32 devices in a mesh: dp: 4 (over x, core), fsdp: 8 (over z, y).
Axes of the slice: x: 2, y: 2, z: 4, core: 2. Of those that a mesh axis runs over, the one named last changes fastest.
Arguments:
- tokens: bfloat16 [8192, 2048], P(('dp', 'fsdp')), may hold values from -16 to 16
- cotangent: bfloat16 [8192, 2048], P(('dp', 'fsdp')), may hold values from -6 to 6
- destination: int32 [8192], P(('dp', 'fsdp')), may hold values from 0 to 8191, as said below
- lengths: int32 [32, 4], P(('dp', 'fsdp')), may hold values from 1 to 128, 256 in all within a row
- norm_gain: bfloat16 [2048], P('fsdp'), may hold values from 0.5 to 1.5
- in_weight: bfloat16 [2048, 8192], P('fsdp'), may hold values from -0.125 to 0.125
- conv_weight: bfloat16 [4, 4096], P(None, 'fsdp'), may hold values from -3 to 3
- conv_bias: bfloat16 [4096], P('fsdp'), may hold values from -3 to 3
- select_weight: bfloat16 [160, 4096], P(None, 'fsdp'), may hold values from -0.09375 to 0.09375
- step_weight: bfloat16 [128, 4096], P(None, 'fsdp'), may hold values from -0.5 to 0.5
- step_bias: bfloat16 [4096], P('fsdp'), may hold values from -6.875 to -2.296875
- decay_log: bfloat16 [16, 4096], P(None, 'fsdp'), may hold values from 0 to 2.765625
- skip_gain: bfloat16 [4096], P('fsdp'), may hold values from 0.5 to 1.5
- out_weight: bfloat16 [4096, 2048], P('fsdp'), may hold values from -0.25 to 0.25
Outputs:
- layer_output: bfloat16 [8192, 2048], P(('dp', 'fsdp'))
- mixer_output: bfloat16 [8192, 2048], P(('dp', 'fsdp'))
- input_grad: bfloat16 [8192, 2048], P(('dp', 'fsdp'))
- input_rms: float32 [], replicated
- grad_norm_gain: float32 [2048], P('fsdp')
- grad_in_weight: float32 [2048, 8192], P('fsdp')
- grad_conv_weight: float32 [4, 4096], P(None, 'fsdp')
- grad_conv_bias: float32 [4096], P('fsdp')
- grad_select_weight: float32 [160, 4096], P(None, 'fsdp')
- grad_step_weight: float32 [128, 4096], P(None, 'fsdp')
- grad_step_bias: float32 [4096], P('fsdp')
- grad_decay_log: float32 [16, 4096], P(None, 'fsdp')
- grad_skip_gain: float32 [4096], P('fsdp')
- grad_out_weight: float32 [4096, 2048], P('fsdp')
The draws below stay inside these ranges and needn't reach their ends.
Inputs may be any that keep to these rules, and one draw needn't show every extreme that they name: `destination`: a permutation of the 8192 row positions; the 256 tokens of each device's block go exactly 8 to each row. `lengths`: the last entry of each row counts padding positions.
All inputs are finite; a program needn't handle non-finite values.
Results may differ from the reference program's by a relative error of at most 0.012.
Values may be sent and summed in bfloat16 or wider, within the bound.
A program may use at most 512 MiB of HBM per device.

```python
import math
import jax
import jax.numpy as jnp
import numpy as np
from jax import lax

D = 2048
DI = 4096
N = 16
R = 128
KC = 4
TOK_DEV = 256
SEGS = 4
ROWS = 32
TOKENS = 8192


def deal_table(key):
    base = jax.random.fold_in(key, 7)
    rows = TOKENS // TOK_DEV
    row_keys = jax.random.split(jax.random.fold_in(base, 1), rows)
    spots = jax.vmap(lambda item: jax.random.permutation(item, TOK_DEV))(row_keys).astype(jnp.int32)
    spots = spots.reshape(rows, rows, TOK_DEV // rows)
    owners = jnp.arange(rows, dtype=jnp.int32)[:, None, None] * TOK_DEV
    target = jnp.transpose(spots + owners, (1, 0, 2)).reshape(rows, TOK_DEV)
    mix_keys = jax.random.split(jax.random.fold_in(base, 2), rows)
    target = jax.vmap(lambda item, values: jax.random.permutation(item, values))(mix_keys, target)
    return target.reshape(TOKENS).astype(jnp.int32)


def draw_destination(key, part):
    return deal_table(key)


def draw_tokens(key, part):
    rows = TOKENS // TOK_DEV
    owner = deal_table(key) // TOK_DEV
    scale = 1.0 + 2.0 * owner.astype(jnp.float32) / (rows - 1)
    noise_key = jax.random.fold_in(key, 11)
    values = jnp.clip(jax.random.normal(noise_key, (TOKENS, D)), -5.0, 5.0)
    return (values * scale[:, None]).astype(jnp.bfloat16)


def level_of(key, dims, cuts, low, top_value):
    loudness = 1.0
    for position, shards_of in cuts:
        draws = jax.random.uniform(jax.random.fold_in(jax.random.fold_in(key, 6), position), (shards_of,), jnp.float32, low / len(cuts), top_value / len(cuts))
        loudness = loudness * jnp.repeat(jnp.exp(draws), dims[position] // shards_of).reshape((-1,) + (1,) * (len(dims) - 1 - position))
    return loudness


def split_up(number_of, total, limit, lean):
    weights = [(1 << 20) // math.isqrt(rank ** lean) + 1 for rank in range(2, number_of + 1)]
    rest, counts = total - limit - (number_of - 1), [1] * (number_of - 1)
    while rest > 0:
        candidates = [i for i in range(number_of - 1) if counts[i] < limit]
        pool, left = sum([weights[i] for i in candidates]), rest
        for i in candidates:
            addition = min(limit - counts[i], max(1, left * weights[i] // pool), rest)
            counts[i] = counts[i] + addition
            rest = rest - addition
    return np.array([limit] + counts)


def uneven_parts(key, count, total, limit, lean):
    if count == 2:
        one = jax.random.randint(key, (), max(1, total - limit), min(limit, total - 1) + 1)
        return jnp.stack([one, total - one])
    sizes = jnp.asarray(split_up(count, total, limit, lean), jnp.int32)
    twos = (count - 1) // 2
    giver, sink = sizes[1:1 + 2 * twos:2], sizes[2:2 + 2 * twos:2]
    slack = jnp.minimum(giver - 1, limit - sink)
    passed = jax.random.randint(jax.random.fold_in(key, 1), (twos,), 0, 1 << 20) % (slack + 1)
    sizes = sizes.at[1:1 + 2 * twos:2].set(giver - passed).at[2:2 + 2 * twos:2].set(sink + passed)
    return sizes[jax.random.permutation(jax.random.fold_in(key, 2), count)]


def noise(stream_key, shape, width, most, pieces=(), kind=jnp.bfloat16):
    factor_of = level_of(stream_key, shape, pieces, -0.22, 0.18) if pieces else 1.0
    result = jax.random.normal(stream_key, shape, jnp.float32) * width * factor_of
    return jnp.minimum(jnp.maximum(result, -most), most).astype(kind)


def setup_inputs(seed: int = 0) -> dict:
    key_of = jax.random.split(jax.random.key(seed), 15)
    tokens = draw_tokens(jax.random.fold_in(key_of[14], 71), 0)
    cotangent = noise(key_of[1], (TOKENS, D), 1.0, 6.0, ((0, 32),))
    destination = draw_destination(jax.random.fold_in(key_of[14], 71), 0)
    lengths = jax.vmap(lambda own: uneven_parts(own, SEGS, TOK_DEV, TOK_DEV // 2, 2))(jax.random.split(key_of[3], ROWS)).reshape((ROWS, SEGS)).astype(jnp.int32)
    norm_gain = jnp.clip(1.0 + 0.1 * jax.random.normal(key_of[4], (D,), jnp.float32), 0.5, 1.5).astype(jnp.bfloat16)
    in_weight = noise(key_of[5], (D, 2 * DI), D ** -0.5, 0.125, ((0, 8),))
    conv_weight = noise(key_of[6], (KC, DI), KC ** -0.5, 3.0, ((1, 8),))
    conv_bias = noise(key_of[7], (DI,), 0.5, 3.0, ((0, 8),))
    select_weight = noise(key_of[8], (R + 2 * N, DI), DI ** -0.5, 0.09375, ((1, 8),))
    step_weight = noise(key_of[9], (R, DI), R ** -0.5, 0.5, ((1, 8),))
    step_bias = jnp.clip(-6.875 + 4.578125 * jax.random.uniform(key_of[10], (DI,), jnp.float32) ** level_of(key_of[10], (DI,), ((0, 8),), -0.2, 0.2), -6.875, -2.296875).astype(jnp.bfloat16)
    decay_log = jnp.clip(2.765625 * jax.random.uniform(key_of[11], (N, DI), jnp.float32) ** level_of(key_of[11], (N, DI), ((1, 8),), -0.2, 0.2), 0.0, 2.765625).astype(jnp.bfloat16)
    skip_gain = jnp.clip(0.5 + 1.0 * jax.random.uniform(key_of[12], (DI,), jnp.float32) ** level_of(key_of[12], (DI,), ((0, 8),), -0.2, 0.2), 0.5, 1.5).astype(jnp.bfloat16)
    out_weight = noise(key_of[13], (DI, D), (DI // 8) ** -0.5, 0.25, ((0, 8),))
    return {"tokens": tokens, "cotangent": cotangent, "destination": destination, "lengths": lengths, "norm_gain": norm_gain, "in_weight": in_weight, "conv_weight": conv_weight, "conv_bias": conv_bias, "select_weight": select_weight, "step_weight": step_weight, "step_bias": step_bias, "decay_log": decay_log, "skip_gain": skip_gain, "out_weight": out_weight}


eps = 1e-05
highest = lax.Precision.HIGHEST

@jax.custom_vjp
def low(v):
    return lax.optimization_barrier(v.astype(jnp.bfloat16)).astype(jnp.float32)

@jax.custom_vjp
def low_back(v):
    return v

def low_keep(v):
    return (low(v), None)

def low_pass(kept, grad):
    return (grad,)

def back_keep(v):
    return (v, None)

def back_low(kept, grad):
    return (low(grad),)
low.defvjp(low_keep, low_pass)
low_back.defvjp(back_keep, back_low)

def matmul(left, right):
    return jnp.dot(left, right, precision=highest, preferred_element_type=jnp.float32)

def delayed(values, lag, fill):
    if lag == 0:
        return values
    front = jnp.full((lag,) + values.shape[1:], fill, values.dtype)
    return jnp.concatenate([front, values[:-lag]], axis=0)

def selective_scan(delta, bmat, cmat, signal, keep, rate):
    block_len = 64
    count = delta.shape[0] // block_len

    def token_step(state, item):
        step_row, write_row, read_row, signal_row, keep_row = item
        decay = jnp.exp(step_row[None, :] * rate) * keep_row
        state = decay * state + write_row[:, None] * (step_row * signal_row)[None, :]
        return (state, lax.optimization_barrier(jnp.sum(read_row[:, None] * state, axis=0)))

    def block_step(state, items):
        return lax.scan(token_step, state, items)
    items = tuple((value.reshape((count, block_len) + value.shape[1:]) for value in (delta, bmat, cmat, signal, keep)))
    first_state = jnp.zeros(rate.shape, jnp.float32)
    _, outputs = lax.scan(jax.checkpoint(block_step), first_state, items)
    return outputs.reshape(delta.shape)

def mixer_block(weights, x_rows, segment, keep):
    norm_gain, in_weight, conv_weight, conv_bias, select_weight, step_weight, step_bias, decay_log, skip_gain, out_weight = weights
    rstd = lax.rsqrt(lax.optimization_barrier(jnp.mean(x_rows * x_rows, axis=1, keepdims=True)) + eps)
    normed = low(x_rows * rstd * norm_gain[None, :])
    proj = low_back(matmul(normed, in_weight))
    x_in = proj[:, :DI]
    gate = proj[:, DI:]
    conv = jnp.zeros_like(x_in) + conv_bias[None, :]
    for lag in range(KC):
        same = (delayed(segment, lag, -1) == segment).astype(jnp.float32)
        conv = conv + conv_weight[KC - 1 - lag][None, :] * delayed(x_in, lag, 0.0) * same[:, None]
    act = low(jax.nn.silu(conv))
    dbl = low_back(matmul(act, select_weight.T))
    step_low = low(dbl[:, :R])
    bmat = dbl[:, R:R + N]
    cmat = dbl[:, R + N:]
    pre = low_back(matmul(step_low, step_weight) + step_bias[None, :])
    delta = jax.nn.softplus(pre)
    rate = -jnp.exp(decay_log)
    scan_out = selective_scan(delta, bmat, cmat, act, keep, rate) + skip_gain[None, :] * act
    gated = low(scan_out * jax.nn.silu(gate))
    mixed = matmul(gated, out_weight)
    return (x_rows + mixed, mixed)

def reference(tokens, cotangent, destination, lengths, norm_gain, in_weight, conv_weight, conv_bias, select_weight, step_weight, step_bias, decay_log, skip_gain, out_weight):
    rows = TOKENS // TOK_DEV
    x_rows = jnp.zeros((TOKENS, D), jnp.float32).at[destination].set(tokens.astype(jnp.float32))
    dy_rows = jnp.zeros((TOKENS, D), jnp.float32).at[destination].set(cotangent.astype(jnp.float32))
    ends = jnp.cumsum(lengths, axis=1).astype(jnp.int32)
    begins = ends - lengths
    positions = jnp.arange(TOK_DEV, dtype=jnp.int32)
    starts = jnp.any(positions[None, :, None] == begins[:, None, :], axis=2)
    segment = lax.optimization_barrier(jnp.sum((positions[None, :, None] >= ends[:, None, :]).astype(jnp.int32), axis=2))
    segment = (segment + SEGS * jnp.arange(rows, dtype=jnp.int32)[:, None]).reshape(TOKENS).astype(jnp.int32)
    keep = (1.0 - starts.astype(jnp.float32)).reshape(TOKENS)
    valid = (positions[None, :] < ends[:, SEGS - 2:SEGS - 1]).astype(jnp.float32).reshape(TOKENS)
    group = 1
    while group * 2 <= max(1, 4096 // TOK_DEV) and rows % (group * 2) == 0:
        group = group * 2
    span = group * TOK_DEV
    count = rows // group
    weights = tuple((value.astype(jnp.float32) for value in (norm_gain, in_weight, conv_weight, conv_bias, select_weight, step_weight, step_bias, decay_log, skip_gain, out_weight)))

    def forward(weights, x_rows):

        def one_group(items):
            x_part, seg_part, keep_part = items
            return mixer_block(weights, x_part, seg_part, keep_part)
        items = (x_rows.reshape(count, span, D), segment.reshape(count, span), keep.reshape(count, span))
        layer, mixed = lax.map(jax.checkpoint(one_group), items)
        return (layer.reshape(TOKENS, D), mixed.reshape(TOKENS, D))
    (layer, mixed), pull = jax.vjp(forward, weights, x_rows)
    grads, grad_rows = pull((dy_rows, jnp.zeros_like(mixed)))
    layer_output = layer[destination].astype(jnp.bfloat16)
    mixer_output = mixed[destination].astype(jnp.bfloat16)
    input_grad = grad_rows[destination].astype(jnp.bfloat16)
    input_rms = jnp.sqrt(jnp.sum(valid * lax.optimization_barrier(jnp.sum(x_rows * x_rows, axis=1))) / (jnp.sum(valid) * D))
    return (layer_output, mixer_output, input_grad, input_rms, grads[0], grads[1], grads[2], grads[3], grads[4], grads[5], grads[6], grads[7], grads[8], grads[9])
```

```python
import functools
import math

import jax
import jax.numpy as jnp
from jax import lax
from jax.experimental import pallas as pl
from jax.experimental.pallas import tpu as pltpu
from jax.sharding import PartitionSpec as P

EPS = 1e-05
TB = 16
LOG2E = math.log2(math.e)
RESET = 1.0e4
BF16 = jnp.bfloat16
F32 = jnp.float32


def silu_slope(value):
    sigma = jax.nn.sigmoid(value)
    return sigma * (1.0 + value * (1.0 - sigma))


def fwd_kernel(chunks, lanes, delta_ref, act_ref, big_ref, bt_ref, cw_ref, rate_ref, skip_ref,
               y_ref, s_ref, carry, d_s, u_s, sc):
    n, ch = rate_ref.shape

    @pl.when(pl.program_id(1) == 0)
    def _():
        carry[...] = jnp.zeros_like(carry)

    def chunk(i, _):
        base = pl.multiple_of(i * TB, TB)
        dl = delta_ref[pl.ds(base, TB), :]
        ac = act_ref[pl.ds(base, TB), :].astype(F32)
        d_s[...] = dl + big_ref[pl.ds(base, TB), :]
        u_s[...] = dl * ac
        bt = bt_ref[i]
        for lo in range(0, ch, lanes):
            cs = pl.ds(lo, lanes)
            rate = rate_ref[:, cs]
            s = carry[:, cs]
            for t in range(TB):
                dec = jnp.exp2(d_s[t : t + 1, cs] * rate)
                s = dec * s + bt[:, t : t + 1] * u_s[t : t + 1, cs]
                sc[t * n : (t + 1) * n, cs] = s.astype(BF16)
            carry[:, cs] = s
        states = sc[...]
        y = jnp.dot(cw_ref[i], states, preferred_element_type=F32)
        y_ref[pl.ds(base, TB), :] = y + skip_ref[...] * ac
        s_ref[pl.ds(pl.multiple_of(base * n, TB * n), TB * n), :] = states
        return 0

    lax.fori_loop(0, chunks, chunk, 0)


def block_coef(m):
    t, n = m.shape
    eye = jnp.eye(TB, dtype=m.dtype)
    spread = m.reshape(t // TB, TB, 1, n) * eye[None, :, :, None]
    return spread.reshape(t // TB, TB, TB * n).astype(BF16)


def turned(m):
    t, n = m.shape
    return m.reshape(t // TB, TB, n).transpose(0, 2, 1)


def scan_forward(delta, act, big, bmat, cmat, rate2, skip, row_len, tblk=64, lanes=512):
    t, ch = delta.shape
    n = bmat.shape[1]
    nb = row_len // tblk
    k = tblk // TB
    at = lambda r, j: (r * nb + j, 0)
    at3 = lambda r, j: (r * nb + j, 0, 0)
    zero = lambda r, j: (0, 0)
    return pl.pallas_call(
        functools.partial(fwd_kernel, k, min(lanes, ch)),
        grid=(t // row_len, nb),
        in_specs=[
            pl.BlockSpec((tblk, ch), at),
            pl.BlockSpec((tblk, ch), at),
            pl.BlockSpec((tblk, 1), at),
            pl.BlockSpec((k, n, TB), at3),
            pl.BlockSpec((k, TB, TB * n), at3),
            pl.BlockSpec((n, ch), zero),
            pl.BlockSpec((1, ch), zero),
        ],
        out_specs=[pl.BlockSpec((tblk, ch), at), pl.BlockSpec((tblk * n, ch), at)],
        out_shape=[jax.ShapeDtypeStruct((t, ch), F32), jax.ShapeDtypeStruct((t * n, ch), BF16)],
        scratch_shapes=[
            pltpu.VMEM((n, ch), F32),
            pltpu.VMEM((TB, ch), F32),
            pltpu.VMEM((TB, ch), F32),
            pltpu.VMEM((TB * n, ch), BF16),
        ],
        compiler_params=pltpu.CompilerParams(vmem_limit_bytes=24 * 2**20),
        cost_estimate=pl.CostEstimate(flops=t * n * ch * 40, bytes_accessed=t * ch * 44, transcendentals=t * n * ch),
    )(delta, act, big, turned(bmat), block_coef(cmat), rate2, skip)


def bwd_kernel(chunks, lanes, delta_ref, act_ref, big_ref, gy_ref, ct_ref, bw_ref, rate_ref, s_ref, sp_ref,
               dd_ref, da_ref, db_ref, dc_ref, dl_ref, carry, d_s, u_s, g_s, h_s):
    n, ch = rate_ref.shape

    @pl.when(pl.program_id(1) == 0)
    def _():
        carry[...] = jnp.zeros_like(carry)

    @pl.when((pl.program_id(0) == 0) & (pl.program_id(1) == 0))
    def _():
        dl_ref[...] = jnp.zeros_like(dl_ref)

    row = lax.broadcasted_iota(jnp.int32, (TB, TB * n), 0)
    col = lax.broadcasted_iota(jnp.int32, (TB, TB * n), 1)
    ones = jnp.where(row == col // n, 1.0, 0.0).astype(BF16)
    nt = (((1,), (1,)), ((), ()))

    def chunk(back, _):
        i = chunks - 1 - back
        base = pl.multiple_of(i * TB, TB)
        sbase = pl.multiple_of(i * TB * n, TB * n)
        dl = delta_ref[pl.ds(base, TB), :]
        ac = act_ref[pl.ds(base, TB), :].astype(F32)
        d_s[...] = dl + big_ref[pl.ds(base, TB), :]
        u_s[...] = dl * ac
        ct = ct_ref[i]
        before = pl.multiple_of(jnp.maximum(sbase - n, 0), n)
        for lo in range(0, ch, lanes):
            cs = pl.ds(lo, lanes)
            rate = rate_ref[:, cs]
            flow = carry[:, cs]
            acc = dl_ref[:, cs]
            for t in reversed(range(TB)):
                dr = d_s[t : t + 1, cs]
                dec = jnp.exp2(dr * rate)
                g = ct[:, t : t + 1] * gy_ref[pl.ds(base + t, 1), cs] + flow
                flow = dec * g
                if t > 0:
                    prev = s_ref[pl.ds(sbase + (t - 1) * n, n), cs]
                else:
                    prev = jnp.where(i > 0, s_ref[pl.ds(before, n), cs], sp_ref[:, cs])
                h = flow * prev.astype(F32)
                acc = acc + h * dr
                g_s[t * n : (t + 1) * n, cs] = g.astype(BF16)
                h_s[t * n : (t + 1) * n, cs] = (h * rate).astype(BF16)
            carry[:, cs] = flow
            dl_ref[:, cs] = acc
        gb = g_s[...]
        du = jnp.dot(bw_ref[i], gb, preferred_element_type=F32)
        hr = jnp.dot(ones, h_s[...], preferred_element_type=F32)
        dd_ref[pl.ds(base, TB), :] = hr * (1.0 / LOG2E) + du * ac
        da_ref[pl.ds(base, TB), :] = du * dl
        db_ref[pl.ds(sbase, TB * n), :] = lax.dot_general(
            gb, u_s[...].astype(BF16), nt, preferred_element_type=F32
        )
        dc_ref[pl.ds(sbase, TB * n), :] = lax.dot_general(
            s_ref[pl.ds(sbase, TB * n), :], gy_ref[pl.ds(base, TB), :].astype(BF16), nt, preferred_element_type=F32
        )
        return 0

    lax.fori_loop(0, chunks, chunk, 0)


def scan_backward(delta, act, big, gy, bmat, cmat, rate2, states, row_len, tblk=64, lanes=512):
    t, ch = delta.shape
    n = bmat.shape[1]
    nb = row_len // tblk
    k = tblk // TB
    at = lambda r, j: (r * nb + nb - 1 - j, 0)
    at3 = lambda r, j: (r * nb + nb - 1 - j, 0, 0)
    zero = lambda r, j: (0, 0)
    entry = lambda r, j: (jnp.maximum((r * nb + nb - 1 - j) * tblk - 1, 0), 0)
    dd, da, db, dc, dl = pl.pallas_call(
        functools.partial(bwd_kernel, k, min(lanes, ch)),
        grid=(t // row_len, nb),
        in_specs=[
            pl.BlockSpec((tblk, ch), at),
            pl.BlockSpec((tblk, ch), at),
            pl.BlockSpec((tblk, 1), at),
            pl.BlockSpec((tblk, ch), at),
            pl.BlockSpec((k, n, TB), at3),
            pl.BlockSpec((k, TB, TB * n), at3),
            pl.BlockSpec((n, ch), zero),
            pl.BlockSpec((tblk * n, ch), at),
            pl.BlockSpec((n, ch), entry),
        ],
        out_specs=[
            pl.BlockSpec((tblk, ch), at),
            pl.BlockSpec((tblk, ch), at),
            pl.BlockSpec((tblk * n, TB), at),
            pl.BlockSpec((tblk * n, TB), at),
            pl.BlockSpec((n, ch), zero),
        ],
        out_shape=[
            jax.ShapeDtypeStruct((t, ch), F32),
            jax.ShapeDtypeStruct((t, ch), F32),
            jax.ShapeDtypeStruct((t * n, TB), F32),
            jax.ShapeDtypeStruct((t * n, TB), F32),
            jax.ShapeDtypeStruct((n, ch), F32),
        ],
        scratch_shapes=[
            pltpu.VMEM((n, ch), F32),
            pltpu.VMEM((TB, ch), F32),
            pltpu.VMEM((TB, ch), F32),
            pltpu.VMEM((TB * n, ch), BF16),
            pltpu.VMEM((TB * n, ch), BF16),
        ],
        compiler_params=pltpu.CompilerParams(vmem_limit_bytes=32 * 2**20),
        cost_estimate=pl.CostEstimate(flops=t * n * ch * 80, bytes_accessed=t * ch * 60, transcendentals=t * n * ch),
    )(delta, act, big, gy, turned(cmat), block_coef(bmat), rate2, states, states)

    def diagonal(m):
        m = m.reshape(t // TB, TB, n, TB)
        return jnp.sum(m * jnp.eye(TB, dtype=m.dtype)[None, :, None, :], axis=3).reshape(t, n)

    return dd, da, diagonal(db), diagonal(dc), dl


def ring_order(count):
    half = count // 2
    if count % 2:
        return list(range(count))
    return [2 * p if p < half else 2 * (count - 1 - p) + 1 for p in range(count)]


def ring_step(value, count, by):
    order = ring_order(count)
    pairs = [(order[p], order[(p + by) % count]) for p in range(count)]
    return lax.ppermute(value, "fsdp", pairs)


def ring_gather(block, count, down):
    blocks = [None] * count
    blocks[0] = block
    here = block
    for hop in range(1, down + 1):
        here = ring_step(here, count, -1)
        blocks[hop] = here
    here = block
    for hop in range(1, count - down):
        here = ring_step(here, count, 1)
        blocks[count - hop] = here
    return blocks


def ring_reduce(part, count, down, dtype):
    total = part(0).astype(F32)
    if down:
        moving = part(count - down).astype(dtype)
        for hop in range(down):
            moving = ring_step(moving, count, -1)
            if hop < down - 1:
                moving = (moving.astype(F32) + part(count - down + hop + 1).astype(F32)).astype(dtype)
        total = total + moving.astype(F32)
    up = count - 1 - down
    if up:
        moving = part(up).astype(dtype)
        for hop in range(up):
            moving = ring_step(moving, count, 1)
            if hop < up - 1:
                moving = (moving.astype(F32) + part(up - hop - 1).astype(F32)).astype(dtype)
        total = total + moving.astype(F32)
    return total


def swap(value, count, mask):
    return lax.ppermute(value, "dp", [(i, i ^ mask) for i in range(count)])


def masks_of(count):
    return [1 << b for b in range(count.bit_length() - 1)]


def group_gather(block, count):
    blocks = {0: block}
    for mask in reversed(masks_of(count)):
        keys = sorted(blocks)
        got = swap(jnp.stack([blocks[m] for m in keys]), count, mask)
        for place, m in enumerate(keys):
            blocks[m | mask] = got[place]
    return [blocks[m] for m in range(count)]


def group_reduce(blocks, count, dtype):
    held = {m: b for m, b in enumerate(blocks)}
    for mask in masks_of(count):
        keep = [m for m in sorted(held) if not m & mask]
        got = swap(jnp.stack([held[m | mask].astype(dtype) for m in keep]), count, mask)
        held = {m: held[m].astype(F32) + got[place].astype(F32) for place, m in enumerate(keep)}
    return held[0]


def group_sum(blocks, count):
    held = {m: b for m, b in enumerate(blocks)}
    masks = masks_of(count)
    keep = [m for m in sorted(held) if not m & 1]
    got = swap(jnp.stack([held[m | 1] for m in keep]), count, 1)
    held = {m: held[m] + got[place] for place, m in enumerate(keep)}
    for mask in masks[1:]:
        keys = sorted(held)
        got = swap(jnp.stack([held[m] for m in keys]), count, mask)
        held = {m: held[m] + got[keys.index(m ^ mask)] for m in keys}
    keys = sorted(held)
    got = swap(jnp.stack([held[m] for m in keys]), count, 1)
    for place, m in enumerate(keys):
        held[m | 1] = got[place]
    return [held[m] for m in range(count)]


def per_device(
    tokens,
    cotangent,
    destination,
    lengths,
    norm_gain,
    in_weight,
    conv_weight,
    conv_bias,
    select_weight,
    step_weight,
    step_bias,
    decay_log,
    skip_gain,
    out_weight,
):
    n_dp = lax.axis_size("dp")
    n_f = lax.axis_size("fsdp")
    rows = n_dp * n_f
    tok = tokens.shape[0]
    width = tokens.shape[1]
    pair = tok // rows
    inner = conv_bias.shape[0] * n_f
    cs = conv_bias.shape[0] // n_dp
    ch = cs * n_f
    taps = conv_weight.shape[0]
    n = decay_log.shape[0]
    rank_of = step_weight.shape[0]
    dcols = width // n_f
    group = n_dp * tok
    both = ("dp", "fsdp")
    me_d = lax.axis_index("dp")
    me_f = lax.axis_index("fsdp")
    order = ring_order(n_f)
    place_of = jnp.asarray([order.index(f) for f in range(n_f)], jnp.int32)
    order_arr = jnp.asarray(order, jnp.int32)
    q = place_of[me_f]
    at_ring = [order_arr[(q + k) % n_f] for k in range(n_f)]
    flat_dot = lambda a, b: jnp.dot(a, b, preferred_element_type=F32)
    nt_dot = lambda a, b: lax.dot_general(a, b, (((1,), (1,)), ((), ())), preferred_element_type=F32)
    tn_dot = lambda a, b: lax.dot_general(a, b, (((0,), (0,)), ((), ())), preferred_element_type=F32)

    rank = jnp.sum((destination[None, :] < destination[:, None]).astype(jnp.int32), axis=1)
    slots = jnp.arange(tok, dtype=jnp.int32)
    to_send = (rank[None, :] == slots[:, None]).astype(BF16)
    from_send = (rank[:, None] == slots[None, :]).astype(BF16)
    spot = jnp.sum(
        jnp.where(rank[None, :] == slots[:, None], (destination % tok)[None, :], 0), axis=1
    )
    tag = jnp.broadcast_to(spot[:, None], (tok, 128)).astype(BF16)
    payload = jnp.concatenate([flat_dot(to_send, tokens).astype(BF16), tag], axis=1)
    got_x = lax.all_to_all(payload.reshape(rows, pair, width + 128), both, 0, 0, tiled=True)
    got_x = got_x.reshape(tok, width + 128)
    got_dy = lax.all_to_all(
        flat_dot(to_send, cotangent).astype(BF16).reshape(rows, pair, width), both, 0, 0, tiled=True
    ).reshape(tok, width)
    got_spot = got_x[:, width].astype(jnp.int32)
    to_row = (got_spot[None, :] == slots[:, None]).astype(BF16)
    from_row = (got_spot[:, None] == slots[None, :]).astype(BF16)
    x_own = flat_dot(to_row, got_x[:, :width]).astype(BF16)
    dy_own = flat_dot(to_row, got_dy).astype(BF16)

    def ring_columns(value):
        return jnp.concatenate(
            [lax.dynamic_slice_in_dim(value, at_ring[k] * dcols, dcols, 1) for k in range(n_f)], axis=1
        )

    def plain_columns(value):
        return jnp.concatenate(
            [lax.dynamic_slice_in_dim(value, ((place_of[f] - q) % n_f) * dcols, dcols, 1) for f in range(n_f)],
            axis=1,
        )

    x_all = jnp.concatenate(group_gather(ring_columns(x_own), n_dp), axis=0)
    dy_all = jnp.concatenate(group_gather(dy_own, n_dp), axis=0)

    lens = group_gather(jnp.broadcast_to(lengths, (8, lengths.shape[1])), n_dp)
    positions = jnp.arange(tok, dtype=jnp.int32)
    starts, segments = [], []
    for m in range(n_dp):
        total = jnp.int32(0)
        start = jnp.zeros((tok,), jnp.bool_)
        segment = jnp.zeros((tok,), jnp.int32)
        for s in range(lengths.shape[1]):
            start = start | (positions == total)
            total = total + lens[m][0, s]
            segment = segment + (positions >= total).astype(jnp.int32)
            if m == 0 and s == lengths.shape[1] - 2:
                valid = (positions < total).astype(F32)
        starts.append(start)
        segments.append(segment + m * (lengths.shape[1] + 1))
    big = jnp.where(jnp.concatenate(starts), RESET, 0.0).astype(F32)[:, None]
    segment = jnp.concatenate(segments)
    x_own32 = x_own.astype(F32)
    square = jnp.sum(x_own32 * x_own32, axis=1)
    totals = lax.psum(jnp.stack([jnp.sum(square * valid), jnp.sum(valid)]), both)
    input_rms = jnp.sqrt(totals[0] / (totals[1] * width))

    def mine(shard):
        return lax.dynamic_slice_in_dim(shard.reshape(-1, n_dp * cs), me_d * cs, cs, 1)

    smalls = [conv_weight, conv_bias, step_bias, skip_gain, decay_log, select_weight, step_weight]
    heights = [math.prod(s.shape) // (n_dp * cs) for s in smalls]
    gain_rows = dcols // cs
    used = sum(heights) + gain_rows
    filler = -used % 16
    small_block = jnp.concatenate(
        [mine(s) for s in smalls] + [norm_gain.reshape(gain_rows, cs), jnp.zeros((filler, cs), BF16)], axis=0
    )

    def my_columns(half):
        return jnp.concatenate(
            [
                lax.dynamic_slice_in_dim(in_weight, half * inner + f * n_dp * cs + me_d * cs, cs, 1)
                for f in range(n_f)
            ],
            axis=1,
        )

    small_ring = ring_gather(small_block, n_f, n_f // 2)
    wx = jnp.concatenate(ring_gather(my_columns(0), n_f, n_f // 2), axis=0)
    wg = jnp.concatenate(ring_gather(my_columns(1), n_f, n_f - 1 - n_f // 2), axis=0)
    wo_ring = ring_gather(lax.dynamic_slice_in_dim(out_weight, me_d * cs, cs, 0), n_f, n_f // 2)
    wo = jnp.zeros((n_f * cs, width), BF16)
    for k in range(n_f):
        wo = lax.dynamic_update_slice_in_dim(wo, wo_ring[k], at_ring[k] * cs, 0)
    small = jnp.zeros((used + filler, ch), BF16)
    for k in range(n_f):
        small = lax.dynamic_update_slice_in_dim(small, small_ring[k], at_ring[k] * cs, 1)
    gain = jnp.concatenate([b[used - gain_rows : used].reshape(dcols) for b in small_ring]).astype(F32)
    pieces, at = [], 0
    for height in heights:
        pieces.append(small[at : at + height])
        at += height
    conv_w, conv_b, step_b, skip, dlog, sel, stepw = pieces
    conv_w = conv_w.astype(F32)
    skip = skip.astype(F32)
    rate = -jnp.exp(dlog.astype(F32))

    x_all32 = x_all.astype(F32)
    rstd = lax.rsqrt(jnp.mean(x_all32 * x_all32, axis=1, keepdims=True) + EPS)
    normed = (x_all32 * rstd * gain[None]).astype(BF16)
    x_in = flat_dot(normed, wx)

    def shifted(values, lag):
        if lag == 0:
            return values
        edge = jnp.zeros((abs(lag),) + values.shape[1:], values.dtype)
        if lag > 0:
            return jnp.concatenate([edge, values[:-lag]], axis=0)
        return jnp.concatenate([values[-lag:], edge], axis=0)

    same = [(shifted(segment + 1, lag) == segment + 1).astype(F32)[:, None] for lag in range(taps)]
    same_next = [(shifted(segment + 1, -lag) == segment + 1).astype(F32)[:, None] for lag in range(taps)]
    conv = conv_b.astype(F32) + sum(
        conv_w[taps - 1 - lag][None] * shifted(x_in, lag) * same[lag] for lag in range(taps)
    )
    act = jax.nn.silu(conv).astype(BF16)
    dbl_part = nt_dot(act, sel)
    split = lambda value: [value[m * tok : (m + 1) * tok] for m in range(n_dp)]
    dbl = jnp.concatenate(group_sum(split(dbl_part), n_dp), axis=0)
    step_low = dbl[:, :rank_of].astype(BF16)
    bmat = dbl[:, rank_of : rank_of + n]
    cmat = dbl[:, rank_of + n :]
    pre = flat_dot(step_low, stepw) + step_b.astype(F32)
    delta = jax.nn.softplus(pre)
    rate2 = rate * LOG2E
    scan_out, states = scan_forward(delta, act, big, bmat, cmat, rate2, skip, tok)
    gate = flat_dot(normed, wg)
    gate_silu = jax.nn.silu(gate)
    gated = (scan_out * gate_silu).astype(BF16)
    mixed_part = flat_dot(gated, wo).astype(BF16)
    mixed = group_reduce(split(mixed_part), n_dp, BF16)

    gated_grad = nt_dot(dy_all, wo)
    scan_grad = gated_grad * gate_silu
    gate_grad = (gated_grad * scan_out * silu_slope(gate)).astype(BF16)
    wg_grad = tn_dot(normed, gate_grad).astype(BF16)
    wo_grad = tn_dot(gated, dy_all).astype(BF16)
    wg_own = ring_reduce(lambda k: wg_grad[k * dcols : (k + 1) * dcols], n_f, n_f // 2, BF16)
    wo_own = ring_reduce(
        lambda k: lax.dynamic_slice_in_dim(wo_grad, at_ring[k] * cs, cs, 0), n_f, n_f - 1 - n_f // 2, BF16
    )
    dd, da, bmat_grad, cmat_grad, decay_sum = scan_backward(
        delta, act, big, scan_grad, bmat, cmat, rate2, states, tok
    )
    pre_grad = (dd * jax.nn.sigmoid(pre)).astype(BF16)
    low_grad = nt_dot(pre_grad, stepw)
    dbl_grad = jnp.concatenate(
        group_sum(split(jnp.concatenate([low_grad, bmat_grad, cmat_grad], axis=1)), n_dp), axis=0
    ).astype(BF16)
    act32 = act.astype(F32)
    act_grad = da + skip * scan_grad + flat_dot(dbl_grad, sel)
    conv_grad = act_grad * silu_slope(conv)
    in_grad = sum(
        conv_w[taps - 1 - lag][None] * shifted(conv_grad, -lag) * same_next[lag] for lag in range(taps)
    ).astype(BF16)
    wx_grad = tn_dot(normed, in_grad).astype(BF16)
    wx_own = ring_reduce(lambda k: wx_grad[k * dcols : (k + 1) * dcols], n_f, n_f // 2, BF16)
    normed_grad_part = (nt_dot(in_grad, wx) + nt_dot(gate_grad, wg)).astype(BF16)
    normed_grad = group_reduce(split(normed_grad_part), n_dp, BF16)

    tap_grads = [
        jnp.sum(conv_grad * shifted(x_in, taps - 1 - tap) * same[taps - 1 - tap], axis=0) for tap in range(taps)
    ]
    small_grads = jnp.concatenate(
        [jnp.stack(tap_grads)]
        + [
            jnp.sum(conv_grad, axis=0, keepdims=True),
            jnp.sum(pre_grad.astype(F32), axis=0, keepdims=True),
            jnp.sum(scan_grad * act32, axis=0, keepdims=True),
            decay_sum * rate,
            tn_dot(dbl_grad, act),
            tn_dot(step_low, pre_grad),
            jnp.zeros((-sum(heights) % 16, ch), F32),
        ],
        axis=0,
    )
    small_own = ring_reduce(
        lambda k: lax.dynamic_slice_in_dim(small_grads, at_ring[k] * cs, cs, 1), n_f, n_f - 1 - n_f // 2, F32
    )

    def in_group_order(blocks):
        stacked = jnp.stack(blocks)
        return [lax.dynamic_index_in_dim(stacked, me_d ^ i, 0, keepdims=False) for i in range(n_dp)]

    def interleaved(blocks):
        parts = in_group_order(blocks)
        return jnp.concatenate(
            [p[:, f * cs : (f + 1) * cs] for f in range(parts[0].shape[1] // cs) for p in parts], axis=1
        )

    gx = interleaved(group_gather(wx_own.astype(BF16), n_dp))
    gg = interleaved(group_gather(wg_own.astype(BF16), n_dp))
    grad_in_weight = jnp.concatenate([gx, gg], axis=1).astype(F32)
    grad_out_weight = jnp.concatenate(in_group_order(group_gather(wo_own.astype(BF16), n_dp)), axis=0).astype(F32)
    small_full = interleaved(group_gather(small_own, n_dp))
    out_small, at = [], 0
    for height, s in zip(heights, smalls):
        out_small.append(small_full[at : at + height].reshape(s.shape))
        at += height
    grad_norm_gain = jnp.sum(grad_in_weight * in_weight.astype(F32), axis=1) / norm_gain.astype(F32)

    hat = x_all32[:tok] * rstd[:tok]
    hat_grad = normed_grad * gain[None]
    change = rstd[:tok] * (hat_grad - hat * jnp.mean(hat_grad * hat, axis=1, keepdims=True))
    row_grad = (dy_own.astype(F32) + plain_columns(change)).astype(BF16)
    layer = (x_own32 + mixed).astype(BF16)

    def returned(value):
        cols = value.shape[1]
        out = flat_dot(from_row, value).astype(BF16).reshape(rows, pair, cols)
        back = lax.all_to_all(out, both, 0, 0, tiled=True).reshape(tok, cols)
        return flat_dot(from_send, back).astype(BF16)

    ahead = returned(jnp.concatenate([layer, mixed.astype(BF16)], axis=1))
    layer_output = ahead[:, :width]
    mixer_output = ahead[:, width:]
    input_grad = returned(row_grad)
    return (
        layer_output,
        mixer_output,
        input_grad,
        input_rms,
        grad_norm_gain,
        grad_in_weight,
        out_small[0],
        out_small[1],
        out_small[5],
        out_small[6],
        out_small[2],
        out_small[4],
        out_small[3],
        grad_out_weight,
    )


def solution(mesh):
    return jax.shard_map(
        per_device,
        mesh=mesh,
        in_specs=(
            P(("dp", "fsdp"), None),
            P(("dp", "fsdp"), None),
            P(("dp", "fsdp")),
            P(("dp", "fsdp"), None),
            P("fsdp"),
            P("fsdp", None),
            P(None, "fsdp"),
            P("fsdp"),
            P(None, "fsdp"),
            P(None, "fsdp"),
            P("fsdp"),
            P(None, "fsdp"),
            P("fsdp"),
            P("fsdp", None),
        ),
        out_specs=(
            P(("dp", "fsdp"), None),
            P(("dp", "fsdp"), None),
            P(("dp", "fsdp"), None),
            P(),
            P("fsdp"),
            P("fsdp", None),
            P(None, "fsdp"),
            P("fsdp"),
            P(None, "fsdp"),
            P(None, "fsdp"),
            P("fsdp"),
            P(None, "fsdp"),
            P("fsdp"),
            P("fsdp", None),
        ),
        check_vma=False,
    )
```

```python
import functools
import math

import jax
import jax.numpy as jnp
from jax import lax
from jax.experimental import pallas as pl
from jax.experimental.pallas import tpu as pltpu
from jax.sharding import PartitionSpec as P

EPS = 1e-05
TB = 16
LOG2E = math.log2(math.e)
RESET = 1.0e4
BF16 = jnp.bfloat16
F32 = jnp.float32


def silu_slope(value):
    sigma = jax.nn.sigmoid(value)
    return sigma * (1.0 + value * (1.0 - sigma))


def fwd_kernel(chunks, lanes, delta_ref, act_ref, big_ref, bt_ref, cw_ref, rate_ref, skip_ref,
               y_ref, s_ref, carry, d_s, u_s, sc):
    n, ch = rate_ref.shape

    @pl.when(pl.program_id(1) == 0)
    def _():
        carry[...] = jnp.zeros_like(carry)

    def chunk(i, _):
        base = pl.multiple_of(i * TB, TB)
        dl = delta_ref[pl.ds(base, TB), :]
        ac = act_ref[pl.ds(base, TB), :].astype(F32)
        d_s[...] = dl + big_ref[pl.ds(base, TB), :]
        u_s[...] = dl * ac
        bt = bt_ref[i]
        for lo in range(0, ch, lanes):
            cs = pl.ds(lo, lanes)
            rate = rate_ref[:, cs]
            s = carry[:, cs]
            for t in range(TB):
                dec = jnp.exp2(d_s[t : t + 1, cs] * rate)
                s = dec * s + bt[:, t : t + 1] * u_s[t : t + 1, cs]
                sc[t * n : (t + 1) * n, cs] = s.astype(BF16)
            carry[:, cs] = s
        states = sc[...]
        y = jnp.dot(cw_ref[i], states, preferred_element_type=F32)
        y_ref[pl.ds(base, TB), :] = y + skip_ref[...] * ac
        s_ref[pl.ds(pl.multiple_of(base * n, TB * n), TB * n), :] = states
        return 0

    lax.fori_loop(0, chunks, chunk, 0)


def block_coef(m):
    t, n = m.shape
    eye = jnp.eye(TB, dtype=m.dtype)
    spread = m.reshape(t // TB, TB, 1, n) * eye[None, :, :, None]
    return spread.reshape(t // TB, TB, TB * n).astype(BF16)


def turned(m):
    t, n = m.shape
    return m.reshape(t // TB, TB, n).transpose(0, 2, 1)


def scan_forward(delta, act, big, bmat, cmat, rate2, skip, row_len, tblk=64, lanes=512):
    t, ch = delta.shape
    n = bmat.shape[1]
    nb = row_len // tblk
    k = tblk // TB
    at = lambda r, j: (r * nb + j, 0)
    at3 = lambda r, j: (r * nb + j, 0, 0)
    zero = lambda r, j: (0, 0)
    return pl.pallas_call(
        functools.partial(fwd_kernel, k, min(lanes, ch)),
        grid=(t // row_len, nb),
        in_specs=[
            pl.BlockSpec((tblk, ch), at),
            pl.BlockSpec((tblk, ch), at),
            pl.BlockSpec((tblk, 1), at),
            pl.BlockSpec((k, n, TB), at3),
            pl.BlockSpec((k, TB, TB * n), at3),
            pl.BlockSpec((n, ch), zero),
            pl.BlockSpec((1, ch), zero),
        ],
        out_specs=[pl.BlockSpec((tblk, ch), at), pl.BlockSpec((tblk * n, ch), at)],
        out_shape=[jax.ShapeDtypeStruct((t, ch), F32), jax.ShapeDtypeStruct((t * n, ch), BF16)],
        scratch_shapes=[
            pltpu.VMEM((n, ch), F32),
            pltpu.VMEM((TB, ch), F32),
            pltpu.VMEM((TB, ch), F32),
            pltpu.VMEM((TB * n, ch), BF16),
        ],
        compiler_params=pltpu.CompilerParams(vmem_limit_bytes=24 * 2**20),
        cost_estimate=pl.CostEstimate(flops=t * n * ch * 40, bytes_accessed=t * ch * 44, transcendentals=t * n * ch),
    )(delta, act, big, turned(bmat), block_coef(cmat), rate2, skip)


def bwd_kernel(chunks, lanes, delta_ref, act_ref, big_ref, gy_ref, ct_ref, bw_ref, rate_ref, s_ref, sp_ref,
               dd_ref, da_ref, db_ref, dc_ref, dl_ref, carry, d_s, u_s, g_s, h_s):
    n, ch = rate_ref.shape

    @pl.when(pl.program_id(1) == 0)
    def _():
        carry[...] = jnp.zeros_like(carry)

    @pl.when((pl.program_id(0) == 0) & (pl.program_id(1) == 0))
    def _():
        dl_ref[...] = jnp.zeros_like(dl_ref)

    row = lax.broadcasted_iota(jnp.int32, (TB, TB * n), 0)
    col = lax.broadcasted_iota(jnp.int32, (TB, TB * n), 1)
    ones = jnp.where(row == col // n, 1.0, 0.0).astype(BF16)
    nt = (((1,), (1,)), ((), ()))

    def chunk(back, _):
        i = chunks - 1 - back
        base = pl.multiple_of(i * TB, TB)
        sbase = pl.multiple_of(i * TB * n, TB * n)
        dl = delta_ref[pl.ds(base, TB), :]
        ac = act_ref[pl.ds(base, TB), :].astype(F32)
        d_s[...] = dl + big_ref[pl.ds(base, TB), :]
        u_s[...] = dl * ac
        ct = ct_ref[i]
        before = pl.multiple_of(jnp.maximum(sbase - n, 0), n)
        for lo in range(0, ch, lanes):
            cs = pl.ds(lo, lanes)
            rate = rate_ref[:, cs]
            flow = carry[:, cs]
            acc = dl_ref[:, cs]
            for t in reversed(range(TB)):
                dr = d_s[t : t + 1, cs]
                dec = jnp.exp2(dr * rate)
                g = ct[:, t : t + 1] * gy_ref[pl.ds(base + t, 1), cs] + flow
                flow = dec * g
                if t > 0:
                    prev = s_ref[pl.ds(sbase + (t - 1) * n, n), cs]
                else:
                    prev = jnp.where(i > 0, s_ref[pl.ds(before, n), cs], sp_ref[:, cs])
                h = flow * prev.astype(F32)
                acc = acc + h * dr
                g_s[t * n : (t + 1) * n, cs] = g.astype(BF16)
                h_s[t * n : (t + 1) * n, cs] = (h * rate).astype(BF16)
            carry[:, cs] = flow
            dl_ref[:, cs] = acc
        gb = g_s[...]
        du = jnp.dot(bw_ref[i], gb, preferred_element_type=F32)
        hr = jnp.dot(ones, h_s[...], preferred_element_type=F32)
        dd_ref[pl.ds(base, TB), :] = hr * (1.0 / LOG2E) + du * ac
        da_ref[pl.ds(base, TB), :] = du * dl
        db_ref[pl.ds(sbase, TB * n), :] = lax.dot_general(
            gb, u_s[...].astype(BF16), nt, preferred_element_type=F32
        )
        dc_ref[pl.ds(sbase, TB * n), :] = lax.dot_general(
            s_ref[pl.ds(sbase, TB * n), :], gy_ref[pl.ds(base, TB), :].astype(BF16), nt, preferred_element_type=F32
        )
        return 0

    lax.fori_loop(0, chunks, chunk, 0)


def scan_backward(delta, act, big, gy, bmat, cmat, rate2, states, row_len, tblk=64, lanes=512):
    t, ch = delta.shape
    n = bmat.shape[1]
    nb = row_len // tblk
    k = tblk // TB
    at = lambda r, j: (r * nb + nb - 1 - j, 0)
    at3 = lambda r, j: (r * nb + nb - 1 - j, 0, 0)
    zero = lambda r, j: (0, 0)
    entry = lambda r, j: (jnp.maximum((r * nb + nb - 1 - j) * tblk - 1, 0), 0)
    dd, da, db, dc, dl = pl.pallas_call(
        functools.partial(bwd_kernel, k, min(lanes, ch)),
        grid=(t // row_len, nb),
        in_specs=[
            pl.BlockSpec((tblk, ch), at),
            pl.BlockSpec((tblk, ch), at),
            pl.BlockSpec((tblk, 1), at),
            pl.BlockSpec((tblk, ch), at),
            pl.BlockSpec((k, n, TB), at3),
            pl.BlockSpec((k, TB, TB * n), at3),
            pl.BlockSpec((n, ch), zero),
            pl.BlockSpec((tblk * n, ch), at),
            pl.BlockSpec((n, ch), entry),
        ],
        out_specs=[
            pl.BlockSpec((tblk, ch), at),
            pl.BlockSpec((tblk, ch), at),
            pl.BlockSpec((tblk * n, TB), at),
            pl.BlockSpec((tblk * n, TB), at),
            pl.BlockSpec((n, ch), zero),
        ],
        out_shape=[
            jax.ShapeDtypeStruct((t, ch), F32),
            jax.ShapeDtypeStruct((t, ch), F32),
            jax.ShapeDtypeStruct((t * n, TB), F32),
            jax.ShapeDtypeStruct((t * n, TB), F32),
            jax.ShapeDtypeStruct((n, ch), F32),
        ],
        scratch_shapes=[
            pltpu.VMEM((n, ch), F32),
            pltpu.VMEM((TB, ch), F32),
            pltpu.VMEM((TB, ch), F32),
            pltpu.VMEM((TB * n, ch), BF16),
            pltpu.VMEM((TB * n, ch), BF16),
        ],
        compiler_params=pltpu.CompilerParams(vmem_limit_bytes=32 * 2**20),
        cost_estimate=pl.CostEstimate(flops=t * n * ch * 80, bytes_accessed=t * ch * 60, transcendentals=t * n * ch),
    )(delta, act, big, gy, turned(cmat), block_coef(bmat), rate2, states, states)

    def diagonal(m):
        m = m.reshape(t // TB, TB, n, TB)
        return jnp.sum(m * jnp.eye(TB, dtype=m.dtype)[None, :, None, :], axis=3).reshape(t, n)

    return dd, da, diagonal(db), diagonal(dc), dl


def ring_order(count):
    half = count // 2
    if count % 2:
        return list(range(count))
    return [2 * p if p < half else 2 * (count - 1 - p) + 1 for p in range(count)]


def ring_step(value, count, by):
    order = ring_order(count)
    pairs = [(order[p], order[(p + by) % count]) for p in range(count)]
    return lax.ppermute(value, "fsdp", pairs)


def ring_reduce(part, count, down, dtype):
    total = part(0).astype(F32)
    if down:
        moving = part(count - down).astype(dtype)
        for hop in range(down):
            moving = ring_step(moving, count, -1)
            if hop < down - 1:
                moving = (moving.astype(F32) + part(count - down + hop + 1).astype(F32)).astype(dtype)
        total = total + moving.astype(F32)
    up = count - 1 - down
    if up:
        moving = part(up).astype(dtype)
        for hop in range(up):
            moving = ring_step(moving, count, 1)
            if hop < up - 1:
                moving = (moving.astype(F32) + part(up - hop - 1).astype(F32)).astype(dtype)
        total = total + moving.astype(F32)
    return total


def swap(value, count, mask):
    return lax.ppermute(value, "dp", [(i, i ^ mask) for i in range(count)])


def masks_of(count):
    return [1 << b for b in range(count.bit_length() - 1)]


def group_gather(block, count):
    blocks = {0: block}
    for mask in reversed(masks_of(count)):
        keys = sorted(blocks)
        got = swap(jnp.stack([blocks[m] for m in keys]), count, mask)
        for place, m in enumerate(keys):
            blocks[m | mask] = got[place]
    return [blocks[m] for m in range(count)]


def group_reduce(blocks, count, dtype):
    held = {m: b for m, b in enumerate(blocks)}
    for mask in masks_of(count):
        keep = [m for m in sorted(held) if not m & mask]
        got = swap(jnp.stack([held[m | mask].astype(dtype) for m in keep]), count, mask)
        held = {m: held[m].astype(F32) + got[place].astype(F32) for place, m in enumerate(keep)}
    return held[0]


def group_sum(blocks, count):
    held = {m: b for m, b in enumerate(blocks)}
    masks = masks_of(count)
    keep = [m for m in sorted(held) if not m & 1]
    got = swap(jnp.stack([held[m | 1] for m in keep]), count, 1)
    held = {m: held[m] + got[place] for place, m in enumerate(keep)}
    for mask in masks[1:]:
        keys = sorted(held)
        got = swap(jnp.stack([held[m] for m in keys]), count, mask)
        held = {m: held[m] + got[keys.index(m ^ mask)] for m in keys}
    keys = sorted(held)
    got = swap(jnp.stack([held[m] for m in keys]), count, 1)
    for place, m in enumerate(keys):
        held[m | 1] = got[place]
    return [held[m] for m in range(count)]


def mesh_at(index, n_f):
    return (index // n_f, lax.rem(index, n_f))


def ring_index(p, n_f):
    if n_f % 2:
        return p
    return jnp.where(p < n_f // 2, 2 * p, 2 * (n_f - 1 - p) + 1)


def ring_place(f, n_f):
    if n_f % 2:
        return f
    return jnp.where(lax.rem(f, 2) == 0, f // 2, n_f - 1 - f // 2)


def gather_kernel(n_dp, n_f, downs, send_ref, *refs):
    streams = len(downs)
    blocks = refs[:streams]
    x_all, dy_all, x_own_ref, dy_own_ref, tag_ref = refs[streams : streams + 5]
    outs = refs[streams + 5 : 2 * streams + 5]
    got, x_own, dy_own, own_sem, deal_sem, loc_sem, pair_send, pair_recv, ring_send, ring_recv = refs[2 * streams + 5 :]
    count = n_dp * n_f
    me_d = lax.axis_index("dp")
    me_f = lax.axis_index("fsdp")
    me = me_d * n_f + me_f
    q = ring_place(me_f, n_f)
    below = ring_index(lax.rem(q + n_f - 1, n_f), n_f)
    above = ring_index(lax.rem(q + 1, n_f), n_f)

    barrier = pltpu.get_barrier_semaphore()

    def greet(p, _):
        pl.semaphore_signal(
            barrier, inc=1, device_id=mesh_at(lax.rem(me + p, count), n_f), device_id_type=pl.DeviceIdType.MESH
        )
        return 0

    lax.fori_loop(1, count, greet, 0)
    own = pltpu.make_async_copy(send_ref.at[0], got.at[0], own_sem)
    own.start()
    locals_ = [
        pltpu.make_async_copy(blocks[s], outs[s].at[me_f], loc_sem.at[s]) for s in range(streams)
    ]
    for c in locals_:
        c.start()
    pl.semaphore_wait(barrier, count - 1)

    def deal(p, _):
        pltpu.make_async_remote_copy(
            src_ref=send_ref.at[p],
            dst_ref=got.at[p],
            send_sem=deal_sem.at[0],
            recv_sem=deal_sem.at[1],
            device_id=mesh_at(lax.rem(me + p, count), n_f),
            device_id_type=pl.DeviceIdType.MESH,
        ).start()
        return 0

    def hop(s, h, up):
        k = lax.rem(q + (n_f - h if up else h), n_f)
        index = ring_index(k, n_f)
        src = blocks[s] if h == 0 else outs[s].at[index]
        return pltpu.make_async_remote_copy(
            src_ref=src,
            dst_ref=outs[s].at[index],
            send_sem=ring_send.at[s, int(up), h],
            recv_sem=ring_recv.at[s, int(up), h],
            device_id=(me_d, above if up else below),
            device_id_type=pl.DeviceIdType.MESH,
        )

    hops = [[downs[s], n_f - 1 - downs[s]] for s in range(streams)]
    for s in range(streams):
        for up in (0, 1):
            if hops[s][up]:
                hop(s, 0, up).start()
        if s == 1:
            lax.fori_loop(1, count, deal, 0)

    def advance(h):
        for s in range(streams):
            for up in (0, 1):
                if h < hops[s][up]:
                    hop(s, h - 1, up).wait_recv()
                    hop(s, h, up).start()

    own.wait()
    rest = got.at[pl.ds(1, count - 1)]
    pltpu.make_async_copy(send_ref.at[pl.ds(1, count - 1)], rest, deal_sem.at[1]).wait()
    tok, width = x_own.shape
    pair2 = got.shape[1]
    total = count * pair2
    tag = got[:, :, width : width + 128].astype(F32).reshape(total, 128)
    reps = tok // 128
    spots = jnp.concatenate([tag] * reps, axis=1)
    lane = lax.broadcasted_iota(jnp.int32, (total, tok), 1).astype(F32)
    row = lax.broadcasted_iota(jnp.int32, (total, tok), 0)
    first = lax.rem(row, pair2) < pair2 // 2
    match = spots == lane
    x_pick = jnp.where(match & first, 1.0, 0.0).astype(BF16)
    dy_pick = jnp.where(match & jnp.logical_not(first), 1.0, 0.0).astype(BF16)
    tn = (((0,), (0,)), ((), ()))
    tag_ref[...] = tag

    def place(pick, out):
        def part(j, _):
            cols = pl.ds(pl.multiple_of(j * 256, 256), 256)
            values = got[:, :, cols].reshape(total, 256)
            out[:, cols] = lax.dot_general(pick, values, tn, preferred_element_type=F32).astype(BF16)
            return 0

        lax.fori_loop(0, width // 256, part, 0)

    masks = list(reversed(masks_of(n_dp)))

    def partner(mask):
        return me_d + mask - 2 * mask * lax.rem(me_d // mask, 2)

    def share(a, m, mask):
        out = (x_all, dy_all)[a]
        own_block = (x_own, dy_own)[a]
        return pltpu.make_async_remote_copy(
            src_ref=own_block if m == 0 else out.at[m],
            dst_ref=out.at[m | mask],
            send_sem=pair_send.at[a, m | mask],
            recv_sem=pair_recv.at[a, m | mask],
            device_id=(partner(mask), me_f),
            device_id_type=pl.DeviceIdType.MESH,
        )

    copies = []

    def keep(a):
        own_block = (x_own, dy_own)[a]
        for j, dst in enumerate(((x_all, dy_all)[a].at[0], (x_own_ref, dy_own_ref)[a])):
            c = pltpu.make_async_copy(own_block, dst, loc_sem.at[streams + 2 * a + j])
            c.start()
            copies.append(c)

    advance(1)
    place(x_pick, x_own)
    for mask in masks:
        share(0, 0, mask).start()
    keep(0)
    place(dy_pick, dy_own)
    for mask in masks:
        share(1, 0, mask).start()
    keep(1)

    def relay(a):
        held = [0]
        for step, mask in enumerate(masks):
            for m in held:
                if m:
                    share(a, m, mask).start()
            for m in held:
                share(a, m, mask).wait_recv()
            held = held + [m | mask for m in held]

    most = max(max(h) for h in hops)
    for h in range(2, most):
        advance(h)
        if h == 2:
            relay(0)
    if most <= 2:
        relay(0)
    relay(1)
    for s in range(streams):
        for up in (0, 1):
            if hops[s][up]:
                hop(s, hops[s][up] - 1, up).wait_recv()
    for s in range(streams):
        for up in (0, 1):
            for h in range(hops[s][up]):
                hop(s, h, up).wait_send()
    for a in (0, 1):
        held = [0]
        for mask in masks:
            for m in held:
                share(a, m, mask).wait_send()
            held = held + [m | mask for m in held]
    for c in locals_ + copies:
        c.wait()
    pltpu.make_async_copy(send_ref.at[pl.ds(1, count - 1)], rest, deal_sem.at[0]).wait()


def gather_all(send, blocks, downs, n_dp, n_f, tok, width):
    streams = len(blocks)
    count, pair2, _ = send.shape
    hops = max(max(d, n_f - 1 - d) for d in downs)
    any_ = pl.BlockSpec(memory_space=pl.ANY)
    row = jax.ShapeDtypeStruct((tok, width), BF16)
    rows = jax.ShapeDtypeStruct((n_dp, tok, width), BF16)
    return pl.pallas_call(
        functools.partial(gather_kernel, n_dp, n_f, downs),
        in_specs=[any_] * (1 + streams),
        out_specs=[any_] * 4 + [pl.BlockSpec(memory_space=pltpu.VMEM)] + [any_] * streams,
        out_shape=[rows, rows, row, row, jax.ShapeDtypeStruct((count * pair2, 128), F32)]
        + [jax.ShapeDtypeStruct((n_f,) + b.shape, b.dtype) for b in blocks],
        scratch_shapes=[
            pltpu.VMEM(send.shape, BF16),
            pltpu.VMEM((tok, width), BF16),
            pltpu.VMEM((tok, width), BF16),
            pltpu.SemaphoreType.DMA,
            pltpu.SemaphoreType.DMA((2,)),
            pltpu.SemaphoreType.DMA((streams + 4,)),
            pltpu.SemaphoreType.DMA((2, n_dp)),
            pltpu.SemaphoreType.DMA((2, n_dp)),
            pltpu.SemaphoreType.DMA((streams, 2, hops)),
            pltpu.SemaphoreType.DMA((streams, 2, hops)),
        ],
        compiler_params=pltpu.CompilerParams(
            collective_id=0, has_side_effects=True, vmem_limit_bytes=32 * 2**20
        ),
        cost_estimate=pl.CostEstimate(flops=10**10, bytes_accessed=2 * 10**8, transcendentals=0),
    )(send, *blocks)


def columns_kernel(starts, cs, w_ref, *outs):
    me_d = lax.axis_index("dp")
    for o, out in enumerate(outs):
        for j, start in enumerate(starts[o]):
            out[:, j * cs : (j + 1) * cs] = w_ref[:, pl.ds(pl.multiple_of(start + me_d * cs, 128), cs)]


def take_columns(w, halves, n_f, n_dp, cs):
    inner = n_f * n_dp * cs
    starts = [[h * inner + f * n_dp * cs for f in range(n_f)] for h in range(halves)]
    me_d = lax.axis_index("dp")
    if cs % 128:
        return [
            jnp.concatenate([lax.dynamic_slice_in_dim(w, s + me_d * cs, cs, 1) for s in group], axis=1)
            for group in starts
        ]
    height = w.shape[0]
    blk = min(height, 64)
    return pl.pallas_call(
        functools.partial(columns_kernel, starts, cs),
        grid=(height // blk,),
        in_specs=[pl.BlockSpec((blk, w.shape[1]), lambda i: (i, 0))],
        out_specs=[pl.BlockSpec((blk, n_f * cs), lambda i: (i, 0))] * halves,
        out_shape=[jax.ShapeDtypeStruct((height, n_f * cs), w.dtype)] * halves,
    )(w)


def spread_kernel(cs, x_ref, w_ref, out_ref, sum_ref):
    me_d = lax.axis_index("dp")
    total = jnp.zeros(sum_ref.shape, F32)
    for i in range(x_ref.shape[0]):
        m = me_d + i - 2 * ((me_d // 2 % 2) * (i // 2 % 2) * 2 + (me_d % 2) * (i % 2))
        part = x_ref[m].astype(F32)
        cols = slice(i * cs, (i + 1) * cs)
        out_ref[:, cols] = part
        product = part * w_ref[:, cols].astype(F32)
        for j in range(0, cs, 128):
            total = total + product[:, j : j + 128]

    @pl.when(pl.program_id(0) == 0)
    def _():
        sum_ref[...] = jnp.zeros_like(sum_ref)

    sum_ref[...] += total


def spread_columns(rel, w, cs):
    n_dp, height, cols = rel.shape
    if cs % 128 or n_dp != 4:
        me_d = lax.axis_index("dp")
        parts = [lax.dynamic_index_in_dim(rel, me_d ^ i, 0, keepdims=False) for i in range(n_dp)]
        out = jnp.concatenate(
            [p[:, f * cs : (f + 1) * cs] for f in range(cols // cs) for p in parts], axis=1
        ).astype(F32)
        return out, jnp.sum(out * w.astype(F32), axis=1)
    out, sums = pl.pallas_call(
        functools.partial(spread_kernel, cs),
        grid=(cols // cs,),
        in_specs=[
            pl.BlockSpec((n_dp, height, cs), lambda f: (0, 0, f)),
            pl.BlockSpec((height, n_dp * cs), lambda f: (0, f)),
        ],
        out_specs=[
            pl.BlockSpec((height, n_dp * cs), lambda f: (0, f)),
            pl.BlockSpec((height, 128), lambda f: (0, 0)),
        ],
        out_shape=[jax.ShapeDtypeStruct((height, n_dp * cols), F32), jax.ShapeDtypeStruct((height, 128), F32)],
        cost_estimate=pl.CostEstimate(flops=4 * height * cols * n_dp, bytes_accessed=8 * height * cols * n_dp, transcendentals=0),
    )(rel, w)
    return out, jnp.sum(sums, axis=1)


def per_device(
    tokens,
    cotangent,
    destination,
    lengths,
    norm_gain,
    in_weight,
    conv_weight,
    conv_bias,
    select_weight,
    step_weight,
    step_bias,
    decay_log,
    skip_gain,
    out_weight,
):
    n_dp = lax.axis_size("dp")
    n_f = lax.axis_size("fsdp")
    rows = n_dp * n_f
    tok = tokens.shape[0]
    width = tokens.shape[1]
    pair = tok // rows
    inner = conv_bias.shape[0] * n_f
    cs = conv_bias.shape[0] // n_dp
    ch = cs * n_f
    taps = conv_weight.shape[0]
    n = decay_log.shape[0]
    rank_of = step_weight.shape[0]
    dcols = width // n_f
    group = n_dp * tok
    both = ("dp", "fsdp")
    me_d = lax.axis_index("dp")
    me_f = lax.axis_index("fsdp")
    order = ring_order(n_f)
    place_of = jnp.asarray([order.index(f) for f in range(n_f)], jnp.int32)
    order_arr = jnp.asarray(order, jnp.int32)
    q = place_of[me_f]
    at_ring = [order_arr[(q + k) % n_f] for k in range(n_f)]
    flat_dot = lambda a, b: jnp.dot(a, b, preferred_element_type=F32)
    nt_dot = lambda a, b: lax.dot_general(a, b, (((1,), (1,)), ((), ())), preferred_element_type=F32)
    tn_dot = lambda a, b: lax.dot_general(a, b, (((0,), (0,)), ((), ())), preferred_element_type=F32)

    me = me_d * n_f + me_f
    row_to = destination // tok
    in_row = destination % tok
    rank = jnp.sum((destination[None, :] < destination[:, None]).astype(jnp.int32), axis=1)
    slots = jnp.arange(tok, dtype=jnp.int32)
    rel_rank = ((row_to - me) % rows) * pair + rank % pair
    to_send = rel_rank[None, :] == slots[:, None]
    from_send = (rank[:, None] == slots[None, :]).astype(BF16)
    spot = jnp.sum(jnp.where(to_send, in_row[None, :], 0), axis=1)
    tag = jnp.broadcast_to(spot[:, None], (tok, 128)).astype(BF16).reshape(rows, pair, 128)
    to_send = to_send.astype(BF16)
    sorted_x = flat_dot(to_send, tokens).astype(BF16).reshape(rows, pair, width)
    sorted_dy = flat_dot(to_send, cotangent).astype(BF16).reshape(rows, pair, width)
    payload = jnp.concatenate(
        [jnp.concatenate([sorted_x, tag], axis=2), jnp.concatenate([sorted_dy, tag], axis=2)], axis=1
    )

    def mine(shard):
        return lax.dynamic_slice_in_dim(shard.reshape(-1, n_dp * cs), me_d * cs, cs, 1)

    smalls = [conv_weight, conv_bias, step_bias, skip_gain, decay_log, select_weight, step_weight]
    heights = [math.prod(s.shape) // (n_dp * cs) for s in smalls]
    gain_rows = dcols // cs
    used = sum(heights) + gain_rows
    filler = -used % 16
    small_block = jnp.concatenate(
        [mine(s) for s in smalls] + [norm_gain.reshape(gain_rows, cs), jnp.zeros((filler, cs), BF16)], axis=0
    )
    wx_block, wg_block = take_columns(in_weight, 2, n_f, n_dp, cs)
    wo_block = lax.dynamic_slice_in_dim(out_weight, me_d * cs, cs, 0)
    x_all, dy_all, x_own, dy_own, tags, small_all, wx, wg, wo = gather_all(
        payload, [small_block, wx_block, wg_block, wo_block], [n_f // 2, n_f // 2, n_f - 1 - n_f // 2, n_f // 2],
        n_dp, n_f, tok, width,
    )
    x_all = x_all.reshape(group, width)
    dy_all = dy_all.reshape(group, width)
    wx = wx.reshape(width, ch)
    wg = wg.reshape(width, ch)
    wo = wo.reshape(ch, width)
    small = small_all.transpose(1, 0, 2).reshape(used + filler, ch)
    gain = small_all[:, used - gain_rows : used].reshape(width).astype(F32)
    tags = tags.reshape(rows, 2 * pair, 128)[:, :pair, 0].astype(jnp.int32)
    tags = tags[(me - jnp.arange(rows, dtype=jnp.int32)) % rows].reshape(tok)
    from_row = (tags[:, None] == slots[None, :]).astype(BF16)

    lens = group_gather(jnp.broadcast_to(lengths, (8, lengths.shape[1])), n_dp)
    positions = jnp.arange(tok, dtype=jnp.int32)
    starts, segments = [], []
    for m in range(n_dp):
        total = jnp.int32(0)
        start = jnp.zeros((tok,), jnp.bool_)
        segment = jnp.zeros((tok,), jnp.int32)
        for s in range(lengths.shape[1]):
            start = start | (positions == total)
            total = total + lens[m][0, s]
            segment = segment + (positions >= total).astype(jnp.int32)
            if m == 0 and s == lengths.shape[1] - 2:
                valid = (positions < total).astype(F32)
        starts.append(start)
        segments.append(segment + m * (lengths.shape[1] + 1))
    big = jnp.where(jnp.concatenate(starts), RESET, 0.0).astype(F32)[:, None]
    segment = jnp.concatenate(segments)
    x_own32 = x_own.astype(F32)
    square = jnp.sum(x_own32 * x_own32, axis=1)
    mine_sums = [jnp.sum(square * valid), jnp.sum(valid)]

    pieces, at = [], 0
    for height in heights:
        pieces.append(small[at : at + height])
        at += height
    conv_w, conv_b, step_b, skip, dlog, sel, stepw = pieces
    conv_w = conv_w.astype(F32)
    skip = skip.astype(F32)
    rate = -jnp.exp(dlog.astype(F32))

    x_all32 = x_all.astype(F32)
    rstd = lax.rsqrt(jnp.mean(x_all32 * x_all32, axis=1, keepdims=True) + EPS)
    normed = (x_all32 * rstd * gain[None]).astype(BF16)
    x_in = flat_dot(normed, wx)

    def shifted(values, lag):
        if lag == 0:
            return values
        edge = jnp.zeros((abs(lag),) + values.shape[1:], values.dtype)
        if lag > 0:
            return jnp.concatenate([edge, values[:-lag]], axis=0)
        return jnp.concatenate([values[-lag:], edge], axis=0)

    same = [(shifted(segment + 1, lag) == segment + 1).astype(F32)[:, None] for lag in range(taps)]
    same_next = [(shifted(segment + 1, -lag) == segment + 1).astype(F32)[:, None] for lag in range(taps)]
    conv = conv_b.astype(F32) + sum(
        conv_w[taps - 1 - lag][None] * shifted(x_in, lag) * same[lag] for lag in range(taps)
    )
    act = jax.nn.silu(conv).astype(BF16)
    dbl_part = nt_dot(act, sel)
    split = lambda value: [value[m * tok : (m + 1) * tok] for m in range(n_dp)]
    dbl = jnp.concatenate(group_sum(split(dbl_part), n_dp), axis=0)
    step_low = dbl[:, :rank_of].astype(BF16)
    bmat = dbl[:, rank_of : rank_of + n]
    cmat = dbl[:, rank_of + n :]
    pre = flat_dot(step_low, stepw) + step_b.astype(F32)
    delta = jax.nn.softplus(pre)
    rate2 = rate * LOG2E
    scan_out, states = scan_forward(delta, act, big, bmat, cmat, rate2, skip, tok)
    gate = flat_dot(normed, wg)
    gate_silu = jax.nn.silu(gate)
    gated = (scan_out * gate_silu).astype(BF16)
    mixed_part = flat_dot(gated, wo).astype(BF16)
    mixed = group_reduce(split(mixed_part), n_dp, BF16)

    gated_grad = nt_dot(dy_all, wo)
    scan_grad = gated_grad * gate_silu
    gate_grad = (gated_grad * scan_out * silu_slope(gate)).astype(BF16)
    wg_grad = tn_dot(normed, gate_grad).astype(BF16)
    wo_grad = tn_dot(gated, dy_all).astype(BF16)
    wg_own = ring_reduce(
        lambda k: lax.dynamic_slice_in_dim(wg_grad, at_ring[k] * dcols, dcols, 0), n_f, n_f // 2, BF16
    )
    wo_own = ring_reduce(
        lambda k: lax.dynamic_slice_in_dim(wo_grad, at_ring[k] * cs, cs, 0), n_f, n_f - 1 - n_f // 2, BF16
    )
    dd, da, bmat_grad, cmat_grad, decay_sum = scan_backward(
        delta, act, big, scan_grad, bmat, cmat, rate2, states, tok
    )
    pre_grad = (dd * jax.nn.sigmoid(pre)).astype(BF16)
    low_grad = nt_dot(pre_grad, stepw)
    dbl_grad = jnp.concatenate(
        group_sum(split(jnp.concatenate([low_grad, bmat_grad, cmat_grad], axis=1)), n_dp), axis=0
    ).astype(BF16)
    act32 = act.astype(F32)
    act_grad = da + skip * scan_grad + flat_dot(dbl_grad, sel)
    conv_grad = act_grad * silu_slope(conv)
    in_grad = sum(
        conv_w[taps - 1 - lag][None] * shifted(conv_grad, -lag) * same_next[lag] for lag in range(taps)
    ).astype(BF16)
    wx_grad = tn_dot(normed, in_grad).astype(BF16)
    wx_own = ring_reduce(
        lambda k: lax.dynamic_slice_in_dim(wx_grad, at_ring[k] * dcols, dcols, 0), n_f, n_f // 2, BF16
    )
    normed_grad_part = (nt_dot(in_grad, wx) + nt_dot(gate_grad, wg)).astype(BF16)
    normed_grad = group_reduce(split(normed_grad_part), n_dp, BF16)

    tap_grads = [
        jnp.sum(conv_grad * shifted(x_in, taps - 1 - tap) * same[taps - 1 - tap], axis=0) for tap in range(taps)
    ]
    small_grads = jnp.concatenate(
        [jnp.stack(tap_grads)]
        + [
            jnp.sum(conv_grad, axis=0, keepdims=True),
            jnp.sum(pre_grad.astype(F32), axis=0, keepdims=True),
            jnp.sum(scan_grad * act32, axis=0, keepdims=True),
            decay_sum * rate,
            tn_dot(dbl_grad, act),
            tn_dot(step_low, pre_grad),
            jnp.zeros((-sum(heights) % 16, ch), F32),
        ],
        axis=0,
    )
    small_own = ring_reduce(
        lambda k: lax.dynamic_slice_in_dim(small_grads, at_ring[k] * cs, cs, 1), n_f, n_f - 1 - n_f // 2, F32
    )

    def in_group_order(blocks):
        stacked = jnp.stack(blocks)
        return [lax.dynamic_index_in_dim(stacked, me_d ^ i, 0, keepdims=False) for i in range(n_dp)]

    def interleaved(blocks):
        return jnp.stack(in_group_order(blocks), axis=1)

    own_in = jnp.concatenate(
        [
            jnp.stack(group_gather(wx_own.astype(BF16), n_dp)),
            jnp.stack(group_gather(wg_own.astype(BF16), n_dp)),
        ],
        axis=2,
    )
    grad_in_weight, gain_sum = spread_columns(own_in, in_weight, cs)
    grad_out_weight = jnp.concatenate(in_group_order(group_gather(wo_own.astype(BF16), n_dp)), axis=0).astype(F32)
    small_full = interleaved(group_gather(small_own, n_dp)).reshape(-1, n_dp * cs)
    out_small, at = [], 0
    for height, s in zip(heights, smalls):
        out_small.append(small_full[at : at + height].reshape(s.shape))
        at += height
    grad_norm_gain = gain_sum / norm_gain.astype(F32)

    hat = x_all32[:tok] * rstd[:tok]
    hat_grad = normed_grad * gain[None]
    change = rstd[:tok] * (hat_grad - hat * jnp.mean(hat_grad * hat, axis=1, keepdims=True))
    row_grad = (dy_own.astype(F32) + change).astype(BF16)
    layer = (x_own32 + mixed).astype(BF16)

    def returned(value):
        cols = value.shape[1]
        out = flat_dot(from_row, value).astype(BF16).reshape(rows, pair, cols)
        back = lax.all_to_all(out, both, 0, 0, tiled=True).reshape(tok, cols)
        return flat_dot(from_send, back).astype(BF16)

    lanes = lax.broadcasted_iota(jnp.int32, (tok, 128), 1)
    ride = jnp.zeros((tok, 128), F32)
    for j, value in enumerate(mine_sums):
        high = value.astype(BF16).astype(F32)
        ride = ride + jnp.where(lanes == 2 * j, high, 0.0) + jnp.where(lanes == 2 * j + 1, value - high, 0.0)
    out = flat_dot(from_row, jnp.concatenate([layer, mixed.astype(BF16)], axis=1)).astype(BF16)
    out = jnp.concatenate([out, ride.astype(BF16)], axis=1).reshape(rows, pair, 2 * width + 128)
    back = lax.all_to_all(out, both, 0, 0, tiled=True).reshape(tok, 2 * width + 128)
    totals = jnp.sum(back.reshape(rows, pair, -1)[:, 0, 2 * width : 2 * width + 4].astype(F32), axis=0)
    input_rms = jnp.sqrt((totals[0] + totals[1]) / ((totals[2] + totals[3]) * width))
    layer_output = flat_dot(from_send, back[:, :width]).astype(BF16)
    mixer_output = flat_dot(from_send, back[:, width : 2 * width]).astype(BF16)
    input_grad = returned(row_grad)
    return (
        layer_output,
        mixer_output,
        input_grad,
        input_rms,
        grad_norm_gain,
        grad_in_weight,
        out_small[0],
        out_small[1],
        out_small[5],
        out_small[6],
        out_small[2],
        out_small[4],
        out_small[3],
        grad_out_weight,
    )


def solution(mesh):
    return jax.shard_map(
        per_device,
        mesh=mesh,
        in_specs=(
            P(("dp", "fsdp"), None),
            P(("dp", "fsdp"), None),
            P(("dp", "fsdp")),
            P(("dp", "fsdp"), None),
            P("fsdp"),
            P("fsdp", None),
            P(None, "fsdp"),
            P("fsdp"),
            P(None, "fsdp"),
            P(None, "fsdp"),
            P("fsdp"),
            P(None, "fsdp"),
            P("fsdp"),
            P("fsdp", None),
        ),
        out_specs=(
            P(("dp", "fsdp"), None),
            P(("dp", "fsdp"), None),
            P(("dp", "fsdp"), None),
            P(),
            P("fsdp"),
            P("fsdp", None),
            P(None, "fsdp"),
            P("fsdp"),
            P(None, "fsdp"),
            P(None, "fsdp"),
            P("fsdp"),
            P(None, "fsdp"),
            P("fsdp"),
            P("fsdp", None),
        ),
        check_vma=False,
    )
```

```python
import functools
import math

import jax
import jax.numpy as jnp
from jax import lax
from jax.experimental import pallas as pl
from jax.experimental.pallas import tpu as pltpu
from jax.sharding import PartitionSpec as P

EPS = 1e-05
TB = 16
LOG2E = math.log2(math.e)
RESET = 1.0e4
BF16 = jnp.bfloat16
F32 = jnp.float32


def silu_slope(value):
    sigma = jax.nn.sigmoid(value)
    return sigma * (1.0 + value * (1.0 - sigma))


def row_at(g, n_dp):
    return lax.rem(2 * g + 1, n_dp + 1)


def flip(d, mask):
    return d + mask - 2 * mask * lax.rem(d // mask, 2)


class GroupSum:
    def __init__(self, part, near, far, total, send, recv):
        self.part, self.near, self.far, self.total = part, near, far, total
        me_d, me_f = lax.axis_index("dp"), lax.axis_index("fsdp")
        plan = [
            (part.at[1], near.at[0], 1),
            (part.at[3], near.at[1], 1),
            (part.at[0], far.at[1], 2),
            (part.at[2], far.at[0], 2),
            (total.at[0], total.at[1], 1),
            (total.at[2], total.at[3], 1),
        ]
        self.copies = [
            pltpu.make_async_remote_copy(
                src_ref=src,
                dst_ref=dst,
                send_sem=send.at[i],
                recv_sem=recv.at[i],
                device_id=(flip(me_d, mask), me_f),
                device_id_type=pl.DeviceIdType.MESH,
            )
            for i, (src, dst, mask) in enumerate(plan)
        ]

    def row_done(self, g):
        for j in (0, 1):

            @pl.when(g == j)
            def _(j=j):
                self.copies[j].start()

            @pl.when(g == j + 2)
            def _(j=j):
                self.copies[j].wait_recv()
                self.part[2 * j] = self.part[2 * j] + self.near[j]
                self.copies[j + 2].start()

    def first(self):
        for j in (0, 1):
            self.copies[j].start()

    def second(self):
        for j in (0, 1):
            self.copies[j].wait_recv()
            self.part[2 * j] = self.part[2 * j] + self.near[j]
            self.copies[j + 2].start()

    def finish(self):
        for j in (0, 1):
            self.copies[3 - j].wait_recv()
            self.total[2 * j] = self.part[2 * j] + self.far[j]
            self.copies[4 + j].start()
        for j in (0, 1):
            self.copies[4 + j].wait_recv()
        for c in self.copies:
            c.wait_send()

    @staticmethod
    def scratch(tok, wide):
        return [
            pltpu.VMEM((4, tok, wide), F32),
            pltpu.VMEM((2, tok, wide), F32),
            pltpu.VMEM((2, tok, wide), F32),
            pltpu.VMEM((4, tok, wide), F32),
            pltpu.SemaphoreType.DMA((6,)),
            pltpu.SemaphoreType.DMA((6,)),
        ]


def greet_neighbours(n_f, ring):
    me_d, me_f = lax.axis_index("dp"), lax.axis_index("fsdp")
    barrier = pltpu.get_barrier_semaphore()
    others = [(flip(me_d, 1), me_f), (flip(me_d, 2), me_f)]
    if ring:
        q = ring_place(me_f, n_f)
        others.append((me_d, ring_index(lax.rem(q + n_f - 1, n_f), n_f)))
        others.append((me_d, ring_index(lax.rem(q + 1, n_f), n_f)))
    for other in others:
        pl.semaphore_signal(barrier, inc=1, device_id=other, device_id_type=pl.DeviceIdType.MESH)
    pl.semaphore_wait(barrier, len(others))


def ring_copy(n_f, src, dst, send, recv, up):
    me_d, me_f = lax.axis_index("dp"), lax.axis_index("fsdp")
    q = ring_place(me_f, n_f)
    to = ring_index(lax.rem(q + (1 if up else n_f - 1), n_f), n_f)
    return pltpu.make_async_remote_copy(
        src_ref=src,
        dst_ref=dst,
        send_sem=send,
        recv_sem=recv,
        device_id=(me_d, to),
        device_id_type=pl.DeviceIdType.MESH,
    )


def segment_span(lens_ref, m, first, rows):
    t = lax.broadcasted_iota(jnp.int32, (rows, 1), 0) + first
    begin = jnp.zeros((rows, 1), jnp.int32)
    end = jnp.zeros((rows, 1), jnp.int32)
    total = jnp.int32(0)
    for j in range(lens_ref.shape[1]):
        after = total + lens_ref[m, j]
        inside = t >= total
        begin = jnp.where(inside, total, begin)
        end = jnp.where(inside, after, end)
        total = after
    return t - begin, end - 1 - t


def enter_kernel(n_f, half, lens_ref, x_ref, gain_ref, wx_ref, wg_ref, taps_ref, bias_ref, sel_ref, wo_ref,
                 normed_ref, xin_ref, conv_ref, act_ref, gate_ref, dbl_ref, next_ref,
                 part, near, far, total, gs_send, gs_recv, hop_send, hop_recv):
    g = pl.program_id(0)
    n_dp, tok = part.shape[:2]
    rows, width = x_ref.shape
    hops = [ring_copy(n_f, wo_ref, next_ref.at[up], hop_send.at[up], hop_recv.at[up], up) for up in (0, 1)]
    group = GroupSum(part, near, far, total, gs_send, gs_recv)
    piece = 256

    @pl.when(g == 0)
    def _():
        greet_neighbours(n_f, True)
        for c in hops:
            c.start()
        part[...] = jnp.zeros_like(part)

        def norm(i, _):
            at = pl.ds(pl.multiple_of(i * 32, 32), 32)
            v = x_ref[at, :].astype(F32)
            rstd = lax.rsqrt(jnp.mean(v * v, axis=1, keepdims=True) + EPS)
            normed_ref[at, :] = (v * rstd * gain_ref[...]).astype(BF16)
            return 0

        lax.fori_loop(0, rows // 32, norm, 0)

    @pl.when(g < half)
    def _():
        n_taps = taps_ref.shape[0]
        for m in range(n_dp):
            at = slice(m * tok, (m + 1) * tok)
            v = jnp.dot(normed_ref[at, :], wx_ref[...], preferred_element_type=F32)
            since, _ = segment_span(lens_ref, m, 0, tok)
            xin_ref[at, :] = v
            conv = bias_ref[...] + taps_ref[n_taps - 1 : n_taps, :] * v
            for lag in range(1, n_taps):
                keep = (since >= lag).astype(F32)
                conv = conv + taps_ref[n_taps - 1 - lag : n_taps - lag, :] * (pltpu.roll(v, lag, 0) * keep)
            conv_ref[at, :] = conv
            act = jax.nn.silu(conv).astype(BF16)
            act_ref[at, :] = act
            part[m] += lax.dot_general(act, sel_ref[...], (((1,), (1,)), ((), ())), preferred_element_type=F32)

    @pl.when(g == half - 1)
    def _():
        group.first()

    @pl.when(g >= half)
    def _():
        for m in range(n_dp):
            at = slice(m * tok, (m + 1) * tok)
            gate_ref[at, :] = jnp.dot(normed_ref[at, :], wg_ref[...], preferred_element_type=F32)

    @pl.when(g == half)
    def _():
        group.second()

    @pl.when(g == 2 * half - 1)
    def _():
        group.finish()
        dbl_ref[...] = total[...]
        for c in hops:
            c.wait()


def enter(lens, x_all, gain, wx, wg, taps, bias, sel, wo_block, n_f):
    n_dp = lens.shape[0]
    rows, width = x_all.shape
    tok = rows // n_dp
    ch = wx.shape[1]
    wide = sel.shape[0]
    piece = 256
    half = ch // piece
    whole = lambda g: (0, 0)
    early = lambda g: (0, jnp.minimum(g, half - 1))
    late = lambda g: (0, jnp.maximum(g - half, 0))
    once = pl.Buffered(1)
    any_ = pl.BlockSpec(memory_space=pl.ANY)
    shaped = lambda d, t: jax.ShapeDtypeStruct((rows, d), t)
    return pl.pallas_call(
        functools.partial(enter_kernel, n_f, half),
        grid=(2 * half,),
        in_specs=[
            pl.BlockSpec(memory_space=pltpu.SMEM),
            pl.BlockSpec((rows, width), whole, pipeline_mode=once),
            pl.BlockSpec((1, width), whole),
            pl.BlockSpec((width, piece), early),
            pl.BlockSpec((width, piece), late),
            pl.BlockSpec((taps.shape[0], piece), early),
            pl.BlockSpec((1, piece), early),
            pl.BlockSpec((wide, piece), early),
            any_,
        ],
        out_specs=[
            pl.BlockSpec((rows, width), whole),
            pl.BlockSpec((rows, piece), early),
            pl.BlockSpec((rows, piece), early),
            pl.BlockSpec((rows, piece), early),
            pl.BlockSpec((rows, piece), late),
            pl.BlockSpec((n_dp, tok, wide), lambda g: (0, 0, 0)),
            any_,
        ],
        out_shape=[
            shaped(width, BF16),
            shaped(ch, F32),
            shaped(ch, F32),
            shaped(ch, BF16),
            shaped(ch, F32),
            jax.ShapeDtypeStruct((n_dp, tok, wide), F32),
            jax.ShapeDtypeStruct((2,) + wo_block.shape, BF16),
        ],
        scratch_shapes=GroupSum.scratch(tok, wide)
        + [pltpu.SemaphoreType.DMA((2,)), pltpu.SemaphoreType.DMA((2,))],
        compiler_params=pltpu.CompilerParams(
            collective_id=1, has_side_effects=True, vmem_limit_bytes=48 * 2**20
        ),
        cost_estimate=pl.CostEstimate(flops=10**10, bytes_accessed=4 * 10**7, transcendentals=10**6),
    )(lens, x_all, gain, wx, wg, taps, bias, sel, wo_block)


def fold_matrix(n):
    i = lax.broadcasted_iota(jnp.int32, (n, TB * n), 0)
    j = lax.broadcasted_iota(jnp.int32, (n, TB * n), 1)
    return jnp.where(lax.rem(j, n) == i, 1.0, 0.0)


def own_token(n):
    i = lax.broadcasted_iota(jnp.int32, (TB, TB * n), 0)
    j = lax.broadcasted_iota(jnp.int32, (TB, TB * n), 1)
    return i == j // n


def block_rows(m, n):
    spread = jnp.dot(m.astype(BF16), fold_matrix(n).astype(BF16), preferred_element_type=F32)
    i = lax.broadcasted_iota(jnp.int32, spread.shape, 0)
    j = lax.broadcasted_iota(jnp.int32, spread.shape, 1)
    return jnp.where(lax.rem(i, TB) == j // n, spread, 0.0).astype(BF16)


def columns_of(m):
    n = m.shape[1]
    i = lax.broadcasted_iota(jnp.int32, (n, n), 0)
    j = lax.broadcasted_iota(jnp.int32, (n, n), 1)
    eye = jnp.where(i == j, 1.0, 0.0)
    return jnp.sum(m[:, None, :] * eye[None], axis=2, keepdims=True)


def softplus(v):
    return jnp.maximum(v, 0.0) + jnp.log1p(jnp.exp(-jnp.abs(v)))


class RingGather:
    def __init__(self, n_f, mine, near, out, local, send, recv):
        q = ring_place(lax.axis_index("fsdp"), n_f)
        at = lambda k: ring_index(lax.rem(q + k, n_f), n_f)
        count = [n_f // 2, n_f - 1 - n_f // 2]
        self.locals = [
            pltpu.make_async_copy(mine, out.at[at(0)], local.at[0]),
            pltpu.make_async_copy(near.at[0], out.at[at(1)], local.at[1]),
            pltpu.make_async_copy(near.at[1], out.at[at(n_f - 1)], local.at[2]),
        ]
        self.hops = [[], []]
        for up in (0, 1):
            for h in range(1, count[up]):
                index = at(n_f - h if up else h)
                src = near.at[up] if h == 1 else out.at[index]
                self.hops[up].append(
                    ring_copy(n_f, src, out.at[index], send.at[up, h], recv.at[up, h], up)
                )
        self.events = max(len(h) for h in self.hops)

    def start(self):
        for c in self.locals:
            c.start()
        for up in (0, 1):
            if self.hops[up]:
                self.hops[up][0].start()

    def event(self, e):
        for up in (0, 1):
            if e < len(self.hops[up]):
                self.hops[up][e - 1].wait_recv()
                self.hops[up][e].start()

    def finish(self):
        for up in (0, 1):
            if self.hops[up]:
                self.hops[up][-1].wait_recv()
            for c in self.hops[up]:
                c.wait_send()
        for c in self.locals:
            c.wait()


def fwd_kernel(lanes, n_f, lens_ref, dbl_ref, act_ref, stepw_ref, stepb_ref, rate_ref, skip_ref, wo_ref, next_ref,
               y_ref, s_ref, delta_ref, pre_ref, wo_all, carry, big_s, cw_s, d_s, u_s, sc, local, hop_send, hop_recv):
    n, ch = rate_ref.shape
    tblk = act_ref.shape[0]
    low_n = stepw_ref.shape[0]
    steps = pl.num_programs(0) * pl.num_programs(1)
    now = pl.program_id(0) * pl.num_programs(1) + pl.program_id(1)
    ring = RingGather(n_f, wo_ref, next_ref, wo_all, local, hop_send, hop_recv)

    @pl.when(now == 0)
    def _():
        greet_neighbours(n_f, True)
        ring.start()

    for e in range(1, ring.events):

        @pl.when(now == min(7 * e, 15))
        def _(e=e):
            ring.event(e)

    @pl.when(pl.program_id(1) == 0)
    def _():
        carry[...] = jnp.zeros_like(carry)

    pre = jnp.dot(dbl_ref[:, :low_n].astype(BF16), stepw_ref[...], preferred_element_type=F32) + stepb_ref[...]
    pre_ref[...] = pre
    delta_ref[...] = softplus(pre)
    since, _ = segment_span(lens_ref, pl.program_id(0), pl.program_id(1) * tblk, tblk)
    big_s[...] = jnp.where(since == 0, RESET, 0.0)
    cw_s[...] = block_rows(dbl_ref[:, low_n + n : low_n + 2 * n], n)

    def chunk(i, _):
        base = pl.multiple_of(i * TB, TB)
        dl = delta_ref[pl.ds(base, TB), :]
        ac = act_ref[pl.ds(base, TB), :].astype(F32)
        d_s[...] = dl + big_s[pl.ds(base, TB), :]
        u_s[...] = dl * ac
        bt = columns_of(dbl_ref[pl.ds(base, TB), low_n : low_n + n])
        for lo in range(0, ch, lanes):
            cs = pl.ds(lo, lanes)
            rate = rate_ref[:, cs]
            s = carry[:, cs]
            for t in range(TB):
                dec = jnp.exp2(d_s[t : t + 1, cs] * rate)
                s = dec * s + bt[t] * u_s[t : t + 1, cs]
                sc[t * n : (t + 1) * n, cs] = s.astype(BF16)
            carry[:, cs] = s
        states = sc[...]
        y = jnp.dot(cw_s[pl.ds(base, TB), :], states, preferred_element_type=F32)
        y_ref[pl.ds(base, TB), :] = y + skip_ref[...] * ac
        s_ref[pl.ds(pl.multiple_of(base * n, TB * n), TB * n), :] = states
        return 0

    lax.fori_loop(0, tblk // TB, chunk, 0)

    @pl.when(now == steps - 1)
    def _():
        ring.finish()


def scan_forward(lens, dbl, act, stepw, stepb, rate2, skip, wo_block, wo_next, n_f, row_len, tblk=64, lanes=512):
    t, ch = act.shape
    n = rate2.shape[0]
    nb = row_len // tblk
    at = lambda r, j: (r * nb + j, 0)
    zero = lambda r, j: (0, 0)
    any_ = pl.BlockSpec(memory_space=pl.ANY)
    wide = jax.ShapeDtypeStruct((t, ch), F32)
    return pl.pallas_call(
        functools.partial(fwd_kernel, min(lanes, ch), n_f),
        grid=(t // row_len, nb),
        in_specs=[
            pl.BlockSpec(memory_space=pltpu.SMEM),
            pl.BlockSpec((tblk, dbl.shape[1]), at),
            pl.BlockSpec((tblk, ch), at),
            pl.BlockSpec(stepw.shape, zero),
            pl.BlockSpec((1, ch), zero),
            pl.BlockSpec((n, ch), zero),
            pl.BlockSpec((1, ch), zero),
            any_,
            any_,
        ],
        out_specs=[
            pl.BlockSpec((tblk, ch), at),
            pl.BlockSpec((tblk * n, ch), at),
            pl.BlockSpec((tblk, ch), at),
            pl.BlockSpec((tblk, ch), at),
            any_,
        ],
        out_shape=[
            wide,
            jax.ShapeDtypeStruct((t * n, ch), BF16),
            wide,
            wide,
            jax.ShapeDtypeStruct((n_f,) + wo_block.shape, BF16),
        ],
        scratch_shapes=[
            pltpu.VMEM((n, ch), F32),
            pltpu.VMEM((tblk, 1), F32),
            pltpu.VMEM((tblk, TB * n), BF16),
            pltpu.VMEM((TB, ch), F32),
            pltpu.VMEM((TB, ch), F32),
            pltpu.VMEM((TB * n, ch), BF16),
            pltpu.SemaphoreType.DMA((3,)),
            pltpu.SemaphoreType.DMA((2, n_f)),
            pltpu.SemaphoreType.DMA((2, n_f)),
        ],
        compiler_params=pltpu.CompilerParams(
            collective_id=2, has_side_effects=True, vmem_limit_bytes=32 * 2**20
        ),
        cost_estimate=pl.CostEstimate(flops=t * n * ch * 40, bytes_accessed=t * ch * 52, transcendentals=t * n * ch),
    )(lens, dbl, act, stepw, stepb, rate2, skip, wo_block, wo_next)


def bwd_kernel(lanes, n_f, lens_ref, dbl_ref, delta_ref, pre_ref, act_ref, gy_ref, stepw_ref, rate_ref, skip_ref,
               s_ref, sp_ref,
               pg_ref, da_ref, dbl_grad_ref, dl_ref, sums_ref, stepg_ref,
               carry, big_s, bw_s, d_s, u_s, g_s, h_s, part, near, far, total, gs_send, gs_recv):
    n, ch = rate_ref.shape
    tblk = act_ref.shape[0]
    low_n = stepw_ref.shape[0]
    r, j = pl.program_id(0), pl.program_id(1)
    n_dp, nb = pl.num_programs(0), pl.num_programs(1)
    m = row_at(r, n_dp)
    group = GroupSum(part, near, far, total, gs_send, gs_recv)

    @pl.when(j == 0)
    def _():
        carry[...] = jnp.zeros_like(carry)

    @pl.when((r == 0) & (j == 0))
    def _():
        greet_neighbours(n_f, False)
        dl_ref[...] = jnp.zeros_like(dl_ref)
        sums_ref[...] = jnp.zeros_like(sums_ref)
        stepg_ref[...] = jnp.zeros_like(stepg_ref)

    ones = jnp.where(own_token(n), 1.0, 0.0).astype(BF16)
    nt = (((1,), (1,)), ((), ()))
    row = lax.broadcasted_iota(jnp.int32, (TB * n, TB), 0)
    col = lax.broadcasted_iota(jnp.int32, (TB * n, TB), 1)
    mask = row // n == col
    row = lax.broadcasted_iota(jnp.int32, (TB * n, n), 0)
    col = lax.broadcasted_iota(jnp.int32, (TB * n, n), 1)
    fold = jnp.where(lax.rem(row, n) == col, 1.0, 0.0)
    since, _ = segment_span(lens_ref, m, (nb - 1 - j) * tblk, tblk)
    big_s[...] = jnp.where(since == 0, RESET, 0.0)
    bw_s[...] = block_rows(dbl_ref[:, low_n : low_n + n], n)

    def diagonal(left, right):
        every = lax.dot_general(left, right, nt, preferred_element_type=F32)
        column = jnp.sum(jnp.where(mask, every, 0.0), axis=1, keepdims=True)
        return jnp.sum((column * fold).reshape(TB, n, n), axis=1)

    def chunk(back, _):
        i = tblk // TB - 1 - back
        base = pl.multiple_of(i * TB, TB)
        sbase = pl.multiple_of(i * TB * n, TB * n)
        dl = delta_ref[pl.ds(base, TB), :]
        ac = act_ref[pl.ds(base, TB), :].astype(F32)
        d_s[...] = dl + big_s[pl.ds(base, TB), :]
        u_s[...] = dl * ac
        ct = columns_of(dbl_ref[pl.ds(base, TB), low_n + n : low_n + 2 * n])
        before = pl.multiple_of(jnp.maximum(sbase - n, 0), n)
        for lo in range(0, ch, lanes):
            cs = pl.ds(lo, lanes)
            rate = rate_ref[:, cs]
            flow = carry[:, cs]
            acc = dl_ref[:, cs]
            for t in reversed(range(TB)):
                dr = d_s[t : t + 1, cs]
                dec = jnp.exp2(dr * rate)
                g = ct[t] * gy_ref[pl.ds(base + t, 1), cs] + flow
                flow = dec * g
                if t > 0:
                    prev = s_ref[pl.ds(sbase + (t - 1) * n, n), cs]
                else:
                    prev = jnp.where(i > 0, s_ref[pl.ds(before, n), cs], sp_ref[:, cs])
                h = flow * prev.astype(F32)
                acc = acc + h * dr
                g_s[t * n : (t + 1) * n, cs] = g.astype(BF16)
                h_s[t * n : (t + 1) * n, cs] = (h * rate).astype(BF16)
            carry[:, cs] = flow
            dl_ref[:, cs] = acc
        gb = g_s[...]
        gy = gy_ref[pl.ds(base, TB), :]
        du = jnp.dot(bw_s[pl.ds(base, TB), :], gb, preferred_element_type=F32)
        hr = jnp.dot(ones, h_s[...], preferred_element_type=F32)
        dd = hr * (1.0 / LOG2E) + du * ac
        pg_ref[pl.ds(base, TB), :] = (dd * jax.nn.sigmoid(pre_ref[pl.ds(base, TB), :])).astype(BF16)
        da_ref[pl.ds(base, TB), :] = du * dl + skip_ref[...] * gy
        at = pl.ds(pl.multiple_of((nb - 1 - j) * tblk + base, TB), TB)
        part[m, at, low_n : low_n + n] = diagonal(gb, u_s[...].astype(BF16))
        part[m, at, low_n + n : low_n + 2 * n] = diagonal(s_ref[pl.ds(sbase, TB * n), :], gy.astype(BF16))
        return 0

    lax.fori_loop(0, tblk // TB, chunk, 0)
    pg = pg_ref[...]
    part[m, pl.ds(pl.multiple_of((nb - 1 - j) * tblk, tblk), tblk), :low_n] = lax.dot_general(
        pg, stepw_ref[...], nt, preferred_element_type=F32
    )
    stepg_ref[...] += lax.dot_general(
        dbl_ref[:, :low_n].astype(BF16), pg, (((0,), (0,)), ((), ())), preferred_element_type=F32
    )
    sums_ref[0:1, :] += jnp.sum(pg.astype(F32), axis=0, keepdims=True)
    sums_ref[1:2, :] += jnp.sum(gy_ref[...] * act_ref[...].astype(F32), axis=0, keepdims=True)

    @pl.when(j == nb - 1)
    def _():
        group.row_done(r)

    @pl.when((j == nb - 1) & (r == n_dp - 1))
    def _():
        group.finish()
        dbl_grad_ref[...] = total[...]


def scan_backward(lens, dbl, delta, pre, act, gy, stepw, rate2, skip, states, n_f, row_len, tblk=64, lanes=512):
    t, ch = delta.shape
    n = rate2.shape[0]
    nb = row_len // tblk
    n_dp = t // row_len
    wide = dbl.shape[1]
    spot = lambda r, j: row_at(r, n_dp) * nb + nb - 1 - j
    at = lambda r, j: (spot(r, j), 0)
    zero = lambda r, j: (0, 0)
    entry = lambda r, j: (jnp.maximum(spot(r, j) * tblk - 1, 0), 0)
    return pl.pallas_call(
        functools.partial(bwd_kernel, min(lanes, ch), n_f),
        grid=(n_dp, nb),
        in_specs=[
            pl.BlockSpec(memory_space=pltpu.SMEM),
            pl.BlockSpec((tblk, wide), at),
            pl.BlockSpec((tblk, ch), at),
            pl.BlockSpec((tblk, ch), at),
            pl.BlockSpec((tblk, ch), at),
            pl.BlockSpec((tblk, ch), at),
            pl.BlockSpec(stepw.shape, zero),
            pl.BlockSpec((n, ch), zero),
            pl.BlockSpec((1, ch), zero),
            pl.BlockSpec((tblk * n, ch), at),
            pl.BlockSpec((n, ch), entry),
        ],
        out_specs=[
            pl.BlockSpec((tblk, ch), at),
            pl.BlockSpec((tblk, ch), at),
            pl.BlockSpec((n_dp, row_len, wide), lambda r, j: (0, 0, 0)),
            pl.BlockSpec((n, ch), zero),
            pl.BlockSpec((8, ch), zero),
            pl.BlockSpec(stepw.shape, zero),
        ],
        out_shape=[
            jax.ShapeDtypeStruct((t, ch), BF16),
            jax.ShapeDtypeStruct((t, ch), F32),
            jax.ShapeDtypeStruct((n_dp, row_len, wide), F32),
            jax.ShapeDtypeStruct((n, ch), F32),
            jax.ShapeDtypeStruct((8, ch), F32),
            jax.ShapeDtypeStruct(stepw.shape, F32),
        ],
        scratch_shapes=[
            pltpu.VMEM((n, ch), F32),
            pltpu.VMEM((tblk, 1), F32),
            pltpu.VMEM((tblk, TB * n), BF16),
            pltpu.VMEM((TB, ch), F32),
            pltpu.VMEM((TB, ch), F32),
            pltpu.VMEM((TB * n, ch), BF16),
            pltpu.VMEM((TB * n, ch), BF16),
        ]
        + GroupSum.scratch(row_len, wide),
        compiler_params=pltpu.CompilerParams(
            collective_id=3, has_side_effects=True, vmem_limit_bytes=40 * 2**20
        ),
        cost_estimate=pl.CostEstimate(flops=t * n * ch * 80, bytes_accessed=t * ch * 60, transcendentals=t * n * ch),
    )(lens, dbl, delta, pre, act, gy, stepw, rate2, skip, states, states)


def ring_order(count):
    half = count // 2
    if count % 2:
        return list(range(count))
    return [2 * p if p < half else 2 * (count - 1 - p) + 1 for p in range(count)]


def ring_step(value, count, by):
    order = ring_order(count)
    pairs = [(order[p], order[(p + by) % count]) for p in range(count)]
    return lax.ppermute(value, "fsdp", pairs)


def ring_reduce(part, count, down, dtype):
    total = part(0).astype(F32)
    if down:
        moving = part(count - down).astype(dtype)
        for hop in range(down):
            moving = ring_step(moving, count, -1)
            if hop < down - 1:
                moving = (moving.astype(F32) + part(count - down + hop + 1).astype(F32)).astype(dtype)
        total = total + moving.astype(F32)
    up = count - 1 - down
    if up:
        moving = part(up).astype(dtype)
        for hop in range(up):
            moving = ring_step(moving, count, 1)
            if hop < up - 1:
                moving = (moving.astype(F32) + part(up - hop - 1).astype(F32)).astype(dtype)
        total = total + moving.astype(F32)
    return total


def swap(value, count, mask):
    return lax.ppermute(value, "dp", [(i, i ^ mask) for i in range(count)])


def masks_of(count):
    return [1 << b for b in range(count.bit_length() - 1)]


def group_gather(block, count):
    blocks = {0: block}
    for mask in reversed(masks_of(count)):
        keys = sorted(blocks)
        got = swap(jnp.stack([blocks[m] for m in keys]), count, mask)
        for place, m in enumerate(keys):
            blocks[m | mask] = got[place]
    return [blocks[m] for m in range(count)]


def group_reduce(blocks, count, dtype):
    held = {m: b for m, b in enumerate(blocks)}
    for mask in masks_of(count):
        keep = [m for m in sorted(held) if not m & mask]
        got = swap(jnp.stack([held[m | mask].astype(dtype) for m in keep]), count, mask)
        held = {m: held[m].astype(F32) + got[place].astype(F32) for place, m in enumerate(keep)}
    return held[0]


def mesh_at(index, n_f):
    return (index // n_f, lax.rem(index, n_f))


def ring_index(p, n_f):
    if n_f % 2:
        return p
    return jnp.where(p < n_f // 2, 2 * p, 2 * (n_f - 1 - p) + 1)


def ring_place(f, n_f):
    if n_f % 2:
        return f
    return jnp.where(lax.rem(f, 2) == 0, f // 2, n_f - 1 - f // 2)


def gather_kernel(n_dp, n_f, downs, x_ref, dy_ref, meta_ref, dest_ref, lens_ref, *refs):
    streams = len(downs)
    blocks = refs[:streams]
    x_all, dy_all, lens_all, x_own_ref, dy_own_ref, tag_ref, rank_ref = refs[streams : streams + 7]
    outs = refs[streams + 7 : 2 * streams + 7]
    send_ref, got, x_own, dy_own, deal_sem, loc_sem, pair_send, pair_recv, ring_send, ring_recv = refs[
        2 * streams + 7 :
    ]
    count = n_dp * n_f
    me_d = lax.axis_index("dp")
    me_f = lax.axis_index("fsdp")
    me = me_d * n_f + me_f
    q = ring_place(me_f, n_f)
    below = ring_index(lax.rem(q + n_f - 1, n_f), n_f)
    above = ring_index(lax.rem(q + 1, n_f), n_f)

    barrier = pltpu.get_barrier_semaphore()

    def greet(p, _):
        pl.semaphore_signal(
            barrier, inc=1, device_id=mesh_at(lax.rem(me + p, count), n_f), device_id_type=pl.DeviceIdType.MESH
        )
        return 0

    lax.fori_loop(1, count, greet, 0)
    locals_ = [
        pltpu.make_async_copy(blocks[s], outs[s].at[me_f], loc_sem.at[s]) for s in range(streams)
    ]
    for c in locals_:
        c.start()
    pl.semaphore_wait(barrier, count - 1)

    def deal(p, _):
        pltpu.make_async_remote_copy(
            src_ref=send_ref.at[p],
            dst_ref=got.at[p],
            send_sem=deal_sem.at[0],
            recv_sem=deal_sem.at[1],
            device_id=mesh_at(lax.rem(me + p, count), n_f),
            device_id_type=pl.DeviceIdType.MESH,
        ).start()
        return 0

    def hop(s, h, up):
        k = lax.rem(q + (n_f - h if up else h), n_f)
        index = ring_index(k, n_f)
        src = blocks[s] if h == 0 else outs[s].at[index]
        return pltpu.make_async_remote_copy(
            src_ref=src,
            dst_ref=outs[s].at[index],
            send_sem=ring_send.at[s, int(up), h],
            recv_sem=ring_recv.at[s, int(up), h],
            device_id=(me_d, above if up else below),
            device_id_type=pl.DeviceIdType.MESH,
        )

    hops = [[downs[s], n_f - 1 - downs[s]] for s in range(streams)]
    for s in range(streams):
        for up in (0, 1):
            if hops[s][up]:
                hop(s, 0, up).start()
    tok, width = x_own.shape
    pair2 = got.shape[1]
    total = count * pair2

    dest_row, rel_row, abs_row, in_row = (meta_ref[i : i + 1, :] for i in range(4))
    rank = jnp.sum((dest_ref[...] < dest_row).astype(F32), axis=0, keepdims=True)
    rank_ref[...] = jnp.broadcast_to(rank, rank_ref.shape)
    half = pair2 // 2
    goal = rel_row * half + rank - abs_row * half
    row = lax.broadcasted_iota(jnp.int32, (total, tok), 0)
    place_in = lax.rem(row, pair2)
    first = place_in < half
    slot = (row // pair2) * half + jnp.where(first, place_in, place_in - half)
    chosen = slot.astype(F32) == goal
    spot = jnp.sum(jnp.where(chosen, in_row, 0.0), axis=1, keepdims=True)
    send_ref[:, :, width:] = jnp.broadcast_to(spot, (total, 128)).astype(BF16).reshape(count, pair2, 128)
    x_pick = jnp.where(chosen & first, 1.0, 0.0).astype(BF16)
    dy_pick = jnp.where(chosen & jnp.logical_not(first), 1.0, 0.0).astype(BF16)

    def sort(j, _):
        cols = pl.ds(pl.multiple_of(j * 256, 256), 256)
        mixed = jnp.dot(x_pick, x_ref[:, cols], preferred_element_type=F32)
        mixed = mixed + jnp.dot(dy_pick, dy_ref[:, cols], preferred_element_type=F32)
        send_ref[:, :, cols] = mixed.astype(BF16).reshape(count, pair2, 256)
        return 0

    lax.fori_loop(0, width // 256, sort, 0)
    lax.fori_loop(1, count, deal, 0)
    got[0] = send_ref[0]

    def advance(h):
        for s in range(streams):
            for up in (0, 1):
                if h < hops[s][up]:
                    hop(s, h - 1, up).wait_recv()
                    hop(s, h, up).start()

    rest = got.at[pl.ds(1, count - 1)]
    pltpu.make_async_copy(send_ref.at[pl.ds(1, count - 1)], rest, deal_sem.at[1]).wait()
    tag = got[:, :, width : width + 128].astype(F32).reshape(total, 128)
    reps = tok // 128
    spots = jnp.concatenate([tag] * reps, axis=1)
    lane = lax.broadcasted_iota(jnp.int32, (total, tok), 1).astype(F32)
    match = spots == lane
    x_pick = jnp.where(match & first, 1.0, 0.0).astype(BF16)
    dy_pick = jnp.where(match & jnp.logical_not(first), 1.0, 0.0).astype(BF16)
    tn = (((0,), (0,)), ((), ()))
    tag_ref[...] = tag

    def place(pick, out):
        def part(j, _):
            cols = pl.ds(pl.multiple_of(j * 256, 256), 256)
            values = got[:, :, cols].reshape(total, 256)
            out[:, cols] = lax.dot_general(pick, values, tn, preferred_element_type=F32).astype(BF16)
            return 0

        lax.fori_loop(0, width // 256, part, 0)

    masks = list(reversed(masks_of(n_dp)))

    def partner(mask):
        return me_d + mask - 2 * mask * lax.rem(me_d // mask, 2)

    def share(a, m, mask):
        out = (x_all, dy_all, lens_all)[a]
        own_block = (x_own, dy_own, lens_ref)[a]
        return pltpu.make_async_remote_copy(
            src_ref=own_block if m == 0 else out.at[m],
            dst_ref=out.at[m | mask],
            send_sem=pair_send.at[a, m | mask],
            recv_sem=pair_recv.at[a, m | mask],
            device_id=(partner(mask), me_f),
            device_id_type=pl.DeviceIdType.MESH,
        )

    copies = []

    def keep(a):
        own_block = (x_own, dy_own, lens_ref)[a]
        dsts = (x_all, dy_all, lens_all)[a].at[0], (x_own_ref, dy_own_ref, None)[a]
        for j, dst in enumerate(dsts[: 1 if a == 2 else 2]):
            c = pltpu.make_async_copy(own_block, dst, loc_sem.at[streams + 2 * a + j])
            c.start()
            copies.append(c)

    for mask in masks:
        share(2, 0, mask).start()
    keep(2)
    advance(1)
    place(x_pick, x_own)
    for mask in masks:
        share(0, 0, mask).start()
    keep(0)
    place(dy_pick, dy_own)
    for mask in masks:
        share(1, 0, mask).start()
    keep(1)

    def relay(a):
        held = [0]
        for step, mask in enumerate(masks):
            for m in held:
                if m:
                    share(a, m, mask).start()
            for m in held:
                share(a, m, mask).wait_recv()
            held = held + [m | mask for m in held]

    most = max(max(h) for h in hops)
    for h in range(2, most):
        advance(h)
        if h == 2:
            relay(0)
    if most <= 2:
        relay(0)
    relay(1)
    relay(2)
    for s in range(streams):
        for up in (0, 1):
            if hops[s][up]:
                hop(s, hops[s][up] - 1, up).wait_recv()
    for s in range(streams):
        for up in (0, 1):
            for h in range(hops[s][up]):
                hop(s, h, up).wait_send()
    for a in (0, 1, 2):
        held = [0]
        for mask in masks:
            for m in held:
                share(a, m, mask).wait_send()
            held = held + [m | mask for m in held]
    for c in locals_ + copies:
        c.wait()
    pltpu.make_async_copy(send_ref.at[pl.ds(1, count - 1)], rest, deal_sem.at[0]).wait()


def gather_all(x, dy, meta, dest, lens, blocks, downs, n_dp, n_f):
    streams = len(blocks)
    tok, width = x.shape
    count = n_dp * n_f
    sent = (count, 2 * tok // count, width + 128)
    hops = max(max(d, n_f - 1 - d) for d in downs)
    any_ = pl.BlockSpec(memory_space=pl.ANY)
    vmem = pl.BlockSpec(memory_space=pltpu.VMEM)
    row = jax.ShapeDtypeStruct((tok, width), BF16)
    rows = jax.ShapeDtypeStruct((n_dp, tok, width), BF16)
    return pl.pallas_call(
        functools.partial(gather_kernel, n_dp, n_f, downs),
        in_specs=[vmem] * 5 + [any_] * streams,
        out_specs=[any_] * 5 + [vmem] * 2 + [any_] * streams,
        out_shape=[
            rows,
            rows,
            jax.ShapeDtypeStruct((n_dp,) + lens.shape, lens.dtype),
            row,
            row,
            jax.ShapeDtypeStruct((2 * tok, 128), F32),
            jax.ShapeDtypeStruct((8, tok), F32),
        ]
        + [jax.ShapeDtypeStruct((n_f,) + b.shape, b.dtype) for b in blocks],
        scratch_shapes=[
            pltpu.VMEM(sent, BF16),
            pltpu.VMEM(sent, BF16),
            pltpu.VMEM((tok, width), BF16),
            pltpu.VMEM((tok, width), BF16),
            pltpu.SemaphoreType.DMA((2,)),
            pltpu.SemaphoreType.DMA((streams + 5,)),
            pltpu.SemaphoreType.DMA((3, n_dp)),
            pltpu.SemaphoreType.DMA((3, n_dp)),
            pltpu.SemaphoreType.DMA((streams, 2, hops)),
            pltpu.SemaphoreType.DMA((streams, 2, hops)),
        ],
        compiler_params=pltpu.CompilerParams(
            collective_id=0, has_side_effects=True, vmem_limit_bytes=40 * 2**20
        ),
        cost_estimate=pl.CostEstimate(flops=10**10, bytes_accessed=2 * 10**8, transcendentals=0),
    )(x, dy, meta, dest, lens, *blocks)


def columns_kernel(starts, cs, w_ref, *outs):
    me_d = lax.axis_index("dp")
    for o, out in enumerate(outs):
        for j, start in enumerate(starts[o]):
            out[:, j * cs : (j + 1) * cs] = w_ref[:, pl.ds(pl.multiple_of(start + me_d * cs, 128), cs)]


def take_columns(w, halves, n_f, n_dp, cs):
    inner = n_f * n_dp * cs
    starts = [[h * inner + f * n_dp * cs for f in range(n_f)] for h in range(halves)]
    me_d = lax.axis_index("dp")
    if cs % 128:
        return [
            jnp.concatenate([lax.dynamic_slice_in_dim(w, s + me_d * cs, cs, 1) for s in group], axis=1)
            for group in starts
        ]
    height = w.shape[0]
    blk = min(height, 64)
    return pl.pallas_call(
        functools.partial(columns_kernel, starts, cs),
        grid=(height // blk,),
        in_specs=[pl.BlockSpec((blk, w.shape[1]), lambda i: (i, 0))],
        out_specs=[pl.BlockSpec((blk, n_f * cs), lambda i: (i, 0))] * halves,
        out_shape=[jax.ShapeDtypeStruct((height, n_f * cs), w.dtype)] * halves,
    )(w)


def spread_kernel(cs, x_ref, w_ref, out_ref, sum_ref):
    me_d = lax.axis_index("dp")
    total = jnp.zeros(sum_ref.shape, F32)
    for i in range(x_ref.shape[0]):
        m = me_d + i - 2 * ((me_d // 2 % 2) * (i // 2 % 2) * 2 + (me_d % 2) * (i % 2))
        part = x_ref[m].astype(F32)
        cols = slice(i * cs, (i + 1) * cs)
        out_ref[:, cols] = part
        product = part * w_ref[:, cols].astype(F32)
        for j in range(0, cs, 128):
            total = total + product[:, j : j + 128]

    @pl.when(pl.program_id(0) == 0)
    def _():
        sum_ref[...] = jnp.zeros_like(sum_ref)

    sum_ref[...] += total


def spread_columns(rel, w, cs):
    n_dp, height, cols = rel.shape
    if cs % 128 or n_dp != 4:
        me_d = lax.axis_index("dp")
        parts = [lax.dynamic_index_in_dim(rel, me_d ^ i, 0, keepdims=False) for i in range(n_dp)]
        out = jnp.concatenate(
            [p[:, f * cs : (f + 1) * cs] for f in range(cols // cs) for p in parts], axis=1
        ).astype(F32)
        return out, jnp.sum(out * w.astype(F32), axis=1)
    out, sums = pl.pallas_call(
        functools.partial(spread_kernel, cs),
        grid=(cols // cs,),
        in_specs=[
            pl.BlockSpec((n_dp, height, cs), lambda f: (0, 0, f)),
            pl.BlockSpec((height, n_dp * cs), lambda f: (0, f)),
        ],
        out_specs=[
            pl.BlockSpec((height, n_dp * cs), lambda f: (0, f)),
            pl.BlockSpec((height, 128), lambda f: (0, 0)),
        ],
        out_shape=[jax.ShapeDtypeStruct((height, n_dp * cols), F32), jax.ShapeDtypeStruct((height, 128), F32)],
        cost_estimate=pl.CostEstimate(flops=4 * height * cols * n_dp, bytes_accessed=8 * height * cols * n_dp, transcendentals=0),
    )(rel, w)
    return out, jnp.sum(sums, axis=1)


def per_device(
    tokens,
    cotangent,
    destination,
    lengths,
    norm_gain,
    in_weight,
    conv_weight,
    conv_bias,
    select_weight,
    step_weight,
    step_bias,
    decay_log,
    skip_gain,
    out_weight,
):
    n_dp = lax.axis_size("dp")
    n_f = lax.axis_size("fsdp")
    rows = n_dp * n_f
    tok = tokens.shape[0]
    width = tokens.shape[1]
    pair = tok // rows
    inner = conv_bias.shape[0] * n_f
    cs = conv_bias.shape[0] // n_dp
    ch = cs * n_f
    taps = conv_weight.shape[0]
    n = decay_log.shape[0]
    rank_of = step_weight.shape[0]
    dcols = width // n_f
    group = n_dp * tok
    both = ("dp", "fsdp")
    me_d = lax.axis_index("dp")
    me_f = lax.axis_index("fsdp")
    order = ring_order(n_f)
    place_of = jnp.asarray([order.index(f) for f in range(n_f)], jnp.int32)
    order_arr = jnp.asarray(order, jnp.int32)
    q = place_of[me_f]
    at_ring = [order_arr[(q + k) % n_f] for k in range(n_f)]
    flat_dot = lambda a, b: jnp.dot(a, b, preferred_element_type=F32)
    nt_dot = lambda a, b: lax.dot_general(a, b, (((1,), (1,)), ((), ())), preferred_element_type=F32)
    tn_dot = lambda a, b: lax.dot_general(a, b, (((0,), (0,)), ((), ())), preferred_element_type=F32)

    me = me_d * n_f + me_f
    row_to = destination // tok
    meta = jnp.stack(
        [destination, (row_to - me) % rows, row_to, destination % tok] + [jnp.zeros_like(destination)] * 4
    ).astype(F32)
    segs = lengths.shape[1]
    lens_tile = jnp.pad(lengths, ((0, 7), (0, 128 - segs)))
    slots = jnp.arange(tok, dtype=jnp.int32)

    def mine(shard):
        return lax.dynamic_slice_in_dim(shard.reshape(-1, n_dp * cs), me_d * cs, cs, 1)

    smalls = [conv_weight, conv_bias, step_bias, skip_gain, decay_log, select_weight, step_weight]
    heights = [math.prod(s.shape) // (n_dp * cs) for s in smalls]
    gain_rows = dcols // cs
    used = sum(heights) + gain_rows
    filler = -used % 16
    small_block = jnp.concatenate(
        [mine(s) for s in smalls] + [norm_gain.reshape(gain_rows, cs), jnp.zeros((filler, cs), BF16)], axis=0
    )
    wx_block, wg_block = take_columns(in_weight, 2, n_f, n_dp, cs)
    wo_block = lax.dynamic_slice_in_dim(out_weight, me_d * cs, cs, 0)
    x_all, dy_all, lens_all, x_own, dy_own, tags, ranks, small_all, wx, wg = gather_all(
        tokens, cotangent, meta, destination[:, None].astype(F32), lens_tile,
        [small_block, wx_block, wg_block], [n_f // 2, n_f // 2, n_f - 1 - n_f // 2], n_dp, n_f,
    )
    x_all = x_all.reshape(group, width)
    lens = lens_all[:, 0, :segs]
    from_send = (ranks[0].astype(jnp.int32)[:, None] == slots[None, :]).astype(BF16)
    dy_all = dy_all.reshape(group, width)
    wx = wx.reshape(width, ch)
    wg = wg.reshape(width, ch)
    small = small_all.transpose(1, 0, 2).reshape(used + filler, ch)
    gain = small_all[:, used - gain_rows : used].reshape(width).astype(F32)
    tags = tags.reshape(rows, 2 * pair, 128)[:, :pair, 0].astype(jnp.int32)
    tags = tags[(me - jnp.arange(rows, dtype=jnp.int32)) % rows].reshape(tok)
    from_row = (tags[:, None] == slots[None, :]).astype(BF16)

    valid = (slots < jnp.sum(lengths[0, : segs - 1])).astype(F32)
    x_own32 = x_own.astype(F32)
    square = jnp.sum(x_own32 * x_own32, axis=1)
    mine_sums = [jnp.sum(square * valid), jnp.sum(valid)]

    pieces, at = [], 0
    for height in heights:
        pieces.append(small[at : at + height])
        at += height
    conv_w, conv_b, step_b, skip, dlog, sel, stepw = pieces
    conv_w = conv_w.astype(F32)
    skip = skip.astype(F32)
    rate = -jnp.exp(dlog.astype(F32))

    def shifted(values, lag):
        if lag == 0:
            return values
        edge = jnp.zeros((abs(lag),) + values.shape[1:], values.dtype)
        if lag > 0:
            return jnp.concatenate([edge, values[:-lag]], axis=0)
        return jnp.concatenate([values[-lag:], edge], axis=0)

    within = jnp.arange(tok, dtype=jnp.int32)
    since, left = [], []
    for m in range(n_dp):
        begin, end, total = 0, 0, 0
        for j in range(segs):
            after = total + lens[m, j]
            begin = jnp.where(within >= total, total, begin)
            end = jnp.where(within >= total, after, end)
            total = after
        since.append(within - begin)
        left.append(end - 1 - within)
    since = jnp.concatenate(since)[:, None]
    left = jnp.concatenate(left)[:, None]
    same = [(since >= lag).astype(F32) for lag in range(taps)]
    same_next = [(left >= lag).astype(F32) for lag in range(taps)]
    split = lambda value: [value[m * tok : (m + 1) * tok] for m in range(n_dp)]
    normed, x_in, conv, act, gate, dbl, wo_next = enter(
        lens, x_all, gain[None], wx, wg, conv_w, conv_b.astype(F32), sel, wo_block, n_f
    )
    dbl = dbl.reshape(group, -1)
    rate2 = rate * LOG2E
    scan_out, states, delta, pre, wo = scan_forward(
        lens, dbl, act, stepw, step_b.astype(F32), rate2, skip, wo_block, wo_next, n_f, tok
    )
    wo = wo.reshape(ch, width)
    gate_silu = jax.nn.silu(gate)
    gated = (scan_out * gate_silu).astype(BF16)
    mixed_part = flat_dot(gated, wo).astype(BF16)
    mixed = group_reduce(split(mixed_part), n_dp, BF16)

    gated_grad = nt_dot(dy_all, wo)
    scan_grad = gated_grad * gate_silu
    gate_grad = (gated_grad * scan_out * silu_slope(gate)).astype(BF16)
    wg_grad = tn_dot(normed, gate_grad).astype(BF16)
    wo_grad = tn_dot(gated, dy_all).astype(BF16)
    wg_own = ring_reduce(
        lambda k: lax.dynamic_slice_in_dim(wg_grad, at_ring[k] * dcols, dcols, 0), n_f, n_f // 2, BF16
    )
    wo_own = ring_reduce(
        lambda k: lax.dynamic_slice_in_dim(wo_grad, at_ring[k] * cs, cs, 0), n_f, n_f - 1 - n_f // 2, BF16
    )
    pre_grad, act_grad, dbl_grad, decay_sum, sums, step_grad = scan_backward(
        lens, dbl, delta, pre, act, scan_grad, stepw, rate2, skip, states, n_f, tok
    )
    dbl_grad = dbl_grad.reshape(group, -1).astype(BF16)
    act_grad = act_grad + flat_dot(dbl_grad, sel)
    conv_grad = act_grad * silu_slope(conv)
    in_grad = sum(
        conv_w[taps - 1 - lag][None] * shifted(conv_grad, -lag) * same_next[lag] for lag in range(taps)
    ).astype(BF16)
    wx_grad = tn_dot(normed, in_grad).astype(BF16)
    wx_own = ring_reduce(
        lambda k: lax.dynamic_slice_in_dim(wx_grad, at_ring[k] * dcols, dcols, 0), n_f, n_f // 2, BF16
    )
    normed_grad_part = (nt_dot(in_grad, wx) + nt_dot(gate_grad, wg)).astype(BF16)
    normed_grad = group_reduce(split(normed_grad_part), n_dp, BF16)

    tap_grads = [
        jnp.sum(conv_grad * shifted(x_in, taps - 1 - tap) * same[taps - 1 - tap], axis=0) for tap in range(taps)
    ]
    small_grads = jnp.concatenate(
        [jnp.stack(tap_grads)]
        + [
            jnp.sum(conv_grad, axis=0, keepdims=True),
            sums[:2],
            decay_sum * rate,
            tn_dot(dbl_grad, act),
            step_grad,
            jnp.zeros((-sum(heights) % 16, ch), F32),
        ],
        axis=0,
    )
    small_own = ring_reduce(
        lambda k: lax.dynamic_slice_in_dim(small_grads, at_ring[k] * cs, cs, 1), n_f, n_f - 1 - n_f // 2, F32
    )

    def in_group_order(blocks):
        stacked = jnp.stack(blocks)
        return [lax.dynamic_index_in_dim(stacked, me_d ^ i, 0, keepdims=False) for i in range(n_dp)]

    def interleaved(blocks):
        return jnp.stack(in_group_order(blocks), axis=1)

    own_in = jnp.concatenate(
        [
            jnp.stack(group_gather(wx_own.astype(BF16), n_dp)),
            jnp.stack(group_gather(wg_own.astype(BF16), n_dp)),
        ],
        axis=2,
    )
    grad_in_weight, gain_sum = spread_columns(own_in, in_weight, cs)
    grad_out_weight = jnp.concatenate(in_group_order(group_gather(wo_own.astype(BF16), n_dp)), axis=0).astype(F32)
    small_full = interleaved(group_gather(small_own, n_dp)).reshape(-1, n_dp * cs)
    out_small, at = [], 0
    for height, s in zip(heights, smalls):
        out_small.append(small_full[at : at + height].reshape(s.shape))
        at += height
    grad_norm_gain = gain_sum / norm_gain.astype(F32)

    rstd = lax.rsqrt(jnp.mean(x_own32 * x_own32, axis=1, keepdims=True) + EPS)
    hat = x_own32 * rstd
    hat_grad = normed_grad * gain[None]
    change = rstd * (hat_grad - hat * jnp.mean(hat_grad * hat, axis=1, keepdims=True))
    row_grad = (dy_own.astype(F32) + change).astype(BF16)
    layer = (x_own32 + mixed).astype(BF16)

    def returned(value):
        cols = value.shape[1]
        out = flat_dot(from_row, value).astype(BF16).reshape(rows, pair, cols)
        back = lax.all_to_all(out, both, 0, 0, tiled=True).reshape(tok, cols)
        return flat_dot(from_send, back).astype(BF16)

    lanes = lax.broadcasted_iota(jnp.int32, (tok, 128), 1)
    ride = jnp.zeros((tok, 128), F32)
    for j, value in enumerate(mine_sums):
        high = value.astype(BF16).astype(F32)
        ride = ride + jnp.where(lanes == 2 * j, high, 0.0) + jnp.where(lanes == 2 * j + 1, value - high, 0.0)
    out = flat_dot(from_row, jnp.concatenate([layer, mixed.astype(BF16)], axis=1)).astype(BF16)
    out = jnp.concatenate([out, ride.astype(BF16)], axis=1).reshape(rows, pair, 2 * width + 128)
    back = lax.all_to_all(out, both, 0, 0, tiled=True).reshape(tok, 2 * width + 128)
    totals = jnp.sum(back.reshape(rows, pair, -1)[:, 0, 2 * width : 2 * width + 4].astype(F32), axis=0)
    input_rms = jnp.sqrt((totals[0] + totals[1]) / ((totals[2] + totals[3]) * width))
    layer_output = flat_dot(from_send, back[:, :width]).astype(BF16)
    mixer_output = flat_dot(from_send, back[:, width : 2 * width]).astype(BF16)
    input_grad = returned(row_grad)
    return (
        layer_output,
        mixer_output,
        input_grad,
        input_rms,
        grad_norm_gain,
        grad_in_weight,
        out_small[0],
        out_small[1],
        out_small[5],
        out_small[6],
        out_small[2],
        out_small[4],
        out_small[3],
        grad_out_weight,
    )


def solution(mesh):
    return jax.shard_map(
        per_device,
        mesh=mesh,
        in_specs=(
            P(("dp", "fsdp"), None),
            P(("dp", "fsdp"), None),
            P(("dp", "fsdp")),
            P(("dp", "fsdp"), None),
            P("fsdp"),
            P("fsdp", None),
            P(None, "fsdp"),
            P("fsdp"),
            P(None, "fsdp"),
            P(None, "fsdp"),
            P("fsdp"),
            P(None, "fsdp"),
            P("fsdp"),
            P("fsdp", None),
        ),
        out_specs=(
            P(("dp", "fsdp"), None),
            P(("dp", "fsdp"), None),
            P(("dp", "fsdp"), None),
            P(),
            P("fsdp"),
            P("fsdp", None),
            P(None, "fsdp"),
            P("fsdp"),
            P(None, "fsdp"),
            P(None, "fsdp"),
            P("fsdp"),
            P(None, "fsdp"),
            P("fsdp"),
            P("fsdp", None),
        ),
        check_vma=False,
    )
```

```python
import functools
import math

import jax
import jax.numpy as jnp
from jax import lax
from jax.experimental import pallas as pl
from jax.experimental.pallas import tpu as pltpu
from jax.sharding import PartitionSpec as P

EPS = 1e-05
TB = 16
LOG2E = math.log2(math.e)
RESET = 1.0e4
BF16 = jnp.bfloat16
F32 = jnp.float32


def silu_slope(value):
    sigma = jax.nn.sigmoid(value)
    return sigma * (1.0 + value * (1.0 - sigma))


def row_at(g, n_dp):
    return lax.rem(2 * g + 1, n_dp + 1)


def flip(d, mask):
    return d + mask - 2 * mask * lax.rem(d // mask, 2)


class GroupSum:
    def __init__(self, part, near, far, total, send, recv):
        self.part, self.near, self.far, self.total = part, near, far, total
        me_d, me_f = lax.axis_index("dp"), lax.axis_index("fsdp")
        plan = [
            (part.at[1], near.at[0], 1),
            (part.at[3], near.at[1], 1),
            (part.at[0], far.at[1], 2),
            (part.at[2], far.at[0], 2),
            (total.at[0], total.at[1], 1),
            (total.at[2], total.at[3], 1),
        ]
        self.copies = [
            pltpu.make_async_remote_copy(
                src_ref=src,
                dst_ref=dst,
                send_sem=send.at[i],
                recv_sem=recv.at[i],
                device_id=(flip(me_d, mask), me_f),
                device_id_type=pl.DeviceIdType.MESH,
            )
            for i, (src, dst, mask) in enumerate(plan)
        ]

    def row_done(self, g):
        for j in (0, 1):

            @pl.when(g == j)
            def _(j=j):
                self.copies[j].start()

            @pl.when(g == j + 2)
            def _(j=j):
                self.copies[j].wait_recv()
                self.part[2 * j] = self.part[2 * j] + self.near[j]
                self.copies[j + 2].start()

    def first(self):
        for j in (0, 1):
            self.copies[j].start()

    def second(self):
        for j in (0, 1):
            self.copies[j].wait_recv()
            self.part[2 * j] = self.part[2 * j] + self.near[j]
            self.copies[j + 2].start()

    def finish(self):
        for j in (0, 1):
            self.copies[3 - j].wait_recv()
            self.total[2 * j] = self.part[2 * j] + self.far[j]
            self.copies[4 + j].start()
        for j in (0, 1):
            self.copies[4 + j].wait_recv()
        for c in self.copies:
            c.wait_send()

    @staticmethod
    def scratch(tok, wide):
        return [
            pltpu.VMEM((4, tok, wide), F32),
            pltpu.VMEM((2, tok, wide), F32),
            pltpu.VMEM((2, tok, wide), F32),
            pltpu.VMEM((4, tok, wide), F32),
            pltpu.SemaphoreType.DMA((6,)),
            pltpu.SemaphoreType.DMA((6,)),
        ]


class RingReduce:
    def __init__(self, n_f, part, got, send, recv, down):
        self.part, self.got = part, got
        q = ring_place(lax.axis_index("fsdp"), n_f)
        self.at = lambda k: ring_index(lax.rem(q + k, n_f), n_f)
        self.n_f = n_f
        self.counts = [down, n_f - 1 - down]
        self.copies = [[], []]
        for up in (0, 1):
            for h in range(self.counts[up]):
                src = part.at[self.at(self.goal(up, 0))] if h == 0 else got.at[up, h - 1]
                self.copies[up].append(ring_copy(n_f, src, got.at[up, h], send.at[up, h], recv.at[up, h], up))
        self.events = max(self.counts)

    def goal(self, up, h):
        left = self.counts[up] - h
        return left if up else self.n_f - left

    def add(self, slot, addend):
        rows = slot.shape[0]
        step = min(rows, 64)

        def piece(i, _):
            at = pl.ds(pl.multiple_of(i * step, step), step)
            slot[at, :] = (slot[at, :].astype(F32) + addend[at, :].astype(F32)).astype(slot.dtype)
            return 0

        lax.fori_loop(0, rows // step, piece, 0)

    def start(self):
        for up in (0, 1):
            if self.copies[up]:
                self.copies[up][0].start()

    def event(self, e):
        for up in (0, 1):
            if e < self.counts[up]:
                self.copies[up][e - 1].wait_recv()
                self.add(self.got.at[up, e - 1], self.part.at[self.at(self.goal(up, e))])
                self.copies[up][e].start()

    def finish(self, out):
        last = []
        for up in (0, 1):
            if self.copies[up]:
                self.copies[up][-1].wait_recv()
                last.append(self.got.at[up, self.counts[up] - 1])
        mine = self.part.at[self.at(0)]
        rows = mine.shape[0]
        step = min(rows, 64)

        def piece(i, _):
            at = pl.ds(pl.multiple_of(i * step, step), step)
            total_ = mine[at, :].astype(F32)
            for slot in last:
                total_ = total_ + slot[at, :].astype(F32)
            out[at, :] = total_.astype(out.dtype)
            return 0

        lax.fori_loop(0, rows // step, piece, 0)
        for up in (0, 1):
            for c in self.copies[up]:
                c.wait_send()

    @staticmethod
    def scratch(n_f, block, dtype=BF16):
        return [
            pltpu.VMEM((2, n_f // 2) + block, dtype),
            pltpu.SemaphoreType.DMA((2, n_f // 2)),
            pltpu.SemaphoreType.DMA((2, n_f // 2)),
        ]


class PairReduce:
    def __init__(self, part, near, far, send, recv):
        self.part, self.near, self.far = part, near, far
        me_d, me_f = lax.axis_index("dp"), lax.axis_index("fsdp")
        plan = [
            (part.at[1], near.at[0], 1),
            (part.at[3], near.at[1], 1),
            (part.at[2], far, 2),
        ]
        self.copies = [
            pltpu.make_async_remote_copy(
                src_ref=src,
                dst_ref=dst,
                send_sem=send.at[i],
                recv_sem=recv.at[i],
                device_id=(flip(me_d, mask), me_f),
                device_id_type=pl.DeviceIdType.MESH,
            )
            for i, (src, dst, mask) in enumerate(plan)
        ]

    def start(self):
        for c in self.copies[:2]:
            c.start()

    def middle(self):
        self.copies[1].wait_recv()
        rows_add(self.part.at[2], [self.part.at[2], self.near.at[1]])
        self.copies[2].start()
        self.copies[0].wait_recv()

    def finish(self, out):
        self.copies[2].wait_recv()
        rows_add(out, [self.part.at[0], self.near.at[0], self.far])
        for c in self.copies:
            c.wait_send()

    @staticmethod
    def scratch(block, dtype=BF16):
        return [
            pltpu.VMEM((2,) + block, dtype),
            pltpu.VMEM(block, dtype),
            pltpu.SemaphoreType.DMA((3,)),
            pltpu.SemaphoreType.DMA((3,)),
        ]


def rows_add(out, terms, step=32):
    def piece(i, _):
        at = pl.ds(pl.multiple_of(i * step, step), step)
        total_ = terms[0][at, :].astype(F32)
        for t in terms[1:]:
            total_ = total_ + t[at, :].astype(F32)
        out[at, :] = total_.astype(out.dtype)
        return 0

    lax.fori_loop(0, out.shape[0] // step, piece, 0)


def greet_neighbours(n_f, ring):
    me_d, me_f = lax.axis_index("dp"), lax.axis_index("fsdp")
    barrier = pltpu.get_barrier_semaphore()
    others = [(flip(me_d, 1), me_f), (flip(me_d, 2), me_f)]
    if ring:
        q = ring_place(me_f, n_f)
        others.append((me_d, ring_index(lax.rem(q + n_f - 1, n_f), n_f)))
        others.append((me_d, ring_index(lax.rem(q + 1, n_f), n_f)))
    for other in others:
        pl.semaphore_signal(barrier, inc=1, device_id=other, device_id_type=pl.DeviceIdType.MESH)
    pl.semaphore_wait(barrier, len(others))


def ring_copy(n_f, src, dst, send, recv, up):
    me_d, me_f = lax.axis_index("dp"), lax.axis_index("fsdp")
    q = ring_place(me_f, n_f)
    to = ring_index(lax.rem(q + (1 if up else n_f - 1), n_f), n_f)
    return pltpu.make_async_remote_copy(
        src_ref=src,
        dst_ref=dst,
        send_sem=send,
        recv_sem=recv,
        device_id=(me_d, to),
        device_id_type=pl.DeviceIdType.MESH,
    )


def segment_span(lens_ref, m, first, rows):
    t = lax.broadcasted_iota(jnp.int32, (rows, 1), 0) + first
    begin = jnp.zeros((rows, 1), jnp.int32)
    end = jnp.zeros((rows, 1), jnp.int32)
    total = jnp.int32(0)
    for j in range(lens_ref.shape[1]):
        after = total + lens_ref[m, j]
        inside = t >= total
        begin = jnp.where(inside, total, begin)
        end = jnp.where(inside, after, end)
        total = after
    return t - begin, end - 1 - t


def enter_kernel(n_f, half, lens_ref, x_ref, gain_ref, wx_ref, wg_ref, taps_ref, bias_ref, sel_ref, wo_ref,
                 normed_ref, xin_ref, conv_ref, act_ref, gate_ref, dbl_ref, next_ref,
                 part, near, far, total, gs_send, gs_recv, hop_send, hop_recv):
    g = pl.program_id(0)
    n_dp, tok = part.shape[:2]
    rows, width = x_ref.shape
    hops = [ring_copy(n_f, wo_ref, next_ref.at[up, 0], hop_send.at[up, 0], hop_recv.at[up, 0], up) for up in (0, 1)]
    hops2 = [
        ring_copy(n_f, next_ref.at[up, 0], next_ref.at[up, 1], hop_send.at[up, 1], hop_recv.at[up, 1], up)
        for up in (0, 1)
    ]
    group = GroupSum(part, near, far, total, gs_send, gs_recv)

    @pl.when(g == 0)
    def _():
        greet_neighbours(n_f, True)
        for c in hops:
            c.start()
        part[...] = jnp.zeros_like(part)

        def norm(i, _):
            at = pl.ds(pl.multiple_of(i * 32, 32), 32)
            v = x_ref[at, :].astype(F32)
            rstd = lax.rsqrt(jnp.mean(v * v, axis=1, keepdims=True) + EPS)
            normed_ref[at, :] = (v * rstd * gain_ref[...]).astype(BF16)
            return 0

        lax.fori_loop(0, rows // 32, norm, 0)

    @pl.when(g == half)
    def _():
        for a, b in zip(hops, hops2):
            a.wait_recv()
            b.start()

    @pl.when(g < half)
    def _():
        n_taps = taps_ref.shape[0]
        for m in range(n_dp):
            at = slice(m * tok, (m + 1) * tok)
            v = jnp.dot(normed_ref[at, :], wx_ref[...], preferred_element_type=F32)
            since, _ = segment_span(lens_ref, m, 0, tok)
            xin_ref[at, :] = v
            conv = bias_ref[...] + taps_ref[n_taps - 1 : n_taps, :] * v
            for lag in range(1, n_taps):
                keep = (since >= lag).astype(F32)
                conv = conv + taps_ref[n_taps - 1 - lag : n_taps - lag, :] * (pltpu.roll(v, lag, 0) * keep)
            conv_ref[at, :] = conv
            act = jax.nn.silu(conv).astype(BF16)
            act_ref[at, :] = act
            part[m] += lax.dot_general(act, sel_ref[...], (((1,), (1,)), ((), ())), preferred_element_type=F32)

    @pl.when(g == half - 1)
    def _():
        group.first()

    @pl.when(g >= half)
    def _():
        for m in range(n_dp):
            at = slice(m * tok, (m + 1) * tok)
            gate_ref[at, :] = jnp.dot(normed_ref[at, :], wg_ref[...], preferred_element_type=F32)

    @pl.when(g == half)
    def _():
        group.second()

    @pl.when(g == 2 * half - 1)
    def _():
        group.finish()
        dbl_ref[...] = total[...]
        for a, b in zip(hops, hops2):
            a.wait_send()
            b.wait()


def enter(lens, x_all, gain, wx, wg, taps, bias, sel, wo_block, n_f):
    n_dp = lens.shape[0]
    rows, width = x_all.shape
    tok = rows // n_dp
    ch = wx.shape[1]
    wide = sel.shape[0]
    piece = 256
    half = ch // piece
    whole = lambda g: (0, 0)
    early = lambda g: (0, jnp.minimum(g, half - 1))
    late = lambda g: (0, jnp.maximum(g - half, 0))
    once = pl.Buffered(1)
    any_ = pl.BlockSpec(memory_space=pl.ANY)
    shaped = lambda d, t: jax.ShapeDtypeStruct((rows, d), t)
    return pl.pallas_call(
        functools.partial(enter_kernel, n_f, half),
        grid=(2 * half,),
        in_specs=[
            pl.BlockSpec(memory_space=pltpu.SMEM),
            pl.BlockSpec((rows, width), whole, pipeline_mode=once),
            pl.BlockSpec((1, width), whole),
            pl.BlockSpec((width, piece), early),
            pl.BlockSpec((width, piece), late),
            pl.BlockSpec((taps.shape[0], piece), early),
            pl.BlockSpec((1, piece), early),
            pl.BlockSpec((wide, piece), early),
            any_,
        ],
        out_specs=[
            pl.BlockSpec((rows, width), whole),
            pl.BlockSpec((rows, piece), early),
            pl.BlockSpec((rows, piece), early),
            pl.BlockSpec((rows, piece), early),
            pl.BlockSpec((rows, piece), late),
            pl.BlockSpec((n_dp, tok, wide), lambda g: (0, 0, 0)),
            any_,
        ],
        out_shape=[
            shaped(width, BF16),
            shaped(ch, F32),
            shaped(ch, F32),
            shaped(ch, BF16),
            shaped(ch, F32),
            jax.ShapeDtypeStruct((n_dp, tok, wide), F32),
            jax.ShapeDtypeStruct((2, 2) + wo_block.shape, BF16),
        ],
        scratch_shapes=GroupSum.scratch(tok, wide)
        + [pltpu.SemaphoreType.DMA((2, 2)), pltpu.SemaphoreType.DMA((2, 2))],
        compiler_params=pltpu.CompilerParams(
            collective_id=1, has_side_effects=True, vmem_limit_bytes=48 * 2**20
        ),
        cost_estimate=pl.CostEstimate(flops=10**10, bytes_accessed=4 * 10**7, transcendentals=10**6),
    )(lens, x_all, gain, wx, wg, taps, bias, sel, wo_block)


def fold_matrix(n):
    i = lax.broadcasted_iota(jnp.int32, (n, TB * n), 0)
    j = lax.broadcasted_iota(jnp.int32, (n, TB * n), 1)
    return jnp.where(lax.rem(j, n) == i, 1.0, 0.0)


def own_token(n):
    i = lax.broadcasted_iota(jnp.int32, (TB, TB * n), 0)
    j = lax.broadcasted_iota(jnp.int32, (TB, TB * n), 1)
    return i == j // n


def block_rows(m, n):
    spread = jnp.dot(m.astype(BF16), fold_matrix(n).astype(BF16), preferred_element_type=F32)
    i = lax.broadcasted_iota(jnp.int32, spread.shape, 0)
    j = lax.broadcasted_iota(jnp.int32, spread.shape, 1)
    return jnp.where(lax.rem(i, TB) == j // n, spread, 0.0).astype(BF16)


def turned(m):
    n = m.shape[1]
    i = lax.broadcasted_iota(jnp.int32, (n, n), 0)
    j = lax.broadcasted_iota(jnp.int32, (n, n), 1)
    eye = jnp.where(i == j, 1.0, 0.0)
    return lax.dot_general(
        eye, m, (((1,), (1,)), ((), ())), preferred_element_type=F32, precision=lax.Precision.HIGHEST
    )


def softplus(v):
    return jnp.maximum(v, 0.0) + jnp.log1p(jnp.exp(-jnp.abs(v)))


class RingGather:
    def __init__(self, n_f, mine, near, out, local, send, recv):
        q = ring_place(lax.axis_index("fsdp"), n_f)
        at = lambda k: ring_index(lax.rem(q + k, n_f), n_f)
        count = [n_f // 2, n_f - 1 - n_f // 2]
        known = near.shape[1]
        self.locals = [pltpu.make_async_copy(mine, out.at[at(0)], local.at[0])]
        self.hops = [[], []]
        for up in (0, 1):
            for j in range(known):
                index = at(n_f - 1 - j if up else 1 + j)
                self.locals.append(pltpu.make_async_copy(near.at[up, j], out.at[index], local.at[1 + known * up + j]))
            for h in range(known, count[up]):
                index = at(n_f - h if up else h)
                src = near.at[up, known - 1] if h == known else out.at[index]
                self.hops[up].append(
                    ring_copy(n_f, src, out.at[index], send.at[up, h], recv.at[up, h], up)
                )
        self.events = max(len(h) for h in self.hops)

    def start(self):
        for c in self.locals:
            c.start()
        for up in (0, 1):
            if self.hops[up]:
                self.hops[up][0].start()

    def event(self, e):
        for up in (0, 1):
            if e < len(self.hops[up]):
                self.hops[up][e - 1].wait_recv()
                self.hops[up][e].start()

    def finish(self):
        for up in (0, 1):
            if self.hops[up]:
                self.hops[up][-1].wait_recv()
            for c in self.hops[up]:
                c.wait_send()
        for c in self.locals:
            c.wait()


def fwd_kernel(lanes, n_f, lens_ref, dbl_ref, act_ref, stepw_ref, stepb_ref, rate_ref, skip_ref, wo_ref, next_ref,
               y_ref, s_ref, delta_ref, pre_ref, wo_all, carry, big_s, cw_s, bt_s, d_s, u_s, sc, local, hop_send, hop_recv):
    n, ch = rate_ref.shape
    tblk = act_ref.shape[0]
    low_n = stepw_ref.shape[0]
    steps = pl.num_programs(0) * pl.num_programs(1)
    now = pl.program_id(0) * pl.num_programs(1) + pl.program_id(1)
    ring = RingGather(n_f, wo_ref, next_ref, wo_all, local, hop_send, hop_recv)

    @pl.when(now == 0)
    def _():
        greet_neighbours(n_f, True)
        ring.start()

    for e in range(1, ring.events):

        @pl.when(now == min(7 * e, 15))
        def _(e=e):
            ring.event(e)

    @pl.when(pl.program_id(1) == 0)
    def _():
        carry[...] = jnp.zeros_like(carry)

    pre = jnp.dot(dbl_ref[:, :low_n].astype(BF16), stepw_ref[...], preferred_element_type=F32) + stepb_ref[...]
    pre_ref[...] = pre
    delta_ref[...] = softplus(pre)
    since, _ = segment_span(lens_ref, pl.program_id(0), pl.program_id(1) * tblk, tblk)
    big_s[...] = jnp.where(since == 0, RESET, 0.0)
    cw_s[...] = block_rows(dbl_ref[:, low_n + n : low_n + 2 * n], n)
    flat = turned(dbl_ref[:, low_n : low_n + n])
    for i in range(tblk // TB):
        bt_s[i] = flat[:, i * TB : (i + 1) * TB]

    def chunk(i, _):
        base = pl.multiple_of(i * TB, TB)
        dl = delta_ref[pl.ds(base, TB), :]
        ac = act_ref[pl.ds(base, TB), :].astype(F32)
        d_s[...] = dl + big_s[pl.ds(base, TB), :]
        u_s[...] = dl * ac
        bt = bt_s[i]
        for lo in range(0, ch, lanes):
            cs = pl.ds(lo, lanes)
            rate = rate_ref[:, cs]
            s = carry[:, cs]
            for t in range(TB):
                dec = jnp.exp2(d_s[t : t + 1, cs] * rate)
                s = dec * s + bt[:, t : t + 1] * u_s[t : t + 1, cs]
                sc[t * n : (t + 1) * n, cs] = s.astype(BF16)
            carry[:, cs] = s
        states = sc[...]
        y = jnp.dot(cw_s[pl.ds(base, TB), :], states, preferred_element_type=F32)
        y_ref[pl.ds(base, TB), :] = y + skip_ref[...] * ac
        s_ref[pl.ds(pl.multiple_of(base * n, TB * n), TB * n), :] = states
        return 0

    lax.fori_loop(0, tblk // TB, chunk, 0)

    @pl.when(now == steps - 1)
    def _():
        ring.finish()


def scan_forward(lens, dbl, act, stepw, stepb, rate2, skip, wo_block, wo_next, n_f, row_len, tblk=64, lanes=512):
    t, ch = act.shape
    n = rate2.shape[0]
    nb = row_len // tblk
    at = lambda r, j: (r * nb + j, 0)
    zero = lambda r, j: (0, 0)
    any_ = pl.BlockSpec(memory_space=pl.ANY)
    wide = jax.ShapeDtypeStruct((t, ch), F32)
    return pl.pallas_call(
        functools.partial(fwd_kernel, min(lanes, ch), n_f),
        grid=(t // row_len, nb),
        in_specs=[
            pl.BlockSpec(memory_space=pltpu.SMEM),
            pl.BlockSpec((tblk, dbl.shape[1]), at),
            pl.BlockSpec((tblk, ch), at),
            pl.BlockSpec(stepw.shape, zero),
            pl.BlockSpec((1, ch), zero),
            pl.BlockSpec((n, ch), zero),
            pl.BlockSpec((1, ch), zero),
            any_,
            any_,
        ],
        out_specs=[
            pl.BlockSpec((tblk, ch), at),
            pl.BlockSpec((tblk * n, ch), at),
            pl.BlockSpec((tblk, ch), at),
            pl.BlockSpec((tblk, ch), at),
            any_,
        ],
        out_shape=[
            wide,
            jax.ShapeDtypeStruct((t * n, ch), BF16),
            wide,
            wide,
            jax.ShapeDtypeStruct((n_f,) + wo_block.shape, BF16),
        ],
        scratch_shapes=[
            pltpu.VMEM((n, ch), F32),
            pltpu.VMEM((tblk, 1), F32),
            pltpu.VMEM((tblk, TB * n), BF16),
            pltpu.VMEM((tblk // TB, n, TB), F32),
            pltpu.VMEM((TB, ch), F32),
            pltpu.VMEM((TB, ch), F32),
            pltpu.VMEM((TB * n, ch), BF16),
            pltpu.SemaphoreType.DMA((5,)),
            pltpu.SemaphoreType.DMA((2, n_f)),
            pltpu.SemaphoreType.DMA((2, n_f)),
        ],
        compiler_params=pltpu.CompilerParams(
            collective_id=2, has_side_effects=True, vmem_limit_bytes=32 * 2**20
        ),
        cost_estimate=pl.CostEstimate(flops=t * n * ch * 40, bytes_accessed=t * ch * 52, transcendentals=t * n * ch),
    )(lens, dbl, act, stepw, stepb, rate2, skip, wo_block, wo_next)


def bwd_kernel(lanes, n_f, lens_ref, dbl_ref, delta_ref, pre_ref, act_ref, gy_ref, stepw_ref, rate_ref, skip_ref,
               s_ref, sp_ref, wg_part, mixed_part,
               pg_ref, da_ref, dbl_grad_ref, dl_ref, sums_ref, stepg_ref, wg_own, mixed_own,
               carry, big_s, bw_s, ct_s, d_all, u_all, g_all, h_all, b_all, c_all, part, near, far, total, gs_send, gs_recv,
               ring_got, ring_send, ring_recv, mix, mix_near, mix_far, mix_send, mix_recv, mix_load):
    n, ch = rate_ref.shape
    tblk = act_ref.shape[0]
    low_n = stepw_ref.shape[0]
    r, j = pl.program_id(0), pl.program_id(1)
    n_dp, nb = pl.num_programs(0), pl.num_programs(1)
    m = row_at(r, n_dp)
    group = GroupSum(part, near, far, total, gs_send, gs_recv)
    ring = RingReduce(n_f, wg_part, ring_got, ring_send, ring_recv, n_f // 2)
    pairs = PairReduce(mix, mix_near, mix_far, mix_send, mix_recv)
    now = r * nb + j
    last_step = n_dp * nb - 1
    @pl.when(j == 0)
    def _():
        carry[...] = jnp.zeros_like(carry)

    @pl.when((r == 0) & (j == 0))
    def _():
        load = pltpu.make_async_copy(mixed_part, mix, mix_load)
        load.start()
        greet_neighbours(n_f, True)
        ring.start()
        load.wait()
        pairs.start()
        dl_ref[...] = jnp.zeros_like(dl_ref)
        sums_ref[...] = jnp.zeros_like(sums_ref)
        stepg_ref[...] = jnp.zeros_like(stepg_ref)

    for e in range(1, ring.events):

        @pl.when(now == min(4 * e, 15))
        def _(e=e):
            ring.event(e)

    @pl.when(now == 2)
    def _():
        pairs.middle()

    @pl.when(now == 12)
    def _():
        pairs.finish(mixed_own)

    ones = jnp.where(own_token(n), 1.0, 0.0).astype(BF16)
    nt = (((1,), (1,)), ((), ()))
    row = lax.broadcasted_iota(jnp.int32, (TB * n, n), 0)
    col = lax.broadcasted_iota(jnp.int32, (TB * n, n), 1)
    fold = jnp.where(lax.rem(row, n) == col, 1.0, 0.0)
    since, _ = segment_span(lens_ref, m, (nb - 1 - j) * tblk, tblk)
    big_s[...] = jnp.where(since == 0, RESET, 0.0)
    bw_s[...] = block_rows(dbl_ref[:, low_n : low_n + n], n)

    flat = turned(dbl_ref[:, low_n + n : low_n + 2 * n])
    for i in range(tblk // TB):
        ct_s[i] = flat[:, i * TB : (i + 1) * TB]

    def lane_sum(value):
        total_ = value[:, :128]
        for at in range(128, value.shape[1], 128):
            total_ = total_ + value[:, at : at + 128]
        return total_

    def gathered(sums):
        spread = jnp.sum(sums, axis=1, keepdims=True) * fold
        high = spread.astype(BF16)
        rest = (spread - high.astype(F32)).astype(BF16)
        return jnp.dot(ones, high, preferred_element_type=F32) + jnp.dot(ones, rest, preferred_element_type=F32)

    for i in reversed(range(tblk // TB)):
        base = i * TB
        d_s, u_s, g_s, h_s, b_s, c_s = (v.at[i % 2] for v in (d_all, u_all, g_all, h_all, b_all, c_all))
        dl = delta_ref[base : base + TB, :]
        ac = act_ref[base : base + TB, :].astype(F32)
        d_s[...] = dl + big_s[base : base + TB, :]
        u_s[...] = dl * ac
        ct = ct_s[i]
        for lo in range(0, ch, lanes):
            cs = pl.ds(lo, lanes)
            rate = rate_ref[:, cs]
            flow = carry[:, cs]
            acc = dl_ref[:, cs]
            here = s_ref[(base + TB - 1) * n : (base + TB) * n, cs].astype(F32)
            for t in reversed(range(TB)):
                dr = d_s[t : t + 1, cs]
                dec = jnp.exp2(dr * rate)
                gy = gy_ref[base + t : base + t + 1, cs]
                g = ct[:, t : t + 1] * gy + flow
                flow = dec * g
                if base + t > 0:
                    prev = s_ref[(base + t - 1) * n : (base + t) * n, cs].astype(F32)
                else:
                    prev = sp_ref[:, cs].astype(F32)
                h = flow * prev
                acc = acc + h * dr
                at = slice(t * n, (t + 1) * n)
                b_now = lane_sum(g * u_s[t : t + 1, cs])
                c_now = lane_sum(here * gy)
                if lo:
                    b_now = b_now + b_s[at, :]
                    c_now = c_now + c_s[at, :]
                b_s[at, :] = b_now
                c_s[at, :] = c_now
                here = prev
                g_s[t * n : (t + 1) * n, cs] = g.astype(BF16)
                h_s[t * n : (t + 1) * n, cs] = (h * rate).astype(BF16)
            carry[:, cs] = flow
            dl_ref[:, cs] = acc
        gb = g_s[...]
        gy = gy_ref[base : base + TB, :]
        du = jnp.dot(bw_s[base : base + TB, :], gb, preferred_element_type=F32)
        hr = jnp.dot(ones, h_s[...], preferred_element_type=F32)
        dd = hr * (1.0 / LOG2E) + du * ac
        pg_ref[base : base + TB, :] = (dd * jax.nn.sigmoid(pre_ref[base : base + TB, :])).astype(BF16)
        da_ref[base : base + TB, :] = du * dl + skip_ref[...] * gy
        at = pl.ds(pl.multiple_of((nb - 1 - j) * tblk + base, TB), TB)
        part[m, at, low_n : low_n + n] = gathered(b_s[...])
        part[m, at, low_n + n : low_n + 2 * n] = gathered(c_s[...])

    pg = pg_ref[...]
    part[m, pl.ds(pl.multiple_of((nb - 1 - j) * tblk, tblk), tblk), :low_n] = lax.dot_general(
        pg, stepw_ref[...], nt, preferred_element_type=F32
    )
    stepg_ref[...] += lax.dot_general(
        dbl_ref[:, :low_n].astype(BF16), pg, (((0,), (0,)), ((), ())), preferred_element_type=F32
    )
    sums_ref[0:1, :] += jnp.sum(pg.astype(F32), axis=0, keepdims=True)
    sums_ref[1:2, :] += jnp.sum(gy_ref[...] * act_ref[...].astype(F32), axis=0, keepdims=True)

    @pl.when(j == nb - 1)
    def _():
        group.row_done(r)

    @pl.when((j == nb - 1) & (r == n_dp - 1))
    def _():
        ring.finish(wg_own)
        group.finish()
        dbl_grad_ref[...] = total[...]


def scan_backward(lens, dbl, delta, pre, act, gy, stepw, rate2, skip, states, wg_part, mixed_part, n_f, row_len,
                  tblk=64, lanes=512):
    t, ch = delta.shape
    n = rate2.shape[0]
    nb = row_len // tblk
    n_dp = t // row_len
    wide = dbl.shape[1]
    spot = lambda r, j: row_at(r, n_dp) * nb + nb - 1 - j
    at = lambda r, j: (spot(r, j), 0)
    zero = lambda r, j: (0, 0)
    entry = lambda r, j: (jnp.maximum(spot(r, j) * tblk - 1, 0), 0)
    return pl.pallas_call(
        functools.partial(bwd_kernel, min(lanes, ch), n_f),
        grid=(n_dp, nb),
        in_specs=[
            pl.BlockSpec(memory_space=pltpu.SMEM),
            pl.BlockSpec((tblk, wide), at),
            pl.BlockSpec((tblk, ch), at),
            pl.BlockSpec((tblk, ch), at),
            pl.BlockSpec((tblk, ch), at),
            pl.BlockSpec((tblk, ch), at),
            pl.BlockSpec(stepw.shape, zero),
            pl.BlockSpec((n, ch), zero),
            pl.BlockSpec((1, ch), zero),
            pl.BlockSpec((tblk * n, ch), at),
            pl.BlockSpec((n, ch), entry),
            pl.BlockSpec(memory_space=pltpu.VMEM),
            pl.BlockSpec(memory_space=pl.ANY),
        ],
        out_specs=[
            pl.BlockSpec((tblk, ch), at),
            pl.BlockSpec((tblk, ch), at),
            pl.BlockSpec((n_dp, row_len, wide), lambda r, j: (0, 0, 0)),
            pl.BlockSpec((n, ch), zero),
            pl.BlockSpec((8, ch), zero),
            pl.BlockSpec(stepw.shape, zero),
            pl.BlockSpec(wg_part.shape[1:], zero),
            pl.BlockSpec(mixed_part.shape[1:], zero),
        ],
        out_shape=[
            jax.ShapeDtypeStruct((t, ch), BF16),
            jax.ShapeDtypeStruct((t, ch), F32),
            jax.ShapeDtypeStruct((n_dp, row_len, wide), F32),
            jax.ShapeDtypeStruct((n, ch), F32),
            jax.ShapeDtypeStruct((8, ch), F32),
            jax.ShapeDtypeStruct(stepw.shape, F32),
            jax.ShapeDtypeStruct(wg_part.shape[1:], BF16),
            jax.ShapeDtypeStruct(mixed_part.shape[1:], F32),
        ],
        scratch_shapes=[
            pltpu.VMEM((n, ch), F32),
            pltpu.VMEM((tblk, 1), F32),
            pltpu.VMEM((tblk, TB * n), BF16),
            pltpu.VMEM((tblk // TB, n, TB), F32),
            pltpu.VMEM((2, TB, ch), F32),
            pltpu.VMEM((2, TB, ch), F32),
            pltpu.VMEM((2, TB * n, ch), BF16),
            pltpu.VMEM((2, TB * n, ch), BF16),
            pltpu.VMEM((2, TB * n, 128), F32),
            pltpu.VMEM((2, TB * n, 128), F32),
        ]
        + GroupSum.scratch(row_len, wide)
        + RingReduce.scratch(n_f, wg_part.shape[1:])
        + [pltpu.VMEM(mixed_part.shape, BF16)]
        + PairReduce.scratch(mixed_part.shape[1:])
        + [pltpu.SemaphoreType.DMA],
        compiler_params=pltpu.CompilerParams(
            collective_id=3, has_side_effects=True, vmem_limit_bytes=56 * 2**20
        ),
        cost_estimate=pl.CostEstimate(flops=t * n * ch * 80, bytes_accessed=t * ch * 60, transcendentals=t * n * ch),
    )(lens, dbl, delta, pre, act, gy, stepw, rate2, skip, states, states, wg_part, mixed_part)


def ring_order(count):
    half = count // 2
    if count % 2:
        return list(range(count))
    return [2 * p if p < half else 2 * (count - 1 - p) + 1 for p in range(count)]


def ring_step(value, count, by):
    order = ring_order(count)
    pairs = [(order[p], order[(p + by) % count]) for p in range(count)]
    return lax.ppermute(value, "fsdp", pairs)


def ring_reduce(part, count, down, dtype):
    total = part(0).astype(F32)
    if down:
        moving = part(count - down).astype(dtype)
        for hop in range(down):
            moving = ring_step(moving, count, -1)
            if hop < down - 1:
                moving = (moving.astype(F32) + part(count - down + hop + 1).astype(F32)).astype(dtype)
        total = total + moving.astype(F32)
    up = count - 1 - down
    if up:
        moving = part(up).astype(dtype)
        for hop in range(up):
            moving = ring_step(moving, count, 1)
            if hop < up - 1:
                moving = (moving.astype(F32) + part(up - hop - 1).astype(F32)).astype(dtype)
        total = total + moving.astype(F32)
    return total


def swap(value, count, mask):
    return lax.ppermute(value, "dp", [(i, i ^ mask) for i in range(count)])


def masks_of(count):
    return [1 << b for b in range(count.bit_length() - 1)]


def group_gather(block, count):
    blocks = {0: block}
    for mask in reversed(masks_of(count)):
        keys = sorted(blocks)
        got = swap(jnp.stack([blocks[m] for m in keys]), count, mask)
        for place, m in enumerate(keys):
            blocks[m | mask] = got[place]
    return [blocks[m] for m in range(count)]


def group_reduce(blocks, count, dtype):
    held = {m: b for m, b in enumerate(blocks)}
    for mask in masks_of(count):
        keep = [m for m in sorted(held) if not m & mask]
        got = swap(jnp.stack([held[m | mask].astype(dtype) for m in keep]), count, mask)
        held = {m: held[m].astype(F32) + got[place].astype(F32) for place, m in enumerate(keep)}
    return held[0]


def mesh_at(index, n_f):
    return (index // n_f, lax.rem(index, n_f))


def ring_index(p, n_f):
    if n_f % 2:
        return p
    return jnp.where(p < n_f // 2, 2 * p, 2 * (n_f - 1 - p) + 1)


def ring_place(f, n_f):
    if n_f % 2:
        return f
    return jnp.where(lax.rem(f, 2) == 0, f // 2, n_f - 1 - f // 2)


def gather_kernel(n_dp, n_f, downs, x_ref, dy_ref, meta_ref, dest_ref, lens_ref, *refs):
    streams = len(downs)
    blocks = refs[:streams]
    x_all, dy_all, lens_all, x_own_ref, dy_own_ref, tag_ref, rank_ref = refs[streams : streams + 7]
    outs = refs[streams + 7 : 2 * streams + 7]
    send_ref, got, x_own, dy_own, deal_sem, loc_sem, pair_send, pair_recv, ring_send, ring_recv = refs[
        2 * streams + 7 :
    ]
    count = n_dp * n_f
    me_d = lax.axis_index("dp")
    me_f = lax.axis_index("fsdp")
    me = me_d * n_f + me_f
    q = ring_place(me_f, n_f)
    below = ring_index(lax.rem(q + n_f - 1, n_f), n_f)
    above = ring_index(lax.rem(q + 1, n_f), n_f)

    barrier = pltpu.get_barrier_semaphore()

    def greet(p, _):
        pl.semaphore_signal(
            barrier, inc=1, device_id=mesh_at(lax.rem(me + p, count), n_f), device_id_type=pl.DeviceIdType.MESH
        )
        return 0

    lax.fori_loop(1, count, greet, 0)
    locals_ = [
        pltpu.make_async_copy(blocks[s], outs[s].at[me_f], loc_sem.at[s]) for s in range(streams)
    ]
    for c in locals_:
        c.start()
    pl.semaphore_wait(barrier, count - 1)

    def deal(p, _):
        pltpu.make_async_remote_copy(
            src_ref=send_ref.at[p],
            dst_ref=got.at[p],
            send_sem=deal_sem.at[0],
            recv_sem=deal_sem.at[1],
            device_id=mesh_at(lax.rem(me + p, count), n_f),
            device_id_type=pl.DeviceIdType.MESH,
        ).start()
        return 0

    def hop(s, h, up):
        k = lax.rem(q + (n_f - h if up else h), n_f)
        index = ring_index(k, n_f)
        src = blocks[s] if h == 0 else outs[s].at[index]
        return pltpu.make_async_remote_copy(
            src_ref=src,
            dst_ref=outs[s].at[index],
            send_sem=ring_send.at[s, int(up), h],
            recv_sem=ring_recv.at[s, int(up), h],
            device_id=(me_d, above if up else below),
            device_id_type=pl.DeviceIdType.MESH,
        )

    hops = [[downs[s], n_f - 1 - downs[s]] for s in range(streams)]
    for s in range(streams):
        for up in (0, 1):
            if hops[s][up]:
                hop(s, 0, up).start()
    tok, width = x_own.shape
    pair2 = got.shape[1]
    total = count * pair2

    dest_row, rel_row, abs_row, in_row = (meta_ref[i : i + 1, :] for i in range(4))
    rank = jnp.sum((dest_ref[...] < dest_row).astype(F32), axis=0, keepdims=True)
    rank_ref[...] = jnp.broadcast_to(rank, rank_ref.shape)
    half = pair2 // 2
    goal = rel_row * half + rank - abs_row * half
    row = lax.broadcasted_iota(jnp.int32, (total, tok), 0)
    place_in = lax.rem(row, pair2)
    first = place_in < half
    slot = (row // pair2) * half + jnp.where(first, place_in, place_in - half)
    chosen = slot.astype(F32) == goal
    spot = jnp.sum(jnp.where(chosen, in_row, 0.0), axis=1, keepdims=True)
    send_ref[:, :, width:] = jnp.broadcast_to(spot, (total, 128)).astype(BF16).reshape(count, pair2, 128)
    x_pick = jnp.where(chosen & first, 1.0, 0.0).astype(BF16)
    dy_pick = jnp.where(chosen & jnp.logical_not(first), 1.0, 0.0).astype(BF16)

    def sort(j, _):
        cols = pl.ds(pl.multiple_of(j * 256, 256), 256)
        mixed = jnp.dot(x_pick, x_ref[:, cols], preferred_element_type=F32)
        mixed = mixed + jnp.dot(dy_pick, dy_ref[:, cols], preferred_element_type=F32)
        send_ref[:, :, cols] = mixed.astype(BF16).reshape(count, pair2, 256)
        return 0

    lax.fori_loop(0, width // 256, sort, 0)
    lax.fori_loop(1, count, deal, 0)
    got[0] = send_ref[0]

    def advance(h):
        for s in range(streams):
            for up in (0, 1):
                if h < hops[s][up]:
                    hop(s, h - 1, up).wait_recv()
                    hop(s, h, up).start()

    rest = got.at[pl.ds(1, count - 1)]
    pltpu.make_async_copy(send_ref.at[pl.ds(1, count - 1)], rest, deal_sem.at[1]).wait()
    tag = got[:, :, width : width + 128].astype(F32).reshape(total, 128)
    reps = tok // 128
    spots = jnp.concatenate([tag] * reps, axis=1)
    lane = lax.broadcasted_iota(jnp.int32, (total, tok), 1).astype(F32)
    match = spots == lane
    x_pick = jnp.where(match & first, 1.0, 0.0).astype(BF16)
    dy_pick = jnp.where(match & jnp.logical_not(first), 1.0, 0.0).astype(BF16)
    tn = (((0,), (0,)), ((), ()))
    tag_ref[...] = tag

    def place(pick, out):
        def part(j, _):
            cols = pl.ds(pl.multiple_of(j * 256, 256), 256)
            values = got[:, :, cols].reshape(total, 256)
            out[:, cols] = lax.dot_general(pick, values, tn, preferred_element_type=F32).astype(BF16)
            return 0

        lax.fori_loop(0, width // 256, part, 0)

    masks = list(reversed(masks_of(n_dp)))

    def partner(mask):
        return me_d + mask - 2 * mask * lax.rem(me_d // mask, 2)

    def share(a, m, mask):
        out = (x_all, dy_all, lens_all)[a]
        own_block = (x_own, dy_own, lens_ref)[a]
        return pltpu.make_async_remote_copy(
            src_ref=own_block if m == 0 else out.at[m],
            dst_ref=out.at[m | mask],
            send_sem=pair_send.at[a, m | mask],
            recv_sem=pair_recv.at[a, m | mask],
            device_id=(partner(mask), me_f),
            device_id_type=pl.DeviceIdType.MESH,
        )

    copies = []

    def keep(a):
        own_block = (x_own, dy_own, lens_ref)[a]
        dsts = (x_all, dy_all, lens_all)[a].at[0], (x_own_ref, dy_own_ref, None)[a]
        for j, dst in enumerate(dsts[: 1 if a == 2 else 2]):
            c = pltpu.make_async_copy(own_block, dst, loc_sem.at[streams + 2 * a + j])
            c.start()
            copies.append(c)

    for mask in masks:
        share(2, 0, mask).start()
    keep(2)
    advance(1)
    place(x_pick, x_own)
    for mask in masks:
        share(0, 0, mask).start()
    keep(0)
    place(dy_pick, dy_own)
    for mask in masks:
        share(1, 0, mask).start()
    keep(1)

    def relay(a):
        held = [0]
        for step, mask in enumerate(masks):
            for m in held:
                if m:
                    share(a, m, mask).start()
            for m in held:
                share(a, m, mask).wait_recv()
            held = held + [m | mask for m in held]

    most = max(max(h) for h in hops)
    for h in range(2, most):
        advance(h)
        if h == 2:
            relay(0)
    if most <= 2:
        relay(0)
    relay(1)
    relay(2)
    for s in range(streams):
        for up in (0, 1):
            if hops[s][up]:
                hop(s, hops[s][up] - 1, up).wait_recv()
    for s in range(streams):
        for up in (0, 1):
            for h in range(hops[s][up]):
                hop(s, h, up).wait_send()
    for a in (0, 1, 2):
        held = [0]
        for mask in masks:
            for m in held:
                share(a, m, mask).wait_send()
            held = held + [m | mask for m in held]
    for c in locals_ + copies:
        c.wait()
    pltpu.make_async_copy(send_ref.at[pl.ds(1, count - 1)], rest, deal_sem.at[0]).wait()


def gather_all(x, dy, meta, dest, lens, blocks, downs, n_dp, n_f):
    streams = len(blocks)
    tok, width = x.shape
    count = n_dp * n_f
    sent = (count, 2 * tok // count, width + 128)
    hops = max(max(d, n_f - 1 - d) for d in downs)
    any_ = pl.BlockSpec(memory_space=pl.ANY)
    vmem = pl.BlockSpec(memory_space=pltpu.VMEM)
    row = jax.ShapeDtypeStruct((tok, width), BF16)
    rows = jax.ShapeDtypeStruct((n_dp, tok, width), BF16)
    return pl.pallas_call(
        functools.partial(gather_kernel, n_dp, n_f, downs),
        in_specs=[vmem] * 5 + [any_] * streams,
        out_specs=[any_] * 5 + [vmem] * 2 + [any_] * streams,
        out_shape=[
            rows,
            rows,
            jax.ShapeDtypeStruct((n_dp,) + lens.shape, lens.dtype),
            row,
            row,
            jax.ShapeDtypeStruct((2 * tok, 128), F32),
            jax.ShapeDtypeStruct((8, tok), F32),
        ]
        + [jax.ShapeDtypeStruct((n_f,) + b.shape, b.dtype) for b in blocks],
        scratch_shapes=[
            pltpu.VMEM(sent, BF16),
            pltpu.VMEM(sent, BF16),
            pltpu.VMEM((tok, width), BF16),
            pltpu.VMEM((tok, width), BF16),
            pltpu.SemaphoreType.DMA((2,)),
            pltpu.SemaphoreType.DMA((streams + 5,)),
            pltpu.SemaphoreType.DMA((3, n_dp)),
            pltpu.SemaphoreType.DMA((3, n_dp)),
            pltpu.SemaphoreType.DMA((streams, 2, hops)),
            pltpu.SemaphoreType.DMA((streams, 2, hops)),
        ],
        compiler_params=pltpu.CompilerParams(
            collective_id=0, has_side_effects=True, vmem_limit_bytes=40 * 2**20
        ),
        cost_estimate=pl.CostEstimate(flops=10**10, bytes_accessed=2 * 10**8, transcendentals=0),
    )(x, dy, meta, dest, lens, *blocks)


def columns_kernel(starts, cs, w_ref, *outs):
    me_d = lax.axis_index("dp")
    for o, out in enumerate(outs):
        for j, start in enumerate(starts[o]):
            out[:, j * cs : (j + 1) * cs] = w_ref[:, pl.ds(pl.multiple_of(start + me_d * cs, 128), cs)]


def take_columns(w, halves, n_f, n_dp, cs):
    inner = n_f * n_dp * cs
    starts = [[h * inner + f * n_dp * cs for f in range(n_f)] for h in range(halves)]
    me_d = lax.axis_index("dp")
    if cs % 128:
        return [
            jnp.concatenate([lax.dynamic_slice_in_dim(w, s + me_d * cs, cs, 1) for s in group], axis=1)
            for group in starts
        ]
    height = w.shape[0]
    blk = min(height, 64)
    return pl.pallas_call(
        functools.partial(columns_kernel, starts, cs),
        grid=(height // blk,),
        in_specs=[pl.BlockSpec((blk, w.shape[1]), lambda i: (i, 0))],
        out_specs=[pl.BlockSpec((blk, n_f * cs), lambda i: (i, 0))] * halves,
        out_shape=[jax.ShapeDtypeStruct((height, n_f * cs), w.dtype)] * halves,
    )(w)


def spread_kernel(cs, x_ref, w_ref, out_ref, sum_ref):
    me_d = lax.axis_index("dp")
    total = jnp.zeros(sum_ref.shape, F32)
    for i in range(x_ref.shape[0]):
        m = me_d + i - 2 * ((me_d // 2 % 2) * (i // 2 % 2) * 2 + (me_d % 2) * (i % 2))
        part = x_ref[m].astype(F32)
        cols = slice(i * cs, (i + 1) * cs)
        out_ref[:, cols] = part
        product = part * w_ref[:, cols].astype(F32)
        for j in range(0, cs, 128):
            total = total + product[:, j : j + 128]

    @pl.when(pl.program_id(0) == 0)
    def _():
        sum_ref[...] = jnp.zeros_like(sum_ref)

    sum_ref[...] += total


def spread_columns(rel, w, cs):
    n_dp, height, cols = rel.shape
    if cs % 128 or n_dp != 4:
        me_d = lax.axis_index("dp")
        parts = [lax.dynamic_index_in_dim(rel, me_d ^ i, 0, keepdims=False) for i in range(n_dp)]
        out = jnp.concatenate(
            [p[:, f * cs : (f + 1) * cs] for f in range(cols // cs) for p in parts], axis=1
        ).astype(F32)
        return out, jnp.sum(out * w.astype(F32), axis=1)
    out, sums = pl.pallas_call(
        functools.partial(spread_kernel, cs),
        grid=(cols // cs,),
        in_specs=[
            pl.BlockSpec((n_dp, height, cs), lambda f: (0, 0, f)),
            pl.BlockSpec((height, n_dp * cs), lambda f: (0, f)),
        ],
        out_specs=[
            pl.BlockSpec((height, n_dp * cs), lambda f: (0, f)),
            pl.BlockSpec((height, 128), lambda f: (0, 0)),
        ],
        out_shape=[jax.ShapeDtypeStruct((height, n_dp * cols), F32), jax.ShapeDtypeStruct((height, 128), F32)],
        cost_estimate=pl.CostEstimate(flops=4 * height * cols * n_dp, bytes_accessed=8 * height * cols * n_dp, transcendentals=0),
    )(rel, w)
    return out, jnp.sum(sums, axis=1)


def per_device(
    tokens,
    cotangent,
    destination,
    lengths,
    norm_gain,
    in_weight,
    conv_weight,
    conv_bias,
    select_weight,
    step_weight,
    step_bias,
    decay_log,
    skip_gain,
    out_weight,
):
    n_dp = lax.axis_size("dp")
    n_f = lax.axis_size("fsdp")
    rows = n_dp * n_f
    tok = tokens.shape[0]
    width = tokens.shape[1]
    pair = tok // rows
    inner = conv_bias.shape[0] * n_f
    cs = conv_bias.shape[0] // n_dp
    ch = cs * n_f
    taps = conv_weight.shape[0]
    n = decay_log.shape[0]
    rank_of = step_weight.shape[0]
    dcols = width // n_f
    group = n_dp * tok
    both = ("dp", "fsdp")
    me_d = lax.axis_index("dp")
    me_f = lax.axis_index("fsdp")
    order = ring_order(n_f)
    place_of = jnp.asarray([order.index(f) for f in range(n_f)], jnp.int32)
    order_arr = jnp.asarray(order, jnp.int32)
    q = place_of[me_f]
    at_ring = [order_arr[(q + k) % n_f] for k in range(n_f)]
    flat_dot = lambda a, b: jnp.dot(a, b, preferred_element_type=F32)
    nt_dot = lambda a, b: lax.dot_general(a, b, (((1,), (1,)), ((), ())), preferred_element_type=F32)
    tn_dot = lambda a, b: lax.dot_general(a, b, (((0,), (0,)), ((), ())), preferred_element_type=F32)

    me = me_d * n_f + me_f
    row_to = destination // tok
    meta = jnp.stack(
        [destination, (row_to - me) % rows, row_to, destination % tok] + [jnp.zeros_like(destination)] * 4
    ).astype(F32)
    segs = lengths.shape[1]
    lens_tile = jnp.pad(lengths, ((0, 7), (0, 128 - segs)))
    slots = jnp.arange(tok, dtype=jnp.int32)

    def mine(shard):
        return lax.dynamic_slice_in_dim(shard.reshape(-1, n_dp * cs), me_d * cs, cs, 1)

    smalls = [conv_weight, conv_bias, step_bias, skip_gain, decay_log, select_weight, step_weight]
    heights = [math.prod(s.shape) // (n_dp * cs) for s in smalls]
    gain_rows = dcols // cs
    used = sum(heights) + gain_rows
    filler = -used % 16
    small_block = jnp.concatenate(
        [mine(s) for s in smalls] + [norm_gain.reshape(gain_rows, cs), jnp.zeros((filler, cs), BF16)], axis=0
    )
    wx_block, wg_block = take_columns(in_weight, 2, n_f, n_dp, cs)
    wo_block = lax.dynamic_slice_in_dim(out_weight, me_d * cs, cs, 0)
    x_all, dy_all, lens_all, x_own, dy_own, tags, ranks, small_all, wx, wg = gather_all(
        tokens, cotangent, meta, destination[:, None].astype(F32), lens_tile,
        [small_block, wx_block, wg_block], [n_f // 2, n_f // 2, n_f - 1 - n_f // 2], n_dp, n_f,
    )
    x_all = x_all.reshape(group, width)
    lens = lens_all[:, 0, :segs]
    from_send = (ranks[0].astype(jnp.int32)[:, None] == slots[None, :]).astype(BF16)
    dy_all = dy_all.reshape(group, width)
    wx = wx.reshape(width, ch)
    wg = wg.reshape(width, ch)
    small = small_all.transpose(1, 0, 2).reshape(used + filler, ch)
    gain = small_all[:, used - gain_rows : used].reshape(width).astype(F32)
    tags = tags.reshape(rows, 2 * pair, 128)[:, :pair, 0].astype(jnp.int32)
    tags = tags[(me - jnp.arange(rows, dtype=jnp.int32)) % rows].reshape(tok)
    from_row = (tags[:, None] == slots[None, :]).astype(BF16)

    valid = (slots < jnp.sum(lengths[0, : segs - 1])).astype(F32)
    x_own32 = x_own.astype(F32)
    square = jnp.sum(x_own32 * x_own32, axis=1)
    mine_sums = [jnp.sum(square * valid), jnp.sum(valid)]

    pieces, at = [], 0
    for height in heights:
        pieces.append(small[at : at + height])
        at += height
    conv_w, conv_b, step_b, skip, dlog, sel, stepw = pieces
    conv_w = conv_w.astype(F32)
    skip = skip.astype(F32)
    rate = -jnp.exp(dlog.astype(F32))

    def shifted(values, lag):
        if lag == 0:
            return values
        edge = jnp.zeros((abs(lag),) + values.shape[1:], values.dtype)
        if lag > 0:
            return jnp.concatenate([edge, values[:-lag]], axis=0)
        return jnp.concatenate([values[-lag:], edge], axis=0)

    within = jnp.arange(tok, dtype=jnp.int32)
    since, left = [], []
    for m in range(n_dp):
        begin, end, total = 0, 0, 0
        for j in range(segs):
            after = total + lens[m, j]
            begin = jnp.where(within >= total, total, begin)
            end = jnp.where(within >= total, after, end)
            total = after
        since.append(within - begin)
        left.append(end - 1 - within)
    since = jnp.concatenate(since)[:, None]
    left = jnp.concatenate(left)[:, None]
    same = [(since >= lag).astype(F32) for lag in range(taps)]
    same_next = [(left >= lag).astype(F32) for lag in range(taps)]
    split = lambda value: [value[m * tok : (m + 1) * tok] for m in range(n_dp)]
    normed, x_in, conv, act, gate, dbl, wo_next = enter(
        lens, x_all, gain[None], wx, wg, conv_w, conv_b.astype(F32), sel, wo_block, n_f
    )
    dbl = dbl.reshape(group, -1)
    rate2 = rate * LOG2E
    scan_out, states, delta, pre, wo = scan_forward(
        lens, dbl, act, stepw, step_b.astype(F32), rate2, skip, wo_block, wo_next, n_f, tok
    )
    wo = wo.reshape(ch, width)
    gate_silu = jax.nn.silu(gate)
    gated = (scan_out * gate_silu).astype(BF16)
    mixed_part = flat_dot(gated, wo).astype(BF16).reshape(n_dp, tok, width)

    gated_grad = nt_dot(dy_all, wo)
    scan_grad = gated_grad * gate_silu
    gate_grad = (gated_grad * scan_out * silu_slope(gate)).astype(BF16)
    wg_grad = tn_dot(normed, gate_grad).astype(BF16)
    wo_grad = tn_dot(gated, dy_all).astype(BF16)
    wo_own = ring_reduce(
        lambda k: lax.dynamic_slice_in_dim(wo_grad, at_ring[k] * cs, cs, 0), n_f, n_f - 1 - n_f // 2, BF16
    )
    pre_grad, act_grad, dbl_grad, decay_sum, sums, step_grad, wg_own, mixed = scan_backward(
        lens, dbl, delta, pre, act, scan_grad, stepw, rate2, skip, states,
        wg_grad.reshape(n_f, dcols, ch), mixed_part, n_f, tok,
    )
    dbl_grad = dbl_grad.reshape(group, -1).astype(BF16)
    act_grad = act_grad + flat_dot(dbl_grad, sel)
    conv_grad = act_grad * silu_slope(conv)
    in_grad = sum(
        conv_w[taps - 1 - lag][None] * shifted(conv_grad, -lag) * same_next[lag] for lag in range(taps)
    ).astype(BF16)
    wx_grad = tn_dot(normed, in_grad).astype(BF16)
    wx_own = ring_reduce(
        lambda k: lax.dynamic_slice_in_dim(wx_grad, at_ring[k] * dcols, dcols, 0), n_f, n_f // 2, BF16
    )
    normed_grad_part = (nt_dot(in_grad, wx) + nt_dot(gate_grad, wg)).astype(BF16)
    normed_grad = group_reduce(split(normed_grad_part), n_dp, BF16)

    tap_grads = [
        jnp.sum(conv_grad * shifted(x_in, taps - 1 - tap) * same[taps - 1 - tap], axis=0) for tap in range(taps)
    ]
    small_grads = jnp.concatenate(
        [jnp.stack(tap_grads)]
        + [
            jnp.sum(conv_grad, axis=0, keepdims=True),
            sums[:2],
            decay_sum * rate,
            tn_dot(dbl_grad, act),
            step_grad,
            jnp.zeros((-sum(heights) % 16, ch), F32),
        ],
        axis=0,
    )
    small_own = ring_reduce(
        lambda k: lax.dynamic_slice_in_dim(small_grads, at_ring[k] * cs, cs, 1), n_f, n_f - 1 - n_f // 2, F32
    )

    def in_group_order(blocks):
        stacked = jnp.stack(blocks)
        return [lax.dynamic_index_in_dim(stacked, me_d ^ i, 0, keepdims=False) for i in range(n_dp)]

    def interleaved(blocks):
        return jnp.stack(in_group_order(blocks), axis=1)

    own_in = jnp.concatenate(
        [
            jnp.stack(group_gather(wx_own.astype(BF16), n_dp)),
            jnp.stack(group_gather(wg_own.astype(BF16), n_dp)),
        ],
        axis=2,
    )
    grad_in_weight, gain_sum = spread_columns(own_in, in_weight, cs)
    grad_out_weight = jnp.concatenate(in_group_order(group_gather(wo_own.astype(BF16), n_dp)), axis=0).astype(F32)
    small_full = interleaved(group_gather(small_own, n_dp)).reshape(-1, n_dp * cs)
    out_small, at = [], 0
    for height, s in zip(heights, smalls):
        out_small.append(small_full[at : at + height].reshape(s.shape))
        at += height
    grad_norm_gain = gain_sum / norm_gain.astype(F32)

    rstd = lax.rsqrt(jnp.mean(x_own32 * x_own32, axis=1, keepdims=True) + EPS)
    hat = x_own32 * rstd
    hat_grad = normed_grad * gain[None]
    change = rstd * (hat_grad - hat * jnp.mean(hat_grad * hat, axis=1, keepdims=True))
    row_grad = (dy_own.astype(F32) + change).astype(BF16)

    def returned(value):
        cols = value.shape[1]
        out = flat_dot(from_row, value).astype(BF16).reshape(rows, pair, cols)
        back = lax.all_to_all(out, both, 0, 0, tiled=True).reshape(tok, cols)
        return flat_dot(from_send, back).astype(BF16)

    lanes = lax.broadcasted_iota(jnp.int32, (tok, 128), 1)
    ride = jnp.zeros((tok, 128), F32)
    for j, value in enumerate(mine_sums):
        high = value.astype(BF16).astype(F32)
        ride = ride + jnp.where(lanes == 2 * j, high, 0.0) + jnp.where(lanes == 2 * j + 1, value - high, 0.0)
    out = flat_dot(from_row, mixed.astype(BF16)).astype(BF16)
    out = jnp.concatenate([out, ride.astype(BF16)], axis=1).reshape(rows, pair, width + 128)
    back = lax.all_to_all(out, both, 0, 0, tiled=True).reshape(tok, width + 128)
    totals = jnp.sum(back.reshape(rows, pair, -1)[:, 0, width : width + 4].astype(F32), axis=0)
    input_rms = jnp.sqrt((totals[0] + totals[1]) / ((totals[2] + totals[3]) * width))
    mixer_output = flat_dot(from_send, back[:, :width])
    layer_output = (tokens.astype(F32) + mixer_output).astype(BF16)
    mixer_output = mixer_output.astype(BF16)
    input_grad = returned(row_grad)
    return (
        layer_output,
        mixer_output,
        input_grad,
        input_rms,
        grad_norm_gain,
        grad_in_weight,
        out_small[0],
        out_small[1],
        out_small[5],
        out_small[6],
        out_small[2],
        out_small[4],
        out_small[3],
        grad_out_weight,
    )


def solution(mesh):
    return jax.shard_map(
        per_device,
        mesh=mesh,
        in_specs=(
            P(("dp", "fsdp"), None),
            P(("dp", "fsdp"), None),
            P(("dp", "fsdp")),
            P(("dp", "fsdp"), None),
            P("fsdp"),
            P("fsdp", None),
            P(None, "fsdp"),
            P("fsdp"),
            P(None, "fsdp"),
            P(None, "fsdp"),
            P("fsdp"),
            P(None, "fsdp"),
            P("fsdp"),
            P("fsdp", None),
        ),
        out_specs=(
            P(("dp", "fsdp"), None),
            P(("dp", "fsdp"), None),
            P(("dp", "fsdp"), None),
            P(),
            P("fsdp"),
            P("fsdp", None),
            P(None, "fsdp"),
            P("fsdp"),
            P(None, "fsdp"),
            P(None, "fsdp"),
            P("fsdp"),
            P(None, "fsdp"),
            P("fsdp"),
            P("fsdp", None),
        ),
        check_vma=False,
    )
```

```python
import functools
import math

import jax
import jax.numpy as jnp
from jax import lax
from jax.experimental import pallas as pl
from jax.experimental.pallas import tpu as pltpu
from jax.sharding import PartitionSpec as P

EPS = 1e-05
TB = 16
LOG2E = math.log2(math.e)
RESET = 1.0e4
BF16 = jnp.bfloat16
F32 = jnp.float32


def silu_slope(value):
    sigma = jax.nn.sigmoid(value)
    return sigma * (1.0 + value * (1.0 - sigma))


def row_at(g, n_dp):
    return lax.rem(2 * g + 1, n_dp + 1)


def flip(d, mask):
    return d + mask - 2 * mask * lax.rem(d // mask, 2)


class GroupSum:
    def __init__(self, part, near, far, total, send, recv):
        self.part, self.near, self.far, self.total = part, near, far, total
        me_d, me_f = lax.axis_index("dp"), lax.axis_index("fsdp")
        plan = [
            (part.at[1], near.at[0], 1),
            (part.at[3], near.at[1], 1),
            (part.at[0], far.at[1], 2),
            (part.at[2], far.at[0], 2),
            (total.at[0], total.at[1], 1),
            (total.at[2], total.at[3], 1),
        ]
        self.copies = [
            pltpu.make_async_remote_copy(
                src_ref=src,
                dst_ref=dst,
                send_sem=send.at[i],
                recv_sem=recv.at[i],
                device_id=(flip(me_d, mask), me_f),
                device_id_type=pl.DeviceIdType.MESH,
            )
            for i, (src, dst, mask) in enumerate(plan)
        ]

    def row_done(self, g):
        for j in (0, 1):

            @pl.when(g == j)
            def _(j=j):
                self.copies[j].start()

            @pl.when(g == j + 2)
            def _(j=j):
                self.copies[j].wait_recv()
                self.part[2 * j] = self.part[2 * j] + self.near[j]
                self.copies[j + 2].start()

    def first(self):
        for j in (0, 1):
            self.copies[j].start()

    def second(self):
        for j in (0, 1):
            self.copies[j].wait_recv()
            self.part[2 * j] = self.part[2 * j] + self.near[j]
            self.copies[j + 2].start()

    def finish(self):
        for j in (0, 1):
            self.copies[3 - j].wait_recv()
            self.total[2 * j] = self.part[2 * j] + self.far[j]
            self.copies[4 + j].start()
        for j in (0, 1):
            self.copies[4 + j].wait_recv()
        for c in self.copies:
            c.wait_send()

    @staticmethod
    def scratch(tok, wide):
        return [
            pltpu.VMEM((4, tok, wide), F32),
            pltpu.VMEM((2, tok, wide), F32),
            pltpu.VMEM((2, tok, wide), F32),
            pltpu.VMEM((4, tok, wide), F32),
            pltpu.SemaphoreType.DMA((6,)),
            pltpu.SemaphoreType.DMA((6,)),
        ]


class RingReduce:
    def __init__(self, n_f, part, got, send, recv, down):
        self.part, self.got = part, got
        q = ring_place(lax.axis_index("fsdp"), n_f)
        self.at = lambda k: ring_index(lax.rem(q + k, n_f), n_f)
        self.n_f = n_f
        self.counts = [down, n_f - 1 - down]
        self.copies = [[], []]
        for up in (0, 1):
            for h in range(self.counts[up]):
                src = part.at[self.at(self.goal(up, 0))] if h == 0 else got.at[up, h - 1]
                self.copies[up].append(ring_copy(n_f, src, got.at[up, h], send.at[up, h], recv.at[up, h], up))
        self.events = max(self.counts)

    def goal(self, up, h):
        left = self.counts[up] - h
        return left if up else self.n_f - left

    def add(self, slot, addend):
        rows = slot.shape[0]
        step = min(rows, 64)

        def piece(i, _):
            at = pl.ds(pl.multiple_of(i * step, step), step)
            slot[at, :] = (slot[at, :].astype(F32) + addend[at, :].astype(F32)).astype(slot.dtype)
            return 0

        lax.fori_loop(0, rows // step, piece, 0)

    def start(self):
        for up in (0, 1):
            if self.copies[up]:
                self.copies[up][0].start()

    def event(self, e):
        for up in (0, 1):
            if e < self.counts[up]:
                self.copies[up][e - 1].wait_recv()
                self.add(self.got.at[up, e - 1], self.part.at[self.at(self.goal(up, e))])
                self.copies[up][e].start()

    def finish(self, out):
        last = []
        for up in (0, 1):
            if self.copies[up]:
                self.copies[up][-1].wait_recv()
                last.append(self.got.at[up, self.counts[up] - 1])
        mine = self.part.at[self.at(0)]
        rows = mine.shape[0]
        step = min(rows, 64)

        def piece(i, _):
            at = pl.ds(pl.multiple_of(i * step, step), step)
            total_ = mine[at, :].astype(F32)
            for slot in last:
                total_ = total_ + slot[at, :].astype(F32)
            out[at, :] = total_.astype(out.dtype)
            return 0

        lax.fori_loop(0, rows // step, piece, 0)
        for up in (0, 1):
            for c in self.copies[up]:
                c.wait_send()

    @staticmethod
    def scratch(n_f, block, dtype=BF16):
        return [
            pltpu.VMEM((2, n_f // 2) + block, dtype),
            pltpu.SemaphoreType.DMA((2, n_f // 2)),
            pltpu.SemaphoreType.DMA((2, n_f // 2)),
        ]


class PairReduce:
    def __init__(self, part, near, far, send, recv):
        self.part, self.near, self.far = part, near, far
        me_d, me_f = lax.axis_index("dp"), lax.axis_index("fsdp")
        plan = [
            (part.at[1], near.at[0], 1),
            (part.at[3], near.at[1], 1),
            (part.at[2], far, 2),
        ]
        self.copies = [
            pltpu.make_async_remote_copy(
                src_ref=src,
                dst_ref=dst,
                send_sem=send.at[i],
                recv_sem=recv.at[i],
                device_id=(flip(me_d, mask), me_f),
                device_id_type=pl.DeviceIdType.MESH,
            )
            for i, (src, dst, mask) in enumerate(plan)
        ]

    def start(self):
        for c in self.copies[:2]:
            c.start()

    def middle(self):
        self.copies[1].wait_recv()
        rows_add(self.part.at[2], [self.part.at[2], self.near.at[1]])
        self.copies[2].start()
        self.copies[0].wait_recv()

    def finish(self, out):
        self.copies[2].wait_recv()
        rows_add(out, [self.part.at[0], self.near.at[0], self.far])
        for c in self.copies:
            c.wait_send()

    @staticmethod
    def scratch(block, dtype=BF16):
        return [
            pltpu.VMEM((2,) + block, dtype),
            pltpu.VMEM(block, dtype),
            pltpu.SemaphoreType.DMA((3,)),
            pltpu.SemaphoreType.DMA((3,)),
        ]


def rows_add(out, terms, step=32):
    def piece(i, _):
        at = pl.ds(pl.multiple_of(i * step, step), step)
        total_ = terms[0][at, :].astype(F32)
        for t in terms[1:]:
            total_ = total_ + t[at, :].astype(F32)
        out[at, :] = total_.astype(out.dtype)
        return 0

    lax.fori_loop(0, out.shape[0] // step, piece, 0)


def greet_neighbours(n_f, ring):
    me_d, me_f = lax.axis_index("dp"), lax.axis_index("fsdp")
    barrier = pltpu.get_barrier_semaphore()
    others = [(flip(me_d, 1), me_f), (flip(me_d, 2), me_f)]
    if ring:
        q = ring_place(me_f, n_f)
        others.append((me_d, ring_index(lax.rem(q + n_f - 1, n_f), n_f)))
        others.append((me_d, ring_index(lax.rem(q + 1, n_f), n_f)))
    for other in others:
        pl.semaphore_signal(barrier, inc=1, device_id=other, device_id_type=pl.DeviceIdType.MESH)
    pl.semaphore_wait(barrier, len(others))


def ring_copy(n_f, src, dst, send, recv, up):
    me_d, me_f = lax.axis_index("dp"), lax.axis_index("fsdp")
    q = ring_place(me_f, n_f)
    to = ring_index(lax.rem(q + (1 if up else n_f - 1), n_f), n_f)
    return pltpu.make_async_remote_copy(
        src_ref=src,
        dst_ref=dst,
        send_sem=send,
        recv_sem=recv,
        device_id=(me_d, to),
        device_id_type=pl.DeviceIdType.MESH,
    )


def segment_span(lens_ref, m, first, rows):
    t = lax.broadcasted_iota(jnp.int32, (rows, 1), 0) + first
    begin = jnp.zeros((rows, 1), jnp.int32)
    end = jnp.zeros((rows, 1), jnp.int32)
    total = jnp.int32(0)
    for j in range(lens_ref.shape[1]):
        after = total + lens_ref[m, j]
        inside = t >= total
        begin = jnp.where(inside, total, begin)
        end = jnp.where(inside, after, end)
        total = after
    return t - begin, end - 1 - t


def enter_kernel(n_f, half, lens_ref, x_ref, gain_ref, wx_ref, wg_ref, taps_ref, bias_ref, sel_ref, wo_ref,
                 normed_ref, xin_ref, conv_ref, act_ref, gate_ref, dbl_ref, next_ref,
                 part, near, far, total, gs_send, gs_recv, hop_send, hop_recv):
    g = pl.program_id(0)
    n_dp, tok = part.shape[:2]
    rows, width = x_ref.shape
    hops = [ring_copy(n_f, wo_ref, next_ref.at[up, 0], hop_send.at[up, 0], hop_recv.at[up, 0], up) for up in (0, 1)]
    hops2 = [
        ring_copy(n_f, next_ref.at[up, 0], next_ref.at[up, 1], hop_send.at[up, 1], hop_recv.at[up, 1], up)
        for up in (0, 1)
    ]
    group = GroupSum(part, near, far, total, gs_send, gs_recv)

    @pl.when(g == 0)
    def _():
        greet_neighbours(n_f, True)
        for c in hops:
            c.start()
        part[...] = jnp.zeros_like(part)

        def norm(i, _):
            at = pl.ds(pl.multiple_of(i * 32, 32), 32)
            v = x_ref[at, :].astype(F32)
            rstd = lax.rsqrt(jnp.mean(v * v, axis=1, keepdims=True) + EPS)
            normed_ref[at, :] = (v * rstd * gain_ref[...]).astype(BF16)
            return 0

        lax.fori_loop(0, rows // 32, norm, 0)

    @pl.when(g == half)
    def _():
        for a, b in zip(hops, hops2):
            a.wait_recv()
            b.start()

    @pl.when(g < half)
    def _():
        n_taps = taps_ref.shape[0]
        for m in range(n_dp):
            at = slice(m * tok, (m + 1) * tok)
            v = jnp.dot(normed_ref[at, :], wx_ref[...], preferred_element_type=F32)
            since, _ = segment_span(lens_ref, m, 0, tok)
            xin_ref[at, :] = v
            conv = bias_ref[...] + taps_ref[n_taps - 1 : n_taps, :] * v
            for lag in range(1, n_taps):
                keep = (since >= lag).astype(F32)
                conv = conv + taps_ref[n_taps - 1 - lag : n_taps - lag, :] * (pltpu.roll(v, lag, 0) * keep)
            conv_ref[at, :] = conv
            act = jax.nn.silu(conv).astype(BF16)
            act_ref[at, :] = act
            part[m] += lax.dot_general(act, sel_ref[...], (((1,), (1,)), ((), ())), preferred_element_type=F32)

    @pl.when(g == half - 1)
    def _():
        group.first()

    @pl.when(g >= half)
    def _():
        for m in range(n_dp):
            at = slice(m * tok, (m + 1) * tok)
            gate_ref[at, :] = jnp.dot(normed_ref[at, :], wg_ref[...], preferred_element_type=F32)

    @pl.when(g == half)
    def _():
        group.second()

    @pl.when(g == 2 * half - 1)
    def _():
        group.finish()
        dbl_ref[...] = total[...]
        for a, b in zip(hops, hops2):
            a.wait_send()
            b.wait()


def enter(lens, x_all, gain, wx, wg, taps, bias, sel, wo_block, n_f):
    n_dp = lens.shape[0]
    rows, width = x_all.shape
    tok = rows // n_dp
    ch = wx.shape[1]
    wide = sel.shape[0]
    piece = 256
    half = ch // piece
    whole = lambda g: (0, 0)
    early = lambda g: (0, jnp.minimum(g, half - 1))
    late = lambda g: (0, jnp.maximum(g - half, 0))
    once = pl.Buffered(1)
    any_ = pl.BlockSpec(memory_space=pl.ANY)
    shaped = lambda d, t: jax.ShapeDtypeStruct((rows, d), t)
    return pl.pallas_call(
        functools.partial(enter_kernel, n_f, half),
        grid=(2 * half,),
        in_specs=[
            pl.BlockSpec(memory_space=pltpu.SMEM),
            pl.BlockSpec((rows, width), whole, pipeline_mode=once),
            pl.BlockSpec((1, width), whole),
            pl.BlockSpec((width, piece), early),
            pl.BlockSpec((width, piece), late),
            pl.BlockSpec((taps.shape[0], piece), early),
            pl.BlockSpec((1, piece), early),
            pl.BlockSpec((wide, piece), early),
            any_,
        ],
        out_specs=[
            pl.BlockSpec((rows, width), whole),
            pl.BlockSpec((rows, piece), early),
            pl.BlockSpec((rows, piece), early),
            pl.BlockSpec((rows, piece), early),
            pl.BlockSpec((rows, piece), late),
            pl.BlockSpec((n_dp, tok, wide), lambda g: (0, 0, 0)),
            any_,
        ],
        out_shape=[
            shaped(width, BF16),
            shaped(ch, F32),
            shaped(ch, F32),
            shaped(ch, BF16),
            shaped(ch, F32),
            jax.ShapeDtypeStruct((n_dp, tok, wide), F32),
            jax.ShapeDtypeStruct((2, 2) + wo_block.shape, BF16),
        ],
        scratch_shapes=GroupSum.scratch(tok, wide)
        + [pltpu.SemaphoreType.DMA((2, 2)), pltpu.SemaphoreType.DMA((2, 2))],
        compiler_params=pltpu.CompilerParams(
            collective_id=1, has_side_effects=True, vmem_limit_bytes=48 * 2**20
        ),
        cost_estimate=pl.CostEstimate(flops=10**10, bytes_accessed=4 * 10**7, transcendentals=10**6),
    )(lens, x_all, gain, wx, wg, taps, bias, sel, wo_block)


def fold_matrix(n):
    i = lax.broadcasted_iota(jnp.int32, (n, TB * n), 0)
    j = lax.broadcasted_iota(jnp.int32, (n, TB * n), 1)
    return jnp.where(lax.rem(j, n) == i, 1.0, 0.0)


def own_token(n):
    i = lax.broadcasted_iota(jnp.int32, (TB, TB * n), 0)
    j = lax.broadcasted_iota(jnp.int32, (TB, TB * n), 1)
    return i == j // n


def block_rows(m, n):
    spread = jnp.dot(m.astype(BF16), fold_matrix(n).astype(BF16), preferred_element_type=F32)
    i = lax.broadcasted_iota(jnp.int32, spread.shape, 0)
    j = lax.broadcasted_iota(jnp.int32, spread.shape, 1)
    return jnp.where(lax.rem(i, TB) == j // n, spread, 0.0).astype(BF16)


def turned(m):
    n = m.shape[1]
    i = lax.broadcasted_iota(jnp.int32, (n, n), 0)
    j = lax.broadcasted_iota(jnp.int32, (n, n), 1)
    eye = jnp.where(i == j, 1.0, 0.0)
    return lax.dot_general(
        eye, m, (((1,), (1,)), ((), ())), preferred_element_type=F32, precision=lax.Precision.HIGHEST
    )


def softplus(v):
    return jnp.maximum(v, 0.0) + jnp.log1p(jnp.exp(-jnp.abs(v)))


class RingGather:
    def __init__(self, n_f, mine, near, out, local, send, recv):
        q = ring_place(lax.axis_index("fsdp"), n_f)
        at = lambda k: ring_index(lax.rem(q + k, n_f), n_f)
        count = [n_f // 2, n_f - 1 - n_f // 2]
        known = near.shape[1]
        self.locals = [pltpu.make_async_copy(mine, out.at[at(0)], local.at[0])]
        self.hops = [[], []]
        for up in (0, 1):
            for j in range(known):
                index = at(n_f - 1 - j if up else 1 + j)
                self.locals.append(pltpu.make_async_copy(near.at[up, j], out.at[index], local.at[1 + known * up + j]))
            for h in range(known, count[up]):
                index = at(n_f - h if up else h)
                src = near.at[up, known - 1] if h == known else out.at[index]
                self.hops[up].append(
                    ring_copy(n_f, src, out.at[index], send.at[up, h], recv.at[up, h], up)
                )
        self.events = max(len(h) for h in self.hops)

    def start(self):
        for c in self.locals:
            c.start()
        for up in (0, 1):
            if self.hops[up]:
                self.hops[up][0].start()

    def event(self, e):
        for up in (0, 1):
            if e < len(self.hops[up]):
                self.hops[up][e - 1].wait_recv()
                self.hops[up][e].start()

    def finish(self):
        for up in (0, 1):
            if self.hops[up]:
                self.hops[up][-1].wait_recv()
            for c in self.hops[up]:
                c.wait_send()
        for c in self.locals:
            c.wait()


def fwd_kernel(lanes, n_f, lens_ref, dbl_ref, act_ref, stepw_ref, stepb_ref, rate_ref, skip_ref, wo_ref, next_ref,
               y_ref, s_ref, delta_ref, pre_ref, wo_all, carry, big_s, cw_s, bt_s, d_s, u_s, sc, local, hop_send, hop_recv):
    n, ch = rate_ref.shape
    tblk = act_ref.shape[0]
    low_n = stepw_ref.shape[0]
    steps = pl.num_programs(0) * pl.num_programs(1)
    now = pl.program_id(0) * pl.num_programs(1) + pl.program_id(1)
    ring = RingGather(n_f, wo_ref, next_ref, wo_all, local, hop_send, hop_recv)

    @pl.when(now == 0)
    def _():
        greet_neighbours(n_f, True)
        ring.start()

    for e in range(1, ring.events):

        @pl.when(now == min(7 * e, 15))
        def _(e=e):
            ring.event(e)

    @pl.when(pl.program_id(1) == 0)
    def _():
        carry[...] = jnp.zeros_like(carry)

    pre = jnp.dot(dbl_ref[:, :low_n].astype(BF16), stepw_ref[...], preferred_element_type=F32) + stepb_ref[...]
    pre_ref[...] = pre
    delta_ref[...] = softplus(pre)
    since, _ = segment_span(lens_ref, pl.program_id(0), pl.program_id(1) * tblk, tblk)
    big_s[...] = jnp.where(since == 0, RESET, 0.0)
    cw_s[...] = block_rows(dbl_ref[:, low_n + n : low_n + 2 * n], n)
    flat = turned(dbl_ref[:, low_n : low_n + n])
    for i in range(tblk // TB):
        bt_s[i] = flat[:, i * TB : (i + 1) * TB]

    def chunk(i, _):
        base = pl.multiple_of(i * TB, TB)
        dl = delta_ref[pl.ds(base, TB), :]
        ac = act_ref[pl.ds(base, TB), :].astype(F32)
        d_s[...] = dl + big_s[pl.ds(base, TB), :]
        u_s[...] = dl * ac
        bt = bt_s[i]
        for lo in range(0, ch, lanes):
            cs = pl.ds(lo, lanes)
            rate = rate_ref[:, cs]
            s = carry[:, cs]
            for t in range(TB):
                dec = jnp.exp2(d_s[t : t + 1, cs] * rate)
                s = dec * s + bt[:, t : t + 1] * u_s[t : t + 1, cs]
                sc[t * n : (t + 1) * n, cs] = s.astype(BF16)
            carry[:, cs] = s
        states = sc[...]
        y = jnp.dot(cw_s[pl.ds(base, TB), :], states, preferred_element_type=F32)
        y_ref[pl.ds(base, TB), :] = y + skip_ref[...] * ac
        s_ref[pl.ds(pl.multiple_of(base * n, TB * n), TB * n), :] = states
        return 0

    lax.fori_loop(0, tblk // TB, chunk, 0)

    @pl.when(now == steps - 1)
    def _():
        ring.finish()


def scan_forward(lens, dbl, act, stepw, stepb, rate2, skip, wo_block, wo_next, n_f, row_len, tblk=64, lanes=512):
    t, ch = act.shape
    n = rate2.shape[0]
    nb = row_len // tblk
    at = lambda r, j: (r * nb + j, 0)
    zero = lambda r, j: (0, 0)
    any_ = pl.BlockSpec(memory_space=pl.ANY)
    wide = jax.ShapeDtypeStruct((t, ch), F32)
    return pl.pallas_call(
        functools.partial(fwd_kernel, min(lanes, ch), n_f),
        grid=(t // row_len, nb),
        in_specs=[
            pl.BlockSpec(memory_space=pltpu.SMEM),
            pl.BlockSpec((tblk, dbl.shape[1]), at),
            pl.BlockSpec((tblk, ch), at),
            pl.BlockSpec(stepw.shape, zero),
            pl.BlockSpec((1, ch), zero),
            pl.BlockSpec((n, ch), zero),
            pl.BlockSpec((1, ch), zero),
            any_,
            any_,
        ],
        out_specs=[
            pl.BlockSpec((tblk, ch), at),
            pl.BlockSpec((tblk * n, ch), at),
            pl.BlockSpec((tblk, ch), at),
            pl.BlockSpec((tblk, ch), at),
            any_,
        ],
        out_shape=[
            wide,
            jax.ShapeDtypeStruct((t * n, ch), BF16),
            wide,
            wide,
            jax.ShapeDtypeStruct((n_f,) + wo_block.shape, BF16),
        ],
        scratch_shapes=[
            pltpu.VMEM((n, ch), F32),
            pltpu.VMEM((tblk, 1), F32),
            pltpu.VMEM((tblk, TB * n), BF16),
            pltpu.VMEM((tblk // TB, n, TB), F32),
            pltpu.VMEM((TB, ch), F32),
            pltpu.VMEM((TB, ch), F32),
            pltpu.VMEM((TB * n, ch), BF16),
            pltpu.SemaphoreType.DMA((5,)),
            pltpu.SemaphoreType.DMA((2, n_f)),
            pltpu.SemaphoreType.DMA((2, n_f)),
        ],
        compiler_params=pltpu.CompilerParams(
            collective_id=2, has_side_effects=True, vmem_limit_bytes=32 * 2**20
        ),
        cost_estimate=pl.CostEstimate(flops=t * n * ch * 40, bytes_accessed=t * ch * 52, transcendentals=t * n * ch),
    )(lens, dbl, act, stepw, stepb, rate2, skip, wo_block, wo_next)


def bwd_kernel(lanes, n_f, lens_ref, dbl_ref, delta_ref, pre_ref, act_ref, gy_ref, stepw_ref, rate_ref, skip_ref,
               s_ref, sp_ref, wg_part, mixed_part,
               pg_ref, da_ref, dbl_grad_ref, dl_ref, sums_ref, stepg_ref, wg_own, mixed_own,
               carry, big_s, bw_s, ct_s, d_all, u_all, g_all, h_all, b_all, c_all, part, near, far, total, gs_send, gs_recv,
               ring_got, ring_send, ring_recv, mix, mix_near, mix_far, mix_send, mix_recv, mix_load):
    n, ch = rate_ref.shape
    tblk = act_ref.shape[0]
    low_n = stepw_ref.shape[0]
    r, j = pl.program_id(0), pl.program_id(1)
    n_dp, nb = pl.num_programs(0), pl.num_programs(1)
    m = row_at(r, n_dp)
    group = GroupSum(part, near, far, total, gs_send, gs_recv)
    ring = RingReduce(n_f, wg_part, ring_got, ring_send, ring_recv, n_f // 2)
    pairs = PairReduce(mix, mix_near, mix_far, mix_send, mix_recv)
    now = r * nb + j
    last_step = n_dp * nb - 1
    @pl.when(j == 0)
    def _():
        carry[...] = jnp.zeros_like(carry)

    @pl.when((r == 0) & (j == 0))
    def _():
        load = pltpu.make_async_copy(mixed_part, mix, mix_load)
        load.start()
        greet_neighbours(n_f, True)
        ring.start()
        load.wait()
        pairs.start()
        dl_ref[...] = jnp.zeros_like(dl_ref)
        sums_ref[...] = jnp.zeros_like(sums_ref)
        stepg_ref[...] = jnp.zeros_like(stepg_ref)

    for e in range(1, ring.events):

        @pl.when(now == min(4 * e, 15))
        def _(e=e):
            ring.event(e)

    @pl.when(now == 2)
    def _():
        pairs.middle()

    @pl.when(now == 12)
    def _():
        pairs.finish(mixed_own)

    ones = jnp.where(own_token(n), 1.0, 0.0).astype(BF16)
    nt = (((1,), (1,)), ((), ()))
    row = lax.broadcasted_iota(jnp.int32, (TB * n, n), 0)
    col = lax.broadcasted_iota(jnp.int32, (TB * n, n), 1)
    fold = jnp.where(lax.rem(row, n) == col, 1.0, 0.0)
    since, _ = segment_span(lens_ref, m, (nb - 1 - j) * tblk, tblk)
    big_s[...] = jnp.where(since == 0, RESET, 0.0)
    bw_s[...] = block_rows(dbl_ref[:, low_n : low_n + n], n)

    flat = turned(dbl_ref[:, low_n + n : low_n + 2 * n])
    for i in range(tblk // TB):
        ct_s[i] = flat[:, i * TB : (i + 1) * TB]

    def lane_sum(value):
        total_ = value[:, :128]
        for at in range(128, value.shape[1], 128):
            total_ = total_ + value[:, at : at + 128]
        return total_

    def gathered(sums):
        spread = jnp.sum(sums, axis=1, keepdims=True) * fold
        high = spread.astype(BF16)
        rest = (spread - high.astype(F32)).astype(BF16)
        return jnp.dot(ones, high, preferred_element_type=F32) + jnp.dot(ones, rest, preferred_element_type=F32)

    for i in reversed(range(tblk // TB)):
        base = i * TB
        d_s, u_s, g_s, h_s, b_s, c_s = (v.at[i % 2] for v in (d_all, u_all, g_all, h_all, b_all, c_all))
        dl = delta_ref[base : base + TB, :]
        ac = act_ref[base : base + TB, :].astype(F32)
        d_s[...] = dl + big_s[base : base + TB, :]
        u_s[...] = dl * ac
        ct = ct_s[i]
        for lo in range(0, ch, lanes):
            cs = pl.ds(lo, lanes)
            rate = rate_ref[:, cs]
            flow = carry[:, cs]
            acc = dl_ref[:, cs]
            here = s_ref[(base + TB - 1) * n : (base + TB) * n, cs].astype(F32)
            for t in reversed(range(TB)):
                dr = d_s[t : t + 1, cs]
                dec = jnp.exp2(dr * rate)
                gy = gy_ref[base + t : base + t + 1, cs]
                g = ct[:, t : t + 1] * gy + flow
                flow = dec * g
                if base + t > 0:
                    prev = s_ref[(base + t - 1) * n : (base + t) * n, cs].astype(F32)
                else:
                    prev = sp_ref[:, cs].astype(F32)
                h = flow * prev
                acc = acc + h * dr
                at = slice(t * n, (t + 1) * n)
                b_now = lane_sum(g * u_s[t : t + 1, cs])
                c_now = lane_sum(here * gy)
                if lo:
                    b_now = b_now + b_s[at, :]
                    c_now = c_now + c_s[at, :]
                b_s[at, :] = b_now
                c_s[at, :] = c_now
                here = prev
                g_s[t * n : (t + 1) * n, cs] = g.astype(BF16)
                h_s[t * n : (t + 1) * n, cs] = (h * rate).astype(BF16)
            carry[:, cs] = flow
            dl_ref[:, cs] = acc
        gb = g_s[...]
        gy = gy_ref[base : base + TB, :]
        du = jnp.dot(bw_s[base : base + TB, :], gb, preferred_element_type=F32)
        hr = jnp.dot(ones, h_s[...], preferred_element_type=F32)
        dd = hr * (1.0 / LOG2E) + du * ac
        pg_ref[base : base + TB, :] = (dd * jax.nn.sigmoid(pre_ref[base : base + TB, :])).astype(BF16)
        da_ref[base : base + TB, :] = du * dl + skip_ref[...] * gy
        at = pl.ds(pl.multiple_of((nb - 1 - j) * tblk + base, TB), TB)
        part[m, at, low_n : low_n + n] = gathered(b_s[...])
        part[m, at, low_n + n : low_n + 2 * n] = gathered(c_s[...])

    pg = pg_ref[...]
    part[m, pl.ds(pl.multiple_of((nb - 1 - j) * tblk, tblk), tblk), :low_n] = lax.dot_general(
        pg, stepw_ref[...], nt, preferred_element_type=F32
    )
    stepg_ref[...] += lax.dot_general(
        dbl_ref[:, :low_n].astype(BF16), pg, (((0,), (0,)), ((), ())), preferred_element_type=F32
    )
    sums_ref[0:1, :] += jnp.sum(pg.astype(F32), axis=0, keepdims=True)
    sums_ref[1:2, :] += jnp.sum(gy_ref[...] * act_ref[...].astype(F32), axis=0, keepdims=True)

    @pl.when(j == nb - 1)
    def _():
        group.row_done(r)

    @pl.when((j == nb - 1) & (r == n_dp - 1))
    def _():
        ring.finish(wg_own)
        group.finish()
        dbl_grad_ref[...] = total[...]


def scan_backward(lens, dbl, delta, pre, act, gy, stepw, rate2, skip, states, wg_part, mixed_part, n_f, row_len,
                  tblk=64, lanes=512):
    t, ch = delta.shape
    n = rate2.shape[0]
    nb = row_len // tblk
    n_dp = t // row_len
    wide = dbl.shape[1]
    spot = lambda r, j: row_at(r, n_dp) * nb + nb - 1 - j
    at = lambda r, j: (spot(r, j), 0)
    zero = lambda r, j: (0, 0)
    entry = lambda r, j: (jnp.maximum(spot(r, j) * tblk - 1, 0), 0)
    return pl.pallas_call(
        functools.partial(bwd_kernel, min(lanes, ch), n_f),
        grid=(n_dp, nb),
        in_specs=[
            pl.BlockSpec(memory_space=pltpu.SMEM),
            pl.BlockSpec((tblk, wide), at),
            pl.BlockSpec((tblk, ch), at),
            pl.BlockSpec((tblk, ch), at),
            pl.BlockSpec((tblk, ch), at),
            pl.BlockSpec((tblk, ch), at),
            pl.BlockSpec(stepw.shape, zero),
            pl.BlockSpec((n, ch), zero),
            pl.BlockSpec((1, ch), zero),
            pl.BlockSpec((tblk * n, ch), at),
            pl.BlockSpec((n, ch), entry),
            pl.BlockSpec(memory_space=pltpu.VMEM),
            pl.BlockSpec(memory_space=pl.ANY),
        ],
        out_specs=[
            pl.BlockSpec((tblk, ch), at),
            pl.BlockSpec((tblk, ch), at),
            pl.BlockSpec((n_dp, row_len, wide), lambda r, j: (0, 0, 0)),
            pl.BlockSpec((n, ch), zero),
            pl.BlockSpec((8, ch), zero),
            pl.BlockSpec(stepw.shape, zero),
            pl.BlockSpec(wg_part.shape[1:], zero),
            pl.BlockSpec(mixed_part.shape[1:], zero),
        ],
        out_shape=[
            jax.ShapeDtypeStruct((t, ch), BF16),
            jax.ShapeDtypeStruct((t, ch), F32),
            jax.ShapeDtypeStruct((n_dp, row_len, wide), F32),
            jax.ShapeDtypeStruct((n, ch), F32),
            jax.ShapeDtypeStruct((8, ch), F32),
            jax.ShapeDtypeStruct(stepw.shape, F32),
            jax.ShapeDtypeStruct(wg_part.shape[1:], BF16),
            jax.ShapeDtypeStruct(mixed_part.shape[1:], F32),
        ],
        scratch_shapes=[
            pltpu.VMEM((n, ch), F32),
            pltpu.VMEM((tblk, 1), F32),
            pltpu.VMEM((tblk, TB * n), BF16),
            pltpu.VMEM((tblk // TB, n, TB), F32),
            pltpu.VMEM((2, TB, ch), F32),
            pltpu.VMEM((2, TB, ch), F32),
            pltpu.VMEM((2, TB * n, ch), BF16),
            pltpu.VMEM((2, TB * n, ch), BF16),
            pltpu.VMEM((2, TB * n, 128), F32),
            pltpu.VMEM((2, TB * n, 128), F32),
        ]
        + GroupSum.scratch(row_len, wide)
        + RingReduce.scratch(n_f, wg_part.shape[1:])
        + [pltpu.VMEM(mixed_part.shape, BF16)]
        + PairReduce.scratch(mixed_part.shape[1:])
        + [pltpu.SemaphoreType.DMA],
        compiler_params=pltpu.CompilerParams(
            collective_id=3, has_side_effects=True, vmem_limit_bytes=56 * 2**20
        ),
        cost_estimate=pl.CostEstimate(flops=t * n * ch * 80, bytes_accessed=t * ch * 60, transcendentals=t * n * ch),
    )(lens, dbl, delta, pre, act, gy, stepw, rate2, skip, states, states, wg_part, mixed_part)


class PairShare:
    def __init__(self, mine, out, local, send, recv):
        me_d, me_f = lax.axis_index("dp"), lax.axis_index("fsdp")
        self.local = pltpu.make_async_copy(mine, out.at[0], local)
        self.copies = [
            pltpu.make_async_remote_copy(
                src_ref=src,
                dst_ref=out.at[i + 1],
                send_sem=send.at[i],
                recv_sem=recv.at[i],
                device_id=(flip(me_d, mask), me_f),
                device_id_type=pl.DeviceIdType.MESH,
            )
            for i, (src, mask) in enumerate([(mine, 1), (mine, 2), (out.at[2], 1)])
        ]

    def start(self):
        self.copies[1].start()
        self.copies[0].start()
        self.local.start()

    def relay(self):
        self.copies[1].wait_recv()
        self.copies[2].start()

    def finish(self):
        self.copies[0].wait_recv()
        self.copies[2].wait_recv()
        for c in self.copies:
            c.wait_send()
        self.local.wait()


class Return:
    def __init__(self, count, n_f, buf, out, local, send, recv):
        self.count, self.n_f, self.buf, self.out = count, n_f, buf, out
        self.local, self.send, self.recv = local, send, recv
        self.me = lax.axis_index("dp") * n_f + lax.axis_index("fsdp")

    def fill(self, pick, values):
        count, pair = self.buf.shape[:2]

        def piece(j, _):
            cols = pl.ds(pl.multiple_of(j * 256, 256), 256)
            moved = jnp.dot(pick, values[:, cols].astype(BF16), preferred_element_type=F32)
            self.buf[:, :, cols] = moved.astype(BF16).reshape(count, pair, 256)
            return 0

        lax.fori_loop(0, values.shape[1] // 256, piece, 0)

    def start(self):
        def one(p, _):
            pltpu.make_async_remote_copy(
                src_ref=self.buf.at[p],
                dst_ref=self.out.at[p],
                send_sem=self.send,
                recv_sem=self.recv,
                device_id=mesh_at(lax.rem(self.me + self.count - p, self.count), self.n_f),
                device_id_type=pl.DeviceIdType.MESH,
            ).start()
            return 0

        pltpu.make_async_copy(self.buf.at[0], self.out.at[0], self.local).start()
        lax.fori_loop(1, self.count, one, 0)

    def finish(self):
        pltpu.make_async_copy(self.buf.at[0], self.out.at[0], self.local).wait()
        rest = pl.ds(1, self.count - 1)
        for sem in (self.recv, self.send):
            pltpu.make_async_copy(self.buf.at[rest], self.out.at[rest], sem).wait()


def leave_kernel(n_f, half, lens_ref, da_ref, conv_ref, xin_ref, act_ref, dblg_ref, sel_ref, taps_ref,
                 sums_ref, dsum_ref, rate_ref, stepg_ref, normed_ref, wx_ref, wg_ref, gg_ref,
                 wo_part, wg_own, x_own, dy_own, mixed_own, gain_ref, tags_ref, ride_ref,
                 mix_back, dx_back, gx_all, gg_all, go_all, small_all,
                 ig_s, wx_s, ng_s, small_s, pick_s, ret_mix, ret_dx, change_s,
                 wo_got, wo_send, wo_recv, wx_got, wx_send, wx_recv, sm_got, sm_send, sm_recv,
                 ng_near, ng_far, ng_send, ng_recv, wo_own, wx_own, sm_own, local, sh_send, sh_recv, ret_sem):
    g = pl.program_id(0)
    steps = pl.num_programs(0)
    n_dp, tok, wide = dblg_ref.shape
    count = n_dp * n_f
    width = x_own.shape[1]
    ch = ig_s.shape[1]
    piece = 256
    n_taps = taps_ref.shape[0]
    down = n_f // 2
    ring_o = RingReduce(n_f, wo_part, wo_got, wo_send, wo_recv, n_f - 1 - down)
    ring_x = RingReduce(n_f, wx_s, wx_got, wx_send, wx_recv, down)
    ring_s = RingReduce(n_f, small_s, sm_got, sm_send, sm_recv, down)
    pairs = PairReduce(ng_s, ng_near, ng_far, ng_send, ng_recv)
    shares = [
        PairShare(mine, out, local.at[i], sh_send.at[i], sh_recv.at[i])
        for i, (mine, out) in enumerate(
            [(wg_own, gg_all), (wo_own, go_all), (wx_own, gx_all), (sm_own, small_all)]
        )
    ]
    ret_m = Return(count, n_f, ret_mix, mix_back, local.at[4], ret_sem.at[0], ret_sem.at[1])
    ret_x = Return(count, n_f, ret_dx, dx_back, local.at[5], ret_sem.at[2], ret_sem.at[3])
    tn = (((0,), (0,)), ((), ()))
    nt = (((1,), (1,)), ((), ()))

    @pl.when(g == 0)
    def _():
        me = lax.axis_index("dp") * n_f + lax.axis_index("fsdp")
        barrier = pltpu.get_barrier_semaphore()

        def greet(p, _):
            pl.semaphore_signal(
                barrier, inc=1, device_id=mesh_at(lax.rem(me + p, count), n_f), device_id_type=pl.DeviceIdType.MESH
            )
            return 0

        lax.fori_loop(1, count, greet, 0)
        pl.semaphore_wait(barrier, count - 1)
        ring_o.start()
        shares[0].start()
        spots = jnp.concatenate([tags_ref[...]] * (tok // 128), axis=1)
        lane = lax.broadcasted_iota(jnp.int32, (tok, tok), 1).astype(F32)
        pick_s[...] = jnp.where(spots == lane, 1.0, 0.0).astype(BF16)
        ret_m.fill(pick_s[...], mixed_own)
        ret_mix[:, :, width:] = jnp.broadcast_to(ride_ref[...], (tok, 128)).astype(BF16).reshape(
            count, tok // count, 128
        )
        ret_m.start()

    for e in range(1, ring_o.events - 1):

        @pl.when(g == min(5 * e, 2 * half + 2))
        def _(e=e):
            ring_o.event(e)

    @pl.when(g < half)
    def _():
        cols = pl.ds(pl.multiple_of(g * piece, piece), piece)
        zero = jnp.zeros((1, piece), F32)
        misc = [zero] * (n_taps + 1)
        sel_grad = jnp.zeros((wide, piece), F32)
        for m in range(n_dp):
            at = slice(m * tok, (m + 1) * tok)
            low = dblg_ref[m].astype(BF16)
            since, left = segment_span(lens_ref, m, 0, tok)
            act_grad = da_ref[at, :] + jnp.dot(low, sel_ref[...], preferred_element_type=F32)
            conv_grad = act_grad * silu_slope(conv_ref[at, :])
            back = taps_ref[n_taps - 1 : n_taps, :] * conv_grad
            x_in = xin_ref[at, :]
            misc[n_taps - 1] = misc[n_taps - 1] + jnp.sum(conv_grad * x_in, axis=0, keepdims=True)
            for lag in range(1, n_taps):
                tap = n_taps - 1 - lag
                later = pltpu.roll(conv_grad, tok - lag, 0) * (left >= lag).astype(F32)
                back = back + taps_ref[tap : tap + 1, :] * later
                misc[tap] = misc[tap] + jnp.sum(later * x_in, axis=0, keepdims=True)
            ig_s[at, cols] = back.astype(BF16)
            misc[n_taps] = misc[n_taps] + jnp.sum(conv_grad, axis=0, keepdims=True)
            sel_grad = sel_grad + lax.dot_general(low, act_ref[at, :], tn, preferred_element_type=F32)
        rows = jnp.concatenate(
            [
                sel_grad,
                stepg_ref[...],
                dsum_ref[...] * rate_ref[...],
                jnp.concatenate(misc + [sums_ref[0:2, :], zero], axis=0),
                jnp.zeros((small_s.shape[1] - wide - stepg_ref.shape[0] - rate_ref.shape[0] - 8, piece), F32),
            ],
            axis=0,
        )
        cs = small_s.shape[2]
        for i in range(piece // cs):
            small_s[g * (piece // cs) + i] = rows[:, i * cs : (i + 1) * cs]

    @pl.when(g >= half)
    def _():
        block = g - half
        dcols = wx_s.shape[1]

        def weights(j, _):
            cols = pl.ds(pl.multiple_of(j * piece, piece), piece)
            grad = lax.dot_general(normed_ref[...], ig_s[:, cols], tn, preferred_element_type=F32).astype(BF16)
            for i in range(piece // dcols):
                wx_s[block * (piece // dcols) + i, :, cols] = grad[i * dcols : (i + 1) * dcols]
            return 0

        lax.fori_loop(0, ch // piece, weights, 0)

        def tokens_(m, _):
            at = pl.ds(pl.multiple_of(m * tok, tok), tok)
            grad = lax.dot_general(ig_s[at, :], wx_ref[...], nt, preferred_element_type=F32)
            grad = grad + lax.dot_general(gg_ref[at, :], wg_ref[...], nt, preferred_element_type=F32)
            ng_s[m, :, pl.ds(pl.multiple_of(block * piece, piece), piece)] = grad.astype(BF16)
            return 0

        lax.fori_loop(0, n_dp, tokens_, 0)

    @pl.when(g == steps - 1)
    def _():
        ring_x.start()
        ring_s.start()
        pairs.start()
        shares[0].relay()
        pairs.middle()
        if ring_o.events > 1:
            ring_o.event(ring_o.events - 1)
        if ring_x.events > 1:
            ring_s.event(1)
            ring_x.event(1)
        ring_o.finish(wo_own)
        shares[1].start()
        pairs.finish(change_s)

        def rows(i, _):
            at = pl.ds(pl.multiple_of(i * 16, 16), 16)
            v = x_own[at, :].astype(F32)
            rstd = lax.rsqrt(jnp.mean(v * v, axis=1, keepdims=True) + EPS)
            hat = v * rstd
            grad = change_s[at, :] * gain_ref[...]
            grad = rstd * (grad - hat * jnp.mean(grad * hat, axis=1, keepdims=True))
            change_s[at, :] = dy_own[at, :].astype(F32) + grad
            return 0

        lax.fori_loop(0, tok // 16, rows, 0)
        ret_x.fill(pick_s[...], change_s)
        ret_x.start()
        for e in range(2, ring_x.events):
            ring_s.event(e)
            ring_x.event(e)
        shares[1].relay()
        ring_s.finish(sm_own)
        shares[3].start()
        ring_x.finish(wx_own)
        shares[2].start()
        shares[3].relay()
        shares[2].relay()
        for share in shares:
            share.finish()
        ret_m.finish()
        ret_x.finish()


def leave(lens, da, conv, x_in, act, dbl_grad, sel, taps, sums, decay_sum, rate, stepg, normed, wx, wg, gate_grad,
          wo_part, wg_own, x_own, dy_own, mixed_own, gain, tags, ride, n_f):
    n_dp, tok, wide = dbl_grad.shape
    group, ch = act.shape
    width = x_own.shape[1]
    count = n_dp * n_f
    pair = tok // count
    piece = 256
    half = ch // piece
    dcols = width // n_f
    cs = ch // n_f
    n = rate.shape[0]
    tall = -(-(wide + stepg.shape[0] + n + 8) // 64) * 64
    early = lambda g: (0, jnp.minimum(g, half - 1))
    late = lambda g: (0, jnp.maximum(g - half, 0))
    late_rows = lambda g: (jnp.maximum(g - half, 0), 0)
    any_ = pl.BlockSpec(memory_space=pl.ANY)
    vmem = pl.BlockSpec(memory_space=pltpu.VMEM)
    block = lambda rows: pl.BlockSpec((rows, piece), early)
    shaped = jax.ShapeDtypeStruct
    return pl.pallas_call(
        functools.partial(leave_kernel, n_f, half),
        grid=(half + width // piece,),
        in_specs=[
            pl.BlockSpec(memory_space=pltpu.SMEM),
            block(group),
            block(group),
            block(group),
            block(group),
            vmem,
            block(wide),
            block(taps.shape[0]),
            block(8),
            block(n),
            block(n),
            block(stepg.shape[0]),
            pl.BlockSpec((group, piece), late),
            pl.BlockSpec((piece, ch), late_rows),
            pl.BlockSpec((piece, ch), late_rows),
        ]
        + [vmem] * 9,
        out_specs=[any_] * 6,
        out_shape=[
            shaped((count, pair, width + 128), BF16),
            shaped((count, pair, width), BF16),
            shaped((n_dp, dcols, ch), BF16),
            shaped((n_dp, dcols, ch), BF16),
            shaped((n_dp, cs, width), BF16),
            shaped((n_dp, tall, cs), F32),
        ],
        scratch_shapes=[
            pltpu.VMEM((group, ch), BF16),
            pltpu.VMEM((n_f, dcols, ch), BF16),
            pltpu.VMEM((n_dp, tok, width), BF16),
            pltpu.VMEM((n_f, tall, cs), F32),
            pltpu.VMEM((tok, tok), BF16),
            pltpu.VMEM((count, pair, width + 128), BF16),
            pltpu.VMEM((count, pair, width), BF16),
            pltpu.VMEM((tok, width), F32),
        ]
        + RingReduce.scratch(n_f, (cs, width))
        + RingReduce.scratch(n_f, (dcols, ch))
        + RingReduce.scratch(n_f, (tall, cs), F32)
        + PairReduce.scratch((tok, width))
        + [
            pltpu.VMEM((cs, width), BF16),
            pltpu.VMEM((dcols, ch), BF16),
            pltpu.VMEM((tall, cs), F32),
            pltpu.SemaphoreType.DMA((6,)),
            pltpu.SemaphoreType.DMA((4, 3)),
            pltpu.SemaphoreType.DMA((4, 3)),
            pltpu.SemaphoreType.DMA((4,)),
        ],
        compiler_params=pltpu.CompilerParams(
            collective_id=4, has_side_effects=True, vmem_limit_bytes=62 * 2**20
        ),
        cost_estimate=pl.CostEstimate(flops=2 * 10**10, bytes_accessed=6 * 10**7, transcendentals=10**6),
    )(lens, da, conv, x_in, act, dbl_grad, sel, taps, sums, decay_sum, rate, stepg, normed, wx, wg, gate_grad,
      wo_part, wg_own, x_own, dy_own, mixed_own, gain, tags, ride)


def masks_of(count):
    return [1 << b for b in range(count.bit_length() - 1)]


def mesh_at(index, n_f):
    return (index // n_f, lax.rem(index, n_f))


def ring_index(p, n_f):
    if n_f % 2:
        return p
    return jnp.where(p < n_f // 2, 2 * p, 2 * (n_f - 1 - p) + 1)


def ring_place(f, n_f):
    if n_f % 2:
        return f
    return jnp.where(lax.rem(f, 2) == 0, f // 2, n_f - 1 - f // 2)


def gather_kernel(n_dp, n_f, downs, x_ref, dy_ref, meta_ref, dest_ref, lens_ref, *refs):
    streams = len(downs)
    blocks = refs[:streams]
    x_all, dy_all, lens_all, x_own_ref, dy_own_ref, tag_ref, rank_ref = refs[streams : streams + 7]
    outs = refs[streams + 7 : 2 * streams + 7]
    send_ref, got, x_own, dy_own, deal_sem, loc_sem, pair_send, pair_recv, ring_send, ring_recv = refs[
        2 * streams + 7 :
    ]
    count = n_dp * n_f
    me_d = lax.axis_index("dp")
    me_f = lax.axis_index("fsdp")
    me = me_d * n_f + me_f
    q = ring_place(me_f, n_f)
    below = ring_index(lax.rem(q + n_f - 1, n_f), n_f)
    above = ring_index(lax.rem(q + 1, n_f), n_f)

    barrier = pltpu.get_barrier_semaphore()

    def greet(p, _):
        pl.semaphore_signal(
            barrier, inc=1, device_id=mesh_at(lax.rem(me + p, count), n_f), device_id_type=pl.DeviceIdType.MESH
        )
        return 0

    lax.fori_loop(1, count, greet, 0)
    locals_ = [
        pltpu.make_async_copy(blocks[s], outs[s].at[me_f], loc_sem.at[s]) for s in range(streams)
    ]
    for c in locals_:
        c.start()
    pl.semaphore_wait(barrier, count - 1)

    def deal(p, _):
        pltpu.make_async_remote_copy(
            src_ref=send_ref.at[p],
            dst_ref=got.at[p],
            send_sem=deal_sem.at[0],
            recv_sem=deal_sem.at[1],
            device_id=mesh_at(lax.rem(me + p, count), n_f),
            device_id_type=pl.DeviceIdType.MESH,
        ).start()
        return 0

    def hop(s, h, up):
        k = lax.rem(q + (n_f - h if up else h), n_f)
        index = ring_index(k, n_f)
        src = blocks[s] if h == 0 else outs[s].at[index]
        return pltpu.make_async_remote_copy(
            src_ref=src,
            dst_ref=outs[s].at[index],
            send_sem=ring_send.at[s, int(up), h],
            recv_sem=ring_recv.at[s, int(up), h],
            device_id=(me_d, above if up else below),
            device_id_type=pl.DeviceIdType.MESH,
        )

    hops = [[downs[s], n_f - 1 - downs[s]] for s in range(streams)]
    for s in range(streams):
        for up in (0, 1):
            if hops[s][up]:
                hop(s, 0, up).start()
    tok, width = x_own.shape
    pair2 = got.shape[1]
    total = count * pair2

    dest_row, rel_row, abs_row, in_row = (meta_ref[i : i + 1, :] for i in range(4))
    rank = jnp.sum((dest_ref[...] < dest_row).astype(F32), axis=0, keepdims=True)
    half = pair2 // 2
    goal = rel_row * half + rank - abs_row * half
    rank_ref[...] = jnp.broadcast_to(goal, rank_ref.shape)
    row = lax.broadcasted_iota(jnp.int32, (total, tok), 0)
    place_in = lax.rem(row, pair2)
    first = place_in < half
    slot = (row // pair2) * half + jnp.where(first, place_in, place_in - half)
    chosen = slot.astype(F32) == goal
    spot = jnp.sum(jnp.where(chosen, in_row, 0.0), axis=1, keepdims=True)
    send_ref[:, :, width:] = jnp.broadcast_to(spot, (total, 128)).astype(BF16).reshape(count, pair2, 128)
    x_pick = jnp.where(chosen & first, 1.0, 0.0).astype(BF16)
    dy_pick = jnp.where(chosen & jnp.logical_not(first), 1.0, 0.0).astype(BF16)

    def sort(j, _):
        cols = pl.ds(pl.multiple_of(j * 256, 256), 256)
        mixed = jnp.dot(x_pick, x_ref[:, cols], preferred_element_type=F32)
        mixed = mixed + jnp.dot(dy_pick, dy_ref[:, cols], preferred_element_type=F32)
        send_ref[:, :, cols] = mixed.astype(BF16).reshape(count, pair2, 256)
        return 0

    lax.fori_loop(0, width // 256, sort, 0)
    lax.fori_loop(1, count, deal, 0)
    got[0] = send_ref[0]

    def advance(h):
        for s in range(streams):
            for up in (0, 1):
                if h < hops[s][up]:
                    hop(s, h - 1, up).wait_recv()
                    hop(s, h, up).start()

    rest = got.at[pl.ds(1, count - 1)]
    pltpu.make_async_copy(send_ref.at[pl.ds(1, count - 1)], rest, deal_sem.at[1]).wait()
    tag = got[:, :, width : width + 128].astype(F32).reshape(total, 128)
    reps = tok // 128
    spots = jnp.concatenate([tag] * reps, axis=1)
    lane = lax.broadcasted_iota(jnp.int32, (total, tok), 1).astype(F32)
    match = spots == lane
    x_pick = jnp.where(match & first, 1.0, 0.0).astype(BF16)
    dy_pick = jnp.where(match & jnp.logical_not(first), 1.0, 0.0).astype(BF16)
    tn = (((0,), (0,)), ((), ()))
    tag_ref[...] = tag

    def place(pick, out):
        def part(j, _):
            cols = pl.ds(pl.multiple_of(j * 256, 256), 256)
            values = got[:, :, cols].reshape(total, 256)
            out[:, cols] = lax.dot_general(pick, values, tn, preferred_element_type=F32).astype(BF16)
            return 0

        lax.fori_loop(0, width // 256, part, 0)

    masks = list(reversed(masks_of(n_dp)))

    def partner(mask):
        return me_d + mask - 2 * mask * lax.rem(me_d // mask, 2)

    def share(a, m, mask):
        out = (x_all, dy_all, lens_all)[a]
        own_block = (x_own, dy_own, lens_ref)[a]
        return pltpu.make_async_remote_copy(
            src_ref=own_block if m == 0 else out.at[m],
            dst_ref=out.at[m | mask],
            send_sem=pair_send.at[a, m | mask],
            recv_sem=pair_recv.at[a, m | mask],
            device_id=(partner(mask), me_f),
            device_id_type=pl.DeviceIdType.MESH,
        )

    copies = []

    def keep(a):
        own_block = (x_own, dy_own, lens_ref)[a]
        dsts = (x_all, dy_all, lens_all)[a].at[0], (x_own_ref, dy_own_ref, None)[a]
        for j, dst in enumerate(dsts[: 1 if a == 2 else 2]):
            c = pltpu.make_async_copy(own_block, dst, loc_sem.at[streams + 2 * a + j])
            c.start()
            copies.append(c)

    for mask in masks:
        share(2, 0, mask).start()
    keep(2)
    advance(1)
    place(x_pick, x_own)
    for mask in masks:
        share(0, 0, mask).start()
    keep(0)
    place(dy_pick, dy_own)
    for mask in masks:
        share(1, 0, mask).start()
    keep(1)

    def relay(a):
        held = [0]
        for step, mask in enumerate(masks):
            for m in held:
                if m:
                    share(a, m, mask).start()
            for m in held:
                share(a, m, mask).wait_recv()
            held = held + [m | mask for m in held]

    most = max(max(h) for h in hops)
    for h in range(2, most):
        advance(h)
        if h == 2:
            relay(0)
    if most <= 2:
        relay(0)
    relay(1)
    relay(2)
    for s in range(streams):
        for up in (0, 1):
            if hops[s][up]:
                hop(s, hops[s][up] - 1, up).wait_recv()
    for s in range(streams):
        for up in (0, 1):
            for h in range(hops[s][up]):
                hop(s, h, up).wait_send()
    for a in (0, 1, 2):
        held = [0]
        for mask in masks:
            for m in held:
                share(a, m, mask).wait_send()
            held = held + [m | mask for m in held]
    for c in locals_ + copies:
        c.wait()
    pltpu.make_async_copy(send_ref.at[pl.ds(1, count - 1)], rest, deal_sem.at[0]).wait()


def gather_all(x, dy, meta, dest, lens, blocks, downs, n_dp, n_f):
    streams = len(blocks)
    tok, width = x.shape
    count = n_dp * n_f
    sent = (count, 2 * tok // count, width + 128)
    hops = max(max(d, n_f - 1 - d) for d in downs)
    any_ = pl.BlockSpec(memory_space=pl.ANY)
    vmem = pl.BlockSpec(memory_space=pltpu.VMEM)
    row = jax.ShapeDtypeStruct((tok, width), BF16)
    rows = jax.ShapeDtypeStruct((n_dp, tok, width), BF16)
    return pl.pallas_call(
        functools.partial(gather_kernel, n_dp, n_f, downs),
        in_specs=[vmem] * 5 + [any_] * streams,
        out_specs=[any_] * 5 + [vmem] * 2 + [any_] * streams,
        out_shape=[
            rows,
            rows,
            jax.ShapeDtypeStruct((n_dp,) + lens.shape, lens.dtype),
            row,
            row,
            jax.ShapeDtypeStruct((2 * tok, 128), F32),
            jax.ShapeDtypeStruct((8, tok), F32),
        ]
        + [jax.ShapeDtypeStruct((n_f,) + b.shape, b.dtype) for b in blocks],
        scratch_shapes=[
            pltpu.VMEM(sent, BF16),
            pltpu.VMEM(sent, BF16),
            pltpu.VMEM((tok, width), BF16),
            pltpu.VMEM((tok, width), BF16),
            pltpu.SemaphoreType.DMA((2,)),
            pltpu.SemaphoreType.DMA((streams + 5,)),
            pltpu.SemaphoreType.DMA((3, n_dp)),
            pltpu.SemaphoreType.DMA((3, n_dp)),
            pltpu.SemaphoreType.DMA((streams, 2, hops)),
            pltpu.SemaphoreType.DMA((streams, 2, hops)),
        ],
        compiler_params=pltpu.CompilerParams(
            collective_id=0, has_side_effects=True, vmem_limit_bytes=40 * 2**20
        ),
        cost_estimate=pl.CostEstimate(flops=10**10, bytes_accessed=2 * 10**8, transcendentals=0),
    )(x, dy, meta, dest, lens, *blocks)


def columns_kernel(starts, cs, w_ref, *outs):
    me_d = lax.axis_index("dp")
    for o, out in enumerate(outs):
        for j, start in enumerate(starts[o]):
            out[:, j * cs : (j + 1) * cs] = w_ref[:, pl.ds(pl.multiple_of(start + me_d * cs, 128), cs)]


def take_columns(w, halves, n_f, n_dp, cs):
    inner = n_f * n_dp * cs
    starts = [[h * inner + f * n_dp * cs for f in range(n_f)] for h in range(halves)]
    me_d = lax.axis_index("dp")
    if cs % 128:
        return [
            jnp.concatenate([lax.dynamic_slice_in_dim(w, s + me_d * cs, cs, 1) for s in group], axis=1)
            for group in starts
        ]
    height = w.shape[0]
    blk = min(height, 64)
    return pl.pallas_call(
        functools.partial(columns_kernel, starts, cs),
        grid=(height // blk,),
        in_specs=[pl.BlockSpec((blk, w.shape[1]), lambda i: (i, 0))],
        out_specs=[pl.BlockSpec((blk, n_f * cs), lambda i: (i, 0))] * halves,
        out_shape=[jax.ShapeDtypeStruct((height, n_f * cs), w.dtype)] * halves,
    )(w)


def spread_kernel(cs, x_ref, w_ref, out_ref, sum_ref):
    me_d = lax.axis_index("dp")
    total = jnp.zeros(sum_ref.shape, F32)
    for i in range(x_ref.shape[0]):
        m = me_d + i - 2 * ((me_d // 2 % 2) * (i // 2 % 2) * 2 + (me_d % 2) * (i % 2))
        part = x_ref[m].astype(F32)
        cols = slice(i * cs, (i + 1) * cs)
        out_ref[:, cols] = part
        product = part * w_ref[:, cols].astype(F32)
        for j in range(0, cs, 128):
            total = total + product[:, j : j + 128]

    @pl.when(pl.program_id(0) == 0)
    def _():
        sum_ref[...] = jnp.zeros_like(sum_ref)

    sum_ref[...] += total


def spread_columns(rel, w, cs):
    n_dp, height, cols = rel.shape
    if cs % 128 or n_dp != 4:
        me_d = lax.axis_index("dp")
        parts = [lax.dynamic_index_in_dim(rel, me_d ^ i, 0, keepdims=False) for i in range(n_dp)]
        out = jnp.concatenate(
            [p[:, f * cs : (f + 1) * cs] for f in range(cols // cs) for p in parts], axis=1
        ).astype(F32)
        return out, jnp.sum(out * w.astype(F32), axis=1)
    out, sums = pl.pallas_call(
        functools.partial(spread_kernel, cs),
        grid=(cols // cs,),
        in_specs=[
            pl.BlockSpec((n_dp, height, cs), lambda f: (0, 0, f)),
            pl.BlockSpec((height, n_dp * cs), lambda f: (0, f)),
        ],
        out_specs=[
            pl.BlockSpec((height, n_dp * cs), lambda f: (0, f)),
            pl.BlockSpec((height, 128), lambda f: (0, 0)),
        ],
        out_shape=[jax.ShapeDtypeStruct((height, n_dp * cols), F32), jax.ShapeDtypeStruct((height, 128), F32)],
        cost_estimate=pl.CostEstimate(flops=4 * height * cols * n_dp, bytes_accessed=8 * height * cols * n_dp, transcendentals=0),
    )(rel, w)
    return out, jnp.sum(sums, axis=1)


def per_device(
    tokens,
    cotangent,
    destination,
    lengths,
    norm_gain,
    in_weight,
    conv_weight,
    conv_bias,
    select_weight,
    step_weight,
    step_bias,
    decay_log,
    skip_gain,
    out_weight,
):
    n_dp = lax.axis_size("dp")
    n_f = lax.axis_size("fsdp")
    rows = n_dp * n_f
    tok = tokens.shape[0]
    width = tokens.shape[1]
    pair = tok // rows
    inner = conv_bias.shape[0] * n_f
    cs = conv_bias.shape[0] // n_dp
    ch = cs * n_f
    taps = conv_weight.shape[0]
    n = decay_log.shape[0]
    rank_of = step_weight.shape[0]
    dcols = width // n_f
    group = n_dp * tok
    both = ("dp", "fsdp")
    me_d = lax.axis_index("dp")
    me_f = lax.axis_index("fsdp")
    flat_dot = lambda a, b: jnp.dot(a, b, preferred_element_type=F32)
    nt_dot = lambda a, b: lax.dot_general(a, b, (((1,), (1,)), ((), ())), preferred_element_type=F32)
    tn_dot = lambda a, b: lax.dot_general(a, b, (((0,), (0,)), ((), ())), preferred_element_type=F32)

    me = me_d * n_f + me_f
    row_to = destination // tok
    meta = jnp.stack(
        [destination, (row_to - me) % rows, row_to, destination % tok] + [jnp.zeros_like(destination)] * 4
    ).astype(F32)
    segs = lengths.shape[1]
    lens_tile = jnp.pad(lengths, ((0, 7), (0, 128 - segs)))
    slots = jnp.arange(tok, dtype=jnp.int32)

    def mine(shard):
        return lax.dynamic_slice_in_dim(shard.reshape(-1, n_dp * cs), me_d * cs, cs, 1)

    smalls = [conv_weight, conv_bias, step_bias, skip_gain, decay_log, select_weight, step_weight]
    heights = [math.prod(s.shape) // (n_dp * cs) for s in smalls]
    gain_rows = dcols // cs
    used = sum(heights) + gain_rows
    filler = -used % 16
    small_block = jnp.concatenate(
        [mine(s) for s in smalls] + [norm_gain.reshape(gain_rows, cs), jnp.zeros((filler, cs), BF16)], axis=0
    )
    wx_block, wg_block = take_columns(in_weight, 2, n_f, n_dp, cs)
    wo_block = lax.dynamic_slice_in_dim(out_weight, me_d * cs, cs, 0)
    x_all, dy_all, lens_all, x_own, dy_own, tags, ranks, small_all, wx, wg = gather_all(
        tokens, cotangent, meta, destination[:, None].astype(F32), lens_tile,
        [small_block, wx_block, wg_block], [n_f // 2, n_f // 2, n_f - 1 - n_f // 2], n_dp, n_f,
    )
    x_all = x_all.reshape(group, width)
    lens = lens_all[:, 0, :segs]
    from_send = (ranks[0].astype(jnp.int32)[:, None] == slots[None, :]).astype(BF16)
    x_tags = tags.reshape(rows, 2 * pair, 128)[:, :pair].reshape(tok, 128)
    dy_all = dy_all.reshape(group, width)
    wx = wx.reshape(width, ch)
    wg = wg.reshape(width, ch)
    small = small_all.transpose(1, 0, 2).reshape(used + filler, ch)
    gain = small_all[:, used - gain_rows : used].reshape(width).astype(F32)
    valid = (slots < jnp.sum(lengths[0, : segs - 1])).astype(F32)
    x_own32 = x_own.astype(F32)
    square = jnp.sum(x_own32 * x_own32, axis=1)
    mine_sums = [jnp.sum(square * valid), jnp.sum(valid)]

    pieces, at = [], 0
    for height in heights:
        pieces.append(small[at : at + height])
        at += height
    conv_w, conv_b, step_b, skip, dlog, sel, stepw = pieces
    conv_w = conv_w.astype(F32)
    skip = skip.astype(F32)
    rate = -jnp.exp(dlog.astype(F32))

    normed, x_in, conv, act, gate, dbl, wo_next = enter(
        lens, x_all, gain[None], wx, wg, conv_w, conv_b.astype(F32), sel, wo_block, n_f
    )
    dbl = dbl.reshape(group, -1)
    rate2 = rate * LOG2E
    scan_out, states, delta, pre, wo = scan_forward(
        lens, dbl, act, stepw, step_b.astype(F32), rate2, skip, wo_block, wo_next, n_f, tok
    )
    wo = wo.reshape(ch, width)
    gate_silu = jax.nn.silu(gate)
    gated = (scan_out * gate_silu).astype(BF16)
    mixed_part = flat_dot(gated, wo).astype(BF16).reshape(n_dp, tok, width)

    gated_grad = nt_dot(dy_all, wo)
    scan_grad = gated_grad * gate_silu
    gate_grad = (gated_grad * scan_out * silu_slope(gate)).astype(BF16)
    wg_grad = tn_dot(normed, gate_grad).astype(BF16)
    wo_grad = tn_dot(gated, dy_all).astype(BF16)
    pre_grad, act_grad, dbl_grad, decay_sum, sums, step_grad, wg_own, mixed = scan_backward(
        lens, dbl, delta, pre, act, scan_grad, stepw, rate2, skip, states,
        wg_grad.reshape(n_f, dcols, ch), mixed_part, n_f, tok,
    )
    lanes = lax.broadcasted_iota(jnp.int32, (1, 128), 1)
    ride = jnp.zeros((1, 128), F32)
    for j, value in enumerate(mine_sums):
        high = value.astype(BF16).astype(F32)
        ride = ride + jnp.where(lanes == 2 * j, high, 0.0) + jnp.where(lanes == 2 * j + 1, value - high, 0.0)
    mix_back, dx_back, gx_all, gg_all, go_all, small_full = leave(
        lens, act_grad, conv, x_in, act, dbl_grad, sel, conv_w, sums, decay_sum, rate, step_grad, normed, wx, wg,
        gate_grad, wo_grad.reshape(n_f, cs, width), wg_own, x_own, dy_own, mixed, gain[None], x_tags, ride, n_f,
    )

    def in_group_order(stacked):
        return jnp.concatenate(
            [lax.dynamic_index_in_dim(stacked, me_d ^ i, 0, keepdims=True) for i in range(n_dp)], axis=0
        )

    grad_in_weight, gain_sum = spread_columns(jnp.concatenate([gx_all, gg_all], axis=2), in_weight, cs)
    grad_out_weight = in_group_order(go_all).reshape(n_dp * cs, width).astype(F32)
    small_full = in_group_order(small_full).transpose(1, 0, 2).reshape(-1, n_dp * cs)
    grad_norm_gain = gain_sum / norm_gain.astype(F32)
    wide = select_weight.shape[0]
    at_decay = wide + rank_of
    at_misc = at_decay + n
    grad_select = small_full[:wide]
    grad_step = small_full[wide:at_decay]
    grad_decay = small_full[at_decay:at_misc]
    misc = small_full[at_misc : at_misc + 8]

    back = mix_back.reshape(tok, width + 128)
    totals = jnp.sum(mix_back[:, 0, width : width + 4].astype(F32), axis=0)
    input_rms = jnp.sqrt((totals[0] + totals[1]) / ((totals[2] + totals[3]) * width))
    mixer_output = flat_dot(from_send, back[:, :width])
    layer_output = (tokens.astype(F32) + mixer_output).astype(BF16)
    mixer_output = mixer_output.astype(BF16)
    input_grad = flat_dot(from_send, dx_back.reshape(tok, width)).astype(BF16)
    return (
        layer_output,
        mixer_output,
        input_grad,
        input_rms,
        grad_norm_gain,
        grad_in_weight,
        misc[:taps],
        misc[taps],
        grad_select,
        grad_step,
        misc[taps + 1],
        grad_decay,
        misc[taps + 2],
        grad_out_weight,
    )


def solution(mesh):
    return jax.shard_map(
        per_device,
        mesh=mesh,
        in_specs=(
            P(("dp", "fsdp"), None),
            P(("dp", "fsdp"), None),
            P(("dp", "fsdp")),
            P(("dp", "fsdp"), None),
            P("fsdp"),
            P("fsdp", None),
            P(None, "fsdp"),
            P("fsdp"),
            P(None, "fsdp"),
            P(None, "fsdp"),
            P("fsdp"),
            P(None, "fsdp"),
            P("fsdp"),
            P("fsdp", None),
        ),
        out_specs=(
            P(("dp", "fsdp"), None),
            P(("dp", "fsdp"), None),
            P(("dp", "fsdp"), None),
            P(),
            P("fsdp"),
            P("fsdp", None),
            P(None, "fsdp"),
            P("fsdp"),
            P(None, "fsdp"),
            P(None, "fsdp"),
            P("fsdp"),
            P(None, "fsdp"),
            P("fsdp"),
            P("fsdp", None),
        ),
        check_vma=False,
    )
```

```python
import functools
import math

import jax
import jax.numpy as jnp
from jax import lax
from jax.experimental import pallas as pl
from jax.experimental.pallas import tpu as pltpu
from jax.sharding import PartitionSpec as P

EPS = 1e-05
TB = 16
LOG2E = math.log2(math.e)
RESET = 1.0e4
BF16 = jnp.bfloat16
F32 = jnp.float32


def silu_slope(value):
    sigma = jax.nn.sigmoid(value)
    return sigma * (1.0 + value * (1.0 - sigma))


def row_at(g, n_dp):
    return lax.rem(2 * g + 1, n_dp + 1)


def flip(d, mask):
    return d + mask - 2 * mask * lax.rem(d // mask, 2)


class GroupSum:
    def __init__(self, part, near, far, total, send, recv):
        self.part, self.near, self.far, self.total = part, near, far, total
        me_d, me_f = lax.axis_index("dp"), lax.axis_index("fsdp")
        plan = [
            (part.at[1], near.at[0], 1),
            (part.at[3], near.at[1], 1),
            (part.at[0], far.at[1], 2),
            (part.at[2], far.at[0], 2),
            (total.at[0], total.at[1], 1),
            (total.at[2], total.at[3], 1),
        ]
        self.copies = [
            pltpu.make_async_remote_copy(
                src_ref=src,
                dst_ref=dst,
                send_sem=send.at[i],
                recv_sem=recv.at[i],
                device_id=(flip(me_d, mask), me_f),
                device_id_type=pl.DeviceIdType.MESH,
            )
            for i, (src, dst, mask) in enumerate(plan)
        ]

    def row_done(self, g):
        for j in (0, 1):

            @pl.when(g == j)
            def _(j=j):
                self.copies[j].start()

            @pl.when(g == j + 2)
            def _(j=j):
                self.copies[j].wait_recv()
                self.part[2 * j] = self.part[2 * j] + self.near[j]
                self.copies[j + 2].start()

    def first(self):
        for j in (0, 1):
            self.copies[j].start()

    def second(self):
        for j in (0, 1):
            self.copies[j].wait_recv()
            self.part[2 * j] = self.part[2 * j] + self.near[j]
            self.copies[j + 2].start()

    def finish(self):
        for j in (0, 1):
            self.copies[3 - j].wait_recv()
            self.total[2 * j] = self.part[2 * j] + self.far[j]
            self.copies[4 + j].start()
        for j in (0, 1):
            self.copies[4 + j].wait_recv()
        for c in self.copies:
            c.wait_send()

    @staticmethod
    def scratch(tok, wide):
        return [
            pltpu.VMEM((4, tok, wide), F32),
            pltpu.VMEM((2, tok, wide), F32),
            pltpu.VMEM((2, tok, wide), F32),
            pltpu.VMEM((4, tok, wide), F32),
            pltpu.SemaphoreType.DMA((6,)),
            pltpu.SemaphoreType.DMA((6,)),
        ]


class RingReduce:
    def __init__(self, n_f, part, got, send, recv, down):
        self.part, self.got = part, got
        q = ring_place(lax.axis_index("fsdp"), n_f)
        self.at = lambda k: ring_index(lax.rem(q + k, n_f), n_f)
        self.n_f = n_f
        self.counts = [down, n_f - 1 - down]
        self.copies = [[], []]
        for up in (0, 1):
            for h in range(min(self.counts[up], got.shape[1])):
                src = part.at[self.at(self.goal(up, 0))] if h == 0 else got.at[up, h - 1]
                self.copies[up].append(ring_copy(n_f, src, got.at[up, h], send.at[up, h], recv.at[up, h], up))
        self.events = max(self.counts)

    def goal(self, up, h):
        left = self.counts[up] - h
        return left if up else self.n_f - left

    def add(self, slot, addend):
        rows = slot.shape[0]
        step = min(rows, 64)

        def piece(i, _):
            at = pl.ds(pl.multiple_of(i * step, step), step)
            slot[at, :] = (slot[at, :].astype(F32) + addend[at, :].astype(F32)).astype(slot.dtype)
            return 0

        lax.fori_loop(0, rows // step, piece, 0)

    def start(self):
        for up in (0, 1):
            if self.copies[up]:
                self.copies[up][0].start()

    def stop(self, hops, out):
        for up in (0, 1):
            self.copies[up][hops - 1].wait_recv()
            rows_add(out.at[up], [self.got.at[up, hops - 1]])
            for c in self.copies[up][:hops]:
                c.wait_send()

    def resume(self, hops, arrived):
        for up in (0, 1):
            slot = self.got.at[up, hops - 1]
            rows_add(slot, [arrived.at[up], self.part.at[self.at(self.goal(up, hops))]])
            self.copies[up][hops].start()

    def event(self, e):
        for up in (0, 1):
            if e < self.counts[up]:
                self.copies[up][e - 1].wait_recv()
                self.add(self.got.at[up, e - 1], self.part.at[self.at(self.goal(up, e))])
                self.copies[up][e].start()

    def finish(self, out, since=0):
        last = []
        for up in (0, 1):
            if self.copies[up]:
                self.copies[up][-1].wait_recv()
                last.append(self.got.at[up, self.counts[up] - 1])
        mine = self.part.at[self.at(0)]
        rows = mine.shape[0]
        step = min(rows, 64)

        def piece(i, _):
            at = pl.ds(pl.multiple_of(i * step, step), step)
            total_ = mine[at, :].astype(F32)
            for slot in last:
                total_ = total_ + slot[at, :].astype(F32)
            out[at, :] = total_.astype(out.dtype)
            return 0

        lax.fori_loop(0, rows // step, piece, 0)
        for up in (0, 1):
            for c in self.copies[up][since:]:
                c.wait_send()

    @staticmethod
    def scratch(n_f, block, dtype=BF16, slots=0):
        return [
            pltpu.VMEM((2, slots or n_f // 2) + block, dtype),
            pltpu.SemaphoreType.DMA((2, n_f // 2)),
            pltpu.SemaphoreType.DMA((2, n_f // 2)),
        ]


class PairReduce:
    def __init__(self, part, near, far, send, recv):
        self.part, self.near, self.far = part, near, far
        me_d, me_f = lax.axis_index("dp"), lax.axis_index("fsdp")
        plan = [
            (part.at[1], near.at[0], 1),
            (part.at[3], near.at[1], 1),
            (part.at[2], far, 2),
        ]
        self.copies = [
            pltpu.make_async_remote_copy(
                src_ref=src,
                dst_ref=dst,
                send_sem=send.at[i],
                recv_sem=recv.at[i],
                device_id=(flip(me_d, mask), me_f),
                device_id_type=pl.DeviceIdType.MESH,
            )
            for i, (src, dst, mask) in enumerate(plan)
        ]

    def start(self):
        for c in self.copies[:2]:
            c.start()

    def middle(self):
        self.copies[1].wait_recv()
        rows_add(self.part.at[2], [self.part.at[2], self.near.at[1]])
        self.copies[2].start()
        self.copies[0].wait_recv()

    def finish(self, out):
        self.copies[2].wait_recv()
        rows_add(out, [self.part.at[0], self.near.at[0], self.far])
        for c in self.copies:
            c.wait_send()

    @staticmethod
    def scratch(block, dtype=BF16):
        return [
            pltpu.VMEM((2,) + block, dtype),
            pltpu.VMEM(block, dtype),
            pltpu.SemaphoreType.DMA((3,)),
            pltpu.SemaphoreType.DMA((3,)),
        ]


def rows_add(out, terms, step=32):
    def piece(i, _):
        at = pl.ds(pl.multiple_of(i * step, step), step)
        total_ = terms[0][at, :].astype(F32)
        for t in terms[1:]:
            total_ = total_ + t[at, :].astype(F32)
        out[at, :] = total_.astype(out.dtype)
        return 0

    lax.fori_loop(0, out.shape[0] // step, piece, 0)


class PairShare:
    def __init__(self, mine, out, local, send, recv, relative=False):
        me_d, me_f = lax.axis_index("dp"), lax.axis_index("fsdp")
        far = 2 if relative else flip(me_d, 2)
        here, at_near, at_far, relayed = (0, 1, 2, 3) if relative else (me_d, me_d, me_d, far)
        self.local = pltpu.make_async_copy(mine, out(here), local)
        self.copies = [
            pltpu.make_async_remote_copy(
                src_ref=src,
                dst_ref=dst,
                send_sem=send.at[i],
                recv_sem=recv.at[i],
                device_id=(flip(me_d, mask), me_f),
                device_id_type=pl.DeviceIdType.MESH,
            )
            for i, (src, dst, mask) in enumerate(
                [(mine, out(at_near), 1), (mine, out(at_far), 2), (out(far), out(relayed), 1)]
            )
        ]

    def start(self):
        self.copies[1].start()
        self.copies[0].start()
        self.local.start()

    def relay(self):
        self.copies[1].wait_recv()
        self.copies[2].start()

    def finish(self):
        self.copies[0].wait_recv()
        self.copies[2].wait_recv()
        for c in self.copies:
            c.wait_send()
        self.local.wait()


def side_by_side(count, height, wide):
    return (count, height, wide) if wide % 128 else (height, count * wide)


def lane_block(ref, index, wide):
    if wide % 128:
        return ref.at[index]
    return ref.at[:, pl.ds(pl.multiple_of(index * wide, 128), wide)]


def joined(value):
    if value.ndim == 2:
        return value
    return value.transpose(1, 0, 2).reshape(value.shape[1], -1)


def greet_neighbours(n_f, ring):
    me_d, me_f = lax.axis_index("dp"), lax.axis_index("fsdp")
    barrier = pltpu.get_barrier_semaphore()
    others = [(flip(me_d, 1), me_f), (flip(me_d, 2), me_f)]
    if ring:
        q = ring_place(me_f, n_f)
        others.append((me_d, ring_index(lax.rem(q + n_f - 1, n_f), n_f)))
        others.append((me_d, ring_index(lax.rem(q + 1, n_f), n_f)))
    for other in others:
        pl.semaphore_signal(barrier, inc=1, device_id=other, device_id_type=pl.DeviceIdType.MESH)
    pl.semaphore_wait(barrier, len(others))


def ring_copy(n_f, src, dst, send, recv, up):
    me_d, me_f = lax.axis_index("dp"), lax.axis_index("fsdp")
    q = ring_place(me_f, n_f)
    to = ring_index(lax.rem(q + (1 if up else n_f - 1), n_f), n_f)
    return pltpu.make_async_remote_copy(
        src_ref=src,
        dst_ref=dst,
        send_sem=send,
        recv_sem=recv,
        device_id=(me_d, to),
        device_id_type=pl.DeviceIdType.MESH,
    )


def segment_span(lens_ref, m, first, rows):
    t = lax.broadcasted_iota(jnp.int32, (rows, 1), 0) + first
    begin = jnp.zeros((rows, 1), jnp.int32)
    end = jnp.zeros((rows, 1), jnp.int32)
    total = jnp.int32(0)
    for j in range(lens_ref.shape[1]):
        after = total + lens_ref[m, j]
        inside = t >= total
        begin = jnp.where(inside, total, begin)
        end = jnp.where(inside, after, end)
        total = after
    return t - begin, end - 1 - t


def enter_kernel(n_f, half, lens_ref, x_ref, gain_ref, wx_ref, wg_ref, taps_ref, bias_ref, sel_ref, wo_ref,
                 normed_ref, xin_ref, conv_ref, act_ref, gate_ref, dbl_ref, next_ref,
                 part, near, far, total, gs_send, gs_recv, hop_send, hop_recv):
    g = pl.program_id(0)
    n_dp, tok = part.shape[:2]
    rows, width = x_ref.shape
    hops = [ring_copy(n_f, wo_ref, next_ref.at[up, 0], hop_send.at[up, 0], hop_recv.at[up, 0], up) for up in (0, 1)]
    hops2 = [
        ring_copy(n_f, next_ref.at[up, 0], next_ref.at[up, 1], hop_send.at[up, 1], hop_recv.at[up, 1], up)
        for up in (0, 1)
    ]
    group = GroupSum(part, near, far, total, gs_send, gs_recv)

    @pl.when(g == 0)
    def _():
        greet_neighbours(n_f, True)
        for c in hops:
            c.start()
        part[...] = jnp.zeros_like(part)

        def norm(i, _):
            for j in range(4):
                at = pl.ds(pl.multiple_of(i * 128 + j * 32, 32), 32)
                v = x_ref[at, :].astype(F32)
                rstd = lax.rsqrt(jnp.mean(v * v, axis=1, keepdims=True) + EPS)
                normed_ref[at, :] = (v * rstd * gain_ref[...]).astype(BF16)
            return 0

        lax.fori_loop(0, rows // 128, norm, 0)

    @pl.when(g == half)
    def _():
        for a, b in zip(hops, hops2):
            a.wait_recv()
            b.start()

    @pl.when(g < half)
    def _():
        n_taps = taps_ref.shape[0]
        xin_ref[...] = jnp.dot(normed_ref[...], wx_ref[...], preferred_element_type=F32)
        for m in range(n_dp):
            at = slice(m * tok, (m + 1) * tok)
            v = xin_ref[at, :]
            since, _ = segment_span(lens_ref, m, 0, tok)
            conv = bias_ref[...] + taps_ref[n_taps - 1 : n_taps, :] * v
            for lag in range(1, n_taps):
                keep = (since >= lag).astype(F32)
                conv = conv + taps_ref[n_taps - 1 - lag : n_taps - lag, :] * (pltpu.roll(v, lag, 0) * keep)
            conv_ref[at, :] = conv
            act = jax.nn.silu(conv).astype(BF16)
            act_ref[at, :] = act
            part[m] += lax.dot_general(act, sel_ref[...], (((1,), (1,)), ((), ())), preferred_element_type=F32)

    @pl.when(g == half - 1)
    def _():
        group.first()

    @pl.when(g >= half)
    def _():
        gate_ref[...] = jnp.dot(normed_ref[...], wg_ref[...], preferred_element_type=F32)

    @pl.when(g == half)
    def _():
        group.second()

    @pl.when(g == 2 * half - 1)
    def _():
        group.finish()
        dbl_ref[...] = total[...]
        for a, b in zip(hops, hops2):
            a.wait_send()
            b.wait()


def enter(lens, x_all, gain, wx, wg, taps, bias, sel, wo_block, n_f):
    n_dp = lens.shape[0]
    rows, width = x_all.shape
    tok = rows // n_dp
    ch = wx.shape[1]
    wide = sel.shape[0]
    piece = 256
    half = ch // piece
    whole = lambda g: (0, 0)
    early = lambda g: (0, jnp.minimum(g, half - 1))
    late = lambda g: (0, jnp.maximum(g - half, 0))
    once = pl.Buffered(1)
    any_ = pl.BlockSpec(memory_space=pl.ANY)
    shaped = lambda d, t: jax.ShapeDtypeStruct((rows, d), t)
    return pl.pallas_call(
        functools.partial(enter_kernel, n_f, half),
        grid=(2 * half,),
        in_specs=[
            pl.BlockSpec(memory_space=pltpu.SMEM),
            pl.BlockSpec((rows, width), whole, pipeline_mode=once),
            pl.BlockSpec((1, width), whole),
            pl.BlockSpec((width, piece), early),
            pl.BlockSpec((width, piece), late),
            pl.BlockSpec((taps.shape[0], piece), early),
            pl.BlockSpec((1, piece), early),
            pl.BlockSpec((wide, piece), early),
            any_,
        ],
        out_specs=[
            pl.BlockSpec((rows, width), whole),
            pl.BlockSpec((rows, piece), early),
            pl.BlockSpec((rows, piece), early),
            pl.BlockSpec((rows, piece), early),
            pl.BlockSpec((rows, piece), late),
            pl.BlockSpec((n_dp, tok, wide), lambda g: (0, 0, 0)),
            any_,
        ],
        out_shape=[
            shaped(width, BF16),
            shaped(ch, F32),
            shaped(ch, F32),
            shaped(ch, BF16),
            shaped(ch, F32),
            jax.ShapeDtypeStruct((n_dp, tok, wide), F32),
            jax.ShapeDtypeStruct((2, 2) + wo_block.shape, BF16),
        ],
        scratch_shapes=GroupSum.scratch(tok, wide)
        + [pltpu.SemaphoreType.DMA((2, 2)), pltpu.SemaphoreType.DMA((2, 2))],
        compiler_params=pltpu.CompilerParams(
            collective_id=1, has_side_effects=True, vmem_limit_bytes=48 * 2**20
        ),
        cost_estimate=pl.CostEstimate(flops=10**10, bytes_accessed=4 * 10**7, transcendentals=10**6),
    )(lens, x_all, gain, wx, wg, taps, bias, sel, wo_block)


def fold_matrix(n):
    i = lax.broadcasted_iota(jnp.int32, (n, TB * n), 0)
    j = lax.broadcasted_iota(jnp.int32, (n, TB * n), 1)
    return jnp.where(lax.rem(j, n) == i, 1.0, 0.0)


def own_token(n):
    i = lax.broadcasted_iota(jnp.int32, (TB, TB * n), 0)
    j = lax.broadcasted_iota(jnp.int32, (TB, TB * n), 1)
    return i == j // n


def block_rows(m, n):
    spread = jnp.dot(m.astype(BF16), fold_matrix(n).astype(BF16), preferred_element_type=F32)
    i = lax.broadcasted_iota(jnp.int32, spread.shape, 0)
    j = lax.broadcasted_iota(jnp.int32, spread.shape, 1)
    return jnp.where(lax.rem(i, TB) == j // n, spread, 0.0).astype(BF16)


def turned(m):
    n = m.shape[1]
    i = lax.broadcasted_iota(jnp.int32, (n, n), 0)
    j = lax.broadcasted_iota(jnp.int32, (n, n), 1)
    eye = jnp.where(i == j, 1.0, 0.0)
    return lax.dot_general(
        eye, m, (((1,), (1,)), ((), ())), preferred_element_type=F32, precision=lax.Precision.HIGHEST
    )


def softplus(v):
    return jnp.maximum(v, 0.0) + jnp.log1p(jnp.exp(-jnp.abs(v)))


class RingGather:
    def __init__(self, n_f, mine, near, out, local, send, recv):
        q = ring_place(lax.axis_index("fsdp"), n_f)
        at = lambda k: ring_index(lax.rem(q + k, n_f), n_f)
        count = [n_f // 2, n_f - 1 - n_f // 2]
        known = near.shape[1]
        self.locals = [pltpu.make_async_copy(mine, out.at[at(0)], local.at[0])]
        self.hops = [[], []]
        for up in (0, 1):
            for j in range(known):
                index = at(n_f - 1 - j if up else 1 + j)
                self.locals.append(pltpu.make_async_copy(near.at[up, j], out.at[index], local.at[1 + known * up + j]))
            for h in range(known, count[up]):
                index = at(n_f - h if up else h)
                src = near.at[up, known - 1] if h == known else out.at[index]
                self.hops[up].append(
                    ring_copy(n_f, src, out.at[index], send.at[up, h], recv.at[up, h], up)
                )
        self.events = max(len(h) for h in self.hops)

    def start(self):
        for c in self.locals:
            c.start()
        for up in (0, 1):
            if self.hops[up]:
                self.hops[up][0].start()

    def event(self, e):
        for up in (0, 1):
            if e < len(self.hops[up]):
                self.hops[up][e - 1].wait_recv()
                self.hops[up][e].start()

    def finish(self):
        for up in (0, 1):
            if self.hops[up]:
                self.hops[up][-1].wait_recv()
            for c in self.hops[up]:
                c.wait_send()
        for c in self.locals:
            c.wait()


def fwd_kernel(lanes, n_f, lens_ref, dbl_ref, act_ref, stepw_ref, stepb_ref, rate_ref, skip_ref, wo_ref, next_ref, dy_ref,
               y_ref, s_ref, delta_ref, pre_ref, wo_all, dy_all, carry, big_s, cw_s, bt_s, d_s, u_s, sc, local, hop_send, hop_recv, sh_send, sh_recv):
    n, ch = rate_ref.shape
    tblk = act_ref.shape[0]
    low_n = stepw_ref.shape[0]
    steps = pl.num_programs(0) * pl.num_programs(1)
    now = pl.program_id(0) * pl.num_programs(1) + pl.program_id(1)
    ring = RingGather(n_f, wo_ref, next_ref, wo_all, local, hop_send, hop_recv)
    share = PairShare(dy_ref, lambda m: dy_all.at[m], local.at[5], sh_send, sh_recv, True)

    @pl.when(now == 0)
    def _():
        greet_neighbours(n_f, True)
        ring.start()
        share.start()

    @pl.when(now == 13)
    def _():
        share.relay()

    for e in range(1, ring.events):

        @pl.when(now == min(7 * e, 15))
        def _(e=e):
            ring.event(e)

    @pl.when(pl.program_id(1) == 0)
    def _():
        carry[...] = jnp.zeros_like(carry)

    pre = jnp.dot(dbl_ref[:, :low_n].astype(BF16), stepw_ref[...], preferred_element_type=F32) + stepb_ref[...]
    pre_ref[...] = pre
    delta_ref[...] = softplus(pre)
    since, _ = segment_span(lens_ref, pl.program_id(0), pl.program_id(1) * tblk, tblk)
    big_s[...] = jnp.where(since == 0, RESET, 0.0)
    cw_s[...] = block_rows(dbl_ref[:, low_n + n : low_n + 2 * n], n)
    flat = turned(dbl_ref[:, low_n : low_n + n])
    for i in range(tblk // TB):
        bt_s[i] = flat[:, i * TB : (i + 1) * TB]

    def chunk(i, _):
        base = pl.multiple_of(i * TB, TB)
        dl = delta_ref[pl.ds(base, TB), :]
        ac = act_ref[pl.ds(base, TB), :].astype(F32)
        d_s[...] = dl + big_s[pl.ds(base, TB), :]
        u_s[...] = dl * ac
        bt = bt_s[i]
        for lo in range(0, ch, lanes):
            cs = pl.ds(lo, lanes)
            rate = rate_ref[:, cs]
            s = carry[:, cs]
            for t in range(TB):
                dec = jnp.exp2(d_s[t : t + 1, cs] * rate)
                s = dec * s + bt[:, t : t + 1] * u_s[t : t + 1, cs]
                sc[t * n : (t + 1) * n, cs] = s.astype(BF16)
            carry[:, cs] = s
        states = sc[...]
        y = jnp.dot(cw_s[pl.ds(base, TB), :], states, preferred_element_type=F32)
        y_ref[pl.ds(base, TB), :] = y + skip_ref[...] * ac
        s_ref[pl.ds(pl.multiple_of(base * n, TB * n), TB * n), :] = states
        return 0

    lax.fori_loop(0, tblk // TB, chunk, 0)

    @pl.when(now == steps - 1)
    def _():
        ring.finish()
        share.finish()


def scan_forward(lens, dbl, act, stepw, stepb, rate2, skip, wo_block, wo_next, dy_own, n_f, row_len, tblk=64, lanes=512):
    t, ch = act.shape
    n = rate2.shape[0]
    nb = row_len // tblk
    at = lambda r, j: (r * nb + j, 0)
    zero = lambda r, j: (0, 0)
    any_ = pl.BlockSpec(memory_space=pl.ANY)
    wide = jax.ShapeDtypeStruct((t, ch), F32)
    return pl.pallas_call(
        functools.partial(fwd_kernel, min(lanes, ch), n_f),
        grid=(t // row_len, nb),
        in_specs=[
            pl.BlockSpec(memory_space=pltpu.SMEM),
            pl.BlockSpec((tblk, dbl.shape[1]), at),
            pl.BlockSpec((tblk, ch), at),
            pl.BlockSpec(stepw.shape, zero),
            pl.BlockSpec((1, ch), zero),
            pl.BlockSpec((n, ch), zero),
            pl.BlockSpec((1, ch), zero),
            any_,
            any_,
            any_,
        ],
        out_specs=[
            pl.BlockSpec((tblk, ch), at),
            pl.BlockSpec((tblk * n, ch), at),
            pl.BlockSpec((tblk, ch), at),
            pl.BlockSpec((tblk, ch), at),
            any_,
            any_,
        ],
        out_shape=[
            wide,
            jax.ShapeDtypeStruct((t * n, ch), BF16),
            wide,
            wide,
            jax.ShapeDtypeStruct((n_f,) + wo_block.shape, BF16),
            jax.ShapeDtypeStruct((t // row_len,) + dy_own.shape, BF16),
        ],
        scratch_shapes=[
            pltpu.VMEM((n, ch), F32),
            pltpu.VMEM((tblk, 1), F32),
            pltpu.VMEM((tblk, TB * n), BF16),
            pltpu.VMEM((tblk // TB, n, TB), F32),
            pltpu.VMEM((TB, ch), F32),
            pltpu.VMEM((TB, ch), F32),
            pltpu.VMEM((TB * n, ch), BF16),
            pltpu.SemaphoreType.DMA((6,)),
            pltpu.SemaphoreType.DMA((2, n_f)),
            pltpu.SemaphoreType.DMA((2, n_f)),
            pltpu.SemaphoreType.DMA((3,)),
            pltpu.SemaphoreType.DMA((3,)),
        ],
        compiler_params=pltpu.CompilerParams(
            collective_id=2, has_side_effects=True, vmem_limit_bytes=32 * 2**20
        ),
        cost_estimate=pl.CostEstimate(flops=t * n * ch * 40, bytes_accessed=t * ch * 52, transcendentals=t * n * ch),
    )(lens, dbl, act, stepw, stepb, rate2, skip, wo_block, wo_next, dy_own)


def bwd_kernel(lanes, n_f, lens_ref, dbl_ref, delta_ref, pre_ref, act_ref, gy_ref, stepw_ref, rate_ref, skip_ref,
               s_ref, sp_ref, wg_part, gated_ref, dy_ref, wo_ref,
               pg_ref, da_ref, dbl_grad_ref, dl_ref, sums_ref, stepg_ref, wg_own, wo_out, wo_half, mixed_own,
               carry, big_s, bw_s, ct_s, d_all, u_all, g_all, h_all, b_all, c_all, part, near, far, total, gs_send, gs_recv,
               ring_got, ring_send, ring_recv, wo_got, wo_send, wo_recv, wo_part, mix, mix_near, mix_far, mix_send, mix_recv, wo_save):
    n, ch = rate_ref.shape
    tblk = act_ref.shape[0]
    low_n = stepw_ref.shape[0]
    r, j = pl.program_id(0), pl.program_id(1)
    n_dp, nb = pl.num_programs(0), pl.num_programs(1)
    m = row_at(r, n_dp)
    group = GroupSum(part, near, far, total, gs_send, gs_recv)
    ring = RingReduce(n_f, wg_part, ring_got, ring_send, ring_recv, n_f // 2)
    ring_o = RingReduce(n_f, wo_part, wo_got, wo_send, wo_recv, n_f - 1 - n_f // 2)
    pairs = PairReduce(mix, mix_near, mix_far, mix_send, mix_recv)
    now = r * nb + j
    last_step = n_dp * nb - 1
    @pl.when(j == 0)
    def _():
        carry[...] = jnp.zeros_like(carry)

    @pl.when((r == 0) & (j == 0))
    def _():
        greet_neighbours(n_f, True)
        ring.start()
        dl_ref[...] = jnp.zeros_like(dl_ref)
        sums_ref[...] = jnp.zeros_like(sums_ref)
        stepg_ref[...] = jnp.zeros_like(stepg_ref)

    for e in range(1, ring.events):

        @pl.when(now == min(4 * e, 15))
        def _(e=e):
            ring.event(e)
            if e == 2:
                ring_o.start()

    tile = 256
    parts = ch // tile
    save = pltpu.make_async_copy(wo_part, wo_out, wo_save)

    @pl.when(now < parts)
    def _():
        cs = wo_part.shape[1]
        cols = pl.ds(pl.multiple_of(now * tile, tile), tile)
        grad = lax.dot_general(
            gated_ref[:, cols], dy_ref[...], (((0,), (0,)), ((), ())), preferred_element_type=F32
        ).astype(BF16)
        for i in range(tile // cs):
            wo_part[now * (tile // cs) + i] = grad[i * cs : (i + 1) * cs]

    @pl.when(now == parts - 1)
    def _():
        save.start()

    @pl.when((now >= parts) & (now < parts + n_dp))
    def _():
        row_len = mix.shape[1]
        at = pl.ds(pl.multiple_of((now - parts) * row_len, row_len), row_len)
        mix[now - parts] = jnp.dot(gated_ref[at, :], wo_ref[...], preferred_element_type=F32).astype(BF16)

    @pl.when(now == 8)
    def _():
        pairs.start()

    @pl.when(now == 10)
    def _():
        pairs.middle()

    ones = jnp.where(own_token(n), 1.0, 0.0).astype(BF16)
    nt = (((1,), (1,)), ((), ()))
    row = lax.broadcasted_iota(jnp.int32, (TB * n, n), 0)
    col = lax.broadcasted_iota(jnp.int32, (TB * n, n), 1)
    fold = jnp.where(lax.rem(row, n) == col, 1.0, 0.0)
    since, _ = segment_span(lens_ref, m, (nb - 1 - j) * tblk, tblk)
    big_s[...] = jnp.where(since == 0, RESET, 0.0)
    bw_s[...] = block_rows(dbl_ref[:, low_n : low_n + n], n)

    flat = turned(dbl_ref[:, low_n + n : low_n + 2 * n])
    for i in range(tblk // TB):
        ct_s[i] = flat[:, i * TB : (i + 1) * TB]

    def lane_sum(value):
        total_ = value[:, :128]
        for at in range(128, value.shape[1], 128):
            total_ = total_ + value[:, at : at + 128]
        return total_

    def gathered(sums):
        spread = jnp.sum(sums, axis=1, keepdims=True) * fold
        high = spread.astype(BF16)
        rest = (spread - high.astype(F32)).astype(BF16)
        return jnp.dot(ones, high, preferred_element_type=F32) + jnp.dot(ones, rest, preferred_element_type=F32)

    for i in reversed(range(tblk // TB)):
        base = i * TB
        d_s, u_s, g_s, h_s, b_s, c_s = (v.at[i % 2] for v in (d_all, u_all, g_all, h_all, b_all, c_all))
        dl = delta_ref[base : base + TB, :]
        ac = act_ref[base : base + TB, :].astype(F32)
        d_s[...] = dl + big_s[base : base + TB, :]
        u_s[...] = dl * ac
        ct = ct_s[i]
        for lo in range(0, ch, lanes):
            cs = pl.ds(lo, lanes)
            rate = rate_ref[:, cs]
            flow = carry[:, cs]
            acc = dl_ref[:, cs]
            here = s_ref[(base + TB - 1) * n : (base + TB) * n, cs].astype(F32)
            for t in reversed(range(TB)):
                dr = d_s[t : t + 1, cs]
                dec = jnp.exp2(dr * rate)
                gy = gy_ref[base + t : base + t + 1, cs]
                g = ct[:, t : t + 1] * gy + flow
                flow = dec * g
                if base + t > 0:
                    prev = s_ref[(base + t - 1) * n : (base + t) * n, cs].astype(F32)
                else:
                    prev = sp_ref[:, cs].astype(F32)
                h = flow * prev
                acc = acc + h * dr
                at = slice(t * n, (t + 1) * n)
                b_now = lane_sum(g * u_s[t : t + 1, cs])
                c_now = lane_sum(here * gy)
                if lo:
                    b_now = b_now + b_s[at, :]
                    c_now = c_now + c_s[at, :]
                b_s[at, :] = b_now
                c_s[at, :] = c_now
                here = prev
                g_s[t * n : (t + 1) * n, cs] = g.astype(BF16)
                h_s[t * n : (t + 1) * n, cs] = (h * rate).astype(BF16)
            carry[:, cs] = flow
            dl_ref[:, cs] = acc
        gb = g_s[...]
        gy = gy_ref[base : base + TB, :]
        du = jnp.dot(bw_s[base : base + TB, :], gb, preferred_element_type=F32)
        hr = jnp.dot(ones, h_s[...], preferred_element_type=F32)
        dd = hr * (1.0 / LOG2E) + du * ac
        pg_ref[base : base + TB, :] = (dd * jax.nn.sigmoid(pre_ref[base : base + TB, :])).astype(BF16)
        da_ref[base : base + TB, :] = du * dl + skip_ref[...] * gy
        at = pl.ds(pl.multiple_of((nb - 1 - j) * tblk + base, TB), TB)
        part[m, at, low_n : low_n + n] = gathered(b_s[...])
        part[m, at, low_n + n : low_n + 2 * n] = gathered(c_s[...])

    pg = pg_ref[...]
    part[m, pl.ds(pl.multiple_of((nb - 1 - j) * tblk, tblk), tblk), :low_n] = lax.dot_general(
        pg, stepw_ref[...], nt, preferred_element_type=F32
    )
    stepg_ref[...] += lax.dot_general(
        dbl_ref[:, :low_n].astype(BF16), pg, (((0,), (0,)), ((), ())), preferred_element_type=F32
    )
    sums_ref[0:1, :] += jnp.sum(pg.astype(F32), axis=0, keepdims=True)
    sums_ref[1:2, :] += jnp.sum(gy_ref[...] * act_ref[...].astype(F32), axis=0, keepdims=True)

    @pl.when(j == nb - 1)
    def _():
        group.row_done(r)

    @pl.when((j == nb - 1) & (r == n_dp - 1))
    def _():
        ring_o.event(1)
        ring.finish(wg_own)
        group.finish()
        dbl_grad_ref[...] = total[...]
        pairs.finish(mixed_own)
        ring_o.stop(2, wo_half)
        save.wait()


def scan_backward(lens, dbl, delta, pre, act, gy, stepw, rate2, skip, states, wg_part, gated, dy_all, wo, n_f, row_len,
                  tblk=64, lanes=512):
    t, ch = delta.shape
    n = rate2.shape[0]
    nb = row_len // tblk
    n_dp = t // row_len
    wide = dbl.shape[1]
    width = wo.shape[1]
    cs = ch // n_f
    spot = lambda r, j: row_at(r, n_dp) * nb + nb - 1 - j
    at = lambda r, j: (spot(r, j), 0)
    zero = lambda r, j: (0, 0)
    entry = lambda r, j: (jnp.maximum(spot(r, j) * tblk - 1, 0), 0)
    return pl.pallas_call(
        functools.partial(bwd_kernel, min(lanes, ch), n_f),
        grid=(n_dp, nb),
        in_specs=[
            pl.BlockSpec(memory_space=pltpu.SMEM),
            pl.BlockSpec((tblk, wide), at),
            pl.BlockSpec((tblk, ch), at),
            pl.BlockSpec((tblk, ch), at),
            pl.BlockSpec((tblk, ch), at),
            pl.BlockSpec((tblk, ch), at),
            pl.BlockSpec(stepw.shape, zero),
            pl.BlockSpec((n, ch), zero),
            pl.BlockSpec((1, ch), zero),
            pl.BlockSpec((tblk * n, ch), at),
            pl.BlockSpec((n, ch), entry),
            pl.BlockSpec(memory_space=pltpu.VMEM),
            pl.BlockSpec(memory_space=pltpu.VMEM),
            pl.BlockSpec(memory_space=pltpu.VMEM),
            pl.BlockSpec(memory_space=pltpu.VMEM),
        ],
        out_specs=[
            pl.BlockSpec((tblk, ch), at),
            pl.BlockSpec((tblk, ch), at),
            pl.BlockSpec((n_dp, row_len, wide), lambda r, j: (0, 0, 0)),
            pl.BlockSpec((n, ch), zero),
            pl.BlockSpec((8, ch), zero),
            pl.BlockSpec(stepw.shape, zero),
            pl.BlockSpec(wg_part.shape[1:], zero),
            pl.BlockSpec(memory_space=pl.ANY),
            pl.BlockSpec((2, cs, width), lambda r, j: (0, 0, 0)),
            pl.BlockSpec((row_len, width), zero),
        ],
        out_shape=[
            jax.ShapeDtypeStruct((t, ch), BF16),
            jax.ShapeDtypeStruct((t, ch), F32),
            jax.ShapeDtypeStruct((n_dp, row_len, wide), F32),
            jax.ShapeDtypeStruct((n, ch), F32),
            jax.ShapeDtypeStruct((8, ch), F32),
            jax.ShapeDtypeStruct(stepw.shape, F32),
            jax.ShapeDtypeStruct(wg_part.shape[1:], BF16),
            jax.ShapeDtypeStruct((n_f, cs, width), BF16),
            jax.ShapeDtypeStruct((2, cs, width), BF16),
            jax.ShapeDtypeStruct((row_len, width), BF16),
        ],
        scratch_shapes=[
            pltpu.VMEM((n, ch), F32),
            pltpu.VMEM((tblk, 1), F32),
            pltpu.VMEM((tblk, TB * n), BF16),
            pltpu.VMEM((tblk // TB, n, TB), F32),
            pltpu.VMEM((2, TB, ch), F32),
            pltpu.VMEM((2, TB, ch), F32),
            pltpu.VMEM((2, TB * n, ch), BF16),
            pltpu.VMEM((2, TB * n, ch), BF16),
            pltpu.VMEM((2, TB * n, 128), F32),
            pltpu.VMEM((2, TB * n, 128), F32),
        ]
        + GroupSum.scratch(row_len, wide)
        + RingReduce.scratch(n_f, wg_part.shape[1:])
        + RingReduce.scratch(n_f, (cs, width), BF16, 2)
        + [pltpu.VMEM((n_f, cs, width), BF16), pltpu.VMEM((n_dp, row_len, width), BF16)]
        + PairReduce.scratch((row_len, width))
        + [pltpu.SemaphoreType.DMA],
        compiler_params=pltpu.CompilerParams(
            collective_id=3, has_side_effects=True, vmem_limit_bytes=60 * 2**20
        ),
        cost_estimate=pl.CostEstimate(flops=t * n * ch * 80, bytes_accessed=t * ch * 60, transcendentals=t * n * ch),
    )(lens, dbl, delta, pre, act, gy, stepw, rate2, skip, states, states, wg_part, gated, dy_all, wo)


class Return:
    def __init__(self, count, n_f, buf, out, local, send, recv):
        self.count, self.n_f, self.buf, self.out = count, n_f, buf, out
        self.local, self.send, self.recv = local, send, recv
        self.me = lax.axis_index("dp") * n_f + lax.axis_index("fsdp")

    def fill(self, pick, values):
        count, pair = self.buf.shape[:2]

        def piece(j, _):
            cols = pl.ds(pl.multiple_of(j * 256, 256), 256)
            moved = jnp.dot(pick, values[:, cols].astype(BF16), preferred_element_type=F32)
            self.buf[:, :, cols] = moved.astype(BF16).reshape(count, pair, 256)
            return 0

        lax.fori_loop(0, values.shape[1] // 256, piece, 0)

    def start(self):
        def one(p, _):
            pltpu.make_async_remote_copy(
                src_ref=self.buf.at[p],
                dst_ref=self.out.at[p],
                send_sem=self.send,
                recv_sem=self.recv,
                device_id=mesh_at(lax.rem(self.me + self.count - p, self.count), self.n_f),
                device_id_type=pl.DeviceIdType.MESH,
            ).start()
            return 0

        pltpu.make_async_copy(self.buf.at[0], self.out.at[0], self.local).start()
        lax.fori_loop(1, self.count, one, 0)

    def finish(self):
        pltpu.make_async_copy(self.buf.at[0], self.out.at[0], self.local).wait()
        rest = pl.ds(1, self.count - 1)
        for sem in (self.recv, self.send):
            pltpu.make_async_copy(self.buf.at[rest], self.out.at[rest], sem).wait()


def leave_kernel(n_f, half, lens_ref, da_ref, conv_ref, xin_ref, act_ref, dblg_ref, sel_ref, taps_ref,
                 sums_ref, dsum_ref, rate_ref, stepg_ref, normed_ref, wx_ref, wg_ref, gg_ref,
                 wo_part, wo_half, wg_own, x_own, dy_own, mixed_own, gain_ref, tags_ref, ride_ref,
                 mix_back, dx_back, gin_all, go_all, small_all,
                 ig_s, wx_s, ng_s, small_s, pick_s, ret_mix, ret_dx, change_s,
                 wo_got, wo_send, wo_recv, wx_got, wx_send, wx_recv, sm_got, sm_send, sm_recv,
                 ng_near, ng_far, ng_send, ng_recv, wo_own, wx_own, sm_own, local, sh_send, sh_recv, ret_sem):
    g = pl.program_id(0)
    steps = pl.num_programs(0)
    n_dp, tok, wide = dblg_ref.shape
    count = n_dp * n_f
    width = x_own.shape[1]
    ch = ig_s.shape[1]
    piece = 256
    n_taps = taps_ref.shape[0]
    down = n_f // 2
    ring_o = RingReduce(n_f, wo_part, wo_got, wo_send, wo_recv, n_f - 1 - down)
    ring_x = RingReduce(n_f, wx_s, wx_got, wx_send, wx_recv, down)
    ring_s = RingReduce(n_f, small_s, sm_got, sm_send, sm_recv, down)
    pairs = [
        PairReduce(ng_s.at[h], ng_near.at[h], ng_far.at[h], ng_send.at[h], ng_recv.at[h]) for h in (0, 1)
    ]
    blocks = width // piece
    turn = half + blocks
    shares = [
        PairShare(mine, out, local.at[i], sh_send.at[i], sh_recv.at[i])
        for i, (mine, out) in enumerate(
            [
                (wg_own, lambda d: gin_all.at[d, :, pl.ds(ch, ch)]),
                (wo_own, lambda d: go_all.at[d]),
                (wx_own, lambda d: gin_all.at[d, :, pl.ds(0, ch)]),
                (sm_own, lambda d: lane_block(small_all, d, sm_own.shape[1])),
            ]
        )
    ]
    ret_m = Return(count, n_f, ret_mix, mix_back, local.at[4], ret_sem.at[0], ret_sem.at[1])
    ret_x = Return(count, n_f, ret_dx, dx_back, local.at[5], ret_sem.at[2], ret_sem.at[3])
    tn = (((0,), (0,)), ((), ()))
    nt = (((1,), (1,)), ((), ()))

    @pl.when(g == 0)
    def _():
        me = lax.axis_index("dp") * n_f + lax.axis_index("fsdp")
        barrier = pltpu.get_barrier_semaphore()

        def greet(p, _):
            pl.semaphore_signal(
                barrier, inc=1, device_id=mesh_at(lax.rem(me + p, count), n_f), device_id_type=pl.DeviceIdType.MESH
            )
            return 0

        lax.fori_loop(1, count, greet, 0)
        pl.semaphore_wait(barrier, count - 1)
        ring_o.resume(2, wo_half)
        shares[0].start()
        spots = jnp.concatenate([tags_ref[...]] * (tok // 128), axis=1)
        lane = lax.broadcasted_iota(jnp.int32, (tok, tok), 1).astype(F32)
        pick_s[...] = jnp.where(spots == lane, 1.0, 0.0).astype(BF16)
        ret_m.fill(pick_s[...], mixed_own)
        ret_mix[:, :, width:] = jnp.broadcast_to(ride_ref[...], (tok, 128)).astype(BF16).reshape(
            count, tok // count, 128
        )
        ret_m.start()

    for e in range(3, ring_o.events):

        @pl.when(g == min(turn + e - 2, steps - 2))
        def _(e=e):
            ring_o.event(e)

    @pl.when(g == turn)
    def _():
        ring_x.start()
        ring_s.start()

    @pl.when(g == turn + blocks // 2)
    def _():
        pairs[0].start()

    @pl.when(g == steps - 2)
    def _():
        pairs[0].middle()

    @pl.when(g < half)
    def _():
        cols = pl.ds(pl.multiple_of(g * piece, piece), piece)
        zero = jnp.zeros((1, piece), F32)
        misc = [zero] * (n_taps + 1)
        sel_grad = jnp.zeros((wide, piece), F32)
        for m in range(n_dp):
            at = slice(m * tok, (m + 1) * tok)
            low = dblg_ref[m].astype(BF16)
            since, left = segment_span(lens_ref, m, 0, tok)
            act_grad = da_ref[at, :] + jnp.dot(low, sel_ref[...], preferred_element_type=F32)
            conv_grad = act_grad * silu_slope(conv_ref[at, :])
            back = taps_ref[n_taps - 1 : n_taps, :] * conv_grad
            x_in = xin_ref[at, :]
            misc[n_taps - 1] = misc[n_taps - 1] + jnp.sum(conv_grad * x_in, axis=0, keepdims=True)
            for lag in range(1, n_taps):
                tap = n_taps - 1 - lag
                later = pltpu.roll(conv_grad, tok - lag, 0) * (left >= lag).astype(F32)
                back = back + taps_ref[tap : tap + 1, :] * later
                misc[tap] = misc[tap] + jnp.sum(later * x_in, axis=0, keepdims=True)
            ig_s[at, cols] = back.astype(BF16)
            misc[n_taps] = misc[n_taps] + jnp.sum(conv_grad, axis=0, keepdims=True)
            sel_grad = sel_grad + lax.dot_general(low, act_ref[at, :], tn, preferred_element_type=F32)
        rows = jnp.concatenate(
            [
                sel_grad,
                stepg_ref[...],
                dsum_ref[...] * rate_ref[...],
                jnp.concatenate(misc + [sums_ref[0:2, :], zero], axis=0),
                jnp.zeros((small_s.shape[1] - wide - stepg_ref.shape[0] - rate_ref.shape[0] - 8, piece), F32),
            ],
            axis=0,
        )
        cs = small_s.shape[2]
        for i in range(piece // cs):
            small_s[g * (piece // cs) + i] = rows[:, i * cs : (i + 1) * cs]

    @pl.when((g >= half) & (g < turn))
    def _():
        block = g - half
        dcols = wx_s.shape[1]
        grad = lax.dot_general(normed_ref[...], ig_s[...], tn, preferred_element_type=F32).astype(BF16)
        for i in range(piece // dcols):
            wx_s[block * (piece // dcols) + i] = grad[i * dcols : (i + 1) * dcols]

    @pl.when(g >= turn)
    def _():
        grad = lax.dot_general(ig_s[...], wx_ref[...], nt, preferred_element_type=F32)
        grad = grad + lax.dot_general(gg_ref[...], wg_ref[...], nt, preferred_element_type=F32)
        grad = grad.astype(BF16).reshape(n_dp, tok, piece)
        for h in (0, 1):

            @pl.when((g - turn) // (blocks // 2) == h)
            def _(h=h):
                at = (g - turn - h * (blocks // 2)) * piece
                ng_s[h, :, :, pl.ds(pl.multiple_of(at, piece), piece)] = grad

    @pl.when(g == steps - 1)
    def _():
        pairs[1].start()
        shares[0].relay()
        pairs[1].middle()
        if ring_x.events > 1:
            ring_s.event(1)
            ring_x.event(1)
        ring_o.finish(wo_own, 2)
        shares[1].start()
        for h in (0, 1):
            pairs[h].finish(change_s.at[:, pl.ds(h * (width // 2), width // 2)])

        def rows(i, _):
            at = pl.ds(pl.multiple_of(i * 16, 16), 16)
            v = x_own[at, :].astype(F32)
            rstd = lax.rsqrt(jnp.mean(v * v, axis=1, keepdims=True) + EPS)
            hat = v * rstd
            grad = change_s[at, :] * gain_ref[...]
            grad = rstd * (grad - hat * jnp.mean(grad * hat, axis=1, keepdims=True))
            change_s[at, :] = dy_own[at, :].astype(F32) + grad
            return 0

        lax.fori_loop(0, tok // 16, rows, 0)
        ret_x.fill(pick_s[...], change_s)
        ret_x.start()
        for e in range(2, ring_x.events):
            ring_s.event(e)
            ring_x.event(e)
        shares[1].relay()
        ring_s.finish(sm_own)
        shares[3].start()
        ring_x.finish(wx_own)
        shares[2].start()
        shares[3].relay()
        shares[2].relay()
        for share in shares:
            share.finish()
        ret_m.finish()
        ret_x.finish()


def leave(lens, da, conv, x_in, act, dbl_grad, sel, taps, sums, decay_sum, rate, stepg, normed, wx, wg, gate_grad,
          wo_part, wo_half, wg_own, x_own, dy_own, mixed_own, gain, tags, ride, n_f):
    n_dp, tok, wide = dbl_grad.shape
    group, ch = act.shape
    width = x_own.shape[1]
    count = n_dp * n_f
    pair = tok // count
    piece = 256
    half = ch // piece
    dcols = width // n_f
    cs = ch // n_f
    n = rate.shape[0]
    tall = -(-(wide + stepg.shape[0] + n + 8) // 64) * 64
    blocks = width // piece
    early = lambda g: (0, jnp.minimum(g, half - 1))
    late = lambda g: (0, jnp.clip(g - half, 0, blocks - 1))
    late_rows = lambda g: (jnp.maximum(g - half - blocks, 0), 0)
    any_ = pl.BlockSpec(memory_space=pl.ANY)
    vmem = pl.BlockSpec(memory_space=pltpu.VMEM)
    block = lambda rows: pl.BlockSpec((rows, piece), early)
    shaped = jax.ShapeDtypeStruct
    return pl.pallas_call(
        functools.partial(leave_kernel, n_f, half),
        grid=(half + 2 * blocks,),
        in_specs=[
            pl.BlockSpec(memory_space=pltpu.SMEM),
            block(group),
            block(group),
            block(group),
            block(group),
            vmem,
            block(wide),
            block(taps.shape[0]),
            block(8),
            block(n),
            block(n),
            block(stepg.shape[0]),
            pl.BlockSpec((group, piece), late),
            pl.BlockSpec((piece, ch), late_rows),
            pl.BlockSpec((piece, ch), late_rows),
        ]
        + [vmem] * 10,
        out_specs=[any_] * 5,
        out_shape=[
            shaped((count, pair, width + 128), BF16),
            shaped((count, pair, width), BF16),
            shaped((n_dp, dcols, 2 * ch), BF16),
            shaped((n_dp, cs, width), BF16),
            shaped(side_by_side(n_dp, tall, cs), F32),
        ],
        scratch_shapes=[
            pltpu.VMEM((group, ch), BF16),
            pltpu.VMEM((n_f, dcols, ch), BF16),
            pltpu.VMEM((2, n_dp, tok, width // 2), BF16),
            pltpu.VMEM((n_f, tall, cs), F32),
            pltpu.VMEM((tok, tok), BF16),
            pltpu.VMEM((count, pair, width + 128), BF16),
            pltpu.VMEM((count, pair, width), BF16),
            pltpu.VMEM((tok, width), F32),
        ]
        + RingReduce.scratch(n_f, (cs, width))
        + RingReduce.scratch(n_f, (dcols, ch))
        + RingReduce.scratch(n_f, (tall, cs), F32)
        + [
            pltpu.VMEM((2, 2, tok, width // 2), BF16),
            pltpu.VMEM((2, tok, width // 2), BF16),
            pltpu.SemaphoreType.DMA((2, 3)),
            pltpu.SemaphoreType.DMA((2, 3)),
            pltpu.VMEM((cs, width), BF16),
            pltpu.VMEM((dcols, ch), BF16),
            pltpu.VMEM((tall, cs), F32),
            pltpu.SemaphoreType.DMA((6,)),
            pltpu.SemaphoreType.DMA((4, 3)),
            pltpu.SemaphoreType.DMA((4, 3)),
            pltpu.SemaphoreType.DMA((4,)),
        ],
        compiler_params=pltpu.CompilerParams(
            collective_id=4, has_side_effects=True, vmem_limit_bytes=62 * 2**20
        ),
        cost_estimate=pl.CostEstimate(flops=2 * 10**10, bytes_accessed=6 * 10**7, transcendentals=10**6),
    )(lens, da, conv, x_in, act, dbl_grad, sel, taps, sums, decay_sum, rate, stepg, normed, wx, wg, gate_grad,
      wo_part, wo_half, wg_own, x_own, dy_own, mixed_own, gain, tags, ride)


def masks_of(count):
    return [1 << b for b in range(count.bit_length() - 1)]


def mesh_at(index, n_f):
    return (index // n_f, lax.rem(index, n_f))


def ring_index(p, n_f):
    if n_f % 2:
        return p
    return jnp.where(p < n_f // 2, 2 * p, 2 * (n_f - 1 - p) + 1)


def ring_place(f, n_f):
    if n_f % 2:
        return f
    return jnp.where(lax.rem(f, 2) == 0, f // 2, n_f - 1 - f // 2)


def gather_kernel(n_dp, n_f, downs, x_ref, dy_ref, meta_ref, dest_ref, lens_ref, *refs):
    streams = len(downs)
    blocks = refs[:streams]
    x_all, lens_all, x_own_ref, dy_own_ref, tag_ref, rank_ref = refs[streams : streams + 6]
    outs = refs[streams + 6 : 2 * streams + 6]
    (send_x, send_dy, got_x, got_dy, x_own, dy_own, deal_sem, loc_sem, pair_send, pair_recv, ring_send, ring_recv) = (
        refs[2 * streams + 6 :]
    )
    count = n_dp * n_f
    me_d = lax.axis_index("dp")
    me_f = lax.axis_index("fsdp")
    me = me_d * n_f + me_f
    q = ring_place(me_f, n_f)
    below = ring_index(lax.rem(q + n_f - 1, n_f), n_f)
    above = ring_index(lax.rem(q + 1, n_f), n_f)

    barrier = pltpu.get_barrier_semaphore()

    def greet(p, _):
        pl.semaphore_signal(
            barrier, inc=1, device_id=mesh_at(lax.rem(me + p, count), n_f), device_id_type=pl.DeviceIdType.MESH
        )
        return 0

    lax.fori_loop(1, count, greet, 0)
    def place_of(s, index):
        return lane_block(outs[s], index, blocks[s].shape[1]) if s == 0 else outs[s].at[index]

    locals_ = [
        pltpu.make_async_copy(blocks[s], place_of(s, me_f), loc_sem.at[s]) for s in range(streams)
    ]
    for c in locals_:
        c.start()
    pl.semaphore_wait(barrier, count - 1)

    def deal(a):
        src, dst = ((send_x, got_x), (send_dy, got_dy))[a]

        def one(p, _):
            pltpu.make_async_remote_copy(
                src_ref=src.at[p],
                dst_ref=dst.at[p],
                send_sem=deal_sem.at[a, 0],
                recv_sem=deal_sem.at[a, 1],
                device_id=mesh_at(lax.rem(me + p, count), n_f),
                device_id_type=pl.DeviceIdType.MESH,
            ).start()
            return 0

        lax.fori_loop(1, count, one, 0)
        dst[0] = src[0]

    def dealt(a, way):
        src, dst = ((send_x, got_x), (send_dy, got_dy))[a]
        rest = pl.ds(1, count - 1)
        pltpu.make_async_copy(src.at[rest], dst.at[rest], deal_sem.at[a, way]).wait()

    def hop(s, h, up):
        k = lax.rem(q + (n_f - h if up else h), n_f)
        index = ring_index(k, n_f)
        src = blocks[s] if h == 0 else place_of(s, index)
        return pltpu.make_async_remote_copy(
            src_ref=src,
            dst_ref=place_of(s, index),
            send_sem=ring_send.at[s, int(up), h],
            recv_sem=ring_recv.at[s, int(up), h],
            device_id=(me_d, above if up else below),
            device_id_type=pl.DeviceIdType.MESH,
        )

    hops = [[downs[s], n_f - 1 - downs[s]] for s in range(streams)]
    for s in range(streams):
        for up in (0, 1):
            if hops[s][up]:
                hop(s, 0, up).start()
    tok, width = x_own.shape
    pair = got_x.shape[1]

    dest_row, rel_row, abs_row, in_row = (meta_ref[i : i + 1, :] for i in range(4))
    rank = jnp.sum((dest_ref[...] < dest_row).astype(F32), axis=0, keepdims=True)
    goal = rel_row * pair + rank - abs_row * pair
    rank_ref[...] = jnp.broadcast_to(goal, rank_ref.shape)
    chosen = lax.broadcasted_iota(jnp.int32, (tok, tok), 0).astype(F32) == goal
    spot = jnp.sum(jnp.where(chosen, in_row, 0.0), axis=1, keepdims=True)
    send_x[:, :, width:] = jnp.broadcast_to(spot, (tok, 128)).astype(BF16).reshape(count, pair, 128)
    pick = jnp.where(chosen, 1.0, 0.0).astype(BF16)

    def sort(values, out):
        def part(j, _):
            cols = pl.ds(pl.multiple_of(j * 256, 256), 256)
            moved = jnp.dot(pick, values[:, cols], preferred_element_type=F32)
            out[:, :, cols] = moved.astype(BF16).reshape(count, pair, 256)
            return 0

        lax.fori_loop(0, width // 256, part, 0)

    sort(x_ref, send_x)
    deal(0)
    sort(dy_ref, send_dy)
    deal(1)

    def advance(h):
        for s in range(streams):
            for up in (0, 1):
                if h < hops[s][up]:
                    hop(s, h - 1, up).wait_recv()
                    hop(s, h, up).start()

    dealt(0, 1)
    tag = got_x[:, :, width : width + 128].astype(F32).reshape(tok, 128)
    spots = jnp.concatenate([tag] * (tok // 128), axis=1)
    lane = lax.broadcasted_iota(jnp.int32, (tok, tok), 1).astype(F32)
    settle = jnp.where(spots == lane, 1.0, 0.0).astype(BF16)
    tn = (((0,), (0,)), ((), ()))
    tag_ref[...] = tag

    def place(values, out):
        def part(j, _):
            cols = pl.ds(pl.multiple_of(j * 256, 256), 256)
            block = values[:, :, cols].reshape(tok, 256)
            out[:, cols] = lax.dot_general(settle, block, tn, preferred_element_type=F32).astype(BF16)
            return 0

        lax.fori_loop(0, width // 256, part, 0)

    masks = list(reversed(masks_of(n_dp)))

    def partner(mask):
        return me_d + mask - 2 * mask * lax.rem(me_d // mask, 2)

    def share(a, m, mask):
        out = (x_all, lens_all)[a]
        own_block = (x_own, lens_ref)[a]
        return pltpu.make_async_remote_copy(
            src_ref=own_block if m == 0 else out.at[m],
            dst_ref=out.at[m | mask],
            send_sem=pair_send.at[a, m | mask],
            recv_sem=pair_recv.at[a, m | mask],
            device_id=(partner(mask), me_f),
            device_id_type=pl.DeviceIdType.MESH,
        )

    copies = []

    def keep(src, dst):
        c = pltpu.make_async_copy(src, dst, loc_sem.at[streams + len(copies)])
        c.start()
        copies.append(c)

    place(got_x, x_own)
    for a in (0, 1):
        for mask in masks:
            share(a, 0, mask).start()
    keep(lens_ref, lens_all.at[0])
    keep(x_own, x_all.at[0])
    keep(x_own, x_own_ref)
    advance(1)

    def relay(a):
        held = [0]
        for step, mask in enumerate(masks):
            for m in held:
                if m:
                    share(a, m, mask).start()
            for m in held:
                share(a, m, mask).wait_recv()
            held = held + [m | mask for m in held]

    most = max(max(h) for h in hops)
    for h in range(2, most):
        advance(h)
        if h == 2:
            dealt(1, 1)
            place(got_dy, dy_own)
            keep(dy_own, dy_own_ref)
            relay(0)
    if most <= 2:
        dealt(1, 1)
        place(got_dy, dy_own)
        keep(dy_own, dy_own_ref)
        relay(0)
    relay(1)
    for s in range(streams):
        for up in (0, 1):
            if hops[s][up]:
                hop(s, hops[s][up] - 1, up).wait_recv()
    for s in range(streams):
        for up in (0, 1):
            for h in range(hops[s][up]):
                hop(s, h, up).wait_send()
    for a in (0, 1):
        held = [0]
        for mask in masks:
            for m in held:
                share(a, m, mask).wait_send()
            held = held + [m | mask for m in held]
    for c in locals_ + copies:
        c.wait()
    dealt(0, 0)
    dealt(1, 0)


def gather_all(x, dy, meta, dest, lens, blocks, downs, n_dp, n_f):
    streams = len(blocks)
    tok, width = x.shape
    count = n_dp * n_f
    sent_x = (count, tok // count, width + 128)
    sent_dy = (count, tok // count, width)
    hops = max(max(d, n_f - 1 - d) for d in downs)
    any_ = pl.BlockSpec(memory_space=pl.ANY)
    vmem = pl.BlockSpec(memory_space=pltpu.VMEM)
    row = jax.ShapeDtypeStruct((tok, width), BF16)
    rows = jax.ShapeDtypeStruct((n_dp, tok, width), BF16)
    return pl.pallas_call(
        functools.partial(gather_kernel, n_dp, n_f, downs),
        in_specs=[vmem] * 5 + [any_] * streams,
        out_specs=[any_] * 4 + [vmem] * 2 + [any_] * streams,
        out_shape=[
            rows,
            jax.ShapeDtypeStruct((n_dp,) + lens.shape, lens.dtype),
            row,
            row,
            jax.ShapeDtypeStruct((tok, 128), F32),
            jax.ShapeDtypeStruct((8, tok), F32),
        ]
        + [jax.ShapeDtypeStruct(side_by_side(n_f, *blocks[0].shape), BF16)]
        + [jax.ShapeDtypeStruct((n_f,) + b.shape, b.dtype) for b in blocks[1:]],
        scratch_shapes=[
            pltpu.VMEM(sent_x, BF16),
            pltpu.VMEM(sent_dy, BF16),
            pltpu.VMEM(sent_x, BF16),
            pltpu.VMEM(sent_dy, BF16),
            pltpu.VMEM((tok, width), BF16),
            pltpu.VMEM((tok, width), BF16),
            pltpu.SemaphoreType.DMA((2, 2)),
            pltpu.SemaphoreType.DMA((streams + 4,)),
            pltpu.SemaphoreType.DMA((2, n_dp)),
            pltpu.SemaphoreType.DMA((2, n_dp)),
            pltpu.SemaphoreType.DMA((streams, 2, hops)),
            pltpu.SemaphoreType.DMA((streams, 2, hops)),
        ],
        compiler_params=pltpu.CompilerParams(
            collective_id=0, has_side_effects=True, vmem_limit_bytes=40 * 2**20
        ),
        cost_estimate=pl.CostEstimate(flops=10**10, bytes_accessed=2 * 10**8, transcendentals=0),
    )(x, dy, meta, dest, lens, *blocks)


def columns_kernel(starts, cs, w_ref, *outs):
    me_d = lax.axis_index("dp")
    for o, out in enumerate(outs):
        for j, start in enumerate(starts[o]):
            out[:, j * cs : (j + 1) * cs] = w_ref[:, pl.ds(pl.multiple_of(start + me_d * cs, 128), cs)]


def take_columns(w, halves, n_f, n_dp, cs):
    inner = n_f * n_dp * cs
    starts = [[h * inner + f * n_dp * cs for f in range(n_f)] for h in range(halves)]
    me_d = lax.axis_index("dp")
    if cs % 128:
        return [
            jnp.concatenate([lax.dynamic_slice_in_dim(w, s + me_d * cs, cs, 1) for s in group], axis=1)
            for group in starts
        ]
    height = w.shape[0]
    blk = min(height, 64)
    return pl.pallas_call(
        functools.partial(columns_kernel, starts, cs),
        grid=(height // blk,),
        in_specs=[pl.BlockSpec((blk, w.shape[1]), lambda i: (i, 0))],
        out_specs=[pl.BlockSpec((blk, n_f * cs), lambda i: (i, 0))] * halves,
        out_shape=[jax.ShapeDtypeStruct((height, n_f * cs), w.dtype)] * halves,
    )(w)


def spread_kernel(cs, x_ref, w_ref, out_ref, sum_ref):
    total = jnp.zeros(sum_ref.shape, F32)
    n_dp = x_ref.shape[0]
    for f in range(x_ref.shape[2] // cs):
        for i in range(n_dp):
            part = x_ref[i, :, f * cs : (f + 1) * cs].astype(F32)
            cols = slice((f * n_dp + i) * cs, (f * n_dp + i + 1) * cs)
            out_ref[:, cols] = part
            product = part * w_ref[:, cols].astype(F32)
            for j in range(0, cs, 128):
                total = total + product[:, j : j + 128]

    @pl.when(pl.program_id(0) == 0)
    def _():
        sum_ref[...] = jnp.zeros_like(sum_ref)

    sum_ref[...] += total


def spread_columns(parts, w, cs):
    n_dp, height, cols = parts.shape
    if cs % 128:
        out = parts.reshape(n_dp, height, cols // cs, cs).transpose(1, 2, 0, 3).reshape(height, n_dp * cols).astype(F32)
        return out, jnp.sum(out * w.astype(F32), axis=1)
    wide = 2 * cs
    out, sums = pl.pallas_call(
        functools.partial(spread_kernel, cs),
        grid=(cols // wide,),
        in_specs=[
            pl.BlockSpec((n_dp, height, wide), lambda f: (0, 0, f)),
            pl.BlockSpec((height, n_dp * wide), lambda f: (0, f)),
        ],
        out_specs=[
            pl.BlockSpec((height, n_dp * wide), lambda f: (0, f)),
            pl.BlockSpec((height, 128), lambda f: (0, 0)),
        ],
        out_shape=[jax.ShapeDtypeStruct((height, n_dp * cols), F32), jax.ShapeDtypeStruct((height, 128), F32)],
        compiler_params=pltpu.CompilerParams(vmem_limit_bytes=32 * 2**20),
        cost_estimate=pl.CostEstimate(flops=4 * height * cols * n_dp, bytes_accessed=8 * height * cols * n_dp, transcendentals=0),
    )(parts, w)
    return out, jnp.sum(sums, axis=1)


def per_device(
    tokens,
    cotangent,
    destination,
    lengths,
    norm_gain,
    in_weight,
    conv_weight,
    conv_bias,
    select_weight,
    step_weight,
    step_bias,
    decay_log,
    skip_gain,
    out_weight,
):
    n_dp = lax.axis_size("dp")
    n_f = lax.axis_size("fsdp")
    rows = n_dp * n_f
    tok = tokens.shape[0]
    width = tokens.shape[1]
    pair = tok // rows
    inner = conv_bias.shape[0] * n_f
    cs = conv_bias.shape[0] // n_dp
    ch = cs * n_f
    taps = conv_weight.shape[0]
    n = decay_log.shape[0]
    rank_of = step_weight.shape[0]
    dcols = width // n_f
    group = n_dp * tok
    both = ("dp", "fsdp")
    me_d = lax.axis_index("dp")
    me_f = lax.axis_index("fsdp")
    flat_dot = lambda a, b: jnp.dot(a, b, preferred_element_type=F32)
    nt_dot = lambda a, b: lax.dot_general(a, b, (((1,), (1,)), ((), ())), preferred_element_type=F32)
    tn_dot = lambda a, b: lax.dot_general(a, b, (((0,), (0,)), ((), ())), preferred_element_type=F32)

    me = me_d * n_f + me_f
    row_to = destination // tok
    meta = jnp.stack(
        [destination, (row_to - me) % rows, row_to, destination % tok] + [jnp.zeros_like(destination)] * 4
    ).astype(F32)
    segs = lengths.shape[1]
    lens_tile = jnp.pad(lengths, ((0, 7), (0, 128 - segs)))
    slots = jnp.arange(tok, dtype=jnp.int32)

    def mine(shard):
        return lax.dynamic_slice_in_dim(shard.reshape(-1, n_dp * cs), me_d * cs, cs, 1)

    smalls = [conv_weight, conv_bias, step_bias, skip_gain, decay_log, select_weight, step_weight]
    heights = [math.prod(s.shape) // (n_dp * cs) for s in smalls]
    gain_rows = dcols // cs
    used = sum(heights) + gain_rows
    filler = -used % 16
    small_block = jnp.concatenate(
        [mine(s) for s in smalls] + [norm_gain.reshape(gain_rows, cs), jnp.zeros((filler, cs), BF16)], axis=0
    )
    wx_block, wg_block = take_columns(in_weight, 2, n_f, n_dp, cs)
    wo_block = lax.dynamic_slice_in_dim(out_weight, me_d * cs, cs, 0)
    x_all, lens_all, x_own, dy_own, x_tags, ranks, small_all, wx, wg = gather_all(
        tokens, cotangent, meta, destination[:, None].astype(F32), lens_tile,
        [small_block, wx_block, wg_block], [n_f // 2, n_f // 2, n_f - 1 - n_f // 2], n_dp, n_f,
    )
    x_all = x_all.reshape(group, width)
    lens = lens_all[:, 0, :segs]
    from_send = (ranks[0].astype(jnp.int32)[:, None] == slots[None, :]).astype(BF16)
    wx = wx.reshape(width, ch)
    wg = wg.reshape(width, ch)
    small = joined(small_all)
    gain = small[used - gain_rows : used].reshape(gain_rows, n_f, cs).transpose(1, 0, 2).reshape(width).astype(F32)
    valid = (slots < jnp.sum(lengths[0, : segs - 1])).astype(F32)
    x_own32 = x_own.astype(F32)
    square = jnp.sum(x_own32 * x_own32, axis=1)
    mine_sums = [jnp.sum(square * valid), jnp.sum(valid)]

    pieces, at = [], 0
    for height in heights:
        pieces.append(small[at : at + height])
        at += height
    conv_w, conv_b, step_b, skip, dlog, sel, stepw = pieces
    conv_w = conv_w.astype(F32)
    skip = skip.astype(F32)
    rate = -jnp.exp(dlog.astype(F32))

    normed, x_in, conv, act, gate, dbl, wo_next = enter(
        lens, x_all, gain[None], wx, wg, conv_w, conv_b.astype(F32), sel, wo_block, n_f
    )
    dbl = dbl.reshape(group, -1)
    rate2 = rate * LOG2E
    scan_out, states, delta, pre, wo, dy_all = scan_forward(
        lens, dbl, act, stepw, step_b.astype(F32), rate2, skip, wo_block, wo_next, dy_own, n_f, tok
    )
    dy_all = dy_all.reshape(group, width)
    wo = wo.reshape(ch, width)
    gate_silu = jax.nn.silu(gate)
    gated = (scan_out * gate_silu).astype(BF16)

    gated_grad = nt_dot(dy_all, wo)
    scan_grad = gated_grad * gate_silu
    gate_grad = (gated_grad * scan_out * silu_slope(gate)).astype(BF16)
    wg_grad = tn_dot(normed, gate_grad).astype(BF16)
    pre_grad, act_grad, dbl_grad, decay_sum, sums, step_grad, wg_own, wo_grad, wo_half, mixed = scan_backward(
        lens, dbl, delta, pre, act, scan_grad, stepw, rate2, skip, states,
        wg_grad.reshape(n_f, dcols, ch), gated, dy_all, wo, n_f, tok,
    )
    lanes = lax.broadcasted_iota(jnp.int32, (1, 128), 1)
    ride = jnp.zeros((1, 128), F32)
    for j, value in enumerate(mine_sums):
        high = value.astype(BF16).astype(F32)
        ride = ride + jnp.where(lanes == 2 * j, high, 0.0) + jnp.where(lanes == 2 * j + 1, value - high, 0.0)
    mix_back, dx_back, gin_all, go_all, small_full = leave(
        lens, act_grad, conv, x_in, act, dbl_grad, sel, conv_w, sums, decay_sum, rate, step_grad, normed, wx, wg,
        gate_grad, wo_grad, wo_half, wg_own, x_own, dy_own, mixed, gain[None], x_tags, ride, n_f,
    )

    grad_in_weight, gain_sum = spread_columns(gin_all, in_weight, cs)
    grad_out_weight = go_all.reshape(n_dp * cs, width).astype(F32)
    small_full = joined(small_full)
    grad_norm_gain = gain_sum / norm_gain.astype(F32)
    wide = select_weight.shape[0]
    at_decay = wide + rank_of
    at_misc = at_decay + n
    grad_select = small_full[:wide]
    grad_step = small_full[wide:at_decay]
    grad_decay = small_full[at_decay:at_misc]
    misc = small_full[at_misc : at_misc + 8]

    back = mix_back.reshape(tok, width + 128)
    totals = jnp.sum(mix_back[:, 0, width : width + 4].astype(F32), axis=0)
    input_rms = jnp.sqrt((totals[0] + totals[1]) / ((totals[2] + totals[3]) * width))
    mixer_output = flat_dot(from_send, back[:, :width])
    layer_output = (tokens.astype(F32) + mixer_output).astype(BF16)
    mixer_output = mixer_output.astype(BF16)
    input_grad = flat_dot(from_send, dx_back.reshape(tok, width)).astype(BF16)
    return (
        layer_output,
        mixer_output,
        input_grad,
        input_rms,
        grad_norm_gain,
        grad_in_weight,
        misc[:taps],
        misc[taps],
        grad_select,
        grad_step,
        misc[taps + 1],
        grad_decay,
        misc[taps + 2],
        grad_out_weight,
    )


def solution(mesh):
    return jax.shard_map(
        per_device,
        mesh=mesh,
        in_specs=(
            P(("dp", "fsdp"), None),
            P(("dp", "fsdp"), None),
            P(("dp", "fsdp")),
            P(("dp", "fsdp"), None),
            P("fsdp"),
            P("fsdp", None),
            P(None, "fsdp"),
            P("fsdp"),
            P(None, "fsdp"),
            P(None, "fsdp"),
            P("fsdp"),
            P(None, "fsdp"),
            P("fsdp"),
            P("fsdp", None),
        ),
        out_specs=(
            P(("dp", "fsdp"), None),
            P(("dp", "fsdp"), None),
            P(("dp", "fsdp"), None),
            P(),
            P("fsdp"),
            P("fsdp", None),
            P(None, "fsdp"),
            P("fsdp"),
            P(None, "fsdp"),
            P(None, "fsdp"),
            P("fsdp"),
            P(None, "fsdp"),
            P("fsdp"),
            P("fsdp", None),
        ),
        check_vma=False,
    )
```

```python
import functools
import math

import jax
import jax.numpy as jnp
from jax import lax
from jax.experimental import pallas as pl
from jax.experimental.pallas import tpu as pltpu
from jax.sharding import PartitionSpec as P

EPS = 1e-05
TB = 16
LOG2E = math.log2(math.e)
RESET = 1.0e4
BF16 = jnp.bfloat16
F32 = jnp.float32


def silu_slope(value):
    sigma = jax.nn.sigmoid(value)
    return sigma * (1.0 + value * (1.0 - sigma))


def row_at(g, n_dp):
    return lax.rem(2 * g + 1, n_dp + 1)


def flip(d, mask):
    return d + mask - 2 * mask * lax.rem(d // mask, 2)


class GroupSum:
    def __init__(self, part, near, far, total, send, recv):
        self.part, self.near, self.far, self.total = part, near, far, total
        me_d, me_f = lax.axis_index("dp"), lax.axis_index("fsdp")
        plan = [
            (part.at[1], near.at[0], 1),
            (part.at[3], near.at[1], 1),
            (part.at[0], far.at[1], 2),
            (part.at[2], far.at[0], 2),
            (total.at[0], total.at[1], 1),
            (total.at[2], total.at[3], 1),
        ]
        self.copies = [
            pltpu.make_async_remote_copy(
                src_ref=src,
                dst_ref=dst,
                send_sem=send.at[i],
                recv_sem=recv.at[i],
                device_id=(flip(me_d, mask), me_f),
                device_id_type=pl.DeviceIdType.MESH,
            )
            for i, (src, dst, mask) in enumerate(plan)
        ]

    def row_done(self, g):
        for j in (0, 1):

            @pl.when(g == j)
            def _(j=j):
                self.copies[j].start()

            @pl.when(g == j + 2)
            def _(j=j):
                self.copies[j].wait_recv()
                self.part[2 * j] = self.part[2 * j] + self.near[j]
                self.copies[j + 2].start()

    def first(self):
        for j in (0, 1):
            self.copies[j].start()

    def second(self):
        for j in (0, 1):
            self.copies[j].wait_recv()
            self.part[2 * j] = self.part[2 * j] + self.near[j]
            self.copies[j + 2].start()

    def finish(self):
        for j in (0, 1):
            self.copies[3 - j].wait_recv()
            self.total[2 * j] = self.part[2 * j] + self.far[j]
            self.copies[4 + j].start()
        for j in (0, 1):
            self.copies[4 + j].wait_recv()
        for c in self.copies:
            c.wait_send()

    @staticmethod
    def scratch(tok, wide):
        return [
            pltpu.VMEM((4, tok, wide), F32),
            pltpu.VMEM((2, tok, wide), F32),
            pltpu.VMEM((2, tok, wide), F32),
            pltpu.VMEM((4, tok, wide), F32),
            pltpu.SemaphoreType.DMA((6,)),
            pltpu.SemaphoreType.DMA((6,)),
        ]


class RingReduce:
    def __init__(self, n_f, part, got, send, recv, down):
        self.part, self.got = part, got
        q = ring_place(lax.axis_index("fsdp"), n_f)
        self.at = lambda k: ring_index(lax.rem(q + k, n_f), n_f)
        self.n_f = n_f
        self.counts = [down, n_f - 1 - down]
        self.copies = [[], []]
        for up in (0, 1):
            for h in range(min(self.counts[up], got.shape[1])):
                src = part.at[self.at(self.goal(up, 0))] if h == 0 else got.at[up, h - 1]
                self.copies[up].append(ring_copy(n_f, src, got.at[up, h], send.at[up, h], recv.at[up, h], up))
        self.events = max(self.counts)

    def goal(self, up, h):
        left = self.counts[up] - h
        return left if up else self.n_f - left

    def add(self, slot, addend):
        rows = slot.shape[0]
        step = min(rows, 64)

        def piece(i, _):
            at = pl.ds(pl.multiple_of(i * step, step), step)
            slot[at, :] = (slot[at, :].astype(F32) + addend[at, :].astype(F32)).astype(slot.dtype)
            return 0

        lax.fori_loop(0, rows // step, piece, 0)

    def start(self):
        for up in (0, 1):
            if self.copies[up]:
                self.copies[up][0].start()

    def stop(self, hops, out):
        for up in (0, 1):
            self.copies[up][hops - 1].wait_recv()
            rows_add(out.at[up], [self.got.at[up, hops - 1]])
            for c in self.copies[up][:hops]:
                c.wait_send()

    def resume(self, hops, arrived):
        for up in (0, 1):
            slot = self.got.at[up, hops - 1]
            rows_add(slot, [arrived.at[up], self.part.at[self.at(self.goal(up, hops))]])
            self.copies[up][hops].start()

    def event(self, e):
        for up in (0, 1):
            if e < self.counts[up]:
                self.copies[up][e - 1].wait_recv()
                self.add(self.got.at[up, e - 1], self.part.at[self.at(self.goal(up, e))])
                self.copies[up][e].start()

    def finish(self, out, since=0):
        last = []
        for up in (0, 1):
            if self.copies[up]:
                self.copies[up][-1].wait_recv()
                last.append(self.got.at[up, self.counts[up] - 1])
        mine = self.part.at[self.at(0)]
        rows = mine.shape[0]
        step = min(rows, 64)

        def piece(i, _):
            at = pl.ds(pl.multiple_of(i * step, step), step)
            total_ = mine[at, :].astype(F32)
            for slot in last:
                total_ = total_ + slot[at, :].astype(F32)
            out[at, :] = total_.astype(out.dtype)
            return 0

        lax.fori_loop(0, rows // step, piece, 0)
        for up in (0, 1):
            for c in self.copies[up][since:]:
                c.wait_send()

    @staticmethod
    def scratch(n_f, block, dtype=BF16, slots=0):
        return [
            pltpu.VMEM((2, slots or n_f // 2) + block, dtype),
            pltpu.SemaphoreType.DMA((2, n_f // 2)),
            pltpu.SemaphoreType.DMA((2, n_f // 2)),
        ]


class PairReduce:
    def __init__(self, part, near, far, send, recv):
        self.part, self.near, self.far = part, near, far
        me_d, me_f = lax.axis_index("dp"), lax.axis_index("fsdp")
        plan = [
            (part.at[1], near.at[0], 1),
            (part.at[3], near.at[1], 1),
            (part.at[2], far, 2),
        ]
        self.copies = [
            pltpu.make_async_remote_copy(
                src_ref=src,
                dst_ref=dst,
                send_sem=send.at[i],
                recv_sem=recv.at[i],
                device_id=(flip(me_d, mask), me_f),
                device_id_type=pl.DeviceIdType.MESH,
            )
            for i, (src, dst, mask) in enumerate(plan)
        ]

    def start(self):
        for c in self.copies[:2]:
            c.start()

    def middle(self):
        self.copies[1].wait_recv()
        rows_add(self.part.at[2], [self.part.at[2], self.near.at[1]])
        self.copies[2].start()
        self.copies[0].wait_recv()

    def finish(self, out):
        self.copies[2].wait_recv()
        rows_add(out, [self.part.at[0], self.near.at[0], self.far])
        for c in self.copies:
            c.wait_send()

    @staticmethod
    def scratch(block, dtype=BF16):
        return [
            pltpu.VMEM((2,) + block, dtype),
            pltpu.VMEM(block, dtype),
            pltpu.SemaphoreType.DMA((3,)),
            pltpu.SemaphoreType.DMA((3,)),
        ]


def rows_add(out, terms, step=32):
    def piece(i, _):
        at = pl.ds(pl.multiple_of(i * step, step), step)
        total_ = terms[0][at, :].astype(F32)
        for t in terms[1:]:
            total_ = total_ + t[at, :].astype(F32)
        out[at, :] = total_.astype(out.dtype)
        return 0

    lax.fori_loop(0, out.shape[0] // step, piece, 0)


class PairShare:
    def __init__(self, mine, out, local, send, recv, relative=False):
        me_d, me_f = lax.axis_index("dp"), lax.axis_index("fsdp")
        far = 2 if relative else flip(me_d, 2)
        here, at_near, at_far, relayed = (0, 1, 2, 3) if relative else (me_d, me_d, me_d, far)
        self.local = pltpu.make_async_copy(mine, out(here), local)
        self.copies = [
            pltpu.make_async_remote_copy(
                src_ref=src,
                dst_ref=dst,
                send_sem=send.at[i],
                recv_sem=recv.at[i],
                device_id=(flip(me_d, mask), me_f),
                device_id_type=pl.DeviceIdType.MESH,
            )
            for i, (src, dst, mask) in enumerate(
                [(mine, out(at_near), 1), (mine, out(at_far), 2), (out(far), out(relayed), 1)]
            )
        ]

    def start(self):
        self.copies[1].start()
        self.copies[0].start()
        self.local.start()

    def relay(self):
        self.copies[1].wait_recv()
        self.copies[2].start()

    def finish(self):
        self.copies[0].wait_recv()
        self.copies[2].wait_recv()
        for c in self.copies:
            c.wait_send()
        self.local.wait()


def side_by_side(count, height, wide):
    return (count, height, wide) if wide % 128 else (height, count * wide)


def lane_block(ref, index, wide):
    if wide % 128:
        return ref.at[index]
    return ref.at[:, pl.ds(pl.multiple_of(index * wide, 128), wide)]


def joined(value):
    if value.ndim == 2:
        return value
    return value.transpose(1, 0, 2).reshape(value.shape[1], -1)


def greet_neighbours(n_f, ring):
    me_d, me_f = lax.axis_index("dp"), lax.axis_index("fsdp")
    barrier = pltpu.get_barrier_semaphore()
    others = [(flip(me_d, 1), me_f), (flip(me_d, 2), me_f)]
    if ring:
        q = ring_place(me_f, n_f)
        others.append((me_d, ring_index(lax.rem(q + n_f - 1, n_f), n_f)))
        others.append((me_d, ring_index(lax.rem(q + 1, n_f), n_f)))
    for other in others:
        pl.semaphore_signal(barrier, inc=1, device_id=other, device_id_type=pl.DeviceIdType.MESH)
    pl.semaphore_wait(barrier, len(others))


def ring_copy(n_f, src, dst, send, recv, up):
    me_d, me_f = lax.axis_index("dp"), lax.axis_index("fsdp")
    q = ring_place(me_f, n_f)
    to = ring_index(lax.rem(q + (1 if up else n_f - 1), n_f), n_f)
    return pltpu.make_async_remote_copy(
        src_ref=src,
        dst_ref=dst,
        send_sem=send,
        recv_sem=recv,
        device_id=(me_d, to),
        device_id_type=pl.DeviceIdType.MESH,
    )


def segment_span(lens_ref, m, first, rows):
    t = lax.broadcasted_iota(jnp.int32, (rows, 1), 0) + first
    begin = jnp.zeros((rows, 1), jnp.int32)
    end = jnp.zeros((rows, 1), jnp.int32)
    total = jnp.int32(0)
    for j in range(lens_ref.shape[1]):
        after = total + lens_ref[m, j]
        inside = t >= total
        begin = jnp.where(inside, total, begin)
        end = jnp.where(inside, after, end)
        total = after
    return t - begin, end - 1 - t


def enter_kernel(n_f, half, lens_ref, x_ref, gain_ref, wx_ref, wg_ref, taps_ref, bias_ref, sel_ref, wo_ref,
                 normed_ref, xin_ref, conv_ref, act_ref, gate_ref, dbl_ref, next_ref,
                 part, near, far, total, gs_send, gs_recv, hop_send, hop_recv):
    g = pl.program_id(0)
    n_dp, tok = part.shape[:2]
    rows, width = x_ref.shape
    hops = [ring_copy(n_f, wo_ref, next_ref.at[up, 0], hop_send.at[up, 0], hop_recv.at[up, 0], up) for up in (0, 1)]
    hops2 = [
        ring_copy(n_f, next_ref.at[up, 0], next_ref.at[up, 1], hop_send.at[up, 1], hop_recv.at[up, 1], up)
        for up in (0, 1)
    ]
    group = GroupSum(part, near, far, total, gs_send, gs_recv)

    @pl.when(g == 0)
    def _():
        greet_neighbours(n_f, True)
        for c in hops:
            c.start()
        part[...] = jnp.zeros_like(part)

        def norm(i, _):
            for j in range(4):
                at = pl.ds(pl.multiple_of(i * 128 + j * 32, 32), 32)
                v = x_ref[at, :].astype(F32)
                rstd = lax.rsqrt(jnp.mean(v * v, axis=1, keepdims=True) + EPS)
                normed_ref[at, :] = (v * rstd * gain_ref[...]).astype(BF16)
            return 0

        lax.fori_loop(0, rows // 128, norm, 0)

    @pl.when(g == half)
    def _():
        for a, b in zip(hops, hops2):
            a.wait_recv()
            b.start()

    @pl.when(g < half)
    def _():
        n_taps = taps_ref.shape[0]
        xin_ref[...] = jnp.dot(normed_ref[...], wx_ref[...], preferred_element_type=F32)
        for m in range(n_dp):
            at = slice(m * tok, (m + 1) * tok)
            v = xin_ref[at, :]
            since, _ = segment_span(lens_ref, m, 0, tok)
            conv = bias_ref[...] + taps_ref[n_taps - 1 : n_taps, :] * v
            for lag in range(1, n_taps):
                keep = (since >= lag).astype(F32)
                conv = conv + taps_ref[n_taps - 1 - lag : n_taps - lag, :] * (pltpu.roll(v, lag, 0) * keep)
            conv_ref[at, :] = conv
            act = jax.nn.silu(conv).astype(BF16)
            act_ref[at, :] = act
            part[m] += lax.dot_general(act, sel_ref[...], (((1,), (1,)), ((), ())), preferred_element_type=F32)

    @pl.when(g == half - 1)
    def _():
        group.first()

    @pl.when(g >= half)
    def _():
        gate_ref[...] = jnp.dot(normed_ref[...], wg_ref[...], preferred_element_type=F32)

    @pl.when(g == half)
    def _():
        group.second()

    @pl.when(g == 2 * half - 1)
    def _():
        group.finish()
        dbl_ref[...] = total[...]
        for a, b in zip(hops, hops2):
            a.wait_send()
            b.wait()


def enter(lens, x_all, gain, wx, wg, taps, bias, sel, wo_block, n_f):
    n_dp = lens.shape[0]
    rows, width = x_all.shape
    tok = rows // n_dp
    ch = wx.shape[1]
    wide = sel.shape[0]
    piece = 256
    half = ch // piece
    whole = lambda g: (0, 0)
    early = lambda g: (0, jnp.minimum(g, half - 1))
    late = lambda g: (0, jnp.maximum(g - half, 0))
    once = pl.Buffered(1)
    any_ = pl.BlockSpec(memory_space=pl.ANY)
    shaped = lambda d, t: jax.ShapeDtypeStruct((rows, d), t)
    return pl.pallas_call(
        functools.partial(enter_kernel, n_f, half),
        grid=(2 * half,),
        in_specs=[
            pl.BlockSpec(memory_space=pltpu.SMEM),
            pl.BlockSpec((rows, width), whole, pipeline_mode=once),
            pl.BlockSpec((1, width), whole),
            pl.BlockSpec((width, piece), early),
            pl.BlockSpec((width, piece), late),
            pl.BlockSpec((taps.shape[0], piece), early),
            pl.BlockSpec((1, piece), early),
            pl.BlockSpec((wide, piece), early),
            any_,
        ],
        out_specs=[
            pl.BlockSpec((rows, width), whole),
            pl.BlockSpec((rows, piece), early),
            pl.BlockSpec((rows, piece), early),
            pl.BlockSpec((rows, piece), early),
            pl.BlockSpec((rows, piece), late),
            pl.BlockSpec((n_dp, tok, wide), lambda g: (0, 0, 0)),
            any_,
        ],
        out_shape=[
            shaped(width, BF16),
            shaped(ch, F32),
            shaped(ch, F32),
            shaped(ch, BF16),
            shaped(ch, F32),
            jax.ShapeDtypeStruct((n_dp, tok, wide), F32),
            jax.ShapeDtypeStruct((2, 2) + wo_block.shape, BF16),
        ],
        scratch_shapes=GroupSum.scratch(tok, wide)
        + [pltpu.SemaphoreType.DMA((2, 2)), pltpu.SemaphoreType.DMA((2, 2))],
        compiler_params=pltpu.CompilerParams(
            collective_id=1, has_side_effects=True, vmem_limit_bytes=48 * 2**20
        ),
        cost_estimate=pl.CostEstimate(flops=10**10, bytes_accessed=4 * 10**7, transcendentals=10**6),
    )(lens, x_all, gain, wx, wg, taps, bias, sel, wo_block)


def fold_matrix(n):
    i = lax.broadcasted_iota(jnp.int32, (n, TB * n), 0)
    j = lax.broadcasted_iota(jnp.int32, (n, TB * n), 1)
    return jnp.where(lax.rem(j, n) == i, 1.0, 0.0)


def own_token(n):
    i = lax.broadcasted_iota(jnp.int32, (TB, TB * n), 0)
    j = lax.broadcasted_iota(jnp.int32, (TB, TB * n), 1)
    return i == j // n


def block_rows(m, n):
    spread = jnp.dot(m.astype(BF16), fold_matrix(n).astype(BF16), preferred_element_type=F32)
    i = lax.broadcasted_iota(jnp.int32, spread.shape, 0)
    j = lax.broadcasted_iota(jnp.int32, spread.shape, 1)
    return jnp.where(lax.rem(i, TB) == j // n, spread, 0.0).astype(BF16)


def turned(m):
    n = m.shape[1]
    i = lax.broadcasted_iota(jnp.int32, (n, n), 0)
    j = lax.broadcasted_iota(jnp.int32, (n, n), 1)
    eye = jnp.where(i == j, 1.0, 0.0)
    return lax.dot_general(
        eye, m, (((1,), (1,)), ((), ())), preferred_element_type=F32, precision=lax.Precision.HIGHEST
    )


def softplus(v):
    return jnp.maximum(v, 0.0) + jnp.log1p(jnp.exp(-jnp.abs(v)))


class RingGather:
    def __init__(self, n_f, mine, near, out, local, send, recv):
        q = ring_place(lax.axis_index("fsdp"), n_f)
        at = lambda k: ring_index(lax.rem(q + k, n_f), n_f)
        count = [n_f // 2, n_f - 1 - n_f // 2]
        known = near.shape[1]
        self.locals = [pltpu.make_async_copy(mine, out.at[at(0)], local.at[0])]
        self.hops = [[], []]
        for up in (0, 1):
            for j in range(known):
                index = at(n_f - 1 - j if up else 1 + j)
                self.locals.append(pltpu.make_async_copy(near.at[up, j], out.at[index], local.at[1 + known * up + j]))
            for h in range(known, count[up]):
                index = at(n_f - h if up else h)
                src = near.at[up, known - 1] if h == known else out.at[index]
                self.hops[up].append(
                    ring_copy(n_f, src, out.at[index], send.at[up, h], recv.at[up, h], up)
                )
        self.events = max(len(h) for h in self.hops)

    def start(self):
        for c in self.locals:
            c.start()
        for up in (0, 1):
            if self.hops[up]:
                self.hops[up][0].start()

    def event(self, e):
        for up in (0, 1):
            if e < len(self.hops[up]):
                self.hops[up][e - 1].wait_recv()
                self.hops[up][e].start()

    def finish(self):
        for up in (0, 1):
            if self.hops[up]:
                self.hops[up][-1].wait_recv()
            for c in self.hops[up]:
                c.wait_send()
        for c in self.locals:
            c.wait()


def fwd_kernel(lanes, n_f, lens_ref, dbl_ref, act_ref, stepw_ref, stepb_ref, rate_ref, skip_ref, wo_ref, next_ref, dy_ref,
               y_ref, s_ref, delta_ref, pre_ref, wo_all, dy_all, carry, big_s, cw_s, bt_s, d_s, u_s, sc, local, hop_send, hop_recv, sh_send, sh_recv):
    n, ch = rate_ref.shape
    tblk = act_ref.shape[0]
    low_n = stepw_ref.shape[0]
    steps = pl.num_programs(0) * pl.num_programs(1)
    now = pl.program_id(0) * pl.num_programs(1) + pl.program_id(1)
    ring = RingGather(n_f, wo_ref, next_ref, wo_all, local, hop_send, hop_recv)
    share = PairShare(dy_ref, lambda m: dy_all.at[m], local.at[5], sh_send, sh_recv, True)

    @pl.when(now == 0)
    def _():
        greet_neighbours(n_f, True)
        ring.start()
        share.start()

    @pl.when(now == 13)
    def _():
        share.relay()

    for e in range(1, ring.events):

        @pl.when(now == min(7 * e, 15))
        def _(e=e):
            ring.event(e)

    @pl.when(pl.program_id(1) == 0)
    def _():
        carry[...] = jnp.zeros_like(carry)

    pre = jnp.dot(dbl_ref[:, :low_n].astype(BF16), stepw_ref[...], preferred_element_type=F32) + stepb_ref[...]
    pre_ref[...] = pre
    delta_ref[...] = softplus(pre)
    since, _ = segment_span(lens_ref, pl.program_id(0), pl.program_id(1) * tblk, tblk)
    big_s[...] = jnp.where(since == 0, RESET, 0.0)
    cw_s[...] = block_rows(dbl_ref[:, low_n + n : low_n + 2 * n], n)
    flat = turned(dbl_ref[:, low_n : low_n + n])
    for i in range(tblk // TB):
        bt_s[i] = flat[:, i * TB : (i + 1) * TB]

    def chunk(i, _):
        base = pl.multiple_of(i * TB, TB)
        dl = delta_ref[pl.ds(base, TB), :]
        ac = act_ref[pl.ds(base, TB), :].astype(F32)
        d_s[...] = dl + big_s[pl.ds(base, TB), :]
        u_s[...] = dl * ac
        bt = bt_s[i]
        for lo in range(0, ch, lanes):
            cs = pl.ds(lo, lanes)
            rate = rate_ref[:, cs]
            s = carry[:, cs]
            for t in range(TB):
                dec = jnp.exp2(d_s[t : t + 1, cs] * rate)
                s = dec * s + bt[:, t : t + 1] * u_s[t : t + 1, cs]
                sc[t * n : (t + 1) * n, cs] = s.astype(BF16)
            carry[:, cs] = s
        states = sc[...]
        y = jnp.dot(cw_s[pl.ds(base, TB), :], states, preferred_element_type=F32)
        y_ref[pl.ds(base, TB), :] = y + skip_ref[...] * ac
        s_ref[pl.ds(pl.multiple_of(base * n, TB * n), TB * n), :] = states
        return 0

    lax.fori_loop(0, tblk // TB, chunk, 0)

    @pl.when(now == steps - 1)
    def _():
        ring.finish()
        share.finish()


def scan_forward(lens, dbl, act, stepw, stepb, rate2, skip, wo_block, wo_next, dy_own, n_f, row_len, tblk=64, lanes=512):
    t, ch = act.shape
    n = rate2.shape[0]
    nb = row_len // tblk
    at = lambda r, j: (r * nb + j, 0)
    zero = lambda r, j: (0, 0)
    any_ = pl.BlockSpec(memory_space=pl.ANY)
    wide = jax.ShapeDtypeStruct((t, ch), F32)
    return pl.pallas_call(
        functools.partial(fwd_kernel, min(lanes, ch), n_f),
        grid=(t // row_len, nb),
        in_specs=[
            pl.BlockSpec(memory_space=pltpu.SMEM),
            pl.BlockSpec((tblk, dbl.shape[1]), at),
            pl.BlockSpec((tblk, ch), at),
            pl.BlockSpec(stepw.shape, zero),
            pl.BlockSpec((1, ch), zero),
            pl.BlockSpec((n, ch), zero),
            pl.BlockSpec((1, ch), zero),
            any_,
            any_,
            any_,
        ],
        out_specs=[
            pl.BlockSpec((tblk, ch), at),
            pl.BlockSpec((tblk * n, ch), at),
            pl.BlockSpec((tblk, ch), at),
            pl.BlockSpec((tblk, ch), at),
            any_,
            any_,
        ],
        out_shape=[
            wide,
            jax.ShapeDtypeStruct((t * n, ch), BF16),
            wide,
            wide,
            jax.ShapeDtypeStruct((n_f,) + wo_block.shape, BF16),
            jax.ShapeDtypeStruct((t // row_len,) + dy_own.shape, BF16),
        ],
        scratch_shapes=[
            pltpu.VMEM((n, ch), F32),
            pltpu.VMEM((tblk, 1), F32),
            pltpu.VMEM((tblk, TB * n), BF16),
            pltpu.VMEM((tblk // TB, n, TB), F32),
            pltpu.VMEM((TB, ch), F32),
            pltpu.VMEM((TB, ch), F32),
            pltpu.VMEM((TB * n, ch), BF16),
            pltpu.SemaphoreType.DMA((6,)),
            pltpu.SemaphoreType.DMA((2, n_f)),
            pltpu.SemaphoreType.DMA((2, n_f)),
            pltpu.SemaphoreType.DMA((3,)),
            pltpu.SemaphoreType.DMA((3,)),
        ],
        compiler_params=pltpu.CompilerParams(
            collective_id=2, has_side_effects=True, vmem_limit_bytes=32 * 2**20
        ),
        cost_estimate=pl.CostEstimate(flops=t * n * ch * 40, bytes_accessed=t * ch * 52, transcendentals=t * n * ch),
    )(lens, dbl, act, stepw, stepb, rate2, skip, wo_block, wo_next, dy_own)


def bwd_kernel(lanes, n_f, lens_ref, dbl_ref, delta_ref, pre_ref, act_ref, gy_ref, stepw_ref, rate_ref, skip_ref,
               s_ref, sp_ref, wg_part, gated_ref, dy_ref, wo_ref,
               pg_ref, da_ref, dbl_grad_ref, dl_ref, sums_ref, stepg_ref, wg_own, wo_out, wo_half, mixed_own,
               carry, big_s, bw_s, ct_s, d_all, u_all, g_all, h_all, b_all, c_all, part, near, far, total, gs_send, gs_recv,
               ring_got, ring_send, ring_recv, wo_got, wo_send, wo_recv, wo_part, mix, mix_near, mix_far, mix_send, mix_recv, wo_save):
    n, ch = rate_ref.shape
    tblk = act_ref.shape[0]
    low_n = stepw_ref.shape[0]
    r, j = pl.program_id(0), pl.program_id(1)
    n_dp, nb = pl.num_programs(0), pl.num_programs(1)
    m = row_at(r, n_dp)
    group = GroupSum(part, near, far, total, gs_send, gs_recv)
    ring = RingReduce(n_f, wg_part, ring_got, ring_send, ring_recv, n_f // 2)
    ring_o = RingReduce(n_f, wo_part, wo_got, wo_send, wo_recv, n_f - 1 - n_f // 2)
    pairs = PairReduce(mix, mix_near, mix_far, mix_send, mix_recv)
    now = r * nb + j
    last_step = n_dp * nb - 1
    @pl.when(j == 0)
    def _():
        carry[...] = jnp.zeros_like(carry)

    @pl.when((r == 0) & (j == 0))
    def _():
        greet_neighbours(n_f, True)
        ring.start()
        dl_ref[...] = jnp.zeros_like(dl_ref)
        sums_ref[...] = jnp.zeros_like(sums_ref)
        stepg_ref[...] = jnp.zeros_like(stepg_ref)

    for e in range(1, ring.events):

        @pl.when(now == min(4 * e, 15))
        def _(e=e):
            ring.event(e)

    tile = 256
    parts = ch // tile
    save = pltpu.make_async_copy(wo_part, wo_out, wo_save)

    @pl.when(now < parts)
    def _():
        cs = wo_part.shape[1]
        cols = pl.ds(pl.multiple_of(now * tile, tile), tile)
        grad = lax.dot_general(
            gated_ref[:, cols], dy_ref[...], (((0,), (0,)), ((), ())), preferred_element_type=F32
        ).astype(BF16)
        for i in range(tile // cs):
            wo_part[now * (tile // cs) + i] = grad[i * cs : (i + 1) * cs]

    @pl.when(now == parts - 1)
    def _():
        save.start()

    @pl.when(now == 6)
    def _():
        ring_o.start()

    @pl.when(now == 13)
    def _():
        ring_o.event(1)

    @pl.when((now >= parts) & (now < parts + n_dp))
    def _():
        row_len = mix.shape[1]
        at = pl.ds(pl.multiple_of((now - parts) * row_len, row_len), row_len)
        mix[now - parts] = jnp.dot(gated_ref[at, :], wo_ref[...], preferred_element_type=F32).astype(BF16)

    @pl.when(now == 8)
    def _():
        pairs.start()

    @pl.when(now == 10)
    def _():
        pairs.middle()

    ones = jnp.where(own_token(n), 1.0, 0.0).astype(BF16)
    nt = (((1,), (1,)), ((), ()))
    row = lax.broadcasted_iota(jnp.int32, (TB * n, n), 0)
    col = lax.broadcasted_iota(jnp.int32, (TB * n, n), 1)
    fold = jnp.where(lax.rem(row, n) == col, 1.0, 0.0)
    since, _ = segment_span(lens_ref, m, (nb - 1 - j) * tblk, tblk)
    big_s[...] = jnp.where(since == 0, RESET, 0.0)
    bw_s[...] = block_rows(dbl_ref[:, low_n : low_n + n], n)

    flat = turned(dbl_ref[:, low_n + n : low_n + 2 * n])
    for i in range(tblk // TB):
        ct_s[i] = flat[:, i * TB : (i + 1) * TB]

    def lane_sum(value):
        total_ = value[:, :128]
        for at in range(128, value.shape[1], 128):
            total_ = total_ + value[:, at : at + 128]
        return total_

    def gathered(sums):
        spread = jnp.sum(sums, axis=1, keepdims=True) * fold
        high = spread.astype(BF16)
        rest = (spread - high.astype(F32)).astype(BF16)
        return jnp.dot(ones, high, preferred_element_type=F32) + jnp.dot(ones, rest, preferred_element_type=F32)

    for i in reversed(range(tblk // TB)):
        base = i * TB
        d_s, u_s, g_s, h_s, b_s, c_s = (v.at[i % 2] for v in (d_all, u_all, g_all, h_all, b_all, c_all))
        dl = delta_ref[base : base + TB, :]
        ac = act_ref[base : base + TB, :].astype(F32)
        d_s[...] = dl + big_s[base : base + TB, :]
        u_s[...] = dl * ac
        ct = ct_s[i]
        for lo in range(0, ch, lanes):
            cs = pl.ds(lo, lanes)
            rate = rate_ref[:, cs]
            flow = carry[:, cs]
            acc = dl_ref[:, cs]
            here = s_ref[(base + TB - 1) * n : (base + TB) * n, cs].astype(F32)
            for t in reversed(range(TB)):
                dr = d_s[t : t + 1, cs]
                dec = jnp.exp2(dr * rate)
                gy = gy_ref[base + t : base + t + 1, cs]
                g = ct[:, t : t + 1] * gy + flow
                flow = dec * g
                if base + t > 0:
                    prev = s_ref[(base + t - 1) * n : (base + t) * n, cs].astype(F32)
                else:
                    prev = sp_ref[:, cs].astype(F32)
                h = flow * prev
                acc = acc + h * dr
                at = slice(t * n, (t + 1) * n)
                b_now = lane_sum(g * u_s[t : t + 1, cs])
                c_now = lane_sum(here * gy)
                if lo:
                    b_now = b_now + b_s[at, :]
                    c_now = c_now + c_s[at, :]
                b_s[at, :] = b_now
                c_s[at, :] = c_now
                here = prev
                g_s[t * n : (t + 1) * n, cs] = g.astype(BF16)
                h_s[t * n : (t + 1) * n, cs] = (h * rate).astype(BF16)
            carry[:, cs] = flow
            dl_ref[:, cs] = acc
        gb = g_s[...]
        gy = gy_ref[base : base + TB, :]
        du = jnp.dot(bw_s[base : base + TB, :], gb, preferred_element_type=F32)
        hr = jnp.dot(ones, h_s[...], preferred_element_type=F32)
        dd = hr * (1.0 / LOG2E) + du * ac
        pg_ref[base : base + TB, :] = (dd * jax.nn.sigmoid(pre_ref[base : base + TB, :])).astype(BF16)
        da_ref[base : base + TB, :] = du * dl + skip_ref[...] * gy
        at = pl.ds(pl.multiple_of((nb - 1 - j) * tblk + base, TB), TB)
        part[m, at, low_n : low_n + n] = gathered(b_s[...])
        part[m, at, low_n + n : low_n + 2 * n] = gathered(c_s[...])

    pg = pg_ref[...]
    part[m, pl.ds(pl.multiple_of((nb - 1 - j) * tblk, tblk), tblk), :low_n] = lax.dot_general(
        pg, stepw_ref[...], nt, preferred_element_type=F32
    )
    stepg_ref[...] += lax.dot_general(
        dbl_ref[:, :low_n].astype(BF16), pg, (((0,), (0,)), ((), ())), preferred_element_type=F32
    )
    sums_ref[0:1, :] += jnp.sum(pg.astype(F32), axis=0, keepdims=True)
    sums_ref[1:2, :] += jnp.sum(gy_ref[...] * act_ref[...].astype(F32), axis=0, keepdims=True)

    @pl.when(j == nb - 1)
    def _():
        group.row_done(r)

    @pl.when((j == nb - 1) & (r == n_dp - 1))
    def _():
        ring.finish(wg_own)
        group.finish()
        dbl_grad_ref[...] = total[...]
        pairs.finish(mixed_own)
        ring_o.stop(2, wo_half)
        save.wait()


def scan_backward(lens, dbl, delta, pre, act, gy, stepw, rate2, skip, states, wg_part, gated, dy_all, wo, n_f, row_len,
                  tblk=64, lanes=512):
    t, ch = delta.shape
    n = rate2.shape[0]
    nb = row_len // tblk
    n_dp = t // row_len
    wide = dbl.shape[1]
    width = wo.shape[1]
    cs = ch // n_f
    spot = lambda r, j: row_at(r, n_dp) * nb + nb - 1 - j
    at = lambda r, j: (spot(r, j), 0)
    zero = lambda r, j: (0, 0)
    entry = lambda r, j: (jnp.maximum(spot(r, j) * tblk - 1, 0), 0)
    return pl.pallas_call(
        functools.partial(bwd_kernel, min(lanes, ch), n_f),
        grid=(n_dp, nb),
        in_specs=[
            pl.BlockSpec(memory_space=pltpu.SMEM),
            pl.BlockSpec((tblk, wide), at),
            pl.BlockSpec((tblk, ch), at),
            pl.BlockSpec((tblk, ch), at),
            pl.BlockSpec((tblk, ch), at),
            pl.BlockSpec((tblk, ch), at),
            pl.BlockSpec(stepw.shape, zero),
            pl.BlockSpec((n, ch), zero),
            pl.BlockSpec((1, ch), zero),
            pl.BlockSpec((tblk * n, ch), at),
            pl.BlockSpec((n, ch), entry),
            pl.BlockSpec(memory_space=pltpu.VMEM),
            pl.BlockSpec(memory_space=pltpu.VMEM),
            pl.BlockSpec(memory_space=pltpu.VMEM),
            pl.BlockSpec(memory_space=pltpu.VMEM),
        ],
        out_specs=[
            pl.BlockSpec((tblk, ch), at),
            pl.BlockSpec((tblk, ch), at),
            pl.BlockSpec((n_dp, row_len, wide), lambda r, j: (0, 0, 0)),
            pl.BlockSpec((n, ch), zero),
            pl.BlockSpec((8, ch), zero),
            pl.BlockSpec(stepw.shape, zero),
            pl.BlockSpec(wg_part.shape[1:], zero),
            pl.BlockSpec(memory_space=pl.ANY),
            pl.BlockSpec((2, cs, width), lambda r, j: (0, 0, 0)),
            pl.BlockSpec((row_len, width), zero),
        ],
        out_shape=[
            jax.ShapeDtypeStruct((t, ch), BF16),
            jax.ShapeDtypeStruct((t, ch), F32),
            jax.ShapeDtypeStruct((n_dp, row_len, wide), F32),
            jax.ShapeDtypeStruct((n, ch), F32),
            jax.ShapeDtypeStruct((8, ch), F32),
            jax.ShapeDtypeStruct(stepw.shape, F32),
            jax.ShapeDtypeStruct(wg_part.shape[1:], BF16),
            jax.ShapeDtypeStruct((n_f, cs, width), BF16),
            jax.ShapeDtypeStruct((2, cs, width), BF16),
            jax.ShapeDtypeStruct((row_len, width), BF16),
        ],
        scratch_shapes=[
            pltpu.VMEM((n, ch), F32),
            pltpu.VMEM((tblk, 1), F32),
            pltpu.VMEM((tblk, TB * n), BF16),
            pltpu.VMEM((tblk // TB, n, TB), F32),
            pltpu.VMEM((2, TB, ch), F32),
            pltpu.VMEM((2, TB, ch), F32),
            pltpu.VMEM((2, TB * n, ch), BF16),
            pltpu.VMEM((2, TB * n, ch), BF16),
            pltpu.VMEM((2, TB * n, 128), F32),
            pltpu.VMEM((2, TB * n, 128), F32),
        ]
        + GroupSum.scratch(row_len, wide)
        + RingReduce.scratch(n_f, wg_part.shape[1:])
        + RingReduce.scratch(n_f, (cs, width), BF16, 2)
        + [pltpu.VMEM((n_f, cs, width), BF16), pltpu.VMEM((n_dp, row_len, width), BF16)]
        + PairReduce.scratch((row_len, width))
        + [pltpu.SemaphoreType.DMA],
        compiler_params=pltpu.CompilerParams(
            collective_id=3, has_side_effects=True, vmem_limit_bytes=60 * 2**20
        ),
        cost_estimate=pl.CostEstimate(flops=t * n * ch * 80, bytes_accessed=t * ch * 60, transcendentals=t * n * ch),
    )(lens, dbl, delta, pre, act, gy, stepw, rate2, skip, states, states, wg_part, gated, dy_all, wo)


class Return:
    def __init__(self, count, n_f, buf, out, local, send, recv):
        self.count, self.n_f, self.buf, self.out = count, n_f, buf, out
        self.local, self.send, self.recv = local, send, recv
        self.me = lax.axis_index("dp") * n_f + lax.axis_index("fsdp")

    def fill(self, pick, values):
        count, pair = self.buf.shape[:2]

        def piece(j, _):
            cols = pl.ds(pl.multiple_of(j * 256, 256), 256)
            moved = jnp.dot(pick, values[:, cols].astype(BF16), preferred_element_type=F32)
            self.buf[:, :, cols] = moved.astype(BF16).reshape(count, pair, 256)
            return 0

        lax.fori_loop(0, values.shape[1] // 256, piece, 0)

    def start(self):
        def one(p, _):
            pltpu.make_async_remote_copy(
                src_ref=self.buf.at[p],
                dst_ref=self.out.at[p],
                send_sem=self.send,
                recv_sem=self.recv,
                device_id=mesh_at(lax.rem(self.me + self.count - p, self.count), self.n_f),
                device_id_type=pl.DeviceIdType.MESH,
            ).start()
            return 0

        pltpu.make_async_copy(self.buf.at[0], self.out.at[0], self.local).start()
        lax.fori_loop(1, self.count, one, 0)

    def finish(self):
        pltpu.make_async_copy(self.buf.at[0], self.out.at[0], self.local).wait()
        rest = pl.ds(1, self.count - 1)
        for sem in (self.recv, self.send):
            pltpu.make_async_copy(self.buf.at[rest], self.out.at[rest], sem).wait()


def leave_kernel(n_f, half, lens_ref, da_ref, conv_ref, xin_ref, act_ref, dblg_ref, sel_ref, taps_ref,
                 sums_ref, dsum_ref, rate_ref, stepg_ref, normed_ref, wx_ref, wg_ref, gg_ref,
                 wo_part, wo_half, wg_own, x_own, dy_own, mixed_own, gain_ref, tags_ref, ride_ref,
                 mix_back, dx_back, gin_all, go_all, small_all,
                 ig_s, wx_s, ng_s, small_s, pick_s, ret_mix, ret_dx, change_s,
                 wo_got, wo_send, wo_recv, wx_got, wx_send, wx_recv, sm_got, sm_send, sm_recv,
                 ng_near, ng_far, ng_send, ng_recv, wo_own, wx_own, sm_own, local, sh_send, sh_recv, ret_sem):
    g = pl.program_id(0)
    steps = pl.num_programs(0)
    n_dp, tok, wide = dblg_ref.shape
    count = n_dp * n_f
    width = x_own.shape[1]
    ch = ig_s.shape[1]
    piece = 256
    n_taps = taps_ref.shape[0]
    down = n_f // 2
    ring_o = RingReduce(n_f, wo_part, wo_got, wo_send, wo_recv, n_f - 1 - down)
    ring_x = RingReduce(n_f, wx_s, wx_got, wx_send, wx_recv, down)
    ring_s = RingReduce(n_f, small_s, sm_got, sm_send, sm_recv, down)
    pairs = [
        PairReduce(ng_s.at[h], ng_near.at[h], ng_far.at[h], ng_send.at[h], ng_recv.at[h]) for h in (0, 1)
    ]
    blocks = width // piece
    turn = half + blocks
    shares = [
        PairShare(mine, out, local.at[i], sh_send.at[i], sh_recv.at[i])
        for i, (mine, out) in enumerate(
            [
                (wg_own, lambda d: gin_all.at[d, :, pl.ds(ch, ch)]),
                (wo_own, lambda d: go_all.at[d]),
                (wx_own, lambda d: gin_all.at[d, :, pl.ds(0, ch)]),
                (sm_own, lambda d: lane_block(small_all, d, sm_own.shape[1])),
            ]
        )
    ]
    ret_m = Return(count, n_f, ret_mix, mix_back, local.at[4], ret_sem.at[0], ret_sem.at[1])
    ret_x = Return(count, n_f, ret_dx, dx_back, local.at[5], ret_sem.at[2], ret_sem.at[3])
    tn = (((0,), (0,)), ((), ()))
    nt = (((1,), (1,)), ((), ()))

    @pl.when(g == 0)
    def _():
        me = lax.axis_index("dp") * n_f + lax.axis_index("fsdp")
        barrier = pltpu.get_barrier_semaphore()

        def greet(p, _):
            pl.semaphore_signal(
                barrier, inc=1, device_id=mesh_at(lax.rem(me + p, count), n_f), device_id_type=pl.DeviceIdType.MESH
            )
            return 0

        lax.fori_loop(1, count, greet, 0)
        pl.semaphore_wait(barrier, count - 1)
        ring_o.resume(2, wo_half)
        shares[0].start()
        spots = jnp.concatenate([tags_ref[...]] * (tok // 128), axis=1)
        lane = lax.broadcasted_iota(jnp.int32, (tok, tok), 1).astype(F32)
        pick_s[...] = jnp.where(spots == lane, 1.0, 0.0).astype(BF16)
        ret_m.fill(pick_s[...], mixed_own)
        ret_mix[:, :, width:] = jnp.broadcast_to(ride_ref[...], (tok, 128)).astype(BF16).reshape(
            count, tok // count, 128
        )
        ret_m.start()

    for e in range(3, ring_o.events):

        @pl.when(g == min(turn + e - 2, steps - 2))
        def _(e=e):
            ring_o.event(e)

    @pl.when(g == turn)
    def _():
        ring_x.start()
        ring_s.start()

    @pl.when(g == turn + blocks // 2)
    def _():
        pairs[0].start()

    @pl.when(g == steps - 2)
    def _():
        pairs[0].middle()
        ring_s.event(1)
        ring_x.event(1)

    @pl.when(g < half)
    def _():
        cols = pl.ds(pl.multiple_of(g * piece, piece), piece)
        zero = jnp.zeros((1, piece), F32)
        misc = [zero] * (n_taps + 1)
        sel_grad = jnp.zeros((wide, piece), F32)
        for m in range(n_dp):
            at = slice(m * tok, (m + 1) * tok)
            low = dblg_ref[m].astype(BF16)
            since, left = segment_span(lens_ref, m, 0, tok)
            act_grad = da_ref[at, :] + jnp.dot(low, sel_ref[...], preferred_element_type=F32)
            conv_grad = act_grad * silu_slope(conv_ref[at, :])
            back = taps_ref[n_taps - 1 : n_taps, :] * conv_grad
            x_in = xin_ref[at, :]
            misc[n_taps - 1] = misc[n_taps - 1] + jnp.sum(conv_grad * x_in, axis=0, keepdims=True)
            for lag in range(1, n_taps):
                tap = n_taps - 1 - lag
                later = pltpu.roll(conv_grad, tok - lag, 0) * (left >= lag).astype(F32)
                back = back + taps_ref[tap : tap + 1, :] * later
                misc[tap] = misc[tap] + jnp.sum(later * x_in, axis=0, keepdims=True)
            ig_s[at, cols] = back.astype(BF16)
            misc[n_taps] = misc[n_taps] + jnp.sum(conv_grad, axis=0, keepdims=True)
            sel_grad = sel_grad + lax.dot_general(low, act_ref[at, :], tn, preferred_element_type=F32)
        rows = jnp.concatenate(
            [
                sel_grad,
                stepg_ref[...],
                dsum_ref[...] * rate_ref[...],
                jnp.concatenate(misc + [sums_ref[0:2, :], zero], axis=0),
                jnp.zeros((small_s.shape[1] - wide - stepg_ref.shape[0] - rate_ref.shape[0] - 8, piece), F32),
            ],
            axis=0,
        )
        cs = small_s.shape[2]
        for i in range(piece // cs):
            small_s[g * (piece // cs) + i] = rows[:, i * cs : (i + 1) * cs]

    @pl.when((g >= half) & (g < turn))
    def _():
        block = g - half
        dcols = wx_s.shape[1]
        grad = lax.dot_general(normed_ref[...], ig_s[...], tn, preferred_element_type=F32).astype(BF16)
        for i in range(piece // dcols):
            wx_s[block * (piece // dcols) + i] = grad[i * dcols : (i + 1) * dcols]

    @pl.when(g >= turn)
    def _():
        grad = lax.dot_general(ig_s[...], wx_ref[...], nt, preferred_element_type=F32)
        grad = grad + lax.dot_general(gg_ref[...], wg_ref[...], nt, preferred_element_type=F32)
        grad = grad.astype(BF16).reshape(n_dp, tok, piece)
        for h in (0, 1):

            @pl.when((g - turn) // (blocks // 2) == h)
            def _(h=h):
                at = (g - turn - h * (blocks // 2)) * piece
                ng_s[h, :, :, pl.ds(pl.multiple_of(at, piece), piece)] = grad

    @pl.when(g == steps - 1)
    def _():
        pairs[1].start()
        shares[0].relay()
        pairs[1].middle()
        ring_o.finish(wo_own, 2)
        shares[1].start()
        ring_s.event(2)
        ring_x.event(2)
        for h in (0, 1):
            pairs[h].finish(change_s.at[:, pl.ds(h * (width // 2), width // 2)])

        def rows(i, _):
            at = pl.ds(pl.multiple_of(i * 16, 16), 16)
            v = x_own[at, :].astype(F32)
            rstd = lax.rsqrt(jnp.mean(v * v, axis=1, keepdims=True) + EPS)
            hat = v * rstd
            grad = change_s[at, :] * gain_ref[...]
            grad = rstd * (grad - hat * jnp.mean(grad * hat, axis=1, keepdims=True))
            change_s[at, :] = dy_own[at, :].astype(F32) + grad
            return 0

        lax.fori_loop(0, tok // 16, rows, 0)
        for e in range(3, ring_x.events):
            ring_s.event(e)
            ring_x.event(e)
        ret_x.fill(pick_s[...], change_s)
        ret_x.start()
        shares[1].relay()
        ring_s.finish(sm_own)
        shares[3].start()
        ring_x.finish(wx_own)
        shares[2].start()
        shares[3].relay()
        shares[2].relay()
        for share in shares:
            share.finish()
        ret_m.finish()
        ret_x.finish()


def leave(lens, da, conv, x_in, act, dbl_grad, sel, taps, sums, decay_sum, rate, stepg, normed, wx, wg, gate_grad,
          wo_part, wo_half, wg_own, x_own, dy_own, mixed_own, gain, tags, ride, n_f):
    n_dp, tok, wide = dbl_grad.shape
    group, ch = act.shape
    width = x_own.shape[1]
    count = n_dp * n_f
    pair = tok // count
    piece = 256
    half = ch // piece
    dcols = width // n_f
    cs = ch // n_f
    n = rate.shape[0]
    tall = -(-(wide + stepg.shape[0] + n + 8) // 64) * 64
    blocks = width // piece
    early = lambda g: (0, jnp.minimum(g, half - 1))
    late = lambda g: (0, jnp.clip(g - half, 0, blocks - 1))
    late_rows = lambda g: (jnp.maximum(g - half - blocks, 0), 0)
    any_ = pl.BlockSpec(memory_space=pl.ANY)
    vmem = pl.BlockSpec(memory_space=pltpu.VMEM)
    block = lambda rows: pl.BlockSpec((rows, piece), early)
    shaped = jax.ShapeDtypeStruct
    return pl.pallas_call(
        functools.partial(leave_kernel, n_f, half),
        grid=(half + 2 * blocks,),
        in_specs=[
            pl.BlockSpec(memory_space=pltpu.SMEM),
            block(group),
            block(group),
            block(group),
            block(group),
            vmem,
            block(wide),
            block(taps.shape[0]),
            block(8),
            block(n),
            block(n),
            block(stepg.shape[0]),
            pl.BlockSpec((group, piece), late),
            pl.BlockSpec((piece, ch), late_rows),
            pl.BlockSpec((piece, ch), late_rows),
        ]
        + [vmem] * 10,
        out_specs=[any_] * 5,
        out_shape=[
            shaped((count, pair, width + 128), BF16),
            shaped((count, pair, width), BF16),
            shaped((n_dp, dcols, 2 * ch), BF16),
            shaped((n_dp, cs, width), BF16),
            shaped(side_by_side(n_dp, tall, cs), F32),
        ],
        scratch_shapes=[
            pltpu.VMEM((group, ch), BF16),
            pltpu.VMEM((n_f, dcols, ch), BF16),
            pltpu.VMEM((2, n_dp, tok, width // 2), BF16),
            pltpu.VMEM((n_f, tall, cs), F32),
            pltpu.VMEM((tok, tok), BF16),
            pltpu.VMEM((count, pair, width + 128), BF16),
            pltpu.VMEM((count, pair, width), BF16),
            pltpu.VMEM((tok, width), F32),
        ]
        + RingReduce.scratch(n_f, (cs, width))
        + RingReduce.scratch(n_f, (dcols, ch))
        + RingReduce.scratch(n_f, (tall, cs), F32)
        + [
            pltpu.VMEM((2, 2, tok, width // 2), BF16),
            pltpu.VMEM((2, tok, width // 2), BF16),
            pltpu.SemaphoreType.DMA((2, 3)),
            pltpu.SemaphoreType.DMA((2, 3)),
            pltpu.VMEM((cs, width), BF16),
            pltpu.VMEM((dcols, ch), BF16),
            pltpu.VMEM((tall, cs), F32),
            pltpu.SemaphoreType.DMA((6,)),
            pltpu.SemaphoreType.DMA((4, 3)),
            pltpu.SemaphoreType.DMA((4, 3)),
            pltpu.SemaphoreType.DMA((4,)),
        ],
        compiler_params=pltpu.CompilerParams(
            collective_id=4, has_side_effects=True, vmem_limit_bytes=62 * 2**20
        ),
        cost_estimate=pl.CostEstimate(flops=2 * 10**10, bytes_accessed=6 * 10**7, transcendentals=10**6),
    )(lens, da, conv, x_in, act, dbl_grad, sel, taps, sums, decay_sum, rate, stepg, normed, wx, wg, gate_grad,
      wo_part, wo_half, wg_own, x_own, dy_own, mixed_own, gain, tags, ride)


def masks_of(count):
    return [1 << b for b in range(count.bit_length() - 1)]


def mesh_at(index, n_f):
    return (index // n_f, lax.rem(index, n_f))


def ring_index(p, n_f):
    if n_f % 2:
        return p
    return jnp.where(p < n_f // 2, 2 * p, 2 * (n_f - 1 - p) + 1)


def ring_place(f, n_f):
    if n_f % 2:
        return f
    return jnp.where(lax.rem(f, 2) == 0, f // 2, n_f - 1 - f // 2)


def gather_kernel(n_dp, n_f, downs, x_ref, dy_ref, meta_ref, dest_ref, lens_ref, *refs):
    streams = len(downs)
    blocks = refs[:streams]
    x_all, lens_all, x_own_ref, dy_own_ref, tag_ref, rank_ref = refs[streams : streams + 6]
    outs = refs[streams + 6 : 2 * streams + 6]
    (send_x, send_dy, got_x, got_dy, x_own, dy_own, deal_sem, loc_sem, pair_send, pair_recv, ring_send, ring_recv) = (
        refs[2 * streams + 6 :]
    )
    count = n_dp * n_f
    me_d = lax.axis_index("dp")
    me_f = lax.axis_index("fsdp")
    me = me_d * n_f + me_f
    q = ring_place(me_f, n_f)
    below = ring_index(lax.rem(q + n_f - 1, n_f), n_f)
    above = ring_index(lax.rem(q + 1, n_f), n_f)

    barrier = pltpu.get_barrier_semaphore()

    def greet(p, _):
        pl.semaphore_signal(
            barrier, inc=1, device_id=mesh_at(lax.rem(me + p, count), n_f), device_id_type=pl.DeviceIdType.MESH
        )
        return 0

    lax.fori_loop(1, count, greet, 0)
    def place_of(s, index):
        return lane_block(outs[s], index, blocks[s].shape[1]) if s == 0 else outs[s].at[index]

    locals_ = [
        pltpu.make_async_copy(blocks[s], place_of(s, me_f), loc_sem.at[s]) for s in range(streams)
    ]
    for c in locals_:
        c.start()
    pl.semaphore_wait(barrier, count - 1)

    def deal(a):
        src, dst = ((send_x, got_x), (send_dy, got_dy))[a]

        def one(p, _):
            pltpu.make_async_remote_copy(
                src_ref=src.at[p],
                dst_ref=dst.at[p],
                send_sem=deal_sem.at[a, 0],
                recv_sem=deal_sem.at[a, 1],
                device_id=mesh_at(lax.rem(me + p, count), n_f),
                device_id_type=pl.DeviceIdType.MESH,
            ).start()
            return 0

        lax.fori_loop(1, count, one, 0)
        dst[0] = src[0]

    def dealt(a, way):
        src, dst = ((send_x, got_x), (send_dy, got_dy))[a]
        rest = pl.ds(1, count - 1)
        pltpu.make_async_copy(src.at[rest], dst.at[rest], deal_sem.at[a, way]).wait()

    def hop(s, h, up):
        k = lax.rem(q + (n_f - h if up else h), n_f)
        index = ring_index(k, n_f)
        src = blocks[s] if h == 0 else place_of(s, index)
        return pltpu.make_async_remote_copy(
            src_ref=src,
            dst_ref=place_of(s, index),
            send_sem=ring_send.at[s, int(up), h],
            recv_sem=ring_recv.at[s, int(up), h],
            device_id=(me_d, above if up else below),
            device_id_type=pl.DeviceIdType.MESH,
        )

    hops = [[downs[s], n_f - 1 - downs[s]] for s in range(streams)]
    for s in range(streams):
        for up in (0, 1):
            if hops[s][up]:
                hop(s, 0, up).start()
    tok, width = x_own.shape
    pair = got_x.shape[1]

    dest_row, rel_row, abs_row, in_row = (meta_ref[i : i + 1, :] for i in range(4))
    rank = jnp.sum((dest_ref[...] < dest_row).astype(F32), axis=0, keepdims=True)
    goal = rel_row * pair + rank - abs_row * pair
    rank_ref[...] = jnp.broadcast_to(goal, rank_ref.shape)
    chosen = lax.broadcasted_iota(jnp.int32, (tok, tok), 0).astype(F32) == goal
    spot = jnp.sum(jnp.where(chosen, in_row, 0.0), axis=1, keepdims=True)
    send_x[:, :, width:] = jnp.broadcast_to(spot, (tok, 128)).astype(BF16).reshape(count, pair, 128)
    pick = jnp.where(chosen, 1.0, 0.0).astype(BF16)

    def sort(values, out):
        def part(j, _):
            cols = pl.ds(pl.multiple_of(j * 256, 256), 256)
            moved = jnp.dot(pick, values[:, cols], preferred_element_type=F32)
            out[:, :, cols] = moved.astype(BF16).reshape(count, pair, 256)
            return 0

        lax.fori_loop(0, width // 256, part, 0)

    sort(x_ref, send_x)
    deal(0)
    sort(dy_ref, send_dy)
    deal(1)

    def advance(h):
        for s in range(streams):
            for up in (0, 1):
                if h < hops[s][up]:
                    hop(s, h - 1, up).wait_recv()
                    hop(s, h, up).start()

    advance(1)
    dealt(0, 1)
    tag = got_x[:, :, width : width + 128].astype(F32).reshape(tok, 128)
    spots = jnp.concatenate([tag] * (tok // 128), axis=1)
    lane = lax.broadcasted_iota(jnp.int32, (tok, tok), 1).astype(F32)
    settle = jnp.where(spots == lane, 1.0, 0.0).astype(BF16)
    tn = (((0,), (0,)), ((), ()))
    tag_ref[...] = tag

    def place(values, out):
        def part(j, _):
            cols = pl.ds(pl.multiple_of(j * 256, 256), 256)
            block = values[:, :, cols].reshape(tok, 256)
            out[:, cols] = lax.dot_general(settle, block, tn, preferred_element_type=F32).astype(BF16)
            return 0

        lax.fori_loop(0, width // 256, part, 0)

    masks = list(reversed(masks_of(n_dp)))

    def partner(mask):
        return me_d + mask - 2 * mask * lax.rem(me_d // mask, 2)

    def share(a, m, mask):
        out = (x_all, lens_all)[a]
        own_block = (x_own, lens_ref)[a]
        return pltpu.make_async_remote_copy(
            src_ref=own_block if m == 0 else out.at[m],
            dst_ref=out.at[m | mask],
            send_sem=pair_send.at[a, m | mask],
            recv_sem=pair_recv.at[a, m | mask],
            device_id=(partner(mask), me_f),
            device_id_type=pl.DeviceIdType.MESH,
        )

    copies = []

    def keep(src, dst):
        c = pltpu.make_async_copy(src, dst, loc_sem.at[streams + len(copies)])
        c.start()
        copies.append(c)

    place(got_x, x_own)
    for a in (0, 1):
        for mask in masks:
            share(a, 0, mask).start()
    keep(lens_ref, lens_all.at[0])
    keep(x_own, x_all.at[0])
    keep(x_own, x_own_ref)

    def relay(a):
        held = [0]
        for step, mask in enumerate(masks):
            for m in held:
                if m:
                    share(a, m, mask).start()
            for m in held:
                share(a, m, mask).wait_recv()
            held = held + [m | mask for m in held]

    most = max(max(h) for h in hops)
    for h in range(2, most):
        advance(h)
        if h == 2:
            dealt(1, 1)
            place(got_dy, dy_own)
            keep(dy_own, dy_own_ref)
    if most <= 2:
        dealt(1, 1)
        place(got_dy, dy_own)
        keep(dy_own, dy_own_ref)
    relay(0)
    relay(1)
    for s in range(streams):
        for up in (0, 1):
            if hops[s][up]:
                hop(s, hops[s][up] - 1, up).wait_recv()
    for s in range(streams):
        for up in (0, 1):
            for h in range(hops[s][up]):
                hop(s, h, up).wait_send()
    for a in (0, 1):
        held = [0]
        for mask in masks:
            for m in held:
                share(a, m, mask).wait_send()
            held = held + [m | mask for m in held]
    for c in locals_ + copies:
        c.wait()
    dealt(0, 0)
    dealt(1, 0)


def gather_all(x, dy, meta, dest, lens, blocks, downs, n_dp, n_f):
    streams = len(blocks)
    tok, width = x.shape
    count = n_dp * n_f
    sent_x = (count, tok // count, width + 128)
    sent_dy = (count, tok // count, width)
    hops = max(max(d, n_f - 1 - d) for d in downs)
    any_ = pl.BlockSpec(memory_space=pl.ANY)
    vmem = pl.BlockSpec(memory_space=pltpu.VMEM)
    row = jax.ShapeDtypeStruct((tok, width), BF16)
    rows = jax.ShapeDtypeStruct((n_dp, tok, width), BF16)
    return pl.pallas_call(
        functools.partial(gather_kernel, n_dp, n_f, downs),
        in_specs=[vmem] * 5 + [any_] * streams,
        out_specs=[any_] * 4 + [vmem] * 2 + [any_] * streams,
        out_shape=[
            rows,
            jax.ShapeDtypeStruct((n_dp,) + lens.shape, lens.dtype),
            row,
            row,
            jax.ShapeDtypeStruct((tok, 128), F32),
            jax.ShapeDtypeStruct((8, tok), F32),
        ]
        + [jax.ShapeDtypeStruct(side_by_side(n_f, *blocks[0].shape), BF16)]
        + [jax.ShapeDtypeStruct((n_f,) + b.shape, b.dtype) for b in blocks[1:]],
        scratch_shapes=[
            pltpu.VMEM(sent_x, BF16),
            pltpu.VMEM(sent_dy, BF16),
            pltpu.VMEM(sent_x, BF16),
            pltpu.VMEM(sent_dy, BF16),
            pltpu.VMEM((tok, width), BF16),
            pltpu.VMEM((tok, width), BF16),
            pltpu.SemaphoreType.DMA((2, 2)),
            pltpu.SemaphoreType.DMA((streams + 4,)),
            pltpu.SemaphoreType.DMA((2, n_dp)),
            pltpu.SemaphoreType.DMA((2, n_dp)),
            pltpu.SemaphoreType.DMA((streams, 2, hops)),
            pltpu.SemaphoreType.DMA((streams, 2, hops)),
        ],
        compiler_params=pltpu.CompilerParams(
            collective_id=0, has_side_effects=True, vmem_limit_bytes=40 * 2**20
        ),
        cost_estimate=pl.CostEstimate(flops=10**10, bytes_accessed=2 * 10**8, transcendentals=0),
    )(x, dy, meta, dest, lens, *blocks)


def columns_kernel(starts, cs, w_ref, *outs):
    me_d = lax.axis_index("dp")
    for o, out in enumerate(outs):
        for j, start in enumerate(starts[o]):
            out[:, j * cs : (j + 1) * cs] = w_ref[:, pl.ds(pl.multiple_of(start + me_d * cs, 128), cs)]


def take_columns(w, halves, n_f, n_dp, cs):
    inner = n_f * n_dp * cs
    starts = [[h * inner + f * n_dp * cs for f in range(n_f)] for h in range(halves)]
    me_d = lax.axis_index("dp")
    if cs % 128:
        return [
            jnp.concatenate([lax.dynamic_slice_in_dim(w, s + me_d * cs, cs, 1) for s in group], axis=1)
            for group in starts
        ]
    height = w.shape[0]
    blk = min(height, 64)
    return pl.pallas_call(
        functools.partial(columns_kernel, starts, cs),
        grid=(height // blk,),
        in_specs=[pl.BlockSpec((blk, w.shape[1]), lambda i: (i, 0))],
        out_specs=[pl.BlockSpec((blk, n_f * cs), lambda i: (i, 0))] * halves,
        out_shape=[jax.ShapeDtypeStruct((height, n_f * cs), w.dtype)] * halves,
    )(w)


def spread_kernel(cs, x_ref, w_ref, out_ref, sum_ref):
    total = jnp.zeros(sum_ref.shape, F32)
    n_dp = x_ref.shape[0]
    for f in range(x_ref.shape[2] // cs):
        for i in range(n_dp):
            part = x_ref[i, :, f * cs : (f + 1) * cs].astype(F32)
            cols = slice((f * n_dp + i) * cs, (f * n_dp + i + 1) * cs)
            out_ref[:, cols] = part
            product = part * w_ref[:, cols].astype(F32)
            for j in range(0, cs, 128):
                total = total + product[:, j : j + 128]

    @pl.when(pl.program_id(0) == 0)
    def _():
        sum_ref[...] = jnp.zeros_like(sum_ref)

    sum_ref[...] += total


def spread_columns(parts, w, cs):
    n_dp, height, cols = parts.shape
    if cs % 128:
        out = parts.reshape(n_dp, height, cols // cs, cs).transpose(1, 2, 0, 3).reshape(height, n_dp * cols).astype(F32)
        return out, jnp.sum(out * w.astype(F32), axis=1)
    wide = 2 * cs
    out, sums = pl.pallas_call(
        functools.partial(spread_kernel, cs),
        grid=(cols // wide,),
        in_specs=[
            pl.BlockSpec((n_dp, height, wide), lambda f: (0, 0, f)),
            pl.BlockSpec((height, n_dp * wide), lambda f: (0, f)),
        ],
        out_specs=[
            pl.BlockSpec((height, n_dp * wide), lambda f: (0, f)),
            pl.BlockSpec((height, 128), lambda f: (0, 0)),
        ],
        out_shape=[jax.ShapeDtypeStruct((height, n_dp * cols), F32), jax.ShapeDtypeStruct((height, 128), F32)],
        compiler_params=pltpu.CompilerParams(vmem_limit_bytes=32 * 2**20),
        cost_estimate=pl.CostEstimate(flops=4 * height * cols * n_dp, bytes_accessed=8 * height * cols * n_dp, transcendentals=0),
    )(parts, w)
    return out, jnp.sum(sums, axis=1)


def per_device(
    tokens,
    cotangent,
    destination,
    lengths,
    norm_gain,
    in_weight,
    conv_weight,
    conv_bias,
    select_weight,
    step_weight,
    step_bias,
    decay_log,
    skip_gain,
    out_weight,
):
    n_dp = lax.axis_size("dp")
    n_f = lax.axis_size("fsdp")
    rows = n_dp * n_f
    tok = tokens.shape[0]
    width = tokens.shape[1]
    pair = tok // rows
    inner = conv_bias.shape[0] * n_f
    cs = conv_bias.shape[0] // n_dp
    ch = cs * n_f
    taps = conv_weight.shape[0]
    n = decay_log.shape[0]
    rank_of = step_weight.shape[0]
    dcols = width // n_f
    group = n_dp * tok
    both = ("dp", "fsdp")
    me_d = lax.axis_index("dp")
    me_f = lax.axis_index("fsdp")
    flat_dot = lambda a, b: jnp.dot(a, b, preferred_element_type=F32)
    nt_dot = lambda a, b: lax.dot_general(a, b, (((1,), (1,)), ((), ())), preferred_element_type=F32)
    tn_dot = lambda a, b: lax.dot_general(a, b, (((0,), (0,)), ((), ())), preferred_element_type=F32)

    me = me_d * n_f + me_f
    row_to = destination // tok
    meta = jnp.stack(
        [destination, (row_to - me) % rows, row_to, destination % tok] + [jnp.zeros_like(destination)] * 4
    ).astype(F32)
    segs = lengths.shape[1]
    lens_tile = jnp.pad(lengths, ((0, 7), (0, 128 - segs)))
    slots = jnp.arange(tok, dtype=jnp.int32)

    def mine(shard):
        return lax.dynamic_slice_in_dim(shard.reshape(-1, n_dp * cs), me_d * cs, cs, 1)

    smalls = [conv_weight, conv_bias, step_bias, skip_gain, decay_log, select_weight, step_weight]
    heights = [math.prod(s.shape) // (n_dp * cs) for s in smalls]
    gain_rows = dcols // cs
    used = sum(heights) + gain_rows
    filler = -used % 16
    small_block = jnp.concatenate(
        [mine(s) for s in smalls] + [norm_gain.reshape(gain_rows, cs), jnp.zeros((filler, cs), BF16)], axis=0
    )
    wx_block, wg_block = take_columns(in_weight, 2, n_f, n_dp, cs)
    wo_block = lax.dynamic_slice_in_dim(out_weight, me_d * cs, cs, 0)
    x_all, lens_all, x_own, dy_own, x_tags, ranks, small_all, wx, wg = gather_all(
        tokens, cotangent, meta, destination[:, None].astype(F32), lens_tile,
        [small_block, wx_block, wg_block], [n_f // 2, n_f // 2, n_f - 1 - n_f // 2], n_dp, n_f,
    )
    x_all = x_all.reshape(group, width)
    lens = lens_all[:, 0, :segs]
    from_send = (ranks[0].astype(jnp.int32)[:, None] == slots[None, :]).astype(BF16)
    wx = wx.reshape(width, ch)
    wg = wg.reshape(width, ch)
    small = joined(small_all)
    gain = small[used - gain_rows : used].reshape(gain_rows, n_f, cs).transpose(1, 0, 2).reshape(width).astype(F32)
    valid = (slots < jnp.sum(lengths[0, : segs - 1])).astype(F32)
    x_own32 = x_own.astype(F32)
    square = jnp.sum(x_own32 * x_own32, axis=1)
    mine_sums = [jnp.sum(square * valid), jnp.sum(valid)]

    pieces, at = [], 0
    for height in heights:
        pieces.append(small[at : at + height])
        at += height
    conv_w, conv_b, step_b, skip, dlog, sel, stepw = pieces
    conv_w = conv_w.astype(F32)
    skip = skip.astype(F32)
    rate = -jnp.exp(dlog.astype(F32))

    normed, x_in, conv, act, gate, dbl, wo_next = enter(
        lens, x_all, gain[None], wx, wg, conv_w, conv_b.astype(F32), sel, wo_block, n_f
    )
    dbl = dbl.reshape(group, -1)
    rate2 = rate * LOG2E
    scan_out, states, delta, pre, wo, dy_all = scan_forward(
        lens, dbl, act, stepw, step_b.astype(F32), rate2, skip, wo_block, wo_next, dy_own, n_f, tok
    )
    dy_all = dy_all.reshape(group, width)
    wo = wo.reshape(ch, width)
    gate_silu = jax.nn.silu(gate)
    gated = (scan_out * gate_silu).astype(BF16)

    gated_grad = nt_dot(dy_all, wo)
    scan_grad = gated_grad * gate_silu
    gate_grad = (gated_grad * scan_out * silu_slope(gate)).astype(BF16)
    wg_grad = tn_dot(normed, gate_grad).astype(BF16)
    pre_grad, act_grad, dbl_grad, decay_sum, sums, step_grad, wg_own, wo_grad, wo_half, mixed = scan_backward(
        lens, dbl, delta, pre, act, scan_grad, stepw, rate2, skip, states,
        wg_grad.reshape(n_f, dcols, ch), gated, dy_all, wo, n_f, tok,
    )
    lanes = lax.broadcasted_iota(jnp.int32, (1, 128), 1)
    ride = jnp.zeros((1, 128), F32)
    for j, value in enumerate(mine_sums):
        high = value.astype(BF16).astype(F32)
        ride = ride + jnp.where(lanes == 2 * j, high, 0.0) + jnp.where(lanes == 2 * j + 1, value - high, 0.0)
    mix_back, dx_back, gin_all, go_all, small_full = leave(
        lens, act_grad, conv, x_in, act, dbl_grad, sel, conv_w, sums, decay_sum, rate, step_grad, normed, wx, wg,
        gate_grad, wo_grad, wo_half, wg_own, x_own, dy_own, mixed, gain[None], x_tags, ride, n_f,
    )

    grad_in_weight, gain_sum = spread_columns(gin_all, in_weight, cs)
    grad_out_weight = go_all.reshape(n_dp * cs, width).astype(F32)
    small_full = joined(small_full)
    grad_norm_gain = gain_sum / norm_gain.astype(F32)
    wide = select_weight.shape[0]
    at_decay = wide + rank_of
    at_misc = at_decay + n
    grad_select = small_full[:wide]
    grad_step = small_full[wide:at_decay]
    grad_decay = small_full[at_decay:at_misc]
    misc = small_full[at_misc : at_misc + 8]

    back = mix_back.reshape(tok, width + 128)
    totals = jnp.sum(mix_back[:, 0, width : width + 4].astype(F32), axis=0)
    input_rms = jnp.sqrt((totals[0] + totals[1]) / ((totals[2] + totals[3]) * width))
    mixer_output = flat_dot(from_send, back[:, :width])
    layer_output = (tokens.astype(F32) + mixer_output).astype(BF16)
    mixer_output = mixer_output.astype(BF16)
    input_grad = flat_dot(from_send, dx_back.reshape(tok, width)).astype(BF16)
    return (
        layer_output,
        mixer_output,
        input_grad,
        input_rms,
        grad_norm_gain,
        grad_in_weight,
        misc[:taps],
        misc[taps],
        grad_select,
        grad_step,
        misc[taps + 1],
        grad_decay,
        misc[taps + 2],
        grad_out_weight,
    )


def solution(mesh):
    return jax.shard_map(
        per_device,
        mesh=mesh,
        in_specs=(
            P(("dp", "fsdp"), None),
            P(("dp", "fsdp"), None),
            P(("dp", "fsdp")),
            P(("dp", "fsdp"), None),
            P("fsdp"),
            P("fsdp", None),
            P(None, "fsdp"),
            P("fsdp"),
            P(None, "fsdp"),
            P(None, "fsdp"),
            P("fsdp"),
            P(None, "fsdp"),
            P("fsdp"),
            P("fsdp", None),
        ),
        out_specs=(
            P(("dp", "fsdp"), None),
            P(("dp", "fsdp"), None),
            P(("dp", "fsdp"), None),
            P(),
            P("fsdp"),
            P("fsdp", None),
            P(None, "fsdp"),
            P("fsdp"),
            P(None, "fsdp"),
            P(None, "fsdp"),
            P("fsdp"),
            P(None, "fsdp"),
            P("fsdp"),
            P("fsdp", None),
        ),
        check_vma=False,
    )
```

```python
import functools
import math

import jax
import jax.numpy as jnp
from jax import lax
from jax.experimental import pallas as pl
from jax.experimental.pallas import tpu as pltpu
from jax.sharding import PartitionSpec as P

EPS = 1e-05
TB = 16
LOG2E = math.log2(math.e)
RESET = 1.0e4
BF16 = jnp.bfloat16
F32 = jnp.float32


def silu_slope(value):
    sigma = jax.nn.sigmoid(value)
    return sigma * (1.0 + value * (1.0 - sigma))


def row_at(g, n_dp):
    return lax.rem(2 * g + 1, n_dp + 1)


def flip(d, mask):
    return d + mask - 2 * mask * lax.rem(d // mask, 2)


class GroupSum:
    def __init__(self, part, near, far, total, send, recv):
        self.part, self.near, self.far, self.total = part, near, far, total
        me_d, me_f = lax.axis_index("dp"), lax.axis_index("fsdp")
        plan = [
            (part.at[1], near.at[0], 1),
            (part.at[3], near.at[1], 1),
            (part.at[0], far.at[1], 2),
            (part.at[2], far.at[0], 2),
            (total.at[0], total.at[1], 1),
            (total.at[2], total.at[3], 1),
        ]
        self.copies = [
            pltpu.make_async_remote_copy(
                src_ref=src,
                dst_ref=dst,
                send_sem=send.at[i],
                recv_sem=recv.at[i],
                device_id=(flip(me_d, mask), me_f),
                device_id_type=pl.DeviceIdType.MESH,
            )
            for i, (src, dst, mask) in enumerate(plan)
        ]

    def row_done(self, g):
        for j in (0, 1):

            @pl.when(g == j)
            def _(j=j):
                self.copies[j].start()

            @pl.when(g == j + 2)
            def _(j=j):
                self.copies[j].wait_recv()
                self.part[2 * j] = self.part[2 * j] + self.near[j]
                self.copies[j + 2].start()

    def first(self):
        for j in (0, 1):
            self.copies[j].start()

    def second(self):
        for j in (0, 1):
            self.copies[j].wait_recv()
            self.part[2 * j] = self.part[2 * j] + self.near[j]
            self.copies[j + 2].start()

    def finish(self):
        for j in (0, 1):
            self.copies[3 - j].wait_recv()
            self.total[2 * j] = self.part[2 * j] + self.far[j]
            self.copies[4 + j].start()
        for j in (0, 1):
            self.copies[4 + j].wait_recv()
        for c in self.copies:
            c.wait_send()

    @staticmethod
    def scratch(tok, wide):
        return [
            pltpu.VMEM((4, tok, wide), F32),
            pltpu.VMEM((2, tok, wide), F32),
            pltpu.VMEM((2, tok, wide), F32),
            pltpu.VMEM((4, tok, wide), F32),
            pltpu.SemaphoreType.DMA((6,)),
            pltpu.SemaphoreType.DMA((6,)),
        ]


class RingReduce:
    def __init__(self, n_f, part, got, send, recv, down):
        self.part, self.got = part, got
        q = ring_place(lax.axis_index("fsdp"), n_f)
        self.at = lambda k: ring_index(lax.rem(q + k, n_f), n_f)
        self.n_f = n_f
        self.counts = [down, n_f - 1 - down]
        self.copies = [[], []]
        for up in (0, 1):
            for h in range(min(self.counts[up], got.shape[1])):
                src = part.at[self.at(self.goal(up, 0))] if h == 0 else got.at[up, h - 1]
                self.copies[up].append(ring_copy(n_f, src, got.at[up, h], send.at[up, h], recv.at[up, h], up))
        self.events = max(self.counts)

    def goal(self, up, h):
        left = self.counts[up] - h
        return left if up else self.n_f - left

    def add(self, slot, addend):
        rows = slot.shape[0]
        step = min(rows, 64)

        def piece(i, _):
            at = pl.ds(pl.multiple_of(i * step, step), step)
            slot[at, :] = (slot[at, :].astype(F32) + addend[at, :].astype(F32)).astype(slot.dtype)
            return 0

        lax.fori_loop(0, rows // step, piece, 0)

    def start(self):
        for up in (0, 1):
            if self.copies[up]:
                self.copies[up][0].start()

    def stop(self, hops, out):
        for up in (0, 1):
            self.copies[up][hops - 1].wait_recv()
            rows_add(out.at[up], [self.got.at[up, hops - 1]])
            for c in self.copies[up][:hops]:
                c.wait_send()

    def resume(self, hops, arrived):
        for up in (0, 1):
            slot = self.got.at[up, hops - 1]
            rows_add(slot, [arrived.at[up], self.part.at[self.at(self.goal(up, hops))]])
            self.copies[up][hops].start()

    def event(self, e):
        for up in (0, 1):
            if e < self.counts[up]:
                self.copies[up][e - 1].wait_recv()
                self.add(self.got.at[up, e - 1], self.part.at[self.at(self.goal(up, e))])
                self.copies[up][e].start()

    def finish(self, out, since=0):
        last = []
        for up in (0, 1):
            if self.copies[up]:
                self.copies[up][-1].wait_recv()
                last.append(self.got.at[up, self.counts[up] - 1])
        mine = self.part.at[self.at(0)]
        rows = mine.shape[0]
        step = min(rows, 64)

        def piece(i, _):
            at = pl.ds(pl.multiple_of(i * step, step), step)
            total_ = mine[at, :].astype(F32)
            for slot in last:
                total_ = total_ + slot[at, :].astype(F32)
            out[at, :] = total_.astype(out.dtype)
            return 0

        lax.fori_loop(0, rows // step, piece, 0)
        for up in (0, 1):
            for c in self.copies[up][since:]:
                c.wait_send()

    @staticmethod
    def scratch(n_f, block, dtype=BF16, slots=0):
        return [
            pltpu.VMEM((2, slots or n_f // 2) + block, dtype),
            pltpu.SemaphoreType.DMA((2, n_f // 2)),
            pltpu.SemaphoreType.DMA((2, n_f // 2)),
        ]


class PairReduce:
    def __init__(self, part, near, far, send, recv):
        self.part, self.near, self.far = part, near, far
        me_d, me_f = lax.axis_index("dp"), lax.axis_index("fsdp")
        plan = [
            (part.at[1], near.at[0], 1),
            (part.at[3], near.at[1], 1),
            (part.at[2], far, 2),
        ]
        self.copies = [
            pltpu.make_async_remote_copy(
                src_ref=src,
                dst_ref=dst,
                send_sem=send.at[i],
                recv_sem=recv.at[i],
                device_id=(flip(me_d, mask), me_f),
                device_id_type=pl.DeviceIdType.MESH,
            )
            for i, (src, dst, mask) in enumerate(plan)
        ]

    def start(self):
        for c in self.copies[:2]:
            c.start()

    def middle(self):
        self.copies[1].wait_recv()
        rows_add(self.part.at[2], [self.part.at[2], self.near.at[1]])
        self.copies[2].start()
        self.copies[0].wait_recv()

    def finish(self, out):
        self.copies[2].wait_recv()
        rows_add(out, [self.part.at[0], self.near.at[0], self.far])
        for c in self.copies:
            c.wait_send()

    @staticmethod
    def scratch(block, dtype=BF16):
        return [
            pltpu.VMEM((2,) + block, dtype),
            pltpu.VMEM(block, dtype),
            pltpu.SemaphoreType.DMA((3,)),
            pltpu.SemaphoreType.DMA((3,)),
        ]


def rows_add(out, terms, step=32):
    def piece(i, _):
        at = pl.ds(pl.multiple_of(i * step, step), step)
        total_ = terms[0][at, :].astype(F32)
        for t in terms[1:]:
            total_ = total_ + t[at, :].astype(F32)
        out[at, :] = total_.astype(out.dtype)
        return 0

    lax.fori_loop(0, out.shape[0] // step, piece, 0)


class PairShare:
    def __init__(self, mine, out, local, send, recv, relative=False):
        me_d, me_f = lax.axis_index("dp"), lax.axis_index("fsdp")
        far = 2 if relative else flip(me_d, 2)
        here, at_near, at_far, relayed = (0, 1, 2, 3) if relative else (me_d, me_d, me_d, far)
        self.local = pltpu.make_async_copy(mine, out(here), local)
        self.copies = [
            pltpu.make_async_remote_copy(
                src_ref=src,
                dst_ref=dst,
                send_sem=send.at[i],
                recv_sem=recv.at[i],
                device_id=(flip(me_d, mask), me_f),
                device_id_type=pl.DeviceIdType.MESH,
            )
            for i, (src, dst, mask) in enumerate(
                [(mine, out(at_near), 1), (mine, out(at_far), 2), (out(far), out(relayed), 1)]
            )
        ]

    def start(self):
        self.copies[1].start()
        self.copies[0].start()
        self.local.start()

    def relay(self):
        self.copies[1].wait_recv()
        self.copies[2].start()

    def finish(self):
        self.copies[0].wait_recv()
        self.copies[2].wait_recv()
        for c in self.copies:
            c.wait_send()
        self.local.wait()


def my_rows(ref, height):
    return ref.at[pl.ds(pl.multiple_of(lax.axis_index("dp") * height, height), height), :]


def side_by_side(count, height, wide):
    return (count, height, wide) if wide % 128 else (height, count * wide)


def lane_block(ref, index, wide):
    if wide % 128:
        return ref.at[index]
    return ref.at[:, pl.ds(pl.multiple_of(index * wide, 128), wide)]


def joined(value):
    if value.ndim == 2:
        return value
    return value.transpose(1, 0, 2).reshape(value.shape[1], -1)


def greet_neighbours(n_f, ring):
    me_d, me_f = lax.axis_index("dp"), lax.axis_index("fsdp")
    barrier = pltpu.get_barrier_semaphore()
    others = [(flip(me_d, 1), me_f), (flip(me_d, 2), me_f)]
    if ring:
        q = ring_place(me_f, n_f)
        others.append((me_d, ring_index(lax.rem(q + n_f - 1, n_f), n_f)))
        others.append((me_d, ring_index(lax.rem(q + 1, n_f), n_f)))
    for other in others:
        pl.semaphore_signal(barrier, inc=1, device_id=other, device_id_type=pl.DeviceIdType.MESH)
    pl.semaphore_wait(barrier, len(others))


def ring_copy(n_f, src, dst, send, recv, up):
    me_d, me_f = lax.axis_index("dp"), lax.axis_index("fsdp")
    q = ring_place(me_f, n_f)
    to = ring_index(lax.rem(q + (1 if up else n_f - 1), n_f), n_f)
    return pltpu.make_async_remote_copy(
        src_ref=src,
        dst_ref=dst,
        send_sem=send,
        recv_sem=recv,
        device_id=(me_d, to),
        device_id_type=pl.DeviceIdType.MESH,
    )


def segment_span(lens_ref, m, first, rows):
    t = lax.broadcasted_iota(jnp.int32, (rows, 1), 0) + first
    begin = jnp.zeros((rows, 1), jnp.int32)
    end = jnp.zeros((rows, 1), jnp.int32)
    total = jnp.int32(0)
    for j in range(lens_ref.shape[1]):
        after = total + lens_ref[m, j]
        inside = t >= total
        begin = jnp.where(inside, total, begin)
        end = jnp.where(inside, after, end)
        total = after
    return t - begin, end - 1 - t


def enter_kernel(n_f, half, lens_ref, x_ref, gain_ref, wx_ref, wg_ref, taps_ref, bias_ref, sel_ref, wo_ref,
                 normed_ref, xin_ref, conv_ref, act_ref, gate_ref, dbl_ref, next_ref,
                 part, near, far, total, gs_send, gs_recv, hop_send, hop_recv):
    g = pl.program_id(0)
    n_dp, tok = part.shape[:2]
    rows, width = x_ref.shape
    wo_mine = my_rows(wo_ref, next_ref.shape[2])
    hops = [ring_copy(n_f, wo_mine, next_ref.at[up, 0], hop_send.at[up, 0], hop_recv.at[up, 0], up) for up in (0, 1)]
    hops2 = [
        ring_copy(n_f, next_ref.at[up, 0], next_ref.at[up, 1], hop_send.at[up, 1], hop_recv.at[up, 1], up)
        for up in (0, 1)
    ]
    group = GroupSum(part, near, far, total, gs_send, gs_recv)

    @pl.when(g == 0)
    def _():
        greet_neighbours(n_f, True)
        for c in hops:
            c.start()
        part[...] = jnp.zeros_like(part)

        def norm(i, _):
            for j in range(4):
                at = pl.ds(pl.multiple_of(i * 128 + j * 32, 32), 32)
                v = x_ref[at, :].astype(F32)
                rstd = lax.rsqrt(jnp.mean(v * v, axis=1, keepdims=True) + EPS)
                normed_ref[at, :] = (v * rstd * gain_ref[...]).astype(BF16)
            return 0

        lax.fori_loop(0, rows // 128, norm, 0)

    @pl.when(g == half)
    def _():
        for a, b in zip(hops, hops2):
            a.wait_recv()
            b.start()

    @pl.when(g < half)
    def _():
        n_taps = taps_ref.shape[0]
        xin_ref[...] = jnp.dot(normed_ref[...], wx_ref[...], preferred_element_type=F32)
        for m in range(n_dp):
            at = slice(m * tok, (m + 1) * tok)
            v = xin_ref[at, :]
            since, _ = segment_span(lens_ref, m, 0, tok)
            conv = bias_ref[...] + taps_ref[n_taps - 1 : n_taps, :] * v
            for lag in range(1, n_taps):
                keep = (since >= lag).astype(F32)
                conv = conv + taps_ref[n_taps - 1 - lag : n_taps - lag, :] * (pltpu.roll(v, lag, 0) * keep)
            conv_ref[at, :] = conv
            act = jax.nn.silu(conv).astype(BF16)
            act_ref[at, :] = act
            part[m] += lax.dot_general(act, sel_ref[...], (((1,), (1,)), ((), ())), preferred_element_type=F32)

    @pl.when(g == half - 1)
    def _():
        group.first()

    @pl.when(g >= half)
    def _():
        gate_ref[...] = jnp.dot(normed_ref[...], wg_ref[...], preferred_element_type=F32)

    @pl.when(g == half)
    def _():
        group.second()

    @pl.when(g == 2 * half - 1)
    def _():
        group.finish()
        dbl_ref[...] = total[...]
        for a, b in zip(hops, hops2):
            a.wait_send()
            b.wait()


def enter(lens, x_all, gain, wx, wg, taps, bias, sel, wo, n_f):
    n_dp = lens.shape[0]
    rows, width = x_all.shape
    tok = rows // n_dp
    ch = wx.shape[1]
    wide = sel.shape[0]
    piece = 256
    half = ch // piece
    whole = lambda g: (0, 0)
    early = lambda g: (0, jnp.minimum(g, half - 1))
    late = lambda g: (0, jnp.maximum(g - half, 0))
    once = pl.Buffered(1)
    any_ = pl.BlockSpec(memory_space=pl.ANY)
    shaped = lambda d, t: jax.ShapeDtypeStruct((rows, d), t)
    return pl.pallas_call(
        functools.partial(enter_kernel, n_f, half),
        grid=(2 * half,),
        in_specs=[
            pl.BlockSpec(memory_space=pltpu.SMEM),
            pl.BlockSpec((rows, width), whole, pipeline_mode=once),
            pl.BlockSpec((1, width), whole),
            pl.BlockSpec((width, piece), early),
            pl.BlockSpec((width, piece), late),
            pl.BlockSpec((taps.shape[0], piece), early),
            pl.BlockSpec((1, piece), early),
            pl.BlockSpec((wide, piece), early),
            any_,
        ],
        out_specs=[
            pl.BlockSpec((rows, width), whole),
            pl.BlockSpec((rows, piece), early),
            pl.BlockSpec((rows, piece), early),
            pl.BlockSpec((rows, piece), early),
            pl.BlockSpec((rows, piece), late),
            pl.BlockSpec((n_dp, tok, wide), lambda g: (0, 0, 0)),
            any_,
        ],
        out_shape=[
            shaped(width, BF16),
            shaped(ch, F32),
            shaped(ch, F32),
            shaped(ch, BF16),
            shaped(ch, F32),
            jax.ShapeDtypeStruct((n_dp, tok, wide), F32),
            jax.ShapeDtypeStruct((2, 2, wo.shape[0] // n_dp, wo.shape[1]), BF16),
        ],
        scratch_shapes=GroupSum.scratch(tok, wide)
        + [pltpu.SemaphoreType.DMA((2, 2)), pltpu.SemaphoreType.DMA((2, 2))],
        compiler_params=pltpu.CompilerParams(
            collective_id=1, has_side_effects=True, vmem_limit_bytes=48 * 2**20
        ),
        cost_estimate=pl.CostEstimate(flops=10**10, bytes_accessed=4 * 10**7, transcendentals=10**6),
    )(lens, x_all, gain, wx, wg, taps, bias, sel, wo)


def fold_matrix(n):
    i = lax.broadcasted_iota(jnp.int32, (n, TB * n), 0)
    j = lax.broadcasted_iota(jnp.int32, (n, TB * n), 1)
    return jnp.where(lax.rem(j, n) == i, 1.0, 0.0)


def own_token(n):
    i = lax.broadcasted_iota(jnp.int32, (TB, TB * n), 0)
    j = lax.broadcasted_iota(jnp.int32, (TB, TB * n), 1)
    return i == j // n


def block_rows(m, n):
    spread = jnp.dot(m.astype(BF16), fold_matrix(n).astype(BF16), preferred_element_type=F32)
    i = lax.broadcasted_iota(jnp.int32, spread.shape, 0)
    j = lax.broadcasted_iota(jnp.int32, spread.shape, 1)
    return jnp.where(lax.rem(i, TB) == j // n, spread, 0.0).astype(BF16)


def turned(m):
    n = m.shape[1]
    i = lax.broadcasted_iota(jnp.int32, (n, n), 0)
    j = lax.broadcasted_iota(jnp.int32, (n, n), 1)
    eye = jnp.where(i == j, 1.0, 0.0)
    return lax.dot_general(
        eye, m, (((1,), (1,)), ((), ())), preferred_element_type=F32, precision=lax.Precision.HIGHEST
    )


def softplus(v):
    return jnp.maximum(v, 0.0) + jnp.log1p(jnp.exp(-jnp.abs(v)))


class RingGather:
    def __init__(self, n_f, mine, near, out, local, send, recv):
        q = ring_place(lax.axis_index("fsdp"), n_f)
        at = lambda k: ring_index(lax.rem(q + k, n_f), n_f)
        count = [n_f // 2, n_f - 1 - n_f // 2]
        known = near.shape[1]
        self.locals = [pltpu.make_async_copy(mine, out.at[at(0)], local.at[0])]
        self.hops = [[], []]
        for up in (0, 1):
            for j in range(known):
                index = at(n_f - 1 - j if up else 1 + j)
                self.locals.append(pltpu.make_async_copy(near.at[up, j], out.at[index], local.at[1 + known * up + j]))
            for h in range(known, count[up]):
                index = at(n_f - h if up else h)
                src = near.at[up, known - 1] if h == known else out.at[index]
                self.hops[up].append(
                    ring_copy(n_f, src, out.at[index], send.at[up, h], recv.at[up, h], up)
                )
        self.events = max(len(h) for h in self.hops)

    def start(self):
        for c in self.locals:
            c.start()
        for up in (0, 1):
            if self.hops[up]:
                self.hops[up][0].start()

    def event(self, e):
        for up in (0, 1):
            if e < len(self.hops[up]):
                self.hops[up][e - 1].wait_recv()
                self.hops[up][e].start()

    def finish(self):
        for up in (0, 1):
            if self.hops[up]:
                self.hops[up][-1].wait_recv()
            for c in self.hops[up]:
                c.wait_send()
        for c in self.locals:
            c.wait()


def fwd_kernel(lanes, n_f, lens_ref, dbl_ref, act_ref, stepw_ref, stepb_ref, rate_ref, skip_ref, wo_ref, next_ref, dy_ref,
               y_ref, s_ref, delta_ref, pre_ref, wo_all, dy_all, carry, big_s, cw_s, bt_s, d_s, u_s, sc, local, hop_send, hop_recv, sh_send, sh_recv):
    n, ch = rate_ref.shape
    tblk = act_ref.shape[0]
    low_n = stepw_ref.shape[0]
    steps = pl.num_programs(0) * pl.num_programs(1)
    now = pl.program_id(0) * pl.num_programs(1) + pl.program_id(1)
    ring = RingGather(n_f, my_rows(wo_ref, next_ref.shape[2]), next_ref, wo_all, local, hop_send, hop_recv)
    share = PairShare(dy_ref, lambda m: dy_all.at[m], local.at[5], sh_send, sh_recv, True)

    @pl.when(now == 0)
    def _():
        greet_neighbours(n_f, True)
        ring.start()
        share.start()

    @pl.when(now == 13)
    def _():
        share.relay()

    for e in range(1, ring.events):

        @pl.when(now == min(7 * e, 15))
        def _(e=e):
            ring.event(e)

    @pl.when(pl.program_id(1) == 0)
    def _():
        carry[...] = jnp.zeros_like(carry)

    pre = jnp.dot(dbl_ref[:, :low_n].astype(BF16), stepw_ref[...], preferred_element_type=F32) + stepb_ref[...]
    pre_ref[...] = pre
    delta_ref[...] = softplus(pre)
    since, _ = segment_span(lens_ref, pl.program_id(0), pl.program_id(1) * tblk, tblk)
    big_s[...] = jnp.where(since == 0, RESET, 0.0)
    cw_s[...] = block_rows(dbl_ref[:, low_n + n : low_n + 2 * n], n)
    flat = turned(dbl_ref[:, low_n : low_n + n])
    for i in range(tblk // TB):
        bt_s[i] = flat[:, i * TB : (i + 1) * TB]

    def chunk(i, _):
        base = pl.multiple_of(i * TB, TB)
        dl = delta_ref[pl.ds(base, TB), :]
        ac = act_ref[pl.ds(base, TB), :].astype(F32)
        d_s[...] = dl + big_s[pl.ds(base, TB), :]
        u_s[...] = dl * ac
        bt = bt_s[i]
        for lo in range(0, ch, lanes):
            cs = pl.ds(lo, lanes)
            rate = rate_ref[:, cs]
            s = carry[:, cs]
            for t in range(TB):
                dec = jnp.exp2(d_s[t : t + 1, cs] * rate)
                s = dec * s + bt[:, t : t + 1] * u_s[t : t + 1, cs]
                sc[t * n : (t + 1) * n, cs] = s.astype(BF16)
            carry[:, cs] = s
        states = sc[...]
        y = jnp.dot(cw_s[pl.ds(base, TB), :], states, preferred_element_type=F32)
        y_ref[pl.ds(base, TB), :] = y + skip_ref[...] * ac
        s_ref[pl.ds(pl.multiple_of(base * n, TB * n), TB * n), :] = states
        return 0

    lax.fori_loop(0, tblk // TB, chunk, 0)

    @pl.when(now == steps - 1)
    def _():
        ring.finish()
        share.finish()


def scan_forward(lens, dbl, act, stepw, stepb, rate2, skip, wo, wo_next, dy_own, n_f, row_len, tblk=64, lanes=512):
    t, ch = act.shape
    n = rate2.shape[0]
    nb = row_len // tblk
    at = lambda r, j: (r * nb + j, 0)
    zero = lambda r, j: (0, 0)
    any_ = pl.BlockSpec(memory_space=pl.ANY)
    wide = jax.ShapeDtypeStruct((t, ch), F32)
    return pl.pallas_call(
        functools.partial(fwd_kernel, min(lanes, ch), n_f),
        grid=(t // row_len, nb),
        in_specs=[
            pl.BlockSpec(memory_space=pltpu.SMEM),
            pl.BlockSpec((tblk, dbl.shape[1]), at),
            pl.BlockSpec((tblk, ch), at),
            pl.BlockSpec(stepw.shape, zero),
            pl.BlockSpec((1, ch), zero),
            pl.BlockSpec((n, ch), zero),
            pl.BlockSpec((1, ch), zero),
            any_,
            any_,
            any_,
        ],
        out_specs=[
            pl.BlockSpec((tblk, ch), at),
            pl.BlockSpec((tblk * n, ch), at),
            pl.BlockSpec((tblk, ch), at),
            pl.BlockSpec((tblk, ch), at),
            any_,
            any_,
        ],
        out_shape=[
            wide,
            jax.ShapeDtypeStruct((t * n, ch), BF16),
            wide,
            wide,
            jax.ShapeDtypeStruct((n_f,) + wo_next.shape[2:], BF16),
            jax.ShapeDtypeStruct((t // row_len,) + dy_own.shape, BF16),
        ],
        scratch_shapes=[
            pltpu.VMEM((n, ch), F32),
            pltpu.VMEM((tblk, 1), F32),
            pltpu.VMEM((tblk, TB * n), BF16),
            pltpu.VMEM((tblk // TB, n, TB), F32),
            pltpu.VMEM((TB, ch), F32),
            pltpu.VMEM((TB, ch), F32),
            pltpu.VMEM((TB * n, ch), BF16),
            pltpu.SemaphoreType.DMA((6,)),
            pltpu.SemaphoreType.DMA((2, n_f)),
            pltpu.SemaphoreType.DMA((2, n_f)),
            pltpu.SemaphoreType.DMA((3,)),
            pltpu.SemaphoreType.DMA((3,)),
        ],
        compiler_params=pltpu.CompilerParams(
            collective_id=2, has_side_effects=True, vmem_limit_bytes=32 * 2**20
        ),
        cost_estimate=pl.CostEstimate(flops=t * n * ch * 40, bytes_accessed=t * ch * 52, transcendentals=t * n * ch),
    )(lens, dbl, act, stepw, stepb, rate2, skip, wo, wo_next, dy_own)


def bwd_kernel(lanes, n_f, lens_ref, dbl_ref, delta_ref, pre_ref, act_ref, gy_ref, stepw_ref, rate_ref, skip_ref,
               s_ref, sp_ref, wg_part, gated_ref, dy_ref, wo_ref,
               pg_ref, da_ref, dbl_grad_ref, dl_ref, sums_ref, stepg_ref, wg_own, wo_out, wo_half, mixed_own,
               carry, big_s, bw_s, ct_s, d_all, u_all, g_all, h_all, b_all, c_all, part, near, far, total, gs_send, gs_recv,
               ring_got, ring_send, ring_recv, wo_got, wo_send, wo_recv, wo_part, mix, mix_near, mix_far, mix_send, mix_recv, wo_save):
    n, ch = rate_ref.shape
    tblk = act_ref.shape[0]
    low_n = stepw_ref.shape[0]
    r, j = pl.program_id(0), pl.program_id(1)
    n_dp, nb = pl.num_programs(0), pl.num_programs(1)
    m = row_at(r, n_dp)
    group = GroupSum(part, near, far, total, gs_send, gs_recv)
    ring = RingReduce(n_f, wg_part, ring_got, ring_send, ring_recv, n_f // 2)
    ring_o = RingReduce(n_f, wo_part, wo_got, wo_send, wo_recv, n_f - 1 - n_f // 2)
    pairs = PairReduce(mix, mix_near, mix_far, mix_send, mix_recv)
    now = r * nb + j
    last_step = n_dp * nb - 1
    @pl.when(j == 0)
    def _():
        carry[...] = jnp.zeros_like(carry)

    @pl.when((r == 0) & (j == 0))
    def _():
        greet_neighbours(n_f, True)
        ring.start()
        dl_ref[...] = jnp.zeros_like(dl_ref)
        sums_ref[...] = jnp.zeros_like(sums_ref)
        stepg_ref[...] = jnp.zeros_like(stepg_ref)

    for e in range(1, ring.events):

        @pl.when(now == min(4 * e, 15))
        def _(e=e):
            ring.event(e)

    tile = 256
    parts = ch // tile
    save = pltpu.make_async_copy(wo_part, wo_out, wo_save)

    @pl.when(now < parts)
    def _():
        cs = wo_part.shape[1]
        cols = pl.ds(pl.multiple_of(now * tile, tile), tile)
        grad = lax.dot_general(
            gated_ref[:, cols], dy_ref[...], (((0,), (0,)), ((), ())), preferred_element_type=F32
        ).astype(BF16)
        for i in range(tile // cs):
            wo_part[now * (tile // cs) + i] = grad[i * cs : (i + 1) * cs]

    @pl.when(now == parts - 1)
    def _():
        save.start()

    @pl.when(now == 6)
    def _():
        ring_o.start()

    @pl.when(now == 13)
    def _():
        ring_o.event(1)

    @pl.when((now >= parts) & (now < parts + n_dp))
    def _():
        row_len = mix.shape[1]
        at = pl.ds(pl.multiple_of((now - parts) * row_len, row_len), row_len)
        mix[now - parts] = jnp.dot(gated_ref[at, :], wo_ref[...], preferred_element_type=F32).astype(BF16)

    @pl.when(now == 8)
    def _():
        pairs.start()

    @pl.when(now == 10)
    def _():
        pairs.middle()

    ones = jnp.where(own_token(n), 1.0, 0.0).astype(BF16)
    nt = (((1,), (1,)), ((), ()))
    row = lax.broadcasted_iota(jnp.int32, (TB * n, n), 0)
    col = lax.broadcasted_iota(jnp.int32, (TB * n, n), 1)
    fold = jnp.where(lax.rem(row, n) == col, 1.0, 0.0)
    since, _ = segment_span(lens_ref, m, (nb - 1 - j) * tblk, tblk)
    big_s[...] = jnp.where(since == 0, RESET, 0.0)
    bw_s[...] = block_rows(dbl_ref[:, low_n : low_n + n], n)

    flat = turned(dbl_ref[:, low_n + n : low_n + 2 * n])
    for i in range(tblk // TB):
        ct_s[i] = flat[:, i * TB : (i + 1) * TB]

    def lane_sum(value):
        total_ = value[:, :128]
        for at in range(128, value.shape[1], 128):
            total_ = total_ + value[:, at : at + 128]
        return total_

    def gathered(sums):
        spread = jnp.sum(sums, axis=1, keepdims=True) * fold
        high = spread.astype(BF16)
        rest = (spread - high.astype(F32)).astype(BF16)
        return jnp.dot(ones, high, preferred_element_type=F32) + jnp.dot(ones, rest, preferred_element_type=F32)

    for i in reversed(range(tblk // TB)):
        base = i * TB
        d_s, u_s, g_s, h_s, b_s, c_s = (v.at[i % 2] for v in (d_all, u_all, g_all, h_all, b_all, c_all))
        dl = delta_ref[base : base + TB, :]
        ac = act_ref[base : base + TB, :].astype(F32)
        d_s[...] = dl + big_s[base : base + TB, :]
        u_s[...] = dl * ac
        ct = ct_s[i]
        for lo in range(0, ch, lanes):
            cs = pl.ds(lo, lanes)
            rate = rate_ref[:, cs]
            flow = carry[:, cs]
            acc = dl_ref[:, cs]
            here = s_ref[(base + TB - 1) * n : (base + TB) * n, cs].astype(F32)
            for t in reversed(range(TB)):
                dr = d_s[t : t + 1, cs]
                dec = jnp.exp2(dr * rate)
                gy = gy_ref[base + t : base + t + 1, cs]
                g = ct[:, t : t + 1] * gy + flow
                flow = dec * g
                if base + t > 0:
                    prev = s_ref[(base + t - 1) * n : (base + t) * n, cs].astype(F32)
                else:
                    prev = sp_ref[:, cs].astype(F32)
                h = flow * prev
                acc = acc + h * dr
                at = slice(t * n, (t + 1) * n)
                b_now = lane_sum(g * u_s[t : t + 1, cs])
                c_now = lane_sum(here * gy)
                if lo:
                    b_now = b_now + b_s[at, :]
                    c_now = c_now + c_s[at, :]
                b_s[at, :] = b_now
                c_s[at, :] = c_now
                here = prev
                g_s[t * n : (t + 1) * n, cs] = g.astype(BF16)
                h_s[t * n : (t + 1) * n, cs] = (h * rate).astype(BF16)
            carry[:, cs] = flow
            dl_ref[:, cs] = acc
        gb = g_s[...]
        gy = gy_ref[base : base + TB, :]
        du = jnp.dot(bw_s[base : base + TB, :], gb, preferred_element_type=F32)
        hr = jnp.dot(ones, h_s[...], preferred_element_type=F32)
        dd = hr * (1.0 / LOG2E) + du * ac
        pg_ref[base : base + TB, :] = (dd * jax.nn.sigmoid(pre_ref[base : base + TB, :])).astype(BF16)
        da_ref[base : base + TB, :] = du * dl + skip_ref[...] * gy
        at = pl.ds(pl.multiple_of((nb - 1 - j) * tblk + base, TB), TB)
        part[m, at, low_n : low_n + n] = gathered(b_s[...])
        part[m, at, low_n + n : low_n + 2 * n] = gathered(c_s[...])

    pg = pg_ref[...]
    part[m, pl.ds(pl.multiple_of((nb - 1 - j) * tblk, tblk), tblk), :low_n] = lax.dot_general(
        pg, stepw_ref[...], nt, preferred_element_type=F32
    )
    stepg_ref[...] += lax.dot_general(
        dbl_ref[:, :low_n].astype(BF16), pg, (((0,), (0,)), ((), ())), preferred_element_type=F32
    )
    sums_ref[0:1, :] += jnp.sum(pg.astype(F32), axis=0, keepdims=True)
    sums_ref[1:2, :] += jnp.sum(gy_ref[...] * act_ref[...].astype(F32), axis=0, keepdims=True)

    @pl.when(j == nb - 1)
    def _():
        group.row_done(r)

    @pl.when((j == nb - 1) & (r == n_dp - 1))
    def _():
        ring.finish(wg_own)
        group.finish()
        dbl_grad_ref[...] = total[...]
        pairs.finish(mixed_own)
        ring_o.stop(2, wo_half)
        save.wait()


def scan_backward(lens, dbl, delta, pre, act, gy, stepw, rate2, skip, states, wg_part, gated, dy_all, wo, n_f, row_len,
                  tblk=64, lanes=512):
    t, ch = delta.shape
    n = rate2.shape[0]
    nb = row_len // tblk
    n_dp = t // row_len
    wide = dbl.shape[1]
    width = wo.shape[1]
    cs = ch // n_f
    spot = lambda r, j: row_at(r, n_dp) * nb + nb - 1 - j
    at = lambda r, j: (spot(r, j), 0)
    zero = lambda r, j: (0, 0)
    entry = lambda r, j: (jnp.maximum(spot(r, j) * tblk - 1, 0), 0)
    return pl.pallas_call(
        functools.partial(bwd_kernel, min(lanes, ch), n_f),
        grid=(n_dp, nb),
        in_specs=[
            pl.BlockSpec(memory_space=pltpu.SMEM),
            pl.BlockSpec((tblk, wide), at),
            pl.BlockSpec((tblk, ch), at),
            pl.BlockSpec((tblk, ch), at),
            pl.BlockSpec((tblk, ch), at),
            pl.BlockSpec((tblk, ch), at),
            pl.BlockSpec(stepw.shape, zero),
            pl.BlockSpec((n, ch), zero),
            pl.BlockSpec((1, ch), zero),
            pl.BlockSpec((tblk * n, ch), at),
            pl.BlockSpec((n, ch), entry),
            pl.BlockSpec(memory_space=pltpu.VMEM),
            pl.BlockSpec(memory_space=pltpu.VMEM),
            pl.BlockSpec(memory_space=pltpu.VMEM),
            pl.BlockSpec(memory_space=pltpu.VMEM),
        ],
        out_specs=[
            pl.BlockSpec((tblk, ch), at),
            pl.BlockSpec((tblk, ch), at),
            pl.BlockSpec((n_dp, row_len, wide), lambda r, j: (0, 0, 0)),
            pl.BlockSpec((n, ch), zero),
            pl.BlockSpec((8, ch), zero),
            pl.BlockSpec(stepw.shape, zero),
            pl.BlockSpec(wg_part.shape[1:], zero),
            pl.BlockSpec(memory_space=pl.ANY),
            pl.BlockSpec((2, cs, width), lambda r, j: (0, 0, 0)),
            pl.BlockSpec((row_len, width), zero),
        ],
        out_shape=[
            jax.ShapeDtypeStruct((t, ch), BF16),
            jax.ShapeDtypeStruct((t, ch), F32),
            jax.ShapeDtypeStruct((n_dp, row_len, wide), F32),
            jax.ShapeDtypeStruct((n, ch), F32),
            jax.ShapeDtypeStruct((8, ch), F32),
            jax.ShapeDtypeStruct(stepw.shape, F32),
            jax.ShapeDtypeStruct(wg_part.shape[1:], BF16),
            jax.ShapeDtypeStruct((n_f, cs, width), BF16),
            jax.ShapeDtypeStruct((2, cs, width), BF16),
            jax.ShapeDtypeStruct((row_len, width), BF16),
        ],
        scratch_shapes=[
            pltpu.VMEM((n, ch), F32),
            pltpu.VMEM((tblk, 1), F32),
            pltpu.VMEM((tblk, TB * n), BF16),
            pltpu.VMEM((tblk // TB, n, TB), F32),
            pltpu.VMEM((2, TB, ch), F32),
            pltpu.VMEM((2, TB, ch), F32),
            pltpu.VMEM((2, TB * n, ch), BF16),
            pltpu.VMEM((2, TB * n, ch), BF16),
            pltpu.VMEM((2, TB * n, 128), F32),
            pltpu.VMEM((2, TB * n, 128), F32),
        ]
        + GroupSum.scratch(row_len, wide)
        + RingReduce.scratch(n_f, wg_part.shape[1:])
        + RingReduce.scratch(n_f, (cs, width), BF16, 2)
        + [pltpu.VMEM((n_f, cs, width), BF16), pltpu.VMEM((n_dp, row_len, width), BF16)]
        + PairReduce.scratch((row_len, width))
        + [pltpu.SemaphoreType.DMA],
        compiler_params=pltpu.CompilerParams(
            collective_id=3, has_side_effects=True, vmem_limit_bytes=60 * 2**20
        ),
        cost_estimate=pl.CostEstimate(flops=t * n * ch * 80, bytes_accessed=t * ch * 60, transcendentals=t * n * ch),
    )(lens, dbl, delta, pre, act, gy, stepw, rate2, skip, states, states, wg_part, gated, dy_all, wo)


class Return:
    def __init__(self, count, n_f, buf, out, local, send, recv):
        self.count, self.n_f, self.buf, self.out = count, n_f, buf, out
        self.local, self.send, self.recv = local, send, recv
        self.me = lax.axis_index("dp") * n_f + lax.axis_index("fsdp")

    def fill(self, pick, values):
        count, pair = self.buf.shape[:2]

        def piece(j, _):
            cols = pl.ds(pl.multiple_of(j * 256, 256), 256)
            moved = jnp.dot(pick, values[:, cols].astype(BF16), preferred_element_type=F32)
            self.buf[:, :, cols] = moved.astype(BF16).reshape(count, pair, 256)
            return 0

        lax.fori_loop(0, values.shape[1] // 256, piece, 0)

    def start(self):
        def one(p, _):
            pltpu.make_async_remote_copy(
                src_ref=self.buf.at[p],
                dst_ref=self.out.at[p],
                send_sem=self.send,
                recv_sem=self.recv,
                device_id=mesh_at(lax.rem(self.me + self.count - p, self.count), self.n_f),
                device_id_type=pl.DeviceIdType.MESH,
            ).start()
            return 0

        pltpu.make_async_copy(self.buf.at[0], self.out.at[0], self.local).start()
        lax.fori_loop(1, self.count, one, 0)

    def finish(self):
        pltpu.make_async_copy(self.buf.at[0], self.out.at[0], self.local).wait()
        rest = pl.ds(1, self.count - 1)
        for sem in (self.recv, self.send):
            pltpu.make_async_copy(self.buf.at[rest], self.out.at[rest], sem).wait()


def leave_kernel(n_f, half, lens_ref, da_ref, conv_ref, xin_ref, act_ref, dblg_ref, sel_ref, taps_ref,
                 sums_ref, dsum_ref, rate_ref, stepg_ref, normed_ref, wx_ref, wg_ref, gg_ref,
                 wo_part, wo_half, wg_own, x_own, dy_own, mixed_own, gain_ref, tags_ref, ride_ref,
                 mix_back, dx_back, gin_all, go_all, small_all,
                 ig_s, wx_s, ng_s, small_s, pick_s, ret_mix, ret_dx, change_s,
                 wo_got, wo_send, wo_recv, wx_got, wx_send, wx_recv, sm_got, sm_send, sm_recv,
                 ng_near, ng_far, ng_send, ng_recv, wo_own, wx_own, sm_own, local, sh_send, sh_recv, ret_sem):
    g = pl.program_id(0)
    steps = pl.num_programs(0)
    n_dp, tok, wide = dblg_ref.shape
    count = n_dp * n_f
    width = x_own.shape[1]
    ch = ig_s.shape[1]
    piece = 256
    n_taps = taps_ref.shape[0]
    down = n_f // 2
    ring_o = RingReduce(n_f, wo_part, wo_got, wo_send, wo_recv, n_f - 1 - down)
    ring_x = RingReduce(n_f, wx_s, wx_got, wx_send, wx_recv, down)
    ring_s = RingReduce(n_f, small_s, sm_got, sm_send, sm_recv, down)
    pairs = [
        PairReduce(ng_s.at[h], ng_near.at[h], ng_far.at[h], ng_send.at[h], ng_recv.at[h]) for h in (0, 1)
    ]
    blocks = width // piece
    turn = half + blocks
    shares = [
        PairShare(mine, out, local.at[i], sh_send.at[i], sh_recv.at[i])
        for i, (mine, out) in enumerate(
            [
                (wg_own, lambda d: gin_all.at[d, :, pl.ds(ch, ch)]),
                (wo_own, lambda d: go_all.at[d]),
                (wx_own, lambda d: gin_all.at[d, :, pl.ds(0, ch)]),
                (sm_own, lambda d: lane_block(small_all, d, sm_own.shape[1])),
            ]
        )
    ]
    ret_m = Return(count, n_f, ret_mix, mix_back, local.at[4], ret_sem.at[0], ret_sem.at[1])
    ret_x = Return(count, n_f, ret_dx, dx_back, local.at[5], ret_sem.at[2], ret_sem.at[3])
    tn = (((0,), (0,)), ((), ()))
    nt = (((1,), (1,)), ((), ()))

    @pl.when(g == 0)
    def _():
        me = lax.axis_index("dp") * n_f + lax.axis_index("fsdp")
        barrier = pltpu.get_barrier_semaphore()

        def greet(p, _):
            pl.semaphore_signal(
                barrier, inc=1, device_id=mesh_at(lax.rem(me + p, count), n_f), device_id_type=pl.DeviceIdType.MESH
            )
            return 0

        lax.fori_loop(1, count, greet, 0)
        pl.semaphore_wait(barrier, count - 1)
        ring_o.resume(2, wo_half)
        shares[0].start()
        spots = jnp.concatenate([tags_ref[...]] * (tok // 128), axis=1)
        lane = lax.broadcasted_iota(jnp.int32, (tok, tok), 1).astype(F32)
        pick_s[...] = jnp.where(spots == lane, 1.0, 0.0).astype(BF16)
        ret_m.fill(pick_s[...], mixed_own)
        ret_mix[:, :, width:] = jnp.broadcast_to(ride_ref[...], (tok, 128)).astype(BF16).reshape(
            count, tok // count, 128
        )
        ret_m.start()

    for e in range(3, ring_o.events):

        @pl.when(g == min(turn + e - 2, steps - 2))
        def _(e=e):
            ring_o.event(e)

    @pl.when(g == turn)
    def _():
        ring_x.start()
        ring_s.start()

    @pl.when(g == turn + blocks // 2)
    def _():
        pairs[0].start()

    @pl.when(g == steps - 2)
    def _():
        pairs[0].middle()
        ring_s.event(1)
        ring_x.event(1)

    @pl.when(g < half)
    def _():
        cols = pl.ds(pl.multiple_of(g * piece, piece), piece)
        zero = jnp.zeros((1, piece), F32)
        misc = [zero] * (n_taps + 1)
        sel_grad = jnp.zeros((wide, piece), F32)
        for m in range(n_dp):
            at = slice(m * tok, (m + 1) * tok)
            low = dblg_ref[m].astype(BF16)
            since, left = segment_span(lens_ref, m, 0, tok)
            act_grad = da_ref[at, :] + jnp.dot(low, sel_ref[...], preferred_element_type=F32)
            conv_grad = act_grad * silu_slope(conv_ref[at, :])
            back = taps_ref[n_taps - 1 : n_taps, :] * conv_grad
            x_in = xin_ref[at, :]
            misc[n_taps - 1] = misc[n_taps - 1] + jnp.sum(conv_grad * x_in, axis=0, keepdims=True)
            for lag in range(1, n_taps):
                tap = n_taps - 1 - lag
                later = pltpu.roll(conv_grad, tok - lag, 0) * (left >= lag).astype(F32)
                back = back + taps_ref[tap : tap + 1, :] * later
                misc[tap] = misc[tap] + jnp.sum(later * x_in, axis=0, keepdims=True)
            ig_s[at, cols] = back.astype(BF16)
            misc[n_taps] = misc[n_taps] + jnp.sum(conv_grad, axis=0, keepdims=True)
            sel_grad = sel_grad + lax.dot_general(low, act_ref[at, :], tn, preferred_element_type=F32)
        rows = jnp.concatenate(
            [
                sel_grad,
                stepg_ref[...],
                dsum_ref[...] * rate_ref[...],
                jnp.concatenate(misc + [sums_ref[0:2, :], zero], axis=0),
                jnp.zeros((small_s.shape[1] - wide - stepg_ref.shape[0] - rate_ref.shape[0] - 8, piece), F32),
            ],
            axis=0,
        )
        cs = small_s.shape[2]
        for i in range(piece // cs):
            small_s[g * (piece // cs) + i] = rows[:, i * cs : (i + 1) * cs]

    @pl.when((g >= half) & (g < turn))
    def _():
        block = g - half
        dcols = wx_s.shape[1]
        grad = lax.dot_general(normed_ref[...], ig_s[...], tn, preferred_element_type=F32).astype(BF16)
        for i in range(piece // dcols):
            wx_s[block * (piece // dcols) + i] = grad[i * dcols : (i + 1) * dcols]

    @pl.when(g >= turn)
    def _():
        grad = lax.dot_general(ig_s[...], wx_ref[...], nt, preferred_element_type=F32)
        grad = grad + lax.dot_general(gg_ref[...], wg_ref[...], nt, preferred_element_type=F32)
        grad = grad.astype(BF16).reshape(n_dp, tok, piece)
        for h in (0, 1):

            @pl.when((g - turn) // (blocks // 2) == h)
            def _(h=h):
                at = (g - turn - h * (blocks // 2)) * piece
                ng_s[h, :, :, pl.ds(pl.multiple_of(at, piece), piece)] = grad

    @pl.when(g == steps - 1)
    def _():
        pairs[1].start()
        shares[0].relay()
        pairs[1].middle()
        ring_o.finish(wo_own, 2)
        shares[1].start()
        ring_s.event(2)
        ring_x.event(2)
        for h in (0, 1):
            pairs[h].finish(change_s.at[:, pl.ds(h * (width // 2), width // 2)])

        def rows(i, _):
            at = pl.ds(pl.multiple_of(i * 16, 16), 16)
            v = x_own[at, :].astype(F32)
            rstd = lax.rsqrt(jnp.mean(v * v, axis=1, keepdims=True) + EPS)
            hat = v * rstd
            grad = change_s[at, :] * gain_ref[...]
            grad = rstd * (grad - hat * jnp.mean(grad * hat, axis=1, keepdims=True))
            change_s[at, :] = dy_own[at, :].astype(F32) + grad
            return 0

        lax.fori_loop(0, tok // 16, rows, 0)
        for e in range(3, ring_x.events):
            ring_s.event(e)
            ring_x.event(e)
        ret_x.fill(pick_s[...], change_s)
        ret_x.start()
        shares[1].relay()
        ring_s.finish(sm_own)
        shares[3].start()
        ring_x.finish(wx_own)
        shares[2].start()
        shares[3].relay()
        shares[2].relay()
        for share in shares:
            share.finish()
        ret_m.finish()
        ret_x.finish()


def leave(lens, da, conv, x_in, act, dbl_grad, sel, taps, sums, decay_sum, rate, stepg, normed, wx, wg, gate_grad,
          wo_part, wo_half, wg_own, x_own, dy_own, mixed_own, gain, tags, ride, n_f):
    n_dp, tok, wide = dbl_grad.shape
    group, ch = act.shape
    width = x_own.shape[1]
    count = n_dp * n_f
    pair = tok // count
    piece = 256
    half = ch // piece
    dcols = width // n_f
    cs = ch // n_f
    n = rate.shape[0]
    tall = -(-(wide + stepg.shape[0] + n + 8) // 64) * 64
    blocks = width // piece
    early = lambda g: (0, jnp.minimum(g, half - 1))
    late = lambda g: (0, jnp.clip(g - half, 0, blocks - 1))
    late_rows = lambda g: (jnp.maximum(g - half - blocks, 0), 0)
    any_ = pl.BlockSpec(memory_space=pl.ANY)
    vmem = pl.BlockSpec(memory_space=pltpu.VMEM)
    block = lambda rows: pl.BlockSpec((rows, piece), early)
    shaped = jax.ShapeDtypeStruct
    return pl.pallas_call(
        functools.partial(leave_kernel, n_f, half),
        grid=(half + 2 * blocks,),
        in_specs=[
            pl.BlockSpec(memory_space=pltpu.SMEM),
            block(group),
            block(group),
            block(group),
            block(group),
            vmem,
            block(wide),
            block(taps.shape[0]),
            block(8),
            block(n),
            block(n),
            block(stepg.shape[0]),
            pl.BlockSpec((group, piece), late),
            pl.BlockSpec((piece, ch), late_rows),
            pl.BlockSpec((piece, ch), late_rows),
        ]
        + [vmem] * 10,
        out_specs=[any_] * 5,
        out_shape=[
            shaped((count, pair, width + 128), BF16),
            shaped((count, pair, width), BF16),
            shaped((n_dp, dcols, 2 * ch), BF16),
            shaped((n_dp, cs, width), BF16),
            shaped(side_by_side(n_dp, tall, cs), F32),
        ],
        scratch_shapes=[
            pltpu.VMEM((group, ch), BF16),
            pltpu.VMEM((n_f, dcols, ch), BF16),
            pltpu.VMEM((2, n_dp, tok, width // 2), BF16),
            pltpu.VMEM((n_f, tall, cs), F32),
            pltpu.VMEM((tok, tok), BF16),
            pltpu.VMEM((count, pair, width + 128), BF16),
            pltpu.VMEM((count, pair, width), BF16),
            pltpu.VMEM((tok, width), F32),
        ]
        + RingReduce.scratch(n_f, (cs, width))
        + RingReduce.scratch(n_f, (dcols, ch))
        + RingReduce.scratch(n_f, (tall, cs), F32)
        + [
            pltpu.VMEM((2, 2, tok, width // 2), BF16),
            pltpu.VMEM((2, tok, width // 2), BF16),
            pltpu.SemaphoreType.DMA((2, 3)),
            pltpu.SemaphoreType.DMA((2, 3)),
            pltpu.VMEM((cs, width), BF16),
            pltpu.VMEM((dcols, ch), BF16),
            pltpu.VMEM((tall, cs), F32),
            pltpu.SemaphoreType.DMA((6,)),
            pltpu.SemaphoreType.DMA((4, 3)),
            pltpu.SemaphoreType.DMA((4, 3)),
            pltpu.SemaphoreType.DMA((4,)),
        ],
        compiler_params=pltpu.CompilerParams(
            collective_id=4, has_side_effects=True, vmem_limit_bytes=62 * 2**20
        ),
        cost_estimate=pl.CostEstimate(flops=2 * 10**10, bytes_accessed=6 * 10**7, transcendentals=10**6),
    )(lens, da, conv, x_in, act, dbl_grad, sel, taps, sums, decay_sum, rate, stepg, normed, wx, wg, gate_grad,
      wo_part, wo_half, wg_own, x_own, dy_own, mixed_own, gain, tags, ride)


def masks_of(count):
    return [1 << b for b in range(count.bit_length() - 1)]


def mesh_at(index, n_f):
    return (index // n_f, lax.rem(index, n_f))


def ring_index(p, n_f):
    if n_f % 2:
        return p
    return jnp.where(p < n_f // 2, 2 * p, 2 * (n_f - 1 - p) + 1)


def ring_place(f, n_f):
    if n_f % 2:
        return f
    return jnp.where(lax.rem(f, 2) == 0, f // 2, n_f - 1 - f // 2)


def pack_kernel(cs, me_d, starts, w_ref, small_refs, gain_ref, blocks):
    small, halves = blocks[0], blocks[1:]
    lanes = pl.ds(pl.multiple_of(me_d * cs, 128), cs)
    sel, step, decay, rest = small_refs[0], small_refs[1], small_refs[2], small_refs[3:]
    at = 0
    for ref in (sel, step, decay):
        small[at : at + ref.shape[0], :] = ref[:, lanes]
        at += ref.shape[0]
    rows = [ref[:, lanes].astype(F32) for ref in rest] + [gain_ref[...].astype(F32)]
    filler = small.shape[0] - at - sum(r.shape[0] for r in rows)
    small[at:, :] = jnp.concatenate(rows + [jnp.zeros((filler, cs), F32)], axis=0).astype(BF16)
    for o, out in enumerate(halves):
        for j, start in enumerate(starts[o]):
            out[:, j * cs : (j + 1) * cs] = w_ref[:, pl.ds(pl.multiple_of(start + me_d * cs, 128), cs)]


def gather_kernel(n_dp, n_f, downs, segs, pack, x_ref, dy_ref, dest_row_ref, dest_ref, lens_ref, *refs):
    streams = len(downs)
    given = len(pack[1]) if pack else streams
    x_all, lens_all, x_own_ref, dy_own_ref, tag_ref, rank_ref, ride_ref = refs[given : given + 7]
    outs = refs[given + 7 : given + 7 + streams]
    (send_x, send_dy, got_x, got_dy, x_own, dy_own, deal_sem, loc_sem, pair_send, pair_recv, ring_send, ring_recv) = (
        refs[given + 7 + streams : given + 19 + streams]
    )
    blocks = refs[given + 19 + streams :] if pack else refs[:streams]
    count = n_dp * n_f
    me_d = lax.axis_index("dp")
    me_f = lax.axis_index("fsdp")
    me = me_d * n_f + me_f
    q = ring_place(me_f, n_f)
    below = ring_index(lax.rem(q + n_f - 1, n_f), n_f)
    above = ring_index(lax.rem(q + 1, n_f), n_f)

    barrier = pltpu.get_barrier_semaphore()

    def greet(p, _):
        pl.semaphore_signal(
            barrier, inc=1, device_id=mesh_at(lax.rem(me + p, count), n_f), device_id_type=pl.DeviceIdType.MESH
        )
        return 0

    lax.fori_loop(1, count, greet, 0)
    if pack:
        pack_kernel(pack[0], me_d, pack[2], refs[0], refs[1 : given - 1], refs[given - 1], blocks)

    def place_of(s, index):
        return lane_block(outs[s], index, blocks[s].shape[1]) if s == 0 else outs[s].at[index]

    locals_ = [
        pltpu.make_async_copy(blocks[s], place_of(s, me_f), loc_sem.at[s]) for s in range(streams)
    ]
    for c in locals_:
        c.start()
    pl.semaphore_wait(barrier, count - 1)

    def deal(a):
        src, dst = ((send_x, got_x), (send_dy, got_dy))[a]

        def one(p, _):
            pltpu.make_async_remote_copy(
                src_ref=src.at[p],
                dst_ref=dst.at[p],
                send_sem=deal_sem.at[a, 0],
                recv_sem=deal_sem.at[a, 1],
                device_id=mesh_at(lax.rem(me + p, count), n_f),
                device_id_type=pl.DeviceIdType.MESH,
            ).start()
            return 0

        lax.fori_loop(1, count, one, 0)
        dst[0] = src[0]

    def dealt(a, way):
        src, dst = ((send_x, got_x), (send_dy, got_dy))[a]
        rest = pl.ds(1, count - 1)
        pltpu.make_async_copy(src.at[rest], dst.at[rest], deal_sem.at[a, way]).wait()

    def hop(s, h, up):
        k = lax.rem(q + (n_f - h if up else h), n_f)
        index = ring_index(k, n_f)
        src = blocks[s] if h == 0 else place_of(s, index)
        return pltpu.make_async_remote_copy(
            src_ref=src,
            dst_ref=place_of(s, index),
            send_sem=ring_send.at[s, int(up), h],
            recv_sem=ring_recv.at[s, int(up), h],
            device_id=(me_d, above if up else below),
            device_id_type=pl.DeviceIdType.MESH,
        )

    hops = [[downs[s], n_f - 1 - downs[s]] for s in range(streams)]
    for s in range(streams):
        for up in (0, 1):
            if hops[s][up]:
                hop(s, 0, up).start()
    tok, width = x_own.shape
    pair = got_x.shape[1]

    dest_row = dest_row_ref[...]
    abs_row = jnp.floor((dest_row + 0.5) * (1.0 / tok))
    in_row = dest_row - abs_row * tok
    rel_row = abs_row - me.astype(F32)
    rel_row = jnp.where(rel_row < 0.0, rel_row + count, rel_row)
    rank = jnp.sum((dest_ref[...] < dest_row).astype(F32), axis=0, keepdims=True)
    goal = rel_row * pair + rank - abs_row * pair
    rank_ref[...] = jnp.broadcast_to(goal, rank_ref.shape)
    chosen = lax.broadcasted_iota(jnp.int32, (tok, tok), 0).astype(F32) == goal
    spot = jnp.sum(jnp.where(chosen, in_row, 0.0), axis=1, keepdims=True)
    send_x[:, :, width:] = jnp.broadcast_to(spot, (tok, 128)).astype(BF16).reshape(count, pair, 128)
    pick = jnp.where(chosen, 1.0, 0.0).astype(BF16)

    def sort(values, out):
        def part(j, _):
            cols = pl.ds(pl.multiple_of(j * 256, 256), 256)
            moved = jnp.dot(pick, values[:, cols], preferred_element_type=F32)
            out[:, :, cols] = moved.astype(BF16).reshape(count, pair, 256)
            return 0

        lax.fori_loop(0, width // 256, part, 0)

    sort(x_ref, send_x)
    deal(0)
    sort(dy_ref, send_dy)
    deal(1)

    def advance(h):
        for s in range(streams):
            for up in (0, 1):
                if h < hops[s][up]:
                    hop(s, h - 1, up).wait_recv()
                    hop(s, h, up).start()

    advance(1)
    dealt(0, 1)
    tag = got_x[:, :, width : width + 128].astype(F32).reshape(tok, 128)
    spots = jnp.concatenate([tag] * (tok // 128), axis=1)
    lane = lax.broadcasted_iota(jnp.int32, (tok, tok), 1).astype(F32)
    settle = jnp.where(spots == lane, 1.0, 0.0).astype(BF16)
    tn = (((0,), (0,)), ((), ()))
    tag_ref[...] = tag

    def place(values, out):
        def part(j, _):
            cols = pl.ds(pl.multiple_of(j * 256, 256), 256)
            block = values[:, :, cols].reshape(tok, 256)
            out[:, cols] = lax.dot_general(settle, block, tn, preferred_element_type=F32).astype(BF16)
            return 0

        lax.fori_loop(0, width // 256, part, 0)

    masks = list(reversed(masks_of(n_dp)))

    def partner(mask):
        return me_d + mask - 2 * mask * lax.rem(me_d // mask, 2)

    def share(a, m, mask):
        out = (x_all, lens_all)[a]
        own_block = (x_own, lens_ref)[a]
        return pltpu.make_async_remote_copy(
            src_ref=own_block if m == 0 else out.at[m],
            dst_ref=out.at[m | mask],
            send_sem=pair_send.at[a, m | mask],
            recv_sem=pair_recv.at[a, m | mask],
            device_id=(partner(mask), me_f),
            device_id_type=pl.DeviceIdType.MESH,
        )

    copies = []

    def keep(src, dst):
        c = pltpu.make_async_copy(src, dst, loc_sem.at[streams + len(copies)])
        c.start()
        copies.append(c)

    place(got_x, x_own)
    for a in (0, 1):
        for mask in masks:
            share(a, 0, mask).start()
    keep(lens_ref, lens_all.at[0])
    keep(x_own, x_all.at[0])
    keep(x_own, x_own_ref)

    lane = lax.broadcasted_iota(jnp.int32, (1, 128), 1)
    limit = jnp.sum(jnp.where(lane < segs - 1, lens_ref[0:1, :], 0).astype(F32), axis=1, keepdims=True)

    def squares(i, total_):
        v = x_own[pl.ds(pl.multiple_of(i * 32, 32), 32), :].astype(F32)
        t = (lax.broadcasted_iota(jnp.int32, (32, 1), 0) + i * 32).astype(F32)
        each = jnp.sum(v * v, axis=1, keepdims=True)
        return total_ + jnp.sum(jnp.where(t < limit, each, 0.0), axis=0, keepdims=True)

    ride = jnp.zeros((1, 128), F32)
    for j, value in enumerate((lax.fori_loop(0, tok // 32, squares, jnp.zeros((1, 1), F32)), limit)):
        high = value.astype(BF16).astype(F32)
        ride = ride + jnp.where(lane == 2 * j, high, 0.0) + jnp.where(lane == 2 * j + 1, value - high, 0.0)
    ride_ref[...] = jnp.broadcast_to(ride, ride_ref.shape)

    def relay(a):
        held = [0]
        for step, mask in enumerate(masks):
            for m in held:
                if m:
                    share(a, m, mask).start()
            for m in held:
                share(a, m, mask).wait_recv()
            held = held + [m | mask for m in held]

    most = max(max(h) for h in hops)
    for h in range(2, most):
        advance(h)
        if h == 2:
            dealt(1, 1)
            place(got_dy, dy_own)
            keep(dy_own, dy_own_ref)
    if most <= 2:
        dealt(1, 1)
        place(got_dy, dy_own)
        keep(dy_own, dy_own_ref)
    relay(0)
    relay(1)
    for s in range(streams):
        for up in (0, 1):
            if hops[s][up]:
                hop(s, hops[s][up] - 1, up).wait_recv()
    for s in range(streams):
        for up in (0, 1):
            for h in range(hops[s][up]):
                hop(s, h, up).wait_send()
    for a in (0, 1):
        held = [0]
        for mask in masks:
            for m in held:
                share(a, m, mask).wait_send()
            held = held + [m | mask for m in held]
    for c in locals_ + copies:
        c.wait()
    dealt(0, 0)
    dealt(1, 0)


def gather_all(x, dy, dest, lens, segs, blocks, pack, downs, n_dp, n_f):
    streams = len(blocks)
    tok, width = x.shape
    count = n_dp * n_f
    sent_x = (count, tok // count, width + 128)
    sent_dy = (count, tok // count, width)
    hops = max(max(d, n_f - 1 - d) for d in downs)
    any_ = pl.BlockSpec(memory_space=pl.ANY)
    vmem = pl.BlockSpec(memory_space=pltpu.VMEM)
    row = jax.ShapeDtypeStruct((tok, width), BF16)
    rows = jax.ShapeDtypeStruct((n_dp, tok, width), BF16)
    return pl.pallas_call(
        functools.partial(gather_kernel, n_dp, n_f, downs, segs, pack and (pack[0], [None] * len(pack[1]), pack[2])),
        in_specs=[vmem] * 5 + ([vmem] * len(pack[1]) if pack else [any_] * streams),
        out_specs=[any_] * 4 + [vmem] * 3 + [any_] * streams,
        out_shape=[
            rows,
            jax.ShapeDtypeStruct((n_dp,) + lens.shape, lens.dtype),
            row,
            row,
            jax.ShapeDtypeStruct((tok, 128), F32),
            jax.ShapeDtypeStruct((8, tok), F32),
            jax.ShapeDtypeStruct((8, 128), F32),
        ]
        + [jax.ShapeDtypeStruct(side_by_side(n_f, *blocks[0].shape), BF16)]
        + [jax.ShapeDtypeStruct((n_f,) + b.shape, b.dtype) for b in blocks[1:]],
        scratch_shapes=[
            pltpu.VMEM(sent_x, BF16),
            pltpu.VMEM(sent_dy, BF16),
            pltpu.VMEM(sent_x, BF16),
            pltpu.VMEM(sent_dy, BF16),
            pltpu.VMEM((tok, width), BF16),
            pltpu.VMEM((tok, width), BF16),
            pltpu.SemaphoreType.DMA((2, 2)),
            pltpu.SemaphoreType.DMA((streams + 4,)),
            pltpu.SemaphoreType.DMA((2, n_dp)),
            pltpu.SemaphoreType.DMA((2, n_dp)),
            pltpu.SemaphoreType.DMA((streams, 2, hops)),
            pltpu.SemaphoreType.DMA((streams, 2, hops)),
        ]
        + ([pltpu.VMEM(b.shape, BF16) for b in blocks] if pack else []),
        compiler_params=pltpu.CompilerParams(
            collective_id=0, has_side_effects=True, vmem_limit_bytes=40 * 2**20
        ),
        cost_estimate=pl.CostEstimate(flops=10**10, bytes_accessed=2 * 10**8, transcendentals=0),
    )(x, dy, dest[None, :], dest[:, None], lens, *(pack[1] if pack else blocks))


def spread_kernel(cs, x_ref, w_ref, go_ref, small_ref, out_ref, sum_ref, go_out, *small_outs):
    total = jnp.zeros(sum_ref.shape, F32)
    n_dp = x_ref.shape[0]
    for f in range(x_ref.shape[2] // cs):
        for i in range(n_dp):
            part = x_ref[i, :, f * cs : (f + 1) * cs].astype(F32)
            cols = slice((f * n_dp + i) * cs, (f * n_dp + i + 1) * cs)
            out_ref[:, cols] = part
            product = part * w_ref[:, cols].astype(F32)
            for j in range(0, cs, 128):
                total = total + product[:, j : j + 128]
    go_out[...] = go_ref[...].astype(F32)

    @pl.when(pl.program_id(0) == 0)
    def _():
        sum_ref[...] = jnp.zeros_like(sum_ref)
        at = 0
        for out in small_outs:
            out[...] = small_ref[at : at + out.shape[0], :]
            at += out.shape[0]

    sum_ref[...] += total


def spread_columns(parts, w, go, small, heights, cs):
    n_dp, height, cols = parts.shape
    if cs % 128:
        out = parts.reshape(n_dp, height, cols // cs, cs).transpose(1, 2, 0, 3).reshape(height, n_dp * cols).astype(F32)
        cuts = [small[sum(heights[:i]) : sum(heights[: i + 1])] for i in range(len(heights))]
        return out, jnp.sum(out * w.astype(F32), axis=1), go.astype(F32), cuts
    wide = 2 * cs
    steps = cols // wide
    once = lambda f: (0, 0)
    go_block = (go.shape[0] // steps, go.shape[1])
    shaped = jax.ShapeDtypeStruct
    out, sums, go, *cuts = pl.pallas_call(
        functools.partial(spread_kernel, cs),
        grid=(steps,),
        in_specs=[
            pl.BlockSpec((n_dp, height, wide), lambda f: (0, 0, f)),
            pl.BlockSpec((height, n_dp * wide), lambda f: (0, f)),
            pl.BlockSpec(go_block, lambda f: (f, 0)),
            pl.BlockSpec(small.shape, once),
        ],
        out_specs=[
            pl.BlockSpec((height, n_dp * wide), lambda f: (0, f)),
            pl.BlockSpec((height, 128), once),
            pl.BlockSpec(go_block, lambda f: (f, 0)),
        ]
        + [pl.BlockSpec((h, small.shape[1]), once) for h in heights],
        out_shape=[shaped((height, n_dp * cols), F32), shaped((height, 128), F32), shaped(go.shape, F32)]
        + [shaped((h, small.shape[1]), F32) for h in heights],
        compiler_params=pltpu.CompilerParams(vmem_limit_bytes=32 * 2**20),
        cost_estimate=pl.CostEstimate(flops=4 * height * cols * n_dp, bytes_accessed=8 * height * cols * n_dp, transcendentals=0),
    )(parts, w, go, small)
    return out, jnp.sum(sums, axis=1), go, cuts


def per_device(
    tokens,
    cotangent,
    destination,
    lengths,
    norm_gain,
    in_weight,
    conv_weight,
    conv_bias,
    select_weight,
    step_weight,
    step_bias,
    decay_log,
    skip_gain,
    out_weight,
):
    n_dp = lax.axis_size("dp")
    n_f = lax.axis_size("fsdp")
    rows = n_dp * n_f
    tok = tokens.shape[0]
    width = tokens.shape[1]
    pair = tok // rows
    inner = conv_bias.shape[0] * n_f
    cs = conv_bias.shape[0] // n_dp
    ch = cs * n_f
    taps = conv_weight.shape[0]
    n = decay_log.shape[0]
    rank_of = step_weight.shape[0]
    dcols = width // n_f
    group = n_dp * tok
    both = ("dp", "fsdp")
    me_d = lax.axis_index("dp")
    me_f = lax.axis_index("fsdp")
    flat_dot = lambda a, b: jnp.dot(a, b, preferred_element_type=F32)
    nt_dot = lambda a, b: lax.dot_general(a, b, (((1,), (1,)), ((), ())), preferred_element_type=F32)
    tn_dot = lambda a, b: lax.dot_general(a, b, (((0,), (0,)), ((), ())), preferred_element_type=F32)

    segs = lengths.shape[1]
    lens_tile = jnp.pad(lengths, ((0, 7), (0, 128 - segs)))
    slots = jnp.arange(tok, dtype=jnp.int32)

    flat = lambda shard: shard.reshape(-1, n_dp * cs)
    smalls = [
        flat(v) for v in (select_weight, step_weight, decay_log, conv_weight, conv_bias, step_bias, skip_gain)
    ]
    gain_rows = dcols // cs
    gain_block = norm_gain.reshape(gain_rows, cs)
    used = sum(v.shape[0] for v in smalls) + gain_rows
    tall = used + -used % 16
    starts = [[h * inner + f * n_dp * cs for f in range(n_f)] for h in (0, 1)]
    if cs % 128:
        mine = lambda value, at: lax.dynamic_slice_in_dim(value, at + me_d * cs, cs, 1)
        blocks = [
            jnp.concatenate(
                [mine(v, 0) for v in smalls] + [gain_block, jnp.zeros((tall - used, cs), BF16)], axis=0
            )
        ] + [jnp.concatenate([mine(in_weight, at) for at in half], axis=1) for half in starts]
        pack = None
    else:
        blocks = [jax.ShapeDtypeStruct((tall, cs), BF16)] + [jax.ShapeDtypeStruct((dcols, ch), BF16)] * 2
        pack = (cs, [in_weight] + smalls + [gain_block], starts)
    x_all, lens_all, x_own, dy_own, x_tags, ranks, ride, small_all, wx, wg = gather_all(
        tokens, cotangent, destination.astype(F32), lens_tile, segs, blocks, pack,
        [n_f // 2, n_f // 2, n_f - 1 - n_f // 2], n_dp, n_f,
    )
    x_all = x_all.reshape(group, width)
    lens = lens_all[:, 0, :segs]
    from_send = (ranks[0].astype(jnp.int32)[:, None] == slots[None, :]).astype(BF16)
    wx = wx.reshape(width, ch)
    wg = wg.reshape(width, ch)
    small = joined(small_all)
    at = select_weight.shape[0]
    sel = small[:at]
    stepw = small[at : at + rank_of]
    dlog = small[at + rank_of : at + rank_of + n]
    misc = small[at + rank_of + n :]
    conv_w, conv_b, step_b, skip = misc[:taps], misc[taps : taps + 1], misc[taps + 1 : taps + 2], misc[taps + 2 : taps + 3]
    gain = misc[taps + 3 : taps + 3 + gain_rows]
    gain = gain.reshape(gain_rows, n_f, cs).transpose(1, 0, 2).reshape(width).astype(F32)
    conv_w = conv_w.astype(F32)
    skip = skip.astype(F32)
    rate = -jnp.exp(dlog.astype(F32))

    normed, x_in, conv, act, gate, dbl, wo_next = enter(
        lens, x_all, gain[None], wx, wg, conv_w, conv_b.astype(F32), sel, out_weight, n_f
    )
    dbl = dbl.reshape(group, -1)
    rate2 = rate * LOG2E
    scan_out, states, delta, pre, wo, dy_all = scan_forward(
        lens, dbl, act, stepw, step_b.astype(F32), rate2, skip, out_weight, wo_next, dy_own, n_f, tok
    )
    dy_all = dy_all.reshape(group, width)
    wo = wo.reshape(ch, width)
    gate_silu = jax.nn.silu(gate)
    gated = (scan_out * gate_silu).astype(BF16)

    gated_grad = nt_dot(dy_all, wo)
    scan_grad = gated_grad * gate_silu
    gate_grad = (gated_grad * scan_out * silu_slope(gate)).astype(BF16)
    wg_grad = tn_dot(normed, gate_grad).astype(BF16)
    pre_grad, act_grad, dbl_grad, decay_sum, sums, step_grad, wg_own, wo_grad, wo_half, mixed = scan_backward(
        lens, dbl, delta, pre, act, scan_grad, stepw, rate2, skip, states,
        wg_grad.reshape(n_f, dcols, ch), gated, dy_all, wo, n_f, tok,
    )
    mix_back, dx_back, gin_all, go_all, small_full = leave(
        lens, act_grad, conv, x_in, act, dbl_grad, sel, conv_w, sums, decay_sum, rate, step_grad, normed, wx, wg,
        gate_grad, wo_grad, wo_half, wg_own, x_own, dy_own, mixed, gain[None], x_tags, ride[:1], n_f,
    )

    grad_in_weight, gain_sum, grad_out_weight, cuts = spread_columns(
        gin_all, in_weight, go_all.reshape(n_dp * cs, width), joined(small_full),
        [select_weight.shape[0], rank_of, n, 8], cs,
    )
    grad_select, grad_step, grad_decay, misc = cuts
    grad_norm_gain = gain_sum / norm_gain.astype(F32)

    back = mix_back.reshape(tok, width + 128)
    totals = jnp.sum(mix_back[:, 0, width : width + 4].astype(F32), axis=0)
    input_rms = jnp.sqrt((totals[0] + totals[1]) / ((totals[2] + totals[3]) * width))
    mixer_output = flat_dot(from_send, back[:, :width])
    layer_output = (tokens.astype(F32) + mixer_output).astype(BF16)
    mixer_output = mixer_output.astype(BF16)
    input_grad = flat_dot(from_send, dx_back.reshape(tok, width)).astype(BF16)
    return (
        layer_output,
        mixer_output,
        input_grad,
        input_rms,
        grad_norm_gain,
        grad_in_weight,
        misc[:taps],
        misc[taps],
        grad_select,
        grad_step,
        misc[taps + 1],
        grad_decay,
        misc[taps + 2],
        grad_out_weight,
    )


def solution(mesh):
    return jax.shard_map(
        per_device,
        mesh=mesh,
        in_specs=(
            P(("dp", "fsdp"), None),
            P(("dp", "fsdp"), None),
            P(("dp", "fsdp")),
            P(("dp", "fsdp"), None),
            P("fsdp"),
            P("fsdp", None),
            P(None, "fsdp"),
            P("fsdp"),
            P(None, "fsdp"),
            P(None, "fsdp"),
            P("fsdp"),
            P(None, "fsdp"),
            P("fsdp"),
            P("fsdp", None),
        ),
        out_specs=(
            P(("dp", "fsdp"), None),
            P(("dp", "fsdp"), None),
            P(("dp", "fsdp"), None),
            P(),
            P("fsdp"),
            P("fsdp", None),
            P(None, "fsdp"),
            P("fsdp"),
            P(None, "fsdp"),
            P(None, "fsdp"),
            P("fsdp"),
            P(None, "fsdp"),
            P("fsdp"),
            P("fsdp", None),
        ),
        check_vma=False,
    )
```

```python
import functools
import math

import jax
import jax.numpy as jnp
from jax import lax
from jax.experimental import pallas as pl
from jax.experimental.pallas import tpu as pltpu
from jax.sharding import PartitionSpec as P

EPS = 1e-05
TB = 16
LOG2E = math.log2(math.e)
RESET = 1.0e4
BF16 = jnp.bfloat16
F32 = jnp.float32


def silu_slope(value):
    sigma = jax.nn.sigmoid(value)
    return sigma * (1.0 + value * (1.0 - sigma))


def row_at(g, n_dp):
    return lax.rem(2 * g + 1, n_dp + 1)


def flip(d, mask):
    return d + mask - 2 * mask * lax.rem(d // mask, 2)


class GroupSum:
    def __init__(self, part, near, far, total, send, recv):
        self.part, self.near, self.far, self.total = part, near, far, total
        me_d, me_f = lax.axis_index("dp"), lax.axis_index("fsdp")
        plan = [
            (part.at[1], near.at[0], 1),
            (part.at[3], near.at[1], 1),
            (part.at[0], far.at[1], 2),
            (part.at[2], far.at[0], 2),
            (total.at[0], total.at[1], 1),
            (total.at[2], total.at[3], 1),
        ]
        self.copies = [
            pltpu.make_async_remote_copy(
                src_ref=src,
                dst_ref=dst,
                send_sem=send.at[i],
                recv_sem=recv.at[i],
                device_id=(flip(me_d, mask), me_f),
                device_id_type=pl.DeviceIdType.MESH,
            )
            for i, (src, dst, mask) in enumerate(plan)
        ]

    def row_done(self, g):
        for j in (0, 1):

            @pl.when(g == j)
            def _(j=j):
                self.copies[j].start()

            @pl.when(g == j + 2)
            def _(j=j):
                self.copies[j].wait_recv()
                self.part[2 * j] = self.part[2 * j] + self.near[j]
                self.copies[j + 2].start()

    def first(self):
        for j in (0, 1):
            self.copies[j].start()

    def second(self):
        for j in (0, 1):
            self.copies[j].wait_recv()
            self.part[2 * j] = self.part[2 * j] + self.near[j]
            self.copies[j + 2].start()

    def finish(self):
        for j in (0, 1):
            self.copies[3 - j].wait_recv()
            self.total[2 * j] = self.part[2 * j] + self.far[j]
            self.copies[4 + j].start()
        for j in (0, 1):
            self.copies[4 + j].wait_recv()
        for c in self.copies:
            c.wait_send()

    @staticmethod
    def scratch(tok, wide):
        return [
            pltpu.VMEM((4, tok, wide), F32),
            pltpu.VMEM((2, tok, wide), F32),
            pltpu.VMEM((2, tok, wide), F32),
            pltpu.VMEM((4, tok, wide), F32),
            pltpu.SemaphoreType.DMA((6,)),
            pltpu.SemaphoreType.DMA((6,)),
        ]


class RingReduce:
    def __init__(self, n_f, part, got, send, recv, down):
        self.part, self.got = part, got
        q = ring_place(lax.axis_index("fsdp"), n_f)
        self.at = lambda k: ring_index(lax.rem(q + k, n_f), n_f)
        self.n_f = n_f
        self.counts = [down, n_f - 1 - down]
        self.copies = [[], []]
        for up in (0, 1):
            for h in range(min(self.counts[up], got.shape[1])):
                src = part.at[self.at(self.goal(up, 0))] if h == 0 else got.at[up, h - 1]
                self.copies[up].append(ring_copy(n_f, src, got.at[up, h], send.at[up, h], recv.at[up, h], up))
        self.events = max(self.counts)

    def goal(self, up, h):
        left = self.counts[up] - h
        return left if up else self.n_f - left

    def add(self, slot, addend):
        rows = slot.shape[0]
        step = min(rows, 64)

        def piece(i, _):
            at = pl.ds(pl.multiple_of(i * step, step), step)
            slot[at, :] = (slot[at, :].astype(F32) + addend[at, :].astype(F32)).astype(slot.dtype)
            return 0

        lax.fori_loop(0, rows // step, piece, 0)

    def start(self):
        for up in (0, 1):
            if self.copies[up]:
                self.copies[up][0].start()

    def stop(self, hops, out):
        for up in (0, 1):
            self.copies[up][hops - 1].wait_recv()
            rows_add(out.at[up], [self.got.at[up, hops - 1]])
            for c in self.copies[up][:hops]:
                c.wait_send()

    def resume(self, hops, arrived):
        for up in (0, 1):
            slot = self.got.at[up, hops - 1]
            rows_add(slot, [arrived.at[up], self.part.at[self.at(self.goal(up, hops))]])
            self.copies[up][hops].start()

    def event(self, e):
        for up in (0, 1):
            if e < self.counts[up]:
                self.copies[up][e - 1].wait_recv()
                self.add(self.got.at[up, e - 1], self.part.at[self.at(self.goal(up, e))])
                self.copies[up][e].start()

    def finish(self, out, since=0):
        last = []
        for up in (0, 1):
            if self.copies[up]:
                self.copies[up][-1].wait_recv()
                last.append(self.got.at[up, self.counts[up] - 1])
        mine = self.part.at[self.at(0)]
        rows = mine.shape[0]
        step = min(rows, 64)

        def piece(i, _):
            at = pl.ds(pl.multiple_of(i * step, step), step)
            total_ = mine[at, :].astype(F32)
            for slot in last:
                total_ = total_ + slot[at, :].astype(F32)
            out[at, :] = total_.astype(out.dtype)
            return 0

        lax.fori_loop(0, rows // step, piece, 0)
        for up in (0, 1):
            for c in self.copies[up][since:]:
                c.wait_send()

    @staticmethod
    def scratch(n_f, block, dtype=BF16, slots=0):
        return [
            pltpu.VMEM((2, slots or n_f // 2) + block, dtype),
            pltpu.SemaphoreType.DMA((2, n_f // 2)),
            pltpu.SemaphoreType.DMA((2, n_f // 2)),
        ]


class PairReduce:
    def __init__(self, part, near, far, send, recv):
        self.part, self.near, self.far = part, near, far
        me_d, me_f = lax.axis_index("dp"), lax.axis_index("fsdp")
        plan = [
            (part.at[1], near.at[0], 1),
            (part.at[3], near.at[1], 1),
            (part.at[2], far, 2),
        ]
        self.copies = [
            pltpu.make_async_remote_copy(
                src_ref=src,
                dst_ref=dst,
                send_sem=send.at[i],
                recv_sem=recv.at[i],
                device_id=(flip(me_d, mask), me_f),
                device_id_type=pl.DeviceIdType.MESH,
            )
            for i, (src, dst, mask) in enumerate(plan)
        ]

    def start(self):
        for c in self.copies[:2]:
            c.start()

    def middle(self):
        self.copies[1].wait_recv()
        rows_add(self.part.at[2], [self.part.at[2], self.near.at[1]])
        self.copies[2].start()
        self.copies[0].wait_recv()

    def finish(self, out):
        self.copies[2].wait_recv()
        rows_add(out, [self.part.at[0], self.near.at[0], self.far])
        for c in self.copies:
            c.wait_send()

    @staticmethod
    def scratch(block, dtype=BF16):
        return [
            pltpu.VMEM((2,) + block, dtype),
            pltpu.VMEM(block, dtype),
            pltpu.SemaphoreType.DMA((3,)),
            pltpu.SemaphoreType.DMA((3,)),
        ]


def rows_add(out, terms, step=32):
    def piece(i, _):
        at = pl.ds(pl.multiple_of(i * step, step), step)
        total_ = terms[0][at, :].astype(F32)
        for t in terms[1:]:
            total_ = total_ + t[at, :].astype(F32)
        out[at, :] = total_.astype(out.dtype)
        return 0

    lax.fori_loop(0, out.shape[0] // step, piece, 0)


class PairShare:
    def __init__(self, mine, out, local, send, recv, relative=False):
        me_d, me_f = lax.axis_index("dp"), lax.axis_index("fsdp")
        far = 2 if relative else flip(me_d, 2)
        here, at_near, at_far, relayed = (0, 1, 2, 3) if relative else (me_d, me_d, me_d, far)
        self.local = pltpu.make_async_copy(mine, out(here), local)
        self.copies = [
            pltpu.make_async_remote_copy(
                src_ref=src,
                dst_ref=dst,
                send_sem=send.at[i],
                recv_sem=recv.at[i],
                device_id=(flip(me_d, mask), me_f),
                device_id_type=pl.DeviceIdType.MESH,
            )
            for i, (src, dst, mask) in enumerate(
                [(mine, out(at_near), 1), (mine, out(at_far), 2), (out(far), out(relayed), 1)]
            )
        ]

    def start(self):
        self.copies[1].start()
        self.copies[0].start()
        self.local.start()

    def relay(self):
        self.copies[1].wait_recv()
        self.copies[2].start()

    def finish(self):
        self.copies[0].wait_recv()
        self.copies[2].wait_recv()
        for c in self.copies:
            c.wait_send()
        self.local.wait()


def side_by_side(count, height, wide):
    return (count, height, wide) if wide % 128 else (height, count * wide)


def lane_block(ref, index, wide):
    if wide % 128:
        return ref.at[index]
    return ref.at[:, pl.ds(pl.multiple_of(index * wide, 128), wide)]


def joined(value):
    if value.ndim == 2:
        return value
    return value.transpose(1, 0, 2).reshape(value.shape[1], -1)


def greet_neighbours(n_f, ring):
    me_d, me_f = lax.axis_index("dp"), lax.axis_index("fsdp")
    barrier = pltpu.get_barrier_semaphore()
    others = [(flip(me_d, 1), me_f), (flip(me_d, 2), me_f)]
    if ring:
        q = ring_place(me_f, n_f)
        others.append((me_d, ring_index(lax.rem(q + n_f - 1, n_f), n_f)))
        others.append((me_d, ring_index(lax.rem(q + 1, n_f), n_f)))
    for other in others:
        pl.semaphore_signal(barrier, inc=1, device_id=other, device_id_type=pl.DeviceIdType.MESH)
    pl.semaphore_wait(barrier, len(others))


def ring_copy(n_f, src, dst, send, recv, up):
    me_d, me_f = lax.axis_index("dp"), lax.axis_index("fsdp")
    q = ring_place(me_f, n_f)
    to = ring_index(lax.rem(q + (1 if up else n_f - 1), n_f), n_f)
    return pltpu.make_async_remote_copy(
        src_ref=src,
        dst_ref=dst,
        send_sem=send,
        recv_sem=recv,
        device_id=(me_d, to),
        device_id_type=pl.DeviceIdType.MESH,
    )


def segment_span(lens_ref, m, first, rows):
    t = lax.broadcasted_iota(jnp.int32, (rows, 1), 0) + first
    begin = jnp.zeros((rows, 1), jnp.int32)
    end = jnp.zeros((rows, 1), jnp.int32)
    total = jnp.int32(0)
    for j in range(lens_ref.shape[1]):
        after = total + lens_ref[m, j]
        inside = t >= total
        begin = jnp.where(inside, total, begin)
        end = jnp.where(inside, after, end)
        total = after
    return t - begin, end - 1 - t


def enter_kernel(n_f, half, lens_ref, x_ref, gain_ref, wx_ref, wg_ref, taps_ref, bias_ref, sel_ref, wo_ref,
                 normed_ref, xin_ref, conv_ref, act_ref, gate_ref, dbl_ref, next_ref,
                 part, near, far, total, gs_send, gs_recv, hop_send, hop_recv):
    g = pl.program_id(0)
    n_dp, tok = part.shape[:2]
    rows, width = x_ref.shape
    hops = [ring_copy(n_f, wo_ref, next_ref.at[up, 0], hop_send.at[up, 0], hop_recv.at[up, 0], up) for up in (0, 1)]
    hops2 = [
        ring_copy(n_f, next_ref.at[up, 0], next_ref.at[up, 1], hop_send.at[up, 1], hop_recv.at[up, 1], up)
        for up in (0, 1)
    ]
    group = GroupSum(part, near, far, total, gs_send, gs_recv)

    @pl.when(g == 0)
    def _():
        greet_neighbours(n_f, True)
        for c in hops:
            c.start()
        part[...] = jnp.zeros_like(part)

        def norm(i, _):
            for j in range(4):
                at = pl.ds(pl.multiple_of(i * 128 + j * 32, 32), 32)
                v = x_ref[at, :].astype(F32)
                rstd = lax.rsqrt(jnp.mean(v * v, axis=1, keepdims=True) + EPS)
                normed_ref[at, :] = (v * rstd * gain_ref[...]).astype(BF16)
            return 0

        lax.fori_loop(0, rows // 128, norm, 0)

    @pl.when(g == half)
    def _():
        for a, b in zip(hops, hops2):
            a.wait_recv()
            b.start()

    @pl.when(g < half)
    def _():
        n_taps = taps_ref.shape[0]
        xin_ref[...] = jnp.dot(normed_ref[...], wx_ref[...], preferred_element_type=F32)
        for m in range(n_dp):
            at = slice(m * tok, (m + 1) * tok)
            v = xin_ref[at, :]
            since, _ = segment_span(lens_ref, m, 0, tok)
            conv = bias_ref[...] + taps_ref[n_taps - 1 : n_taps, :] * v
            for lag in range(1, n_taps):
                keep = (since >= lag).astype(F32)
                conv = conv + taps_ref[n_taps - 1 - lag : n_taps - lag, :] * (pltpu.roll(v, lag, 0) * keep)
            conv_ref[at, :] = conv
            act = jax.nn.silu(conv).astype(BF16)
            act_ref[at, :] = act
            part[m] += lax.dot_general(act, sel_ref[...], (((1,), (1,)), ((), ())), preferred_element_type=F32)

    @pl.when(g == half - 1)
    def _():
        group.first()

    @pl.when(g >= half)
    def _():
        gate_ref[...] = jnp.dot(normed_ref[...], wg_ref[...], preferred_element_type=F32)

    @pl.when(g == half)
    def _():
        group.second()

    @pl.when(g == 2 * half - 1)
    def _():
        group.finish()
        dbl_ref[...] = total[...]
        for a, b in zip(hops, hops2):
            a.wait_send()
            b.wait()


def enter(lens, x_all, gain, wx, wg, taps, bias, sel, wo, n_f):
    n_dp = lens.shape[0]
    rows, width = x_all.shape
    tok = rows // n_dp
    ch = wx.shape[1]
    wide = sel.shape[0]
    piece = 256
    half = ch // piece
    whole = lambda g: (0, 0)
    early = lambda g: (0, jnp.minimum(g, half - 1))
    late = lambda g: (0, jnp.maximum(g - half, 0))
    once = pl.Buffered(1)
    any_ = pl.BlockSpec(memory_space=pl.ANY)
    shaped = lambda d, t: jax.ShapeDtypeStruct((rows, d), t)
    return pl.pallas_call(
        functools.partial(enter_kernel, n_f, half),
        grid=(2 * half,),
        in_specs=[
            pl.BlockSpec(memory_space=pltpu.SMEM),
            pl.BlockSpec((rows, width), whole, pipeline_mode=once),
            pl.BlockSpec((1, width), whole),
            pl.BlockSpec((width, piece), early),
            pl.BlockSpec((width, piece), late),
            pl.BlockSpec((taps.shape[0], piece), early),
            pl.BlockSpec((1, piece), early),
            pl.BlockSpec((wide, piece), early),
            any_,
        ],
        out_specs=[
            pl.BlockSpec((rows, width), whole),
            pl.BlockSpec((rows, piece), early),
            pl.BlockSpec((rows, piece), early),
            pl.BlockSpec((rows, piece), early),
            pl.BlockSpec((rows, piece), late),
            pl.BlockSpec((n_dp, tok, wide), lambda g: (0, 0, 0)),
            any_,
        ],
        out_shape=[
            shaped(width, BF16),
            shaped(ch, F32),
            shaped(ch, F32),
            shaped(ch, BF16),
            shaped(ch, F32),
            jax.ShapeDtypeStruct((n_dp, tok, wide), F32),
            jax.ShapeDtypeStruct((2, 2) + wo.shape, BF16),
        ],
        scratch_shapes=GroupSum.scratch(tok, wide)
        + [pltpu.SemaphoreType.DMA((2, 2)), pltpu.SemaphoreType.DMA((2, 2))],
        compiler_params=pltpu.CompilerParams(
            collective_id=1, has_side_effects=True, vmem_limit_bytes=48 * 2**20
        ),
        cost_estimate=pl.CostEstimate(flops=10**10, bytes_accessed=4 * 10**7, transcendentals=10**6),
    )(lens, x_all, gain, wx, wg, taps, bias, sel, wo)


def fold_matrix(n):
    i = lax.broadcasted_iota(jnp.int32, (n, TB * n), 0)
    j = lax.broadcasted_iota(jnp.int32, (n, TB * n), 1)
    return jnp.where(lax.rem(j, n) == i, 1.0, 0.0)


def own_token(n):
    i = lax.broadcasted_iota(jnp.int32, (TB, TB * n), 0)
    j = lax.broadcasted_iota(jnp.int32, (TB, TB * n), 1)
    return i == j // n


def block_rows(m, n):
    spread = jnp.dot(m.astype(BF16), fold_matrix(n).astype(BF16), preferred_element_type=F32)
    i = lax.broadcasted_iota(jnp.int32, spread.shape, 0)
    j = lax.broadcasted_iota(jnp.int32, spread.shape, 1)
    return jnp.where(lax.rem(i, TB) == j // n, spread, 0.0).astype(BF16)


def turned(m):
    n = m.shape[1]
    i = lax.broadcasted_iota(jnp.int32, (n, n), 0)
    j = lax.broadcasted_iota(jnp.int32, (n, n), 1)
    eye = jnp.where(i == j, 1.0, 0.0)
    return lax.dot_general(
        eye, m, (((1,), (1,)), ((), ())), preferred_element_type=F32, precision=lax.Precision.HIGHEST
    )


def softplus(v):
    return jnp.maximum(v, 0.0) + jnp.log1p(jnp.exp(-jnp.abs(v)))


class RingGather:
    def __init__(self, n_f, mine, near, out, local, send, recv):
        q = ring_place(lax.axis_index("fsdp"), n_f)
        at = lambda k: ring_index(lax.rem(q + k, n_f), n_f)
        count = [n_f // 2, n_f - 1 - n_f // 2]
        known = near.shape[1]
        self.locals = [pltpu.make_async_copy(mine, out.at[at(0)], local.at[0])]
        self.hops = [[], []]
        for up in (0, 1):
            for j in range(known):
                index = at(n_f - 1 - j if up else 1 + j)
                self.locals.append(pltpu.make_async_copy(near.at[up, j], out.at[index], local.at[1 + known * up + j]))
            for h in range(known, count[up]):
                index = at(n_f - h if up else h)
                src = near.at[up, known - 1] if h == known else out.at[index]
                self.hops[up].append(
                    ring_copy(n_f, src, out.at[index], send.at[up, h], recv.at[up, h], up)
                )
        self.events = max(len(h) for h in self.hops)

    def start(self):
        for c in self.locals:
            c.start()
        for up in (0, 1):
            if self.hops[up]:
                self.hops[up][0].start()

    def event(self, e):
        for up in (0, 1):
            if e < len(self.hops[up]):
                self.hops[up][e - 1].wait_recv()
                self.hops[up][e].start()

    def finish(self):
        for up in (0, 1):
            if self.hops[up]:
                self.hops[up][-1].wait_recv()
            for c in self.hops[up]:
                c.wait_send()
        for c in self.locals:
            c.wait()


def fwd_kernel(lanes, n_f, lens_ref, dbl_ref, act_ref, stepw_ref, stepb_ref, rate_ref, skip_ref, wo_ref, next_ref, dy_ref,
               y_ref, s_ref, delta_ref, pre_ref, wo_all, dy_all, carry, big_s, cw_s, bt_s, d_s, u_s, sc, local, hop_send, hop_recv, sh_send, sh_recv):
    n, ch = rate_ref.shape
    tblk = act_ref.shape[0]
    low_n = stepw_ref.shape[0]
    steps = pl.num_programs(0) * pl.num_programs(1)
    now = pl.program_id(0) * pl.num_programs(1) + pl.program_id(1)
    ring = RingGather(n_f, wo_ref, next_ref, wo_all, local, hop_send, hop_recv)
    share = PairShare(dy_ref, lambda m: dy_all.at[m], local.at[5], sh_send, sh_recv, True)

    @pl.when(now == 0)
    def _():
        greet_neighbours(n_f, True)
        ring.start()
        share.start()

    @pl.when(now == 13)
    def _():
        share.relay()

    for e in range(1, ring.events):

        @pl.when(now == min(7 * e, 15))
        def _(e=e):
            ring.event(e)

    @pl.when(pl.program_id(1) == 0)
    def _():
        carry[...] = jnp.zeros_like(carry)

    pre = jnp.dot(dbl_ref[:, :low_n].astype(BF16), stepw_ref[...], preferred_element_type=F32) + stepb_ref[...]
    pre_ref[...] = pre
    delta_ref[...] = softplus(pre)
    since, _ = segment_span(lens_ref, pl.program_id(0), pl.program_id(1) * tblk, tblk)
    big_s[...] = jnp.where(since == 0, RESET, 0.0)
    cw_s[...] = block_rows(dbl_ref[:, low_n + n : low_n + 2 * n], n)
    flat = turned(dbl_ref[:, low_n : low_n + n])
    for i in range(tblk // TB):
        bt_s[i] = flat[:, i * TB : (i + 1) * TB]

    def chunk(i, _):
        base = pl.multiple_of(i * TB, TB)
        dl = delta_ref[pl.ds(base, TB), :]
        ac = act_ref[pl.ds(base, TB), :].astype(F32)
        d_s[...] = dl + big_s[pl.ds(base, TB), :]
        u_s[...] = dl * ac
        bt = bt_s[i]
        for lo in range(0, ch, lanes):
            cs = pl.ds(lo, lanes)
            rate = rate_ref[:, cs]
            s = carry[:, cs]
            for t in range(TB):
                dec = jnp.exp2(d_s[t : t + 1, cs] * rate)
                s = dec * s + bt[:, t : t + 1] * u_s[t : t + 1, cs]
                sc[t * n : (t + 1) * n, cs] = s.astype(BF16)
            carry[:, cs] = s
        states = sc[...]
        y = jnp.dot(cw_s[pl.ds(base, TB), :], states, preferred_element_type=F32)
        y_ref[pl.ds(base, TB), :] = y + skip_ref[...] * ac
        s_ref[pl.ds(pl.multiple_of(base * n, TB * n), TB * n), :] = states
        return 0

    lax.fori_loop(0, tblk // TB, chunk, 0)

    @pl.when(now == steps - 1)
    def _():
        ring.finish()
        share.finish()


def scan_forward(lens, dbl, act, stepw, stepb, rate2, skip, wo, wo_next, dy_own, n_f, row_len, tblk=64, lanes=512):
    t, ch = act.shape
    n = rate2.shape[0]
    nb = row_len // tblk
    at = lambda r, j: (r * nb + j, 0)
    zero = lambda r, j: (0, 0)
    any_ = pl.BlockSpec(memory_space=pl.ANY)
    wide = jax.ShapeDtypeStruct((t, ch), F32)
    return pl.pallas_call(
        functools.partial(fwd_kernel, min(lanes, ch), n_f),
        grid=(t // row_len, nb),
        in_specs=[
            pl.BlockSpec(memory_space=pltpu.SMEM),
            pl.BlockSpec((tblk, dbl.shape[1]), at),
            pl.BlockSpec((tblk, ch), at),
            pl.BlockSpec(stepw.shape, zero),
            pl.BlockSpec((1, ch), zero),
            pl.BlockSpec((n, ch), zero),
            pl.BlockSpec((1, ch), zero),
            any_,
            any_,
            any_,
        ],
        out_specs=[
            pl.BlockSpec((tblk, ch), at),
            pl.BlockSpec((tblk * n, ch), at),
            pl.BlockSpec((tblk, ch), at),
            pl.BlockSpec((tblk, ch), at),
            any_,
            any_,
        ],
        out_shape=[
            wide,
            jax.ShapeDtypeStruct((t * n, ch), BF16),
            wide,
            wide,
            jax.ShapeDtypeStruct((n_f,) + wo_next.shape[2:], BF16),
            jax.ShapeDtypeStruct((t // row_len,) + dy_own.shape, BF16),
        ],
        scratch_shapes=[
            pltpu.VMEM((n, ch), F32),
            pltpu.VMEM((tblk, 1), F32),
            pltpu.VMEM((tblk, TB * n), BF16),
            pltpu.VMEM((tblk // TB, n, TB), F32),
            pltpu.VMEM((TB, ch), F32),
            pltpu.VMEM((TB, ch), F32),
            pltpu.VMEM((TB * n, ch), BF16),
            pltpu.SemaphoreType.DMA((6,)),
            pltpu.SemaphoreType.DMA((2, n_f)),
            pltpu.SemaphoreType.DMA((2, n_f)),
            pltpu.SemaphoreType.DMA((3,)),
            pltpu.SemaphoreType.DMA((3,)),
        ],
        compiler_params=pltpu.CompilerParams(
            collective_id=2, has_side_effects=True, vmem_limit_bytes=32 * 2**20
        ),
        cost_estimate=pl.CostEstimate(flops=t * n * ch * 40, bytes_accessed=t * ch * 52, transcendentals=t * n * ch),
    )(lens, dbl, act, stepw, stepb, rate2, skip, wo, wo_next, dy_own)


def bwd_kernel(lanes, n_f, lens_ref, dbl_ref, delta_ref, pre_ref, act_ref, gy_ref, stepw_ref, rate_ref, skip_ref,
               s_ref, sp_ref, wg_part, gated_ref, dy_ref, wo_ref,
               pg_ref, da_ref, dbl_grad_ref, dl_ref, sums_ref, stepg_ref, wg_own, wo_out, wo_half, mixed_own,
               carry, big_s, bw_s, ct_s, d_all, u_all, g_all, h_all, b_all, c_all, part, near, far, total, gs_send, gs_recv,
               ring_got, ring_send, ring_recv, wo_got, wo_send, wo_recv, wo_part, mix, mix_near, mix_far, mix_send, mix_recv, wo_save):
    n, ch = rate_ref.shape
    tblk = act_ref.shape[0]
    low_n = stepw_ref.shape[0]
    r, j = pl.program_id(0), pl.program_id(1)
    n_dp, nb = pl.num_programs(0), pl.num_programs(1)
    m = row_at(r, n_dp)
    group = GroupSum(part, near, far, total, gs_send, gs_recv)
    ring = RingReduce(n_f, wg_part, ring_got, ring_send, ring_recv, n_f // 2)
    ring_o = RingReduce(n_f, wo_part, wo_got, wo_send, wo_recv, n_f - 1 - n_f // 2)
    pairs = PairReduce(mix, mix_near, mix_far, mix_send, mix_recv)
    now = r * nb + j
    last_step = n_dp * nb - 1
    @pl.when(j == 0)
    def _():
        carry[...] = jnp.zeros_like(carry)

    @pl.when((r == 0) & (j == 0))
    def _():
        greet_neighbours(n_f, True)
        ring.start()
        dl_ref[...] = jnp.zeros_like(dl_ref)
        sums_ref[...] = jnp.zeros_like(sums_ref)
        stepg_ref[...] = jnp.zeros_like(stepg_ref)

    for e in range(1, ring.events):

        @pl.when(now == min(4 * e, 15))
        def _(e=e):
            ring.event(e)

    tile = 256
    parts = ch // tile
    save = pltpu.make_async_copy(wo_part, wo_out, wo_save)

    @pl.when(now < parts)
    def _():
        cs = wo_part.shape[1]
        cols = pl.ds(pl.multiple_of(now * tile, tile), tile)
        grad = lax.dot_general(
            gated_ref[:, cols], dy_ref[...], (((0,), (0,)), ((), ())), preferred_element_type=F32
        ).astype(BF16)
        for i in range(tile // cs):
            wo_part[now * (tile // cs) + i] = grad[i * cs : (i + 1) * cs]

    @pl.when(now == parts - 1)
    def _():
        save.start()

    @pl.when(now == 6)
    def _():
        ring_o.start()

    @pl.when(now == 13)
    def _():
        ring_o.event(1)

    @pl.when((now >= parts) & (now < parts + n_dp))
    def _():
        row_len = mix.shape[1]
        at = pl.ds(pl.multiple_of((now - parts) * row_len, row_len), row_len)
        mix[now - parts] = jnp.dot(gated_ref[at, :], wo_ref[...], preferred_element_type=F32).astype(BF16)

    @pl.when(now == 8)
    def _():
        pairs.start()

    @pl.when(now == 10)
    def _():
        pairs.middle()

    ones = jnp.where(own_token(n), 1.0, 0.0).astype(BF16)
    nt = (((1,), (1,)), ((), ()))
    row = lax.broadcasted_iota(jnp.int32, (TB * n, n), 0)
    col = lax.broadcasted_iota(jnp.int32, (TB * n, n), 1)
    fold = jnp.where(lax.rem(row, n) == col, 1.0, 0.0)
    since, _ = segment_span(lens_ref, m, (nb - 1 - j) * tblk, tblk)
    big_s[...] = jnp.where(since == 0, RESET, 0.0)
    bw_s[...] = block_rows(dbl_ref[:, low_n : low_n + n], n)

    flat = turned(dbl_ref[:, low_n + n : low_n + 2 * n])
    for i in range(tblk // TB):
        ct_s[i] = flat[:, i * TB : (i + 1) * TB]

    def lane_sum(value):
        total_ = value[:, :128]
        for at in range(128, value.shape[1], 128):
            total_ = total_ + value[:, at : at + 128]
        return total_

    def gathered(sums):
        spread = jnp.sum(sums, axis=1, keepdims=True) * fold
        high = spread.astype(BF16)
        rest = (spread - high.astype(F32)).astype(BF16)
        return jnp.dot(ones, high, preferred_element_type=F32) + jnp.dot(ones, rest, preferred_element_type=F32)

    for i in reversed(range(tblk // TB)):
        base = i * TB
        d_s, u_s, g_s, h_s, b_s, c_s = (v.at[i % 2] for v in (d_all, u_all, g_all, h_all, b_all, c_all))
        dl = delta_ref[base : base + TB, :]
        ac = act_ref[base : base + TB, :].astype(F32)
        d_s[...] = dl + big_s[base : base + TB, :]
        u_s[...] = dl * ac
        ct = ct_s[i]
        for lo in range(0, ch, lanes):
            cs = pl.ds(lo, lanes)
            rate = rate_ref[:, cs]
            flow = carry[:, cs]
            acc = dl_ref[:, cs]
            here = s_ref[(base + TB - 1) * n : (base + TB) * n, cs].astype(F32)
            for t in reversed(range(TB)):
                dr = d_s[t : t + 1, cs]
                dec = jnp.exp2(dr * rate)
                gy = gy_ref[base + t : base + t + 1, cs]
                g = ct[:, t : t + 1] * gy + flow
                flow = dec * g
                if base + t > 0:
                    prev = s_ref[(base + t - 1) * n : (base + t) * n, cs].astype(F32)
                else:
                    prev = sp_ref[:, cs].astype(F32)
                h = flow * prev
                acc = acc + h * dr
                at = slice(t * n, (t + 1) * n)
                b_now = lane_sum(g * u_s[t : t + 1, cs])
                c_now = lane_sum(here * gy)
                if lo:
                    b_now = b_now + b_s[at, :]
                    c_now = c_now + c_s[at, :]
                b_s[at, :] = b_now
                c_s[at, :] = c_now
                here = prev
                g_s[t * n : (t + 1) * n, cs] = g.astype(BF16)
                h_s[t * n : (t + 1) * n, cs] = (h * rate).astype(BF16)
            carry[:, cs] = flow
            dl_ref[:, cs] = acc
        gb = g_s[...]
        gy = gy_ref[base : base + TB, :]
        du = jnp.dot(bw_s[base : base + TB, :], gb, preferred_element_type=F32)
        hr = jnp.dot(ones, h_s[...], preferred_element_type=F32)
        dd = hr * (1.0 / LOG2E) + du * ac
        pg_ref[base : base + TB, :] = (dd * jax.nn.sigmoid(pre_ref[base : base + TB, :])).astype(BF16)
        da_ref[base : base + TB, :] = du * dl + skip_ref[...] * gy
        at = pl.ds(pl.multiple_of((nb - 1 - j) * tblk + base, TB), TB)
        part[m, at, low_n : low_n + n] = gathered(b_s[...])
        part[m, at, low_n + n : low_n + 2 * n] = gathered(c_s[...])

    pg = pg_ref[...]
    part[m, pl.ds(pl.multiple_of((nb - 1 - j) * tblk, tblk), tblk), :low_n] = lax.dot_general(
        pg, stepw_ref[...], nt, preferred_element_type=F32
    )
    stepg_ref[...] += lax.dot_general(
        dbl_ref[:, :low_n].astype(BF16), pg, (((0,), (0,)), ((), ())), preferred_element_type=F32
    )
    sums_ref[0:1, :] += jnp.sum(pg.astype(F32), axis=0, keepdims=True)
    sums_ref[1:2, :] += jnp.sum(gy_ref[...] * act_ref[...].astype(F32), axis=0, keepdims=True)

    @pl.when(j == nb - 1)
    def _():
        group.row_done(r)

    @pl.when((j == nb - 1) & (r == n_dp - 1))
    def _():
        ring.finish(wg_own)
        group.finish()
        dbl_grad_ref[...] = total[...]
        pairs.finish(mixed_own)
        ring_o.stop(2, wo_half)
        save.wait()


def scan_backward(lens, dbl, delta, pre, act, gy, stepw, rate2, skip, states, wg_part, gated, dy_all, wo, n_f, row_len,
                  tblk=64, lanes=512):
    t, ch = delta.shape
    n = rate2.shape[0]
    nb = row_len // tblk
    n_dp = t // row_len
    wide = dbl.shape[1]
    width = wo.shape[1]
    cs = ch // n_f
    spot = lambda r, j: row_at(r, n_dp) * nb + nb - 1 - j
    at = lambda r, j: (spot(r, j), 0)
    zero = lambda r, j: (0, 0)
    entry = lambda r, j: (jnp.maximum(spot(r, j) * tblk - 1, 0), 0)
    return pl.pallas_call(
        functools.partial(bwd_kernel, min(lanes, ch), n_f),
        grid=(n_dp, nb),
        in_specs=[
            pl.BlockSpec(memory_space=pltpu.SMEM),
            pl.BlockSpec((tblk, wide), at),
            pl.BlockSpec((tblk, ch), at),
            pl.BlockSpec((tblk, ch), at),
            pl.BlockSpec((tblk, ch), at),
            pl.BlockSpec((tblk, ch), at),
            pl.BlockSpec(stepw.shape, zero),
            pl.BlockSpec((n, ch), zero),
            pl.BlockSpec((1, ch), zero),
            pl.BlockSpec((tblk * n, ch), at),
            pl.BlockSpec((n, ch), entry),
            pl.BlockSpec(memory_space=pltpu.VMEM),
            pl.BlockSpec(memory_space=pltpu.VMEM),
            pl.BlockSpec(memory_space=pltpu.VMEM),
            pl.BlockSpec(memory_space=pltpu.VMEM),
        ],
        out_specs=[
            pl.BlockSpec((tblk, ch), at),
            pl.BlockSpec((tblk, ch), at),
            pl.BlockSpec((n_dp, row_len, wide), lambda r, j: (0, 0, 0)),
            pl.BlockSpec((n, ch), zero),
            pl.BlockSpec((8, ch), zero),
            pl.BlockSpec(stepw.shape, zero),
            pl.BlockSpec(wg_part.shape[1:], zero),
            pl.BlockSpec(memory_space=pl.ANY),
            pl.BlockSpec((2, cs, width), lambda r, j: (0, 0, 0)),
            pl.BlockSpec((row_len, width), zero),
        ],
        out_shape=[
            jax.ShapeDtypeStruct((t, ch), BF16),
            jax.ShapeDtypeStruct((t, ch), F32),
            jax.ShapeDtypeStruct((n_dp, row_len, wide), F32),
            jax.ShapeDtypeStruct((n, ch), F32),
            jax.ShapeDtypeStruct((8, ch), F32),
            jax.ShapeDtypeStruct(stepw.shape, F32),
            jax.ShapeDtypeStruct(wg_part.shape[1:], BF16),
            jax.ShapeDtypeStruct((n_f, cs, width), BF16),
            jax.ShapeDtypeStruct((2, cs, width), BF16),
            jax.ShapeDtypeStruct((row_len, width), BF16),
        ],
        scratch_shapes=[
            pltpu.VMEM((n, ch), F32),
            pltpu.VMEM((tblk, 1), F32),
            pltpu.VMEM((tblk, TB * n), BF16),
            pltpu.VMEM((tblk // TB, n, TB), F32),
            pltpu.VMEM((2, TB, ch), F32),
            pltpu.VMEM((2, TB, ch), F32),
            pltpu.VMEM((2, TB * n, ch), BF16),
            pltpu.VMEM((2, TB * n, ch), BF16),
            pltpu.VMEM((2, TB * n, 128), F32),
            pltpu.VMEM((2, TB * n, 128), F32),
        ]
        + GroupSum.scratch(row_len, wide)
        + RingReduce.scratch(n_f, wg_part.shape[1:])
        + RingReduce.scratch(n_f, (cs, width), BF16, 2)
        + [pltpu.VMEM((n_f, cs, width), BF16), pltpu.VMEM((n_dp, row_len, width), BF16)]
        + PairReduce.scratch((row_len, width))
        + [pltpu.SemaphoreType.DMA],
        compiler_params=pltpu.CompilerParams(
            collective_id=3, has_side_effects=True, vmem_limit_bytes=60 * 2**20
        ),
        cost_estimate=pl.CostEstimate(flops=t * n * ch * 80, bytes_accessed=t * ch * 60, transcendentals=t * n * ch),
    )(lens, dbl, delta, pre, act, gy, stepw, rate2, skip, states, states, wg_part, gated, dy_all, wo)


class Return:
    def __init__(self, count, n_f, buf, out, local, send, recv):
        self.count, self.n_f, self.buf, self.out = count, n_f, buf, out
        self.local, self.send, self.recv = local, send, recv
        self.me = lax.axis_index("dp") * n_f + lax.axis_index("fsdp")

    def fill(self, pick, values):
        count, pair = self.buf.shape[:2]

        def piece(j, _):
            cols = pl.ds(pl.multiple_of(j * 256, 256), 256)
            moved = jnp.dot(pick, values[:, cols].astype(BF16), preferred_element_type=F32)
            self.buf[:, :, cols] = moved.astype(BF16).reshape(count, pair, 256)
            return 0

        lax.fori_loop(0, values.shape[1] // 256, piece, 0)

    def start(self):
        def one(p, _):
            pltpu.make_async_remote_copy(
                src_ref=self.buf.at[p],
                dst_ref=self.out.at[p],
                send_sem=self.send,
                recv_sem=self.recv,
                device_id=mesh_at(lax.rem(self.me + self.count - p, self.count), self.n_f),
                device_id_type=pl.DeviceIdType.MESH,
            ).start()
            return 0

        pltpu.make_async_copy(self.buf.at[0], self.out.at[0], self.local).start()
        lax.fori_loop(1, self.count, one, 0)

    def finish(self):
        pltpu.make_async_copy(self.buf.at[0], self.out.at[0], self.local).wait()
        rest = pl.ds(1, self.count - 1)
        for sem in (self.recv, self.send):
            pltpu.make_async_copy(self.buf.at[rest], self.out.at[rest], sem).wait()


def leave_kernel(n_f, half, lens_ref, da_ref, conv_ref, xin_ref, act_ref, dblg_ref, sel_ref, taps_ref,
                 sums_ref, dsum_ref, rate_ref, stepg_ref, normed_ref, wx_ref, wg_ref, gg_ref,
                 wo_part, wo_half, wg_own, x_own, dy_own, mixed_own, gain_ref, tags_ref, ride_ref,
                 mix_back, dx_back, gin_all, go_all, small_all,
                 ig_s, wx_s, ng_s, small_s, pick_s, ret_mix, ret_dx, change_s,
                 wo_got, wo_send, wo_recv, wx_got, wx_send, wx_recv, sm_got, sm_send, sm_recv,
                 ng_near, ng_far, ng_send, ng_recv, wo_own, wx_own, sm_own, local, sh_send, sh_recv, ret_sem):
    g = pl.program_id(0)
    steps = pl.num_programs(0)
    n_dp, tok, wide = dblg_ref.shape
    count = n_dp * n_f
    width = x_own.shape[1]
    ch = ig_s.shape[1]
    piece = 256
    n_taps = taps_ref.shape[0]
    down = n_f // 2
    ring_o = RingReduce(n_f, wo_part, wo_got, wo_send, wo_recv, n_f - 1 - down)
    ring_x = RingReduce(n_f, wx_s, wx_got, wx_send, wx_recv, down)
    ring_s = RingReduce(n_f, small_s, sm_got, sm_send, sm_recv, down)
    pairs = [
        PairReduce(ng_s.at[h], ng_near.at[h], ng_far.at[h], ng_send.at[h], ng_recv.at[h]) for h in (0, 1)
    ]
    blocks = width // piece
    turn = half + blocks
    shares = [
        PairShare(mine, out, local.at[i], sh_send.at[i], sh_recv.at[i])
        for i, (mine, out) in enumerate(
            [
                (wg_own, lambda d: gin_all.at[d, :, pl.ds(ch, ch)]),
                (wo_own, lambda d: go_all.at[d]),
                (wx_own, lambda d: gin_all.at[d, :, pl.ds(0, ch)]),
                (sm_own, lambda d: lane_block(small_all, d, sm_own.shape[1])),
            ]
        )
    ]
    ret_m = Return(count, n_f, ret_mix, mix_back, local.at[4], ret_sem.at[0], ret_sem.at[1])
    ret_x = Return(count, n_f, ret_dx, dx_back, local.at[5], ret_sem.at[2], ret_sem.at[3])
    tn = (((0,), (0,)), ((), ()))
    nt = (((1,), (1,)), ((), ()))

    @pl.when(g == 0)
    def _():
        me = lax.axis_index("dp") * n_f + lax.axis_index("fsdp")
        barrier = pltpu.get_barrier_semaphore()

        def greet(p, _):
            pl.semaphore_signal(
                barrier, inc=1, device_id=mesh_at(lax.rem(me + p, count), n_f), device_id_type=pl.DeviceIdType.MESH
            )
            return 0

        lax.fori_loop(1, count, greet, 0)
        pl.semaphore_wait(barrier, count - 1)
        ring_o.resume(2, wo_half)
        shares[0].start()
        spots = jnp.concatenate([tags_ref[...]] * (tok // 128), axis=1)
        lane = lax.broadcasted_iota(jnp.int32, (tok, tok), 1).astype(F32)
        pick_s[...] = jnp.where(spots == lane, 1.0, 0.0).astype(BF16)
        ret_m.fill(pick_s[...], mixed_own)
        ret_mix[:, :, width:] = jnp.broadcast_to(ride_ref[...], (tok, 128)).astype(BF16).reshape(
            count, tok // count, 128
        )
        ret_m.start()

    for e in range(3, ring_o.events):

        @pl.when(g == min(turn + e - 2, steps - 2))
        def _(e=e):
            ring_o.event(e)

    @pl.when(g == turn)
    def _():
        ring_x.start()
        ring_s.start()

    @pl.when(g == turn + blocks // 2)
    def _():
        pairs[0].start()

    @pl.when(g == steps - 2)
    def _():
        pairs[0].middle()
        ring_s.event(1)
        ring_x.event(1)

    @pl.when(g < half)
    def _():
        cols = pl.ds(pl.multiple_of(g * piece, piece), piece)
        zero = jnp.zeros((1, piece), F32)
        misc = [zero] * (n_taps + 1)
        sel_grad = jnp.zeros((wide, piece), F32)
        for m in range(n_dp):
            at = slice(m * tok, (m + 1) * tok)
            low = dblg_ref[m].astype(BF16)
            since, left = segment_span(lens_ref, m, 0, tok)
            act_grad = da_ref[at, :] + jnp.dot(low, sel_ref[...], preferred_element_type=F32)
            conv_grad = act_grad * silu_slope(conv_ref[at, :])
            back = taps_ref[n_taps - 1 : n_taps, :] * conv_grad
            x_in = xin_ref[at, :]
            misc[n_taps - 1] = misc[n_taps - 1] + jnp.sum(conv_grad * x_in, axis=0, keepdims=True)
            for lag in range(1, n_taps):
                tap = n_taps - 1 - lag
                later = pltpu.roll(conv_grad, tok - lag, 0) * (left >= lag).astype(F32)
                back = back + taps_ref[tap : tap + 1, :] * later
                misc[tap] = misc[tap] + jnp.sum(later * x_in, axis=0, keepdims=True)
            ig_s[at, cols] = back.astype(BF16)
            misc[n_taps] = misc[n_taps] + jnp.sum(conv_grad, axis=0, keepdims=True)
            sel_grad = sel_grad + lax.dot_general(low, act_ref[at, :], tn, preferred_element_type=F32)
        rows = jnp.concatenate(
            [
                sel_grad,
                stepg_ref[...],
                dsum_ref[...] * rate_ref[...],
                jnp.concatenate(misc + [sums_ref[0:2, :], zero], axis=0),
                jnp.zeros((small_s.shape[1] - wide - stepg_ref.shape[0] - rate_ref.shape[0] - 8, piece), F32),
            ],
            axis=0,
        )
        cs = small_s.shape[2]
        for i in range(piece // cs):
            small_s[g * (piece // cs) + i] = rows[:, i * cs : (i + 1) * cs]

    @pl.when((g >= half) & (g < turn))
    def _():
        block = g - half
        dcols = wx_s.shape[1]
        grad = lax.dot_general(normed_ref[...], ig_s[...], tn, preferred_element_type=F32).astype(BF16)
        for i in range(piece // dcols):
            wx_s[block * (piece // dcols) + i] = grad[i * dcols : (i + 1) * dcols]

    @pl.when(g >= turn)
    def _():
        grad = lax.dot_general(ig_s[...], wx_ref[...], nt, preferred_element_type=F32)
        grad = grad + lax.dot_general(gg_ref[...], wg_ref[...], nt, preferred_element_type=F32)
        grad = grad.astype(BF16).reshape(n_dp, tok, piece)
        for h in (0, 1):

            @pl.when((g - turn) // (blocks // 2) == h)
            def _(h=h):
                at = (g - turn - h * (blocks // 2)) * piece
                ng_s[h, :, :, pl.ds(pl.multiple_of(at, piece), piece)] = grad

    @pl.when(g == steps - 1)
    def _():
        pairs[1].start()
        shares[0].relay()
        pairs[1].middle()
        ring_o.finish(wo_own, 2)
        shares[1].start()
        ring_s.event(2)
        ring_x.event(2)
        for h in (0, 1):
            pairs[h].finish(change_s.at[:, pl.ds(h * (width // 2), width // 2)])

        def rows(i, _):
            at = pl.ds(pl.multiple_of(i * 16, 16), 16)
            v = x_own[at, :].astype(F32)
            rstd = lax.rsqrt(jnp.mean(v * v, axis=1, keepdims=True) + EPS)
            hat = v * rstd
            grad = change_s[at, :] * gain_ref[...]
            grad = rstd * (grad - hat * jnp.mean(grad * hat, axis=1, keepdims=True))
            change_s[at, :] = dy_own[at, :].astype(F32) + grad
            return 0

        lax.fori_loop(0, tok // 16, rows, 0)
        for e in range(3, ring_x.events):
            ring_s.event(e)
            ring_x.event(e)
        ret_x.fill(pick_s[...], change_s)
        ret_x.start()
        shares[1].relay()
        ring_s.finish(sm_own)
        shares[3].start()
        ring_x.finish(wx_own)
        shares[2].start()
        shares[3].relay()
        shares[2].relay()
        for share in shares:
            share.finish()
        ret_m.finish()
        ret_x.finish()


def leave(lens, da, conv, x_in, act, dbl_grad, sel, taps, sums, decay_sum, rate, stepg, normed, wx, wg, gate_grad,
          wo_part, wo_half, wg_own, x_own, dy_own, mixed_own, gain, tags, ride, n_f):
    n_dp, tok, wide = dbl_grad.shape
    group, ch = act.shape
    width = x_own.shape[1]
    count = n_dp * n_f
    pair = tok // count
    piece = 256
    half = ch // piece
    dcols = width // n_f
    cs = ch // n_f
    n = rate.shape[0]
    tall = -(-(wide + stepg.shape[0] + n + 8) // 64) * 64
    blocks = width // piece
    early = lambda g: (0, jnp.minimum(g, half - 1))
    late = lambda g: (0, jnp.clip(g - half, 0, blocks - 1))
    late_rows = lambda g: (jnp.maximum(g - half - blocks, 0), 0)
    any_ = pl.BlockSpec(memory_space=pl.ANY)
    vmem = pl.BlockSpec(memory_space=pltpu.VMEM)
    block = lambda rows: pl.BlockSpec((rows, piece), early)
    shaped = jax.ShapeDtypeStruct
    return pl.pallas_call(
        functools.partial(leave_kernel, n_f, half),
        grid=(half + 2 * blocks,),
        in_specs=[
            pl.BlockSpec(memory_space=pltpu.SMEM),
            block(group),
            block(group),
            block(group),
            block(group),
            vmem,
            block(wide),
            block(taps.shape[0]),
            block(8),
            block(n),
            block(n),
            block(stepg.shape[0]),
            pl.BlockSpec((group, piece), late),
            pl.BlockSpec((piece, ch), late_rows),
            pl.BlockSpec((piece, ch), late_rows),
        ]
        + [vmem] * 10,
        out_specs=[any_] * 5,
        out_shape=[
            shaped((count, pair, width + 128), BF16),
            shaped((count, pair, width), BF16),
            shaped((n_dp, dcols, 2 * ch), BF16),
            shaped((n_dp, cs, width), BF16),
            shaped(side_by_side(n_dp, tall, cs), F32),
        ],
        scratch_shapes=[
            pltpu.VMEM((group, ch), BF16),
            pltpu.VMEM((n_f, dcols, ch), BF16),
            pltpu.VMEM((2, n_dp, tok, width // 2), BF16),
            pltpu.VMEM((n_f, tall, cs), F32),
            pltpu.VMEM((tok, tok), BF16),
            pltpu.VMEM((count, pair, width + 128), BF16),
            pltpu.VMEM((count, pair, width), BF16),
            pltpu.VMEM((tok, width), F32),
        ]
        + RingReduce.scratch(n_f, (cs, width))
        + RingReduce.scratch(n_f, (dcols, ch))
        + RingReduce.scratch(n_f, (tall, cs), F32)
        + [
            pltpu.VMEM((2, 2, tok, width // 2), BF16),
            pltpu.VMEM((2, tok, width // 2), BF16),
            pltpu.SemaphoreType.DMA((2, 3)),
            pltpu.SemaphoreType.DMA((2, 3)),
            pltpu.VMEM((cs, width), BF16),
            pltpu.VMEM((dcols, ch), BF16),
            pltpu.VMEM((tall, cs), F32),
            pltpu.SemaphoreType.DMA((6,)),
            pltpu.SemaphoreType.DMA((4, 3)),
            pltpu.SemaphoreType.DMA((4, 3)),
            pltpu.SemaphoreType.DMA((4,)),
        ],
        compiler_params=pltpu.CompilerParams(
            collective_id=4, has_side_effects=True, vmem_limit_bytes=62 * 2**20
        ),
        cost_estimate=pl.CostEstimate(flops=2 * 10**10, bytes_accessed=6 * 10**7, transcendentals=10**6),
    )(lens, da, conv, x_in, act, dbl_grad, sel, taps, sums, decay_sum, rate, stepg, normed, wx, wg, gate_grad,
      wo_part, wo_half, wg_own, x_own, dy_own, mixed_own, gain, tags, ride)


def masks_of(count):
    return [1 << b for b in range(count.bit_length() - 1)]


def mesh_at(index, n_f):
    return (index // n_f, lax.rem(index, n_f))


def ring_index(p, n_f):
    if n_f % 2:
        return p
    return jnp.where(p < n_f // 2, 2 * p, 2 * (n_f - 1 - p) + 1)


def ring_place(f, n_f):
    if n_f % 2:
        return f
    return jnp.where(lax.rem(f, 2) == 0, f // 2, n_f - 1 - f // 2)


def pack_kernel(cs, me_d, starts, w_ref, small_refs, gain_ref, blocks):
    small, halves = blocks[0], blocks[1:]
    lanes = pl.ds(pl.multiple_of(me_d * cs, 128), cs)
    sel, step, decay, rest = small_refs[0], small_refs[1], small_refs[2], small_refs[3:]
    at = 0
    for ref in (sel, step, decay):
        small[at : at + ref.shape[0], :] = ref[:, lanes]
        at += ref.shape[0]
    rows = [ref[:, lanes].astype(F32) for ref in rest] + [gain_ref[...].astype(F32)]
    filler = small.shape[0] - at - sum(r.shape[0] for r in rows)
    small[at:, :] = jnp.concatenate(rows + [jnp.zeros((filler, cs), F32)], axis=0).astype(BF16)
    for o, out in enumerate(halves):
        for j, start in enumerate(starts[o]):
            out[:, j * cs : (j + 1) * cs] = w_ref[:, pl.ds(pl.multiple_of(start + me_d * cs, 128), cs)]


def gather_kernel(n_dp, n_f, downs, segs, pack, x_ref, dy_ref, dest_row_ref, dest_ref, lens_ref, *refs):
    streams = len(downs)
    given = len(pack[1]) if pack else streams
    x_all, lens_all, x_own_ref, dy_own_ref, tag_ref, rank_ref, ride_ref = refs[given : given + 7]
    outs = refs[given + 7 : given + 7 + streams]
    (send_x, send_dy, got_x, got_dy, x_own, dy_own, deal_sem, loc_sem, pair_send, pair_recv, ring_send, ring_recv) = (
        refs[given + 7 + streams : given + 19 + streams]
    )
    blocks = refs[given + 19 + streams :] if pack else refs[:streams]
    count = n_dp * n_f
    me_d = lax.axis_index("dp")
    me_f = lax.axis_index("fsdp")
    me = me_d * n_f + me_f
    q = ring_place(me_f, n_f)
    below = ring_index(lax.rem(q + n_f - 1, n_f), n_f)
    above = ring_index(lax.rem(q + 1, n_f), n_f)

    barrier = pltpu.get_barrier_semaphore()

    def greet(p, _):
        pl.semaphore_signal(
            barrier, inc=1, device_id=mesh_at(lax.rem(me + p, count), n_f), device_id_type=pl.DeviceIdType.MESH
        )
        return 0

    lax.fori_loop(1, count, greet, 0)
    if pack:
        pack_kernel(pack[0], me_d, pack[2], refs[0], refs[1 : given - 1], refs[given - 1], blocks)

    def place_of(s, index):
        return lane_block(outs[s], index, blocks[s].shape[1]) if s == 0 else outs[s].at[index]

    locals_ = [
        pltpu.make_async_copy(blocks[s], place_of(s, me_f), loc_sem.at[s]) for s in range(streams)
    ]
    for c in locals_:
        c.start()
    pl.semaphore_wait(barrier, count - 1)

    def deal(a):
        src, dst = ((send_x, got_x), (send_dy, got_dy))[a]

        def one(p, _):
            pltpu.make_async_remote_copy(
                src_ref=src.at[p],
                dst_ref=dst.at[p],
                send_sem=deal_sem.at[a, 0],
                recv_sem=deal_sem.at[a, 1],
                device_id=mesh_at(lax.rem(me + p, count), n_f),
                device_id_type=pl.DeviceIdType.MESH,
            ).start()
            return 0

        lax.fori_loop(1, count, one, 0)
        dst[0] = src[0]

    def dealt(a, way):
        src, dst = ((send_x, got_x), (send_dy, got_dy))[a]
        rest = pl.ds(1, count - 1)
        pltpu.make_async_copy(src.at[rest], dst.at[rest], deal_sem.at[a, way]).wait()

    def hop(s, h, up):
        k = lax.rem(q + (n_f - h if up else h), n_f)
        index = ring_index(k, n_f)
        src = blocks[s] if h == 0 else place_of(s, index)
        return pltpu.make_async_remote_copy(
            src_ref=src,
            dst_ref=place_of(s, index),
            send_sem=ring_send.at[s, int(up), h],
            recv_sem=ring_recv.at[s, int(up), h],
            device_id=(me_d, above if up else below),
            device_id_type=pl.DeviceIdType.MESH,
        )

    hops = [[downs[s], n_f - 1 - downs[s]] for s in range(streams)]
    for s in range(streams):
        for up in (0, 1):
            if hops[s][up]:
                hop(s, 0, up).start()
    tok, width = x_own.shape
    pair = got_x.shape[1]

    dest_row = dest_row_ref[...]
    abs_row = jnp.floor((dest_row + 0.5) * (1.0 / tok))
    in_row = dest_row - abs_row * tok
    rel_row = abs_row - me.astype(F32)
    rel_row = jnp.where(rel_row < 0.0, rel_row + count, rel_row)
    rank = jnp.sum((dest_ref[...] < dest_row).astype(F32), axis=0, keepdims=True)
    goal = rel_row * pair + rank - abs_row * pair
    rank_ref[...] = jnp.broadcast_to(goal, rank_ref.shape)
    chosen = lax.broadcasted_iota(jnp.int32, (tok, tok), 0).astype(F32) == goal
    spot = jnp.sum(jnp.where(chosen, in_row, 0.0), axis=1, keepdims=True)
    send_x[:, :, width:] = jnp.broadcast_to(spot, (tok, 128)).astype(BF16).reshape(count, pair, 128)
    pick = jnp.where(chosen, 1.0, 0.0).astype(BF16)

    def sort(values, out):
        def part(j, _):
            cols = pl.ds(pl.multiple_of(j * 256, 256), 256)
            moved = jnp.dot(pick, values[:, cols], preferred_element_type=F32)
            out[:, :, cols] = moved.astype(BF16).reshape(count, pair, 256)
            return 0

        lax.fori_loop(0, width // 256, part, 0)

    sort(x_ref, send_x)
    deal(0)
    sort(dy_ref, send_dy)
    deal(1)

    def advance(h):
        for s in range(streams):
            for up in (0, 1):
                if h < hops[s][up]:
                    hop(s, h - 1, up).wait_recv()
                    hop(s, h, up).start()

    advance(1)
    dealt(0, 1)
    tag = got_x[:, :, width : width + 128].astype(F32).reshape(tok, 128)
    spots = jnp.concatenate([tag] * (tok // 128), axis=1)
    lane = lax.broadcasted_iota(jnp.int32, (tok, tok), 1).astype(F32)
    settle = jnp.where(spots == lane, 1.0, 0.0).astype(BF16)
    tn = (((0,), (0,)), ((), ()))
    tag_ref[...] = tag

    def place(values, out):
        def part(j, _):
            cols = pl.ds(pl.multiple_of(j * 256, 256), 256)
            block = values[:, :, cols].reshape(tok, 256)
            out[:, cols] = lax.dot_general(settle, block, tn, preferred_element_type=F32).astype(BF16)
            return 0

        lax.fori_loop(0, width // 256, part, 0)

    masks = list(reversed(masks_of(n_dp)))

    def partner(mask):
        return me_d + mask - 2 * mask * lax.rem(me_d // mask, 2)

    def share(a, m, mask):
        out = (x_all, lens_all)[a]
        own_block = (x_own, lens_ref)[a]
        return pltpu.make_async_remote_copy(
            src_ref=own_block if m == 0 else out.at[m],
            dst_ref=out.at[m | mask],
            send_sem=pair_send.at[a, m | mask],
            recv_sem=pair_recv.at[a, m | mask],
            device_id=(partner(mask), me_f),
            device_id_type=pl.DeviceIdType.MESH,
        )

    copies = []

    def keep(src, dst):
        c = pltpu.make_async_copy(src, dst, loc_sem.at[streams + len(copies)])
        c.start()
        copies.append(c)

    place(got_x, x_own)
    for a in (0, 1):
        for mask in masks:
            share(a, 0, mask).start()
    keep(lens_ref, lens_all.at[0])
    keep(x_own, x_all.at[0])
    keep(x_own, x_own_ref)

    lane = lax.broadcasted_iota(jnp.int32, (1, 128), 1)
    limit = jnp.sum(jnp.where(lane < segs - 1, lens_ref[0:1, :], 0).astype(F32), axis=1, keepdims=True)

    def squares(i, total_):
        v = x_own[pl.ds(pl.multiple_of(i * 32, 32), 32), :].astype(F32)
        t = (lax.broadcasted_iota(jnp.int32, (32, 1), 0) + i * 32).astype(F32)
        each = jnp.sum(v * v, axis=1, keepdims=True)
        return total_ + jnp.sum(jnp.where(t < limit, each, 0.0), axis=0, keepdims=True)

    ride = jnp.zeros((1, 128), F32)
    for j, value in enumerate((lax.fori_loop(0, tok // 32, squares, jnp.zeros((1, 1), F32)), limit)):
        high = value.astype(BF16).astype(F32)
        ride = ride + jnp.where(lane == 2 * j, high, 0.0) + jnp.where(lane == 2 * j + 1, value - high, 0.0)
    ride_ref[...] = jnp.broadcast_to(ride, ride_ref.shape)

    def relay(a):
        held = [0]
        for step, mask in enumerate(masks):
            for m in held:
                if m:
                    share(a, m, mask).start()
            for m in held:
                share(a, m, mask).wait_recv()
            held = held + [m | mask for m in held]

    most = max(max(h) for h in hops)
    for h in range(2, most):
        advance(h)
        if h == 2:
            dealt(1, 1)
            place(got_dy, dy_own)
            keep(dy_own, dy_own_ref)
    if most <= 2:
        dealt(1, 1)
        place(got_dy, dy_own)
        keep(dy_own, dy_own_ref)
    relay(0)
    relay(1)
    for s in range(streams):
        for up in (0, 1):
            if hops[s][up]:
                hop(s, hops[s][up] - 1, up).wait_recv()
    for s in range(streams):
        for up in (0, 1):
            for h in range(hops[s][up]):
                hop(s, h, up).wait_send()
    for a in (0, 1):
        held = [0]
        for mask in masks:
            for m in held:
                share(a, m, mask).wait_send()
            held = held + [m | mask for m in held]
    for c in locals_ + copies:
        c.wait()
    dealt(0, 0)
    dealt(1, 0)


def gather_all(x, dy, dest, lens, segs, blocks, pack, downs, n_dp, n_f):
    streams = len(blocks)
    tok, width = x.shape
    count = n_dp * n_f
    sent_x = (count, tok // count, width + 128)
    sent_dy = (count, tok // count, width)
    hops = max(max(d, n_f - 1 - d) for d in downs)
    any_ = pl.BlockSpec(memory_space=pl.ANY)
    vmem = pl.BlockSpec(memory_space=pltpu.VMEM)
    row = jax.ShapeDtypeStruct((tok, width), BF16)
    rows = jax.ShapeDtypeStruct((n_dp, tok, width), BF16)
    return pl.pallas_call(
        functools.partial(gather_kernel, n_dp, n_f, downs, segs, pack and (pack[0], [None] * len(pack[1]), pack[2])),
        in_specs=[vmem] * 5 + ([vmem] * len(pack[1]) if pack else [any_] * streams),
        out_specs=[any_] * 4 + [vmem] * 3 + [any_] * streams,
        out_shape=[
            rows,
            jax.ShapeDtypeStruct((n_dp,) + lens.shape, lens.dtype),
            row,
            row,
            jax.ShapeDtypeStruct((tok, 128), F32),
            jax.ShapeDtypeStruct((8, tok), F32),
            jax.ShapeDtypeStruct((8, 128), F32),
        ]
        + [jax.ShapeDtypeStruct(side_by_side(n_f, *blocks[0].shape), BF16)]
        + [jax.ShapeDtypeStruct((n_f,) + b.shape, b.dtype) for b in blocks[1:]],
        scratch_shapes=[
            pltpu.VMEM(sent_x, BF16),
            pltpu.VMEM(sent_dy, BF16),
            pltpu.VMEM(sent_x, BF16),
            pltpu.VMEM(sent_dy, BF16),
            pltpu.VMEM((tok, width), BF16),
            pltpu.VMEM((tok, width), BF16),
            pltpu.SemaphoreType.DMA((2, 2)),
            pltpu.SemaphoreType.DMA((streams + 4,)),
            pltpu.SemaphoreType.DMA((2, n_dp)),
            pltpu.SemaphoreType.DMA((2, n_dp)),
            pltpu.SemaphoreType.DMA((streams, 2, hops)),
            pltpu.SemaphoreType.DMA((streams, 2, hops)),
        ]
        + ([pltpu.VMEM(b.shape, BF16) for b in blocks] if pack else []),
        compiler_params=pltpu.CompilerParams(
            collective_id=0, has_side_effects=True, vmem_limit_bytes=40 * 2**20
        ),
        cost_estimate=pl.CostEstimate(flops=10**10, bytes_accessed=2 * 10**8, transcendentals=0),
    )(x, dy, dest[None, :], dest[:, None], lens, *(pack[1] if pack else blocks))


def spread_kernel(cs, x_ref, w_ref, go_ref, small_ref, out_ref, sum_ref, go_out, *small_outs):
    total = jnp.zeros(sum_ref.shape, F32)
    n_dp = x_ref.shape[0]
    for f in range(x_ref.shape[2] // cs):
        for i in range(n_dp):
            part = x_ref[i, :, f * cs : (f + 1) * cs].astype(F32)
            cols = slice((f * n_dp + i) * cs, (f * n_dp + i + 1) * cs)
            out_ref[:, cols] = part
            product = part * w_ref[:, cols].astype(F32)
            for j in range(0, cs, 128):
                total = total + product[:, j : j + 128]
    go_out[...] = go_ref[...].astype(F32)

    @pl.when(pl.program_id(0) == 0)
    def _():
        sum_ref[...] = jnp.zeros_like(sum_ref)
        at = 0
        for out in small_outs:
            out[...] = small_ref[at : at + out.shape[0], :]
            at += out.shape[0]

    sum_ref[...] += total


def spread_columns(parts, w, go, small, heights, cs):
    n_dp, height, cols = parts.shape
    if cs % 128:
        out = parts.reshape(n_dp, height, cols // cs, cs).transpose(1, 2, 0, 3).reshape(height, n_dp * cols).astype(F32)
        cuts = [small[sum(heights[:i]) : sum(heights[: i + 1])] for i in range(len(heights))]
        return out, jnp.sum(out * w.astype(F32), axis=1), go.astype(F32), cuts
    wide = 2 * cs
    steps = cols // wide
    once = lambda f: (0, 0)
    go_block = (go.shape[0] // steps, go.shape[1])
    shaped = jax.ShapeDtypeStruct
    out, sums, go, *cuts = pl.pallas_call(
        functools.partial(spread_kernel, cs),
        grid=(steps,),
        in_specs=[
            pl.BlockSpec((n_dp, height, wide), lambda f: (0, 0, f)),
            pl.BlockSpec((height, n_dp * wide), lambda f: (0, f)),
            pl.BlockSpec(go_block, lambda f: (f, 0)),
            pl.BlockSpec(small.shape, once),
        ],
        out_specs=[
            pl.BlockSpec((height, n_dp * wide), lambda f: (0, f)),
            pl.BlockSpec((height, 128), once),
            pl.BlockSpec(go_block, lambda f: (f, 0)),
        ]
        + [pl.BlockSpec((h, small.shape[1]), once) for h in heights],
        out_shape=[shaped((height, n_dp * cols), F32), shaped((height, 128), F32), shaped(go.shape, F32)]
        + [shaped((h, small.shape[1]), F32) for h in heights],
        compiler_params=pltpu.CompilerParams(vmem_limit_bytes=32 * 2**20),
        cost_estimate=pl.CostEstimate(flops=4 * height * cols * n_dp, bytes_accessed=8 * height * cols * n_dp, transcendentals=0),
    )(parts, w, go, small)
    return out, jnp.sum(sums, axis=1), go, cuts


def per_device(
    tokens,
    cotangent,
    destination,
    lengths,
    norm_gain,
    in_weight,
    conv_weight,
    conv_bias,
    select_weight,
    step_weight,
    step_bias,
    decay_log,
    skip_gain,
    out_weight,
):
    n_dp = lax.axis_size("dp")
    n_f = lax.axis_size("fsdp")
    rows = n_dp * n_f
    tok = tokens.shape[0]
    width = tokens.shape[1]
    pair = tok // rows
    inner = conv_bias.shape[0] * n_f
    cs = conv_bias.shape[0] // n_dp
    ch = cs * n_f
    taps = conv_weight.shape[0]
    n = decay_log.shape[0]
    rank_of = step_weight.shape[0]
    dcols = width // n_f
    group = n_dp * tok
    both = ("dp", "fsdp")
    me_d = lax.axis_index("dp")
    me_f = lax.axis_index("fsdp")
    flat_dot = lambda a, b: jnp.dot(a, b, preferred_element_type=F32)
    nt_dot = lambda a, b: lax.dot_general(a, b, (((1,), (1,)), ((), ())), preferred_element_type=F32)
    tn_dot = lambda a, b: lax.dot_general(a, b, (((0,), (0,)), ((), ())), preferred_element_type=F32)

    segs = lengths.shape[1]
    lens_tile = jnp.pad(lengths, ((0, 7), (0, 128 - segs)))
    slots = jnp.arange(tok, dtype=jnp.int32)

    flat = lambda shard: shard.reshape(-1, n_dp * cs)
    smalls = [
        flat(v) for v in (select_weight, step_weight, decay_log, conv_weight, conv_bias, step_bias, skip_gain)
    ]
    gain_rows = dcols // cs
    gain_block = norm_gain.reshape(gain_rows, cs)
    used = sum(v.shape[0] for v in smalls) + gain_rows
    tall = used + -used % 16
    starts = [[h * inner + f * n_dp * cs for f in range(n_f)] for h in (0, 1)]
    if cs % 128:
        mine = lambda value, at: lax.dynamic_slice_in_dim(value, at + me_d * cs, cs, 1)
        blocks = [
            jnp.concatenate(
                [mine(v, 0) for v in smalls] + [gain_block, jnp.zeros((tall - used, cs), BF16)], axis=0
            )
        ] + [jnp.concatenate([mine(in_weight, at) for at in half], axis=1) for half in starts]
        pack = None
    else:
        blocks = [jax.ShapeDtypeStruct((tall, cs), BF16)] + [jax.ShapeDtypeStruct((dcols, ch), BF16)] * 2
        pack = (cs, [in_weight] + smalls + [gain_block], starts)
    wo_block = lax.dynamic_slice_in_dim(out_weight, me_d * cs, cs, 0)
    x_all, lens_all, x_own, dy_own, x_tags, ranks, ride, small_all, wx, wg = gather_all(
        tokens, cotangent, destination.astype(F32), lens_tile, segs, blocks, pack,
        [n_f // 2, n_f // 2, n_f - 1 - n_f // 2], n_dp, n_f,
    )
    x_all = x_all.reshape(group, width)
    lens = lens_all[:, 0, :segs]
    from_send = (ranks[0].astype(jnp.int32)[:, None] == slots[None, :]).astype(BF16)
    wx = wx.reshape(width, ch)
    wg = wg.reshape(width, ch)
    small = joined(small_all)
    at = select_weight.shape[0]
    sel = small[:at]
    stepw = small[at : at + rank_of]
    dlog = small[at + rank_of : at + rank_of + n]
    misc = small[at + rank_of + n :]
    conv_w, conv_b, step_b, skip = misc[:taps], misc[taps : taps + 1], misc[taps + 1 : taps + 2], misc[taps + 2 : taps + 3]
    gain = misc[taps + 3 : taps + 3 + gain_rows]
    gain = gain.reshape(gain_rows, n_f, cs).transpose(1, 0, 2).reshape(width).astype(F32)
    conv_w = conv_w.astype(F32)
    skip = skip.astype(F32)
    rate = -jnp.exp(dlog.astype(F32))

    normed, x_in, conv, act, gate, dbl, wo_next = enter(
        lens, x_all, gain[None], wx, wg, conv_w, conv_b.astype(F32), sel, wo_block, n_f
    )
    dbl = dbl.reshape(group, -1)
    rate2 = rate * LOG2E
    scan_out, states, delta, pre, wo, dy_all = scan_forward(
        lens, dbl, act, stepw, step_b.astype(F32), rate2, skip, wo_block, wo_next, dy_own, n_f, tok
    )
    dy_all = dy_all.reshape(group, width)
    wo = wo.reshape(ch, width)
    gate_silu = jax.nn.silu(gate)
    gated = (scan_out * gate_silu).astype(BF16)

    gated_grad = nt_dot(dy_all, wo)
    scan_grad = gated_grad * gate_silu
    gate_grad = (gated_grad * scan_out * silu_slope(gate)).astype(BF16)
    wg_grad = tn_dot(normed, gate_grad).astype(BF16)
    pre_grad, act_grad, dbl_grad, decay_sum, sums, step_grad, wg_own, wo_grad, wo_half, mixed = scan_backward(
        lens, dbl, delta, pre, act, scan_grad, stepw, rate2, skip, states,
        wg_grad.reshape(n_f, dcols, ch), gated, dy_all, wo, n_f, tok,
    )
    mix_back, dx_back, gin_all, go_all, small_full = leave(
        lens, act_grad, conv, x_in, act, dbl_grad, sel, conv_w, sums, decay_sum, rate, step_grad, normed, wx, wg,
        gate_grad, wo_grad, wo_half, wg_own, x_own, dy_own, mixed, gain[None], x_tags, ride[:1], n_f,
    )

    grad_in_weight, gain_sum, grad_out_weight, cuts = spread_columns(
        gin_all, in_weight, go_all.reshape(n_dp * cs, width), joined(small_full),
        [select_weight.shape[0], rank_of, n, 8], cs,
    )
    grad_select, grad_step, grad_decay, misc = cuts
    grad_norm_gain = gain_sum / norm_gain.astype(F32)

    back = mix_back.reshape(tok, width + 128)
    totals = jnp.sum(mix_back[:, 0, width : width + 4].astype(F32), axis=0)
    input_rms = jnp.sqrt((totals[0] + totals[1]) / ((totals[2] + totals[3]) * width))
    mixer_output = flat_dot(from_send, back[:, :width])
    layer_output = (tokens.astype(F32) + mixer_output).astype(BF16)
    mixer_output = mixer_output.astype(BF16)
    input_grad = flat_dot(from_send, dx_back.reshape(tok, width)).astype(BF16)
    return (
        layer_output,
        mixer_output,
        input_grad,
        input_rms,
        grad_norm_gain,
        grad_in_weight,
        misc[:taps],
        misc[taps],
        grad_select,
        grad_step,
        misc[taps + 1],
        grad_decay,
        misc[taps + 2],
        grad_out_weight,
    )


def solution(mesh):
    return jax.shard_map(
        per_device,
        mesh=mesh,
        in_specs=(
            P(("dp", "fsdp"), None),
            P(("dp", "fsdp"), None),
            P(("dp", "fsdp")),
            P(("dp", "fsdp"), None),
            P("fsdp"),
            P("fsdp", None),
            P(None, "fsdp"),
            P("fsdp"),
            P(None, "fsdp"),
            P(None, "fsdp"),
            P("fsdp"),
            P(None, "fsdp"),
            P("fsdp"),
            P("fsdp", None),
        ),
        out_specs=(
            P(("dp", "fsdp"), None),
            P(("dp", "fsdp"), None),
            P(("dp", "fsdp"), None),
            P(),
            P("fsdp"),
            P("fsdp", None),
            P(None, "fsdp"),
            P("fsdp"),
            P(None, "fsdp"),
            P(None, "fsdp"),
            P("fsdp"),
            P(None, "fsdp"),
            P("fsdp"),
            P("fsdp", None),
        ),
        check_vma=False,
    )
```

```python
import functools
import math

import jax
import jax.numpy as jnp
from jax import lax
from jax.experimental import pallas as pl
from jax.experimental.pallas import tpu as pltpu
from jax.sharding import PartitionSpec as P

EPS = 1e-05
TB = 16
LOG2E = math.log2(math.e)
RESET = 1.0e4
BF16 = jnp.bfloat16
F32 = jnp.float32


def silu_slope(value):
    sigma = jax.nn.sigmoid(value)
    return sigma * (1.0 + value * (1.0 - sigma))


def row_at(g, n_dp):
    return lax.rem(2 * g + 1, n_dp + 1)


def flip(d, mask):
    return d + mask - 2 * mask * lax.rem(d // mask, 2)


class GroupSum:
    def __init__(self, part, near, far, total, send, recv):
        self.part, self.near, self.far, self.total = part, near, far, total
        me_d, me_f = lax.axis_index("dp"), lax.axis_index("fsdp")
        plan = [
            (part.at[1], near.at[0], 1),
            (part.at[3], near.at[1], 1),
            (part.at[0], far.at[1], 2),
            (part.at[2], far.at[0], 2),
            (total.at[0], total.at[1], 1),
            (total.at[2], total.at[3], 1),
        ]
        self.copies = [
            pltpu.make_async_remote_copy(
                src_ref=src,
                dst_ref=dst,
                send_sem=send.at[i],
                recv_sem=recv.at[i],
                device_id=(flip(me_d, mask), me_f),
                device_id_type=pl.DeviceIdType.MESH,
            )
            for i, (src, dst, mask) in enumerate(plan)
        ]

    def row_done(self, g):
        for j in (0, 1):

            @pl.when(g == j)
            def _(j=j):
                self.copies[j].start()

            @pl.when(g == j + 2)
            def _(j=j):
                self.copies[j].wait_recv()
                self.part[2 * j] = self.part[2 * j] + self.near[j]
                self.copies[j + 2].start()

    def first(self):
        for j in (0, 1):
            self.copies[j].start()

    def second(self):
        for j in (0, 1):
            self.copies[j].wait_recv()
            self.part[2 * j] = self.part[2 * j] + self.near[j]
            self.copies[j + 2].start()

    def finish(self):
        for j in (0, 1):
            self.copies[3 - j].wait_recv()
            self.total[2 * j] = self.part[2 * j] + self.far[j]
            self.copies[4 + j].start()
        for j in (0, 1):
            self.copies[4 + j].wait_recv()
        for c in self.copies:
            c.wait_send()

    @staticmethod
    def scratch(tok, wide):
        return [
            pltpu.VMEM((4, tok, wide), F32),
            pltpu.VMEM((2, tok, wide), F32),
            pltpu.VMEM((2, tok, wide), F32),
            pltpu.VMEM((4, tok, wide), F32),
            pltpu.SemaphoreType.DMA((6,)),
            pltpu.SemaphoreType.DMA((6,)),
        ]


class RingReduce:
    def __init__(self, n_f, part, got, send, recv, down):
        self.part, self.got = part, got
        q = ring_place(lax.axis_index("fsdp"), n_f)
        self.at = lambda k: ring_index(lax.rem(q + k, n_f), n_f)
        self.n_f = n_f
        self.counts = [down, n_f - 1 - down]
        self.copies = [[], []]
        for up in (0, 1):
            for h in range(min(self.counts[up], got.shape[1])):
                src = part.at[self.at(self.goal(up, 0))] if h == 0 else got.at[up, h - 1]
                self.copies[up].append(ring_copy(n_f, src, got.at[up, h], send.at[up, h], recv.at[up, h], up))
        self.events = max(self.counts)

    def goal(self, up, h):
        left = self.counts[up] - h
        return left if up else self.n_f - left

    def add(self, slot, addend):
        rows = slot.shape[0]
        step = min(rows, 64)

        def piece(i, _):
            at = pl.ds(pl.multiple_of(i * step, step), step)
            slot[at, :] = (slot[at, :].astype(F32) + addend[at, :].astype(F32)).astype(slot.dtype)
            return 0

        lax.fori_loop(0, rows // step, piece, 0)

    def start(self):
        for up in (0, 1):
            if self.copies[up]:
                self.copies[up][0].start()

    def stop(self, hops, out):
        for up in (0, 1):
            self.copies[up][hops - 1].wait_recv()
            rows_add(out.at[up], [self.got.at[up, hops - 1]])
            for c in self.copies[up][:hops]:
                c.wait_send()

    def resume(self, hops, arrived):
        for up in (0, 1):
            slot = self.got.at[up, hops - 1]
            rows_add(slot, [arrived.at[up], self.part.at[self.at(self.goal(up, hops))]])
            self.copies[up][hops].start()

    def event(self, e):
        for up in (0, 1):
            if e < self.counts[up]:
                self.copies[up][e - 1].wait_recv()
                self.add(self.got.at[up, e - 1], self.part.at[self.at(self.goal(up, e))])
                self.copies[up][e].start()

    def finish(self, out, since=0):
        last = []
        for up in (0, 1):
            if self.copies[up]:
                self.copies[up][-1].wait_recv()
                last.append(self.got.at[up, self.counts[up] - 1])
        mine = self.part.at[self.at(0)]
        rows = mine.shape[0]
        step = min(rows, 64)

        def piece(i, _):
            at = pl.ds(pl.multiple_of(i * step, step), step)
            total_ = mine[at, :].astype(F32)
            for slot in last:
                total_ = total_ + slot[at, :].astype(F32)
            out[at, :] = total_.astype(out.dtype)
            return 0

        lax.fori_loop(0, rows // step, piece, 0)
        for up in (0, 1):
            for c in self.copies[up][since:]:
                c.wait_send()

    @staticmethod
    def scratch(n_f, block, dtype=BF16, slots=0):
        return [
            pltpu.VMEM((2, slots or n_f // 2) + block, dtype),
            pltpu.SemaphoreType.DMA((2, n_f // 2)),
            pltpu.SemaphoreType.DMA((2, n_f // 2)),
        ]


class PairReduce:
    def __init__(self, part, near, far, send, recv):
        self.part, self.near, self.far = part, near, far
        me_d, me_f = lax.axis_index("dp"), lax.axis_index("fsdp")
        plan = [
            (part.at[1], near.at[0], 1),
            (part.at[3], near.at[1], 1),
            (part.at[2], far, 2),
        ]
        self.copies = [
            pltpu.make_async_remote_copy(
                src_ref=src,
                dst_ref=dst,
                send_sem=send.at[i],
                recv_sem=recv.at[i],
                device_id=(flip(me_d, mask), me_f),
                device_id_type=pl.DeviceIdType.MESH,
            )
            for i, (src, dst, mask) in enumerate(plan)
        ]

    def start(self):
        for c in self.copies[:2]:
            c.start()

    def middle(self):
        self.copies[1].wait_recv()
        rows_add(self.part.at[2], [self.part.at[2], self.near.at[1]])
        self.copies[2].start()
        self.copies[0].wait_recv()

    def finish(self, out):
        self.copies[2].wait_recv()
        rows_add(out, [self.part.at[0], self.near.at[0], self.far])
        for c in self.copies:
            c.wait_send()

    @staticmethod
    def scratch(block, dtype=BF16):
        return [
            pltpu.VMEM((2,) + block, dtype),
            pltpu.VMEM(block, dtype),
            pltpu.SemaphoreType.DMA((3,)),
            pltpu.SemaphoreType.DMA((3,)),
        ]


def rows_add(out, terms, step=32):
    def piece(i, _):
        at = pl.ds(pl.multiple_of(i * step, step), step)
        total_ = terms[0][at, :].astype(F32)
        for t in terms[1:]:
            total_ = total_ + t[at, :].astype(F32)
        out[at, :] = total_.astype(out.dtype)
        return 0

    lax.fori_loop(0, out.shape[0] // step, piece, 0)


class PairShare:
    def __init__(self, mine, out, local, send, recv, relative=False):
        me_d, me_f = lax.axis_index("dp"), lax.axis_index("fsdp")
        far = 2 if relative else flip(me_d, 2)
        here, at_near, at_far, relayed = (0, 1, 2, 3) if relative else (me_d, me_d, me_d, far)
        self.local = pltpu.make_async_copy(mine, out(here), local)
        self.copies = [
            pltpu.make_async_remote_copy(
                src_ref=src,
                dst_ref=dst,
                send_sem=send.at[i],
                recv_sem=recv.at[i],
                device_id=(flip(me_d, mask), me_f),
                device_id_type=pl.DeviceIdType.MESH,
            )
            for i, (src, dst, mask) in enumerate(
                [(mine, out(at_near), 1), (mine, out(at_far), 2), (out(far), out(relayed), 1)]
            )
        ]

    def start(self):
        self.copies[1].start()
        self.copies[0].start()
        self.local.start()

    def relay(self):
        self.copies[1].wait_recv()
        self.copies[2].start()

    def finish(self):
        self.copies[0].wait_recv()
        self.copies[2].wait_recv()
        for c in self.copies:
            c.wait_send()
        self.local.wait()


def side_by_side(count, height, wide):
    return (count, height, wide) if wide % 128 else (height, count * wide)


def lane_block(ref, index, wide):
    if wide % 128:
        return ref.at[index]
    return ref.at[:, pl.ds(pl.multiple_of(index * wide, 128), wide)]


def joined(value):
    if value.ndim == 2:
        return value
    return value.transpose(1, 0, 2).reshape(value.shape[1], -1)


def greet_neighbours(n_f, ring):
    me_d, me_f = lax.axis_index("dp"), lax.axis_index("fsdp")
    barrier = pltpu.get_barrier_semaphore()
    others = [(flip(me_d, 1), me_f), (flip(me_d, 2), me_f)]
    if ring:
        q = ring_place(me_f, n_f)
        others.append((me_d, ring_index(lax.rem(q + n_f - 1, n_f), n_f)))
        others.append((me_d, ring_index(lax.rem(q + 1, n_f), n_f)))
    for other in others:
        pl.semaphore_signal(barrier, inc=1, device_id=other, device_id_type=pl.DeviceIdType.MESH)
    pl.semaphore_wait(barrier, len(others))


def ring_copy(n_f, src, dst, send, recv, up):
    me_d, me_f = lax.axis_index("dp"), lax.axis_index("fsdp")
    q = ring_place(me_f, n_f)
    to = ring_index(lax.rem(q + (1 if up else n_f - 1), n_f), n_f)
    return pltpu.make_async_remote_copy(
        src_ref=src,
        dst_ref=dst,
        send_sem=send,
        recv_sem=recv,
        device_id=(me_d, to),
        device_id_type=pl.DeviceIdType.MESH,
    )


def segment_span(lens_ref, m, first, rows):
    t = lax.broadcasted_iota(jnp.int32, (rows, 1), 0) + first
    begin = jnp.zeros((rows, 1), jnp.int32)
    end = jnp.zeros((rows, 1), jnp.int32)
    total = jnp.int32(0)
    for j in range(lens_ref.shape[1]):
        after = total + lens_ref[m, j]
        inside = t >= total
        begin = jnp.where(inside, total, begin)
        end = jnp.where(inside, after, end)
        total = after
    return t - begin, end - 1 - t


def enter_kernel(n_f, half, lens_ref, x_ref, gain_ref, wx_ref, wg_ref, taps_ref, bias_ref, sel_ref, wo_ref,
                 normed_ref, xin_ref, conv_ref, act_ref, gate_ref, dbl_ref, next_ref,
                 part, near, far, total, gs_send, gs_recv, hop_send, hop_recv):
    g = pl.program_id(0)
    n_dp, tok = part.shape[:2]
    rows, width = x_ref.shape
    hops = [ring_copy(n_f, wo_ref, next_ref.at[up, 0], hop_send.at[up, 0], hop_recv.at[up, 0], up) for up in (0, 1)]
    hops2 = [
        ring_copy(n_f, next_ref.at[up, 0], next_ref.at[up, 1], hop_send.at[up, 1], hop_recv.at[up, 1], up)
        for up in (0, 1)
    ]
    group = GroupSum(part, near, far, total, gs_send, gs_recv)

    @pl.when(g == 0)
    def _():
        greet_neighbours(n_f, True)
        for c in hops:
            c.start()
        part[...] = jnp.zeros_like(part)

        def norm(i, _):
            for j in range(4):
                at = pl.ds(pl.multiple_of(i * 128 + j * 32, 32), 32)
                v = x_ref[at, :].astype(F32)
                rstd = lax.rsqrt(jnp.mean(v * v, axis=1, keepdims=True) + EPS)
                normed_ref[at, :] = (v * rstd * gain_ref[...]).astype(BF16)
            return 0

        lax.fori_loop(0, rows // 128, norm, 0)

    @pl.when(g == half)
    def _():
        for a, b in zip(hops, hops2):
            a.wait_recv()
            b.start()

    @pl.when(g < half)
    def _():
        n_taps = taps_ref.shape[0]
        xin_ref[...] = jnp.dot(normed_ref[...], wx_ref[...], preferred_element_type=F32)
        for m in range(n_dp):
            at = slice(m * tok, (m + 1) * tok)
            v = xin_ref[at, :]
            since, _ = segment_span(lens_ref, m, 0, tok)
            conv = bias_ref[...] + taps_ref[n_taps - 1 : n_taps, :] * v
            for lag in range(1, n_taps):
                keep = (since >= lag).astype(F32)
                conv = conv + taps_ref[n_taps - 1 - lag : n_taps - lag, :] * (pltpu.roll(v, lag, 0) * keep)
            conv_ref[at, :] = conv
            act = jax.nn.silu(conv).astype(BF16)
            act_ref[at, :] = act
            part[m] += lax.dot_general(act, sel_ref[...], (((1,), (1,)), ((), ())), preferred_element_type=F32)

    @pl.when(g == half - 1)
    def _():
        group.first()

    @pl.when(g >= half)
    def _():
        gate_ref[...] = jnp.dot(normed_ref[...], wg_ref[...], preferred_element_type=F32)

    @pl.when(g == half)
    def _():
        group.second()

    @pl.when(g == 2 * half - 1)
    def _():
        group.finish()
        dbl_ref[...] = total[...]
        for a, b in zip(hops, hops2):
            a.wait_send()
            b.wait()


def enter(lens, x_all, gain, wx, wg, taps, bias, sel, wo, n_f):
    n_dp = lens.shape[0]
    rows, width = x_all.shape
    tok = rows // n_dp
    ch = wx.shape[1]
    wide = sel.shape[0]
    piece = 256
    half = ch // piece
    whole = lambda g: (0, 0)
    early = lambda g: (0, jnp.minimum(g, half - 1))
    late = lambda g: (0, jnp.maximum(g - half, 0))
    once = pl.Buffered(1)
    any_ = pl.BlockSpec(memory_space=pl.ANY)
    shaped = lambda d, t: jax.ShapeDtypeStruct((rows, d), t)
    return pl.pallas_call(
        functools.partial(enter_kernel, n_f, half),
        grid=(2 * half,),
        in_specs=[
            pl.BlockSpec(memory_space=pltpu.SMEM),
            pl.BlockSpec((rows, width), whole, pipeline_mode=once),
            pl.BlockSpec((1, width), whole),
            pl.BlockSpec((width, piece), early),
            pl.BlockSpec((width, piece), late),
            pl.BlockSpec((taps.shape[0], piece), early),
            pl.BlockSpec((1, piece), early),
            pl.BlockSpec((wide, piece), early),
            any_,
        ],
        out_specs=[
            pl.BlockSpec((rows, width), whole),
            pl.BlockSpec((rows, piece), early),
            pl.BlockSpec((rows, piece), early),
            pl.BlockSpec((rows, piece), early),
            pl.BlockSpec((rows, piece), late),
            pl.BlockSpec((n_dp, tok, wide), lambda g: (0, 0, 0)),
            any_,
        ],
        out_shape=[
            shaped(width, BF16),
            shaped(ch, F32),
            shaped(ch, F32),
            shaped(ch, BF16),
            shaped(ch, F32),
            jax.ShapeDtypeStruct((n_dp, tok, wide), F32),
            jax.ShapeDtypeStruct((2, 2) + wo.shape, BF16),
        ],
        scratch_shapes=GroupSum.scratch(tok, wide)
        + [pltpu.SemaphoreType.DMA((2, 2)), pltpu.SemaphoreType.DMA((2, 2))],
        compiler_params=pltpu.CompilerParams(
            collective_id=1, has_side_effects=True, vmem_limit_bytes=48 * 2**20
        ),
        cost_estimate=pl.CostEstimate(flops=10**10, bytes_accessed=4 * 10**7, transcendentals=10**6),
    )(lens, x_all, gain, wx, wg, taps, bias, sel, wo)


def fold_matrix(n):
    i = lax.broadcasted_iota(jnp.int32, (n, TB * n), 0)
    j = lax.broadcasted_iota(jnp.int32, (n, TB * n), 1)
    return jnp.where(lax.rem(j, n) == i, 1.0, 0.0)


def own_token(n):
    i = lax.broadcasted_iota(jnp.int32, (TB, TB * n), 0)
    j = lax.broadcasted_iota(jnp.int32, (TB, TB * n), 1)
    return i == j // n


def block_rows(m, n):
    spread = jnp.dot(m.astype(BF16), fold_matrix(n).astype(BF16), preferred_element_type=F32)
    i = lax.broadcasted_iota(jnp.int32, spread.shape, 0)
    j = lax.broadcasted_iota(jnp.int32, spread.shape, 1)
    return jnp.where(lax.rem(i, TB) == j // n, spread, 0.0).astype(BF16)


def turned(m):
    n = m.shape[1]
    i = lax.broadcasted_iota(jnp.int32, (n, n), 0)
    j = lax.broadcasted_iota(jnp.int32, (n, n), 1)
    eye = jnp.where(i == j, 1.0, 0.0)
    return lax.dot_general(
        eye, m, (((1,), (1,)), ((), ())), preferred_element_type=F32, precision=lax.Precision.HIGHEST
    )


def softplus(v):
    return jnp.maximum(v, 0.0) + jnp.log1p(jnp.exp(-jnp.abs(v)))


class RingGather:
    def __init__(self, n_f, mine, near, out, local, send, recv):
        q = ring_place(lax.axis_index("fsdp"), n_f)
        at = lambda k: ring_index(lax.rem(q + k, n_f), n_f)
        count = [n_f // 2, n_f - 1 - n_f // 2]
        known = near.shape[1]
        self.locals = [pltpu.make_async_copy(mine, out.at[at(0)], local.at[0])]
        self.hops = [[], []]
        for up in (0, 1):
            for j in range(known):
                index = at(n_f - 1 - j if up else 1 + j)
                self.locals.append(pltpu.make_async_copy(near.at[up, j], out.at[index], local.at[1 + known * up + j]))
            for h in range(known, count[up]):
                index = at(n_f - h if up else h)
                src = near.at[up, known - 1] if h == known else out.at[index]
                self.hops[up].append(
                    ring_copy(n_f, src, out.at[index], send.at[up, h], recv.at[up, h], up)
                )
        self.events = max(len(h) for h in self.hops)

    def start(self):
        for c in self.locals:
            c.start()
        for up in (0, 1):
            if self.hops[up]:
                self.hops[up][0].start()

    def event(self, e):
        for up in (0, 1):
            if e < len(self.hops[up]):
                self.hops[up][e - 1].wait_recv()
                self.hops[up][e].start()

    def finish(self):
        for up in (0, 1):
            if self.hops[up]:
                self.hops[up][-1].wait_recv()
            for c in self.hops[up]:
                c.wait_send()
        for c in self.locals:
            c.wait()


def fwd_kernel(lanes, n_f, lens_ref, dbl_ref, act_ref, stepw_ref, stepb_ref, rate_ref, skip_ref, wo_ref, next_ref, dy_ref,
               y_ref, s_ref, delta_ref, pre_ref, wo_all, dy_all, carry, big_s, cw_s, bt_s, d_s, u_s, sc, local, hop_send, hop_recv, sh_send, sh_recv):
    n, ch = rate_ref.shape
    tblk = act_ref.shape[0]
    low_n = stepw_ref.shape[0]
    steps = pl.num_programs(0) * pl.num_programs(1)
    now = pl.program_id(0) * pl.num_programs(1) + pl.program_id(1)
    ring = RingGather(n_f, wo_ref, next_ref, wo_all, local, hop_send, hop_recv)
    share = PairShare(dy_ref, lambda m: dy_all.at[m], local.at[5], sh_send, sh_recv, True)

    @pl.when(now == 0)
    def _():
        greet_neighbours(n_f, True)
        ring.start()
        share.start()

    @pl.when(now == 13)
    def _():
        share.relay()

    for e in range(1, ring.events):

        @pl.when(now == min(7 * e, 15))
        def _(e=e):
            ring.event(e)

    @pl.when(pl.program_id(1) == 0)
    def _():
        carry[...] = jnp.zeros_like(carry)

    pre = jnp.dot(dbl_ref[:, :low_n].astype(BF16), stepw_ref[...], preferred_element_type=F32) + stepb_ref[...]
    pre_ref[...] = pre
    delta_ref[...] = softplus(pre)
    since, _ = segment_span(lens_ref, pl.program_id(0), pl.program_id(1) * tblk, tblk)
    big_s[...] = jnp.where(since == 0, RESET, 0.0)
    cw_s[...] = block_rows(dbl_ref[:, low_n + n : low_n + 2 * n], n)
    flat = turned(dbl_ref[:, low_n : low_n + n])
    for i in range(tblk // TB):
        bt_s[i] = flat[:, i * TB : (i + 1) * TB]

    def chunk(i, _):
        base = pl.multiple_of(i * TB, TB)
        dl = delta_ref[pl.ds(base, TB), :]
        ac = act_ref[pl.ds(base, TB), :].astype(F32)
        d_s[...] = dl + big_s[pl.ds(base, TB), :]
        u_s[...] = dl * ac
        bt = bt_s[i]
        for lo in range(0, ch, lanes):
            cs = pl.ds(lo, lanes)
            rate = rate_ref[:, cs]
            s = carry[:, cs]
            for t in range(TB):
                dec = jnp.exp2(d_s[t : t + 1, cs] * rate)
                s = dec * s + bt[:, t : t + 1] * u_s[t : t + 1, cs]
                sc[t * n : (t + 1) * n, cs] = s.astype(BF16)
            carry[:, cs] = s
        states = sc[...]
        y = jnp.dot(cw_s[pl.ds(base, TB), :], states, preferred_element_type=F32)
        y_ref[pl.ds(base, TB), :] = y + skip_ref[...] * ac
        s_ref[pl.ds(pl.multiple_of(base * n, TB * n), TB * n), :] = states
        return 0

    lax.fori_loop(0, tblk // TB, chunk, 0)

    @pl.when(now == steps - 1)
    def _():
        ring.finish()
        share.finish()


def scan_forward(lens, dbl, act, stepw, stepb, rate2, skip, wo, wo_next, dy_own, n_f, row_len, tblk=64, lanes=512):
    t, ch = act.shape
    n = rate2.shape[0]
    nb = row_len // tblk
    at = lambda r, j: (r * nb + j, 0)
    zero = lambda r, j: (0, 0)
    any_ = pl.BlockSpec(memory_space=pl.ANY)
    wide = jax.ShapeDtypeStruct((t, ch), F32)
    return pl.pallas_call(
        functools.partial(fwd_kernel, min(lanes, ch), n_f),
        grid=(t // row_len, nb),
        in_specs=[
            pl.BlockSpec(memory_space=pltpu.SMEM),
            pl.BlockSpec((tblk, dbl.shape[1]), at),
            pl.BlockSpec((tblk, ch), at),
            pl.BlockSpec(stepw.shape, zero),
            pl.BlockSpec((1, ch), zero),
            pl.BlockSpec((n, ch), zero),
            pl.BlockSpec((1, ch), zero),
            any_,
            any_,
            any_,
        ],
        out_specs=[
            pl.BlockSpec((tblk, ch), at),
            pl.BlockSpec((tblk * n, ch), at),
            pl.BlockSpec((tblk, ch), at),
            pl.BlockSpec((tblk, ch), at),
            any_,
            any_,
        ],
        out_shape=[
            wide,
            jax.ShapeDtypeStruct((t * n, ch), BF16),
            wide,
            wide,
            jax.ShapeDtypeStruct((n_f,) + wo_next.shape[2:], BF16),
            jax.ShapeDtypeStruct((t // row_len,) + dy_own.shape, BF16),
        ],
        scratch_shapes=[
            pltpu.VMEM((n, ch), F32),
            pltpu.VMEM((tblk, 1), F32),
            pltpu.VMEM((tblk, TB * n), BF16),
            pltpu.VMEM((tblk // TB, n, TB), F32),
            pltpu.VMEM((TB, ch), F32),
            pltpu.VMEM((TB, ch), F32),
            pltpu.VMEM((TB * n, ch), BF16),
            pltpu.SemaphoreType.DMA((6,)),
            pltpu.SemaphoreType.DMA((2, n_f)),
            pltpu.SemaphoreType.DMA((2, n_f)),
            pltpu.SemaphoreType.DMA((3,)),
            pltpu.SemaphoreType.DMA((3,)),
        ],
        compiler_params=pltpu.CompilerParams(
            collective_id=2, has_side_effects=True, vmem_limit_bytes=32 * 2**20
        ),
        cost_estimate=pl.CostEstimate(flops=t * n * ch * 40, bytes_accessed=t * ch * 52, transcendentals=t * n * ch),
    )(lens, dbl, act, stepw, stepb, rate2, skip, wo, wo_next, dy_own)


def bwd_kernel(lanes, n_f, lens_ref, dbl_ref, delta_ref, pre_ref, act_ref, gy_ref, stepw_ref, rate_ref, skip_ref,
               s_ref, sp_ref, wg_part, gated_ref, dy_ref, wo_ref,
               pg_ref, da_ref, dbl_grad_ref, dl_ref, sums_ref, stepg_ref, wg_own, wo_out, wo_half, mixed_own,
               carry, big_s, bw_s, ct_s, d_all, u_all, g_all, h_all, b_all, c_all, part, near, far, total, gs_send, gs_recv,
               ring_got, ring_send, ring_recv, wo_got, wo_send, wo_recv, wo_part, mix, mix_near, mix_far, mix_send, mix_recv, wo_save):
    n, ch = rate_ref.shape
    tblk = act_ref.shape[0]
    low_n = stepw_ref.shape[0]
    r, j = pl.program_id(0), pl.program_id(1)
    n_dp, nb = pl.num_programs(0), pl.num_programs(1)
    m = row_at(r, n_dp)
    group = GroupSum(part, near, far, total, gs_send, gs_recv)
    ring = RingReduce(n_f, wg_part, ring_got, ring_send, ring_recv, n_f // 2)
    ring_o = RingReduce(n_f, wo_part, wo_got, wo_send, wo_recv, n_f - 1 - n_f // 2)
    pairs = PairReduce(mix, mix_near, mix_far, mix_send, mix_recv)
    now = r * nb + j
    last_step = n_dp * nb - 1
    @pl.when(j == 0)
    def _():
        carry[...] = jnp.zeros_like(carry)

    @pl.when((r == 0) & (j == 0))
    def _():
        greet_neighbours(n_f, True)
        ring.start()
        dl_ref[...] = jnp.zeros_like(dl_ref)
        sums_ref[...] = jnp.zeros_like(sums_ref)
        stepg_ref[...] = jnp.zeros_like(stepg_ref)

    for e in range(1, ring.events):

        @pl.when(now == min(4 * e, 15))
        def _(e=e):
            ring.event(e)

    tile = 256
    parts = ch // tile
    save = pltpu.make_async_copy(wo_part, wo_out, wo_save)

    @pl.when(now < parts)
    def _():
        cs = wo_part.shape[1]
        cols = pl.ds(pl.multiple_of(now * tile, tile), tile)
        grad = lax.dot_general(
            gated_ref[:, cols], dy_ref[...], (((0,), (0,)), ((), ())), preferred_element_type=F32
        ).astype(BF16)
        for i in range(tile // cs):
            wo_part[now * (tile // cs) + i] = grad[i * cs : (i + 1) * cs]

    @pl.when(now == parts - 1)
    def _():
        save.start()

    @pl.when(now == 6)
    def _():
        ring_o.start()

    @pl.when(now == 13)
    def _():
        ring_o.event(1)

    @pl.when((now >= parts) & (now < parts + n_dp))
    def _():
        row_len = mix.shape[1]
        at = pl.ds(pl.multiple_of((now - parts) * row_len, row_len), row_len)
        mix[now - parts] = jnp.dot(gated_ref[at, :], wo_ref[...], preferred_element_type=F32).astype(BF16)

    @pl.when(now == 8)
    def _():
        pairs.start()

    @pl.when(now == 10)
    def _():
        pairs.middle()

    ones = jnp.where(own_token(n), 1.0, 0.0).astype(BF16)
    nt = (((1,), (1,)), ((), ()))
    row = lax.broadcasted_iota(jnp.int32, (TB * n, n), 0)
    col = lax.broadcasted_iota(jnp.int32, (TB * n, n), 1)
    fold = jnp.where(lax.rem(row, n) == col, 1.0, 0.0)
    since, _ = segment_span(lens_ref, m, (nb - 1 - j) * tblk, tblk)
    big_s[...] = jnp.where(since == 0, RESET, 0.0)
    bw_s[...] = block_rows(dbl_ref[:, low_n : low_n + n], n)

    flat = turned(dbl_ref[:, low_n + n : low_n + 2 * n])
    for i in range(tblk // TB):
        ct_s[i] = flat[:, i * TB : (i + 1) * TB]

    def lane_sum(value):
        total_ = value[:, :128]
        for at in range(128, value.shape[1], 128):
            total_ = total_ + value[:, at : at + 128]
        return total_

    def gathered(sums):
        spread = jnp.sum(sums, axis=1, keepdims=True) * fold
        high = spread.astype(BF16)
        rest = (spread - high.astype(F32)).astype(BF16)
        return jnp.dot(ones, high, preferred_element_type=F32) + jnp.dot(ones, rest, preferred_element_type=F32)

    for i in reversed(range(tblk // TB)):
        base = i * TB
        d_s, u_s, g_s, h_s, b_s, c_s = (v.at[i % 2] for v in (d_all, u_all, g_all, h_all, b_all, c_all))
        dl = delta_ref[base : base + TB, :]
        ac = act_ref[base : base + TB, :].astype(F32)
        d_s[...] = dl + big_s[base : base + TB, :]
        u_s[...] = dl * ac
        ct = ct_s[i]
        for lo in range(0, ch, lanes):
            cs = pl.ds(lo, lanes)
            rate = rate_ref[:, cs]
            flow = carry[:, cs]
            acc = dl_ref[:, cs]
            here = s_ref[(base + TB - 1) * n : (base + TB) * n, cs].astype(F32)
            for t in reversed(range(TB)):
                dr = d_s[t : t + 1, cs]
                dec = jnp.exp2(dr * rate)
                gy = gy_ref[base + t : base + t + 1, cs]
                g = ct[:, t : t + 1] * gy + flow
                flow = dec * g
                if base + t > 0:
                    prev = s_ref[(base + t - 1) * n : (base + t) * n, cs].astype(F32)
                else:
                    prev = sp_ref[:, cs].astype(F32)
                h = flow * prev
                acc = acc + h * dr
                at = slice(t * n, (t + 1) * n)
                b_now = lane_sum(g * u_s[t : t + 1, cs])
                c_now = lane_sum(here * gy)
                if lo:
                    b_now = b_now + b_s[at, :]
                    c_now = c_now + c_s[at, :]
                b_s[at, :] = b_now
                c_s[at, :] = c_now
                here = prev
                g_s[t * n : (t + 1) * n, cs] = g.astype(BF16)
                h_s[t * n : (t + 1) * n, cs] = (h * rate).astype(BF16)
            carry[:, cs] = flow
            dl_ref[:, cs] = acc
        gb = g_s[...]
        gy = gy_ref[base : base + TB, :]
        du = jnp.dot(bw_s[base : base + TB, :], gb, preferred_element_type=F32)
        hr = jnp.dot(ones, h_s[...], preferred_element_type=F32)
        dd = hr * (1.0 / LOG2E) + du * ac
        pg_ref[base : base + TB, :] = (dd * jax.nn.sigmoid(pre_ref[base : base + TB, :])).astype(BF16)
        da_ref[base : base + TB, :] = du * dl + skip_ref[...] * gy
        at = pl.ds(pl.multiple_of((nb - 1 - j) * tblk + base, TB), TB)
        part[m, at, low_n : low_n + n] = gathered(b_s[...])
        part[m, at, low_n + n : low_n + 2 * n] = gathered(c_s[...])

    pg = pg_ref[...]
    part[m, pl.ds(pl.multiple_of((nb - 1 - j) * tblk, tblk), tblk), :low_n] = lax.dot_general(
        pg, stepw_ref[...], nt, preferred_element_type=F32
    )
    stepg_ref[...] += lax.dot_general(
        dbl_ref[:, :low_n].astype(BF16), pg, (((0,), (0,)), ((), ())), preferred_element_type=F32
    )
    sums_ref[0:1, :] += jnp.sum(pg.astype(F32), axis=0, keepdims=True)
    sums_ref[1:2, :] += jnp.sum(gy_ref[...] * act_ref[...].astype(F32), axis=0, keepdims=True)

    @pl.when(j == nb - 1)
    def _():
        group.row_done(r)

    @pl.when((j == nb - 1) & (r == n_dp - 1))
    def _():
        ring.finish(wg_own)
        group.finish()
        dbl_grad_ref[...] = total[...]
        pairs.finish(mixed_own)
        ring_o.stop(2, wo_half)
        save.wait()


def scan_backward(lens, dbl, delta, pre, act, gy, stepw, rate2, skip, states, wg_part, gated, dy_all, wo, n_f, row_len,
                  tblk=64, lanes=512):
    t, ch = delta.shape
    n = rate2.shape[0]
    nb = row_len // tblk
    n_dp = t // row_len
    wide = dbl.shape[1]
    width = wo.shape[1]
    cs = ch // n_f
    spot = lambda r, j: row_at(r, n_dp) * nb + nb - 1 - j
    at = lambda r, j: (spot(r, j), 0)
    zero = lambda r, j: (0, 0)
    entry = lambda r, j: (jnp.maximum(spot(r, j) * tblk - 1, 0), 0)
    return pl.pallas_call(
        functools.partial(bwd_kernel, min(lanes, ch), n_f),
        grid=(n_dp, nb),
        in_specs=[
            pl.BlockSpec(memory_space=pltpu.SMEM),
            pl.BlockSpec((tblk, wide), at),
            pl.BlockSpec((tblk, ch), at),
            pl.BlockSpec((tblk, ch), at),
            pl.BlockSpec((tblk, ch), at),
            pl.BlockSpec((tblk, ch), at),
            pl.BlockSpec(stepw.shape, zero),
            pl.BlockSpec((n, ch), zero),
            pl.BlockSpec((1, ch), zero),
            pl.BlockSpec((tblk * n, ch), at),
            pl.BlockSpec((n, ch), entry),
            pl.BlockSpec(memory_space=pltpu.VMEM),
            pl.BlockSpec(memory_space=pltpu.VMEM),
            pl.BlockSpec(memory_space=pltpu.VMEM),
            pl.BlockSpec(memory_space=pltpu.VMEM),
        ],
        out_specs=[
            pl.BlockSpec((tblk, ch), at),
            pl.BlockSpec((tblk, ch), at),
            pl.BlockSpec((n_dp, row_len, wide), lambda r, j: (0, 0, 0)),
            pl.BlockSpec((n, ch), zero),
            pl.BlockSpec((8, ch), zero),
            pl.BlockSpec(stepw.shape, zero),
            pl.BlockSpec(wg_part.shape[1:], zero),
            pl.BlockSpec(memory_space=pl.ANY),
            pl.BlockSpec((2, cs, width), lambda r, j: (0, 0, 0)),
            pl.BlockSpec((row_len, width), zero),
        ],
        out_shape=[
            jax.ShapeDtypeStruct((t, ch), BF16),
            jax.ShapeDtypeStruct((t, ch), F32),
            jax.ShapeDtypeStruct((n_dp, row_len, wide), F32),
            jax.ShapeDtypeStruct((n, ch), F32),
            jax.ShapeDtypeStruct((8, ch), F32),
            jax.ShapeDtypeStruct(stepw.shape, F32),
            jax.ShapeDtypeStruct(wg_part.shape[1:], BF16),
            jax.ShapeDtypeStruct((n_f, cs, width), BF16),
            jax.ShapeDtypeStruct((2, cs, width), BF16),
            jax.ShapeDtypeStruct((row_len, width), BF16),
        ],
        scratch_shapes=[
            pltpu.VMEM((n, ch), F32),
            pltpu.VMEM((tblk, 1), F32),
            pltpu.VMEM((tblk, TB * n), BF16),
            pltpu.VMEM((tblk // TB, n, TB), F32),
            pltpu.VMEM((2, TB, ch), F32),
            pltpu.VMEM((2, TB, ch), F32),
            pltpu.VMEM((2, TB * n, ch), BF16),
            pltpu.VMEM((2, TB * n, ch), BF16),
            pltpu.VMEM((2, TB * n, 128), F32),
            pltpu.VMEM((2, TB * n, 128), F32),
        ]
        + GroupSum.scratch(row_len, wide)
        + RingReduce.scratch(n_f, wg_part.shape[1:])
        + RingReduce.scratch(n_f, (cs, width), BF16, 2)
        + [pltpu.VMEM((n_f, cs, width), BF16), pltpu.VMEM((n_dp, row_len, width), BF16)]
        + PairReduce.scratch((row_len, width))
        + [pltpu.SemaphoreType.DMA],
        compiler_params=pltpu.CompilerParams(
            collective_id=3, has_side_effects=True, vmem_limit_bytes=60 * 2**20
        ),
        cost_estimate=pl.CostEstimate(flops=t * n * ch * 80, bytes_accessed=t * ch * 60, transcendentals=t * n * ch),
    )(lens, dbl, delta, pre, act, gy, stepw, rate2, skip, states, states, wg_part, gated, dy_all, wo)


class Return:
    def __init__(self, count, n_f, buf, out, local, send, recv):
        self.count, self.n_f, self.buf, self.out = count, n_f, buf, out
        self.local, self.send, self.recv = local, send, recv
        self.me = lax.axis_index("dp") * n_f + lax.axis_index("fsdp")

    def fill(self, pick, values):
        count, pair = self.buf.shape[:2]

        def piece(j, _):
            cols = pl.ds(pl.multiple_of(j * 256, 256), 256)
            moved = jnp.dot(pick, values[:, cols].astype(BF16), preferred_element_type=F32)
            self.buf[:, :, cols] = moved.astype(BF16).reshape(count, pair, 256)
            return 0

        lax.fori_loop(0, values.shape[1] // 256, piece, 0)

    def start(self):
        def one(p, _):
            pltpu.make_async_remote_copy(
                src_ref=self.buf.at[p],
                dst_ref=self.out.at[p],
                send_sem=self.send,
                recv_sem=self.recv,
                device_id=mesh_at(lax.rem(self.me + self.count - p, self.count), self.n_f),
                device_id_type=pl.DeviceIdType.MESH,
            ).start()
            return 0

        pltpu.make_async_copy(self.buf.at[0], self.out.at[0], self.local).start()
        lax.fori_loop(1, self.count, one, 0)

    def finish(self):
        pltpu.make_async_copy(self.buf.at[0], self.out.at[0], self.local).wait()
        rest = pl.ds(1, self.count - 1)
        for sem in (self.recv, self.send):
            pltpu.make_async_copy(self.buf.at[rest], self.out.at[rest], sem).wait()


def leave_kernel(n_f, half, lens_ref, da_ref, conv_ref, xin_ref, act_ref, dblg_ref, sel_ref, taps_ref,
                 sums_ref, dsum_ref, rate_ref, stepg_ref, normed_ref, wx_ref, wg_ref, gg_ref,
                 wo_part, wo_half, wg_own, x_own, dy_own, mixed_own, gain_ref, tags_ref, ride_ref,
                 mix_back, dx_back, gin_all, go_all, small_all,
                 ig_s, wx_s, ng_s, small_s, pick_s, ret_mix, ret_dx, change_s,
                 wo_got, wo_send, wo_recv, wx_got, wx_send, wx_recv, sm_got, sm_send, sm_recv,
                 ng_near, ng_far, ng_send, ng_recv, wo_own, wx_own, sm_own, local, sh_send, sh_recv, ret_sem):
    g = pl.program_id(0)
    steps = pl.num_programs(0)
    n_dp, tok, wide = dblg_ref.shape
    count = n_dp * n_f
    width = x_own.shape[1]
    ch = ig_s.shape[1]
    piece = 256
    n_taps = taps_ref.shape[0]
    down = n_f // 2
    ring_o = RingReduce(n_f, wo_part, wo_got, wo_send, wo_recv, n_f - 1 - down)
    ring_x = RingReduce(n_f, wx_s, wx_got, wx_send, wx_recv, down)
    ring_s = RingReduce(n_f, small_s, sm_got, sm_send, sm_recv, down)
    pairs = [
        PairReduce(ng_s.at[h], ng_near.at[h], ng_far.at[h], ng_send.at[h], ng_recv.at[h]) for h in (0, 1)
    ]
    blocks = width // piece
    turn = half + blocks
    shares = [
        PairShare(mine, out, local.at[i], sh_send.at[i], sh_recv.at[i])
        for i, (mine, out) in enumerate(
            [
                (wg_own, lambda d: gin_all.at[d, :, pl.ds(ch, ch)]),
                (wo_own, lambda d: go_all.at[d]),
                (wx_own, lambda d: gin_all.at[d, :, pl.ds(0, ch)]),
                (sm_own, lambda d: lane_block(small_all, d, sm_own.shape[1])),
            ]
        )
    ]
    ret_m = Return(count, n_f, ret_mix, mix_back, local.at[4], ret_sem.at[0], ret_sem.at[1])
    ret_x = Return(count, n_f, ret_dx, dx_back, local.at[5], ret_sem.at[2], ret_sem.at[3])
    tn = (((0,), (0,)), ((), ()))
    nt = (((1,), (1,)), ((), ()))

    @pl.when(g == 0)
    def _():
        me = lax.axis_index("dp") * n_f + lax.axis_index("fsdp")
        barrier = pltpu.get_barrier_semaphore()

        def greet(p, _):
            pl.semaphore_signal(
                barrier, inc=1, device_id=mesh_at(lax.rem(me + p, count), n_f), device_id_type=pl.DeviceIdType.MESH
            )
            return 0

        lax.fori_loop(1, count, greet, 0)
        pl.semaphore_wait(barrier, count - 1)
        ring_o.resume(2, wo_half)
        shares[0].start()
        spots = jnp.concatenate([tags_ref[...]] * (tok // 128), axis=1)
        lane = lax.broadcasted_iota(jnp.int32, (tok, tok), 1).astype(F32)
        pick_s[...] = jnp.where(spots == lane, 1.0, 0.0).astype(BF16)
        ret_m.fill(pick_s[...], mixed_own)
        ret_mix[:, :, width:] = jnp.broadcast_to(ride_ref[...], (tok, 128)).astype(BF16).reshape(
            count, tok // count, 128
        )
        ret_m.start()

    for e in range(3, ring_o.events):

        @pl.when(g == min(turn + e - 2, steps - 2))
        def _(e=e):
            ring_o.event(e)

    @pl.when(g == turn)
    def _():
        ring_x.start()
        ring_s.start()

    @pl.when(g == turn + blocks // 2)
    def _():
        pairs[0].start()

    @pl.when(g == steps - 2)
    def _():
        pairs[0].middle()
        ring_s.event(1)
        ring_x.event(1)

    @pl.when(g < half)
    def _():
        cols = pl.ds(pl.multiple_of(g * piece, piece), piece)
        zero = jnp.zeros((1, piece), F32)
        misc = [zero] * (n_taps + 1)
        sel_grad = jnp.zeros((wide, piece), F32)
        for m in range(n_dp):
            at = slice(m * tok, (m + 1) * tok)
            low = dblg_ref[m].astype(BF16)
            since, left = segment_span(lens_ref, m, 0, tok)
            act_grad = da_ref[at, :] + jnp.dot(low, sel_ref[...], preferred_element_type=F32)
            conv_grad = act_grad * silu_slope(conv_ref[at, :])
            back = taps_ref[n_taps - 1 : n_taps, :] * conv_grad
            x_in = xin_ref[at, :]
            misc[n_taps - 1] = misc[n_taps - 1] + jnp.sum(conv_grad * x_in, axis=0, keepdims=True)
            for lag in range(1, n_taps):
                tap = n_taps - 1 - lag
                later = pltpu.roll(conv_grad, tok - lag, 0) * (left >= lag).astype(F32)
                back = back + taps_ref[tap : tap + 1, :] * later
                misc[tap] = misc[tap] + jnp.sum(later * x_in, axis=0, keepdims=True)
            ig_s[at, cols] = back.astype(BF16)
            misc[n_taps] = misc[n_taps] + jnp.sum(conv_grad, axis=0, keepdims=True)
            sel_grad = sel_grad + lax.dot_general(low, act_ref[at, :], tn, preferred_element_type=F32)
        rows = jnp.concatenate(
            [
                sel_grad,
                stepg_ref[...],
                dsum_ref[...] * rate_ref[...],
                jnp.concatenate(misc + [sums_ref[0:2, :], zero], axis=0),
                jnp.zeros((small_s.shape[1] - wide - stepg_ref.shape[0] - rate_ref.shape[0] - 8, piece), F32),
            ],
            axis=0,
        )
        cs = small_s.shape[2]
        for i in range(piece // cs):
            small_s[g * (piece // cs) + i] = rows[:, i * cs : (i + 1) * cs]

    @pl.when((g >= half) & (g < turn))
    def _():
        block = g - half
        dcols = wx_s.shape[1]
        grad = lax.dot_general(normed_ref[...], ig_s[...], tn, preferred_element_type=F32).astype(BF16)
        for i in range(piece // dcols):
            wx_s[block * (piece // dcols) + i] = grad[i * dcols : (i + 1) * dcols]

    @pl.when(g >= turn)
    def _():
        grad = lax.dot_general(ig_s[...], wx_ref[...], nt, preferred_element_type=F32)
        grad = grad + lax.dot_general(gg_ref[...], wg_ref[...], nt, preferred_element_type=F32)
        grad = grad.astype(BF16).reshape(n_dp, tok, piece)
        for h in (0, 1):

            @pl.when((g - turn) // (blocks // 2) == h)
            def _(h=h):
                at = (g - turn - h * (blocks // 2)) * piece
                ng_s[h, :, :, pl.ds(pl.multiple_of(at, piece), piece)] = grad

    @pl.when(g == steps - 1)
    def _():
        pairs[1].start()
        shares[0].relay()
        pairs[1].middle()
        ring_o.finish(wo_own, 2)
        shares[1].start()
        ring_s.event(2)
        ring_x.event(2)
        for h in (0, 1):
            pairs[h].finish(change_s.at[:, pl.ds(h * (width // 2), width // 2)])

        def rows(i, _):
            at = pl.ds(pl.multiple_of(i * 16, 16), 16)
            v = x_own[at, :].astype(F32)
            rstd = lax.rsqrt(jnp.mean(v * v, axis=1, keepdims=True) + EPS)
            hat = v * rstd
            grad = change_s[at, :] * gain_ref[...]
            grad = rstd * (grad - hat * jnp.mean(grad * hat, axis=1, keepdims=True))
            change_s[at, :] = dy_own[at, :].astype(F32) + grad
            return 0

        lax.fori_loop(0, tok // 16, rows, 0)
        for e in range(3, ring_x.events):
            ring_s.event(e)
            ring_x.event(e)
        ret_x.fill(pick_s[...], change_s)
        ret_x.start()
        shares[1].relay()
        ring_s.finish(sm_own)
        shares[3].start()
        ring_x.finish(wx_own)
        shares[2].start()
        shares[3].relay()
        shares[2].relay()
        for share in shares:
            share.finish()
        ret_m.finish()
        ret_x.finish()


def leave(lens, da, conv, x_in, act, dbl_grad, sel, taps, sums, decay_sum, rate, stepg, normed, wx, wg, gate_grad,
          wo_part, wo_half, wg_own, x_own, dy_own, mixed_own, gain, tags, ride, n_f):
    n_dp, tok, wide = dbl_grad.shape
    group, ch = act.shape
    width = x_own.shape[1]
    count = n_dp * n_f
    pair = tok // count
    piece = 256
    half = ch // piece
    dcols = width // n_f
    cs = ch // n_f
    n = rate.shape[0]
    tall = -(-(wide + stepg.shape[0] + n + 8) // 64) * 64
    blocks = width // piece
    early = lambda g: (0, jnp.minimum(g, half - 1))
    late = lambda g: (0, jnp.clip(g - half, 0, blocks - 1))
    late_rows = lambda g: (jnp.maximum(g - half - blocks, 0), 0)
    any_ = pl.BlockSpec(memory_space=pl.ANY)
    vmem = pl.BlockSpec(memory_space=pltpu.VMEM)
    block = lambda rows: pl.BlockSpec((rows, piece), early)
    shaped = jax.ShapeDtypeStruct
    return pl.pallas_call(
        functools.partial(leave_kernel, n_f, half),
        grid=(half + 2 * blocks,),
        in_specs=[
            pl.BlockSpec(memory_space=pltpu.SMEM),
            block(group),
            block(group),
            block(group),
            block(group),
            vmem,
            block(wide),
            block(taps.shape[0]),
            block(8),
            block(n),
            block(n),
            block(stepg.shape[0]),
            pl.BlockSpec((group, piece), late),
            pl.BlockSpec((piece, ch), late_rows),
            pl.BlockSpec((piece, ch), late_rows),
        ]
        + [vmem] * 10,
        out_specs=[any_] * 5,
        out_shape=[
            shaped((count, pair, width + 128), BF16),
            shaped((count, pair, width), BF16),
            shaped((n_dp, dcols, 2 * ch), BF16),
            shaped((n_dp, cs, width), BF16),
            shaped(side_by_side(n_dp, tall, cs), F32),
        ],
        scratch_shapes=[
            pltpu.VMEM((group, ch), BF16),
            pltpu.VMEM((n_f, dcols, ch), BF16),
            pltpu.VMEM((2, n_dp, tok, width // 2), BF16),
            pltpu.VMEM((n_f, tall, cs), F32),
            pltpu.VMEM((tok, tok), BF16),
            pltpu.VMEM((count, pair, width + 128), BF16),
            pltpu.VMEM((count, pair, width), BF16),
            pltpu.VMEM((tok, width), F32),
        ]
        + RingReduce.scratch(n_f, (cs, width))
        + RingReduce.scratch(n_f, (dcols, ch))
        + RingReduce.scratch(n_f, (tall, cs), F32)
        + [
            pltpu.VMEM((2, 2, tok, width // 2), BF16),
            pltpu.VMEM((2, tok, width // 2), BF16),
            pltpu.SemaphoreType.DMA((2, 3)),
            pltpu.SemaphoreType.DMA((2, 3)),
            pltpu.VMEM((cs, width), BF16),
            pltpu.VMEM((dcols, ch), BF16),
            pltpu.VMEM((tall, cs), F32),
            pltpu.SemaphoreType.DMA((6,)),
            pltpu.SemaphoreType.DMA((4, 3)),
            pltpu.SemaphoreType.DMA((4, 3)),
            pltpu.SemaphoreType.DMA((4,)),
        ],
        compiler_params=pltpu.CompilerParams(
            collective_id=4, has_side_effects=True, vmem_limit_bytes=62 * 2**20
        ),
        cost_estimate=pl.CostEstimate(flops=2 * 10**10, bytes_accessed=6 * 10**7, transcendentals=10**6),
    )(lens, da, conv, x_in, act, dbl_grad, sel, taps, sums, decay_sum, rate, stepg, normed, wx, wg, gate_grad,
      wo_part, wo_half, wg_own, x_own, dy_own, mixed_own, gain, tags, ride)


def masks_of(count):
    return [1 << b for b in range(count.bit_length() - 1)]


def mesh_at(index, n_f):
    return (index // n_f, lax.rem(index, n_f))


def ring_index(p, n_f):
    if n_f % 2:
        return p
    return jnp.where(p < n_f // 2, 2 * p, 2 * (n_f - 1 - p) + 1)


def ring_place(f, n_f):
    if n_f % 2:
        return f
    return jnp.where(lax.rem(f, 2) == 0, f // 2, n_f - 1 - f // 2)


def pack_kernel(cs, me_d, starts, w_ref, small_refs, gain_ref, blocks):
    small, halves = blocks[0], blocks[1:]
    lanes = pl.ds(pl.multiple_of(me_d * cs, 128), cs)
    sel, step, decay, rest = small_refs[0], small_refs[1], small_refs[2], small_refs[3:]
    at = 0
    for ref in (sel, step, decay):
        small[at : at + ref.shape[0], :] = ref[:, lanes]
        at += ref.shape[0]
    rows = [ref[:, lanes].astype(F32) for ref in rest] + [gain_ref[...].astype(F32)]
    filler = small.shape[0] - at - sum(r.shape[0] for r in rows)
    small[at:, :] = jnp.concatenate(rows + [jnp.zeros((filler, cs), F32)], axis=0).astype(BF16)
    for o, out in enumerate(halves):
        for j, start in enumerate(starts[o]):
            out[:, j * cs : (j + 1) * cs] = w_ref[:, pl.ds(pl.multiple_of(start + me_d * cs, 128), cs)]


def gather_kernel(n_dp, n_f, downs, segs, pack, x_ref, dy_ref, dest_row_ref, dest_ref, lens_ref, *refs):
    streams = len(downs)
    given = len(pack[1]) if pack else streams
    x_all, lens_all, x_own_ref, dy_own_ref, tag_ref, rank_ref, ride_ref = refs[given : given + 7]
    outs = refs[given + 7 : given + 7 + streams]
    (send_x, send_dy, got_x, got_dy, x_own, dy_own, deal_sem, loc_sem, pair_send, pair_recv, ring_send, ring_recv) = (
        refs[given + 7 + streams : given + 19 + streams]
    )
    blocks = refs[given + 19 + streams :] if pack else refs[:streams]
    count = n_dp * n_f
    me_d = lax.axis_index("dp")
    me_f = lax.axis_index("fsdp")
    me = me_d * n_f + me_f
    q = ring_place(me_f, n_f)
    below = ring_index(lax.rem(q + n_f - 1, n_f), n_f)
    above = ring_index(lax.rem(q + 1, n_f), n_f)

    barrier = pltpu.get_barrier_semaphore()

    def greet(p, _):
        pl.semaphore_signal(
            barrier, inc=1, device_id=mesh_at(lax.rem(me + p, count), n_f), device_id_type=pl.DeviceIdType.MESH
        )
        return 0

    lax.fori_loop(1, count, greet, 0)
    if pack:
        pack_kernel(pack[0], me_d, pack[2], refs[0], refs[1 : given - 1], refs[given - 1], blocks)

    def place_of(s, index):
        return lane_block(outs[s], index, blocks[s].shape[1]) if s == 0 else outs[s].at[index]

    locals_ = [
        pltpu.make_async_copy(blocks[s], place_of(s, me_f), loc_sem.at[s]) for s in range(streams)
    ]
    for c in locals_:
        c.start()
    pl.semaphore_wait(barrier, count - 1)

    def deal(a):
        src, dst = ((send_x, got_x), (send_dy, got_dy))[a]

        def one(p, _):
            pltpu.make_async_remote_copy(
                src_ref=src.at[p],
                dst_ref=dst.at[p],
                send_sem=deal_sem.at[a, 0],
                recv_sem=deal_sem.at[a, 1],
                device_id=mesh_at(lax.rem(me + p, count), n_f),
                device_id_type=pl.DeviceIdType.MESH,
            ).start()
            return 0

        lax.fori_loop(1, count, one, 0)
        dst[0] = src[0]

    def dealt(a, way):
        src, dst = ((send_x, got_x), (send_dy, got_dy))[a]
        rest = pl.ds(1, count - 1)
        pltpu.make_async_copy(src.at[rest], dst.at[rest], deal_sem.at[a, way]).wait()

    def hop(s, h, up):
        k = lax.rem(q + (n_f - h if up else h), n_f)
        index = ring_index(k, n_f)
        src = blocks[s] if h == 0 else place_of(s, index)
        return pltpu.make_async_remote_copy(
            src_ref=src,
            dst_ref=place_of(s, index),
            send_sem=ring_send.at[s, int(up), h],
            recv_sem=ring_recv.at[s, int(up), h],
            device_id=(me_d, above if up else below),
            device_id_type=pl.DeviceIdType.MESH,
        )

    hops = [[downs[s], n_f - 1 - downs[s]] for s in range(streams)]
    for s in range(streams):
        for up in (0, 1):
            if hops[s][up]:
                hop(s, 0, up).start()
    tok, width = x_own.shape
    pair = got_x.shape[1]

    dest_row = dest_row_ref[...]
    abs_row = jnp.floor((dest_row + 0.5) * (1.0 / tok))
    in_row = dest_row - abs_row * tok
    rel_row = abs_row - me.astype(F32)
    rel_row = jnp.where(rel_row < 0.0, rel_row + count, rel_row)
    rank = jnp.sum((dest_ref[...] < dest_row).astype(F32), axis=0, keepdims=True)
    goal = rel_row * pair + rank - abs_row * pair
    rank_ref[...] = jnp.broadcast_to(goal, rank_ref.shape)
    chosen = lax.broadcasted_iota(jnp.int32, (tok, tok), 0).astype(F32) == goal
    spot = jnp.sum(jnp.where(chosen, in_row, 0.0), axis=1, keepdims=True)
    send_x[:, :, width:] = jnp.broadcast_to(spot, (tok, 128)).astype(BF16).reshape(count, pair, 128)
    pick = jnp.where(chosen, 1.0, 0.0).astype(BF16)

    def sort(values, out):
        def part(j, _):
            cols = pl.ds(pl.multiple_of(j * 256, 256), 256)
            moved = jnp.dot(pick, values[:, cols], preferred_element_type=F32)
            out[:, :, cols] = moved.astype(BF16).reshape(count, pair, 256)
            return 0

        lax.fori_loop(0, width // 256, part, 0)

    sort(x_ref, send_x)
    deal(0)
    sort(dy_ref, send_dy)
    deal(1)

    def advance(h):
        for s in range(streams):
            for up in (0, 1):
                if h < hops[s][up]:
                    hop(s, h - 1, up).wait_recv()
                    hop(s, h, up).start()

    advance(1)
    dealt(0, 1)
    tag = got_x[:, :, width : width + 128].astype(F32).reshape(tok, 128)
    spots = jnp.concatenate([tag] * (tok // 128), axis=1)
    lane = lax.broadcasted_iota(jnp.int32, (tok, tok), 1).astype(F32)
    settle = jnp.where(spots == lane, 1.0, 0.0).astype(BF16)
    tn = (((0,), (0,)), ((), ()))
    tag_ref[...] = tag

    def place(values, out):
        def part(j, _):
            cols = pl.ds(pl.multiple_of(j * 256, 256), 256)
            block = values[:, :, cols].reshape(tok, 256)
            out[:, cols] = lax.dot_general(settle, block, tn, preferred_element_type=F32).astype(BF16)
            return 0

        lax.fori_loop(0, width // 256, part, 0)

    masks = list(reversed(masks_of(n_dp)))

    def partner(mask):
        return me_d + mask - 2 * mask * lax.rem(me_d // mask, 2)

    def share(a, m, mask):
        out = (x_all, lens_all)[a]
        own_block = (x_own, lens_ref)[a]
        return pltpu.make_async_remote_copy(
            src_ref=own_block if m == 0 else out.at[m],
            dst_ref=out.at[m | mask],
            send_sem=pair_send.at[a, m | mask],
            recv_sem=pair_recv.at[a, m | mask],
            device_id=(partner(mask), me_f),
            device_id_type=pl.DeviceIdType.MESH,
        )

    copies = []

    def keep(src, dst):
        c = pltpu.make_async_copy(src, dst, loc_sem.at[streams + len(copies)])
        c.start()
        copies.append(c)

    place(got_x, x_own)
    for a in (0, 1):
        for mask in masks:
            share(a, 0, mask).start()
    keep(lens_ref, lens_all.at[0])
    keep(x_own, x_all.at[0])
    keep(x_own, x_own_ref)

    lane = lax.broadcasted_iota(jnp.int32, (1, 128), 1)
    limit = jnp.sum(jnp.where(lane < segs - 1, lens_ref[0:1, :], 0).astype(F32), axis=1, keepdims=True)

    def squares(i, total_):
        v = x_own[pl.ds(pl.multiple_of(i * 32, 32), 32), :].astype(F32)
        t = (lax.broadcasted_iota(jnp.int32, (32, 1), 0) + i * 32).astype(F32)
        each = jnp.sum(v * v, axis=1, keepdims=True)
        return total_ + jnp.sum(jnp.where(t < limit, each, 0.0), axis=0, keepdims=True)

    ride = jnp.zeros((1, 128), F32)
    for j, value in enumerate((lax.fori_loop(0, tok // 32, squares, jnp.zeros((1, 1), F32)), limit)):
        high = value.astype(BF16).astype(F32)
        ride = ride + jnp.where(lane == 2 * j, high, 0.0) + jnp.where(lane == 2 * j + 1, value - high, 0.0)
    ride_ref[...] = jnp.broadcast_to(ride, ride_ref.shape)

    def relay(a):
        held = [0]
        for step, mask in enumerate(masks):
            for m in held:
                if m:
                    share(a, m, mask).start()
            for m in held:
                share(a, m, mask).wait_recv()
            held = held + [m | mask for m in held]

    most = max(max(h) for h in hops)
    for h in range(2, most):
        advance(h)
        if h == 2:
            dealt(1, 1)
            place(got_dy, dy_own)
            keep(dy_own, dy_own_ref)
    if most <= 2:
        dealt(1, 1)
        place(got_dy, dy_own)
        keep(dy_own, dy_own_ref)
    relay(0)
    relay(1)
    for s in range(streams):
        for up in (0, 1):
            if hops[s][up]:
                hop(s, hops[s][up] - 1, up).wait_recv()
    for s in range(streams):
        for up in (0, 1):
            for h in range(hops[s][up]):
                hop(s, h, up).wait_send()
    for a in (0, 1):
        held = [0]
        for mask in masks:
            for m in held:
                share(a, m, mask).wait_send()
            held = held + [m | mask for m in held]
    for c in locals_ + copies:
        c.wait()
    dealt(0, 0)
    dealt(1, 0)


def gather_all(x, dy, dest, lens, segs, blocks, pack, downs, n_dp, n_f):
    streams = len(blocks)
    tok, width = x.shape
    count = n_dp * n_f
    sent_x = (count, tok // count, width + 128)
    sent_dy = (count, tok // count, width)
    hops = max(max(d, n_f - 1 - d) for d in downs)
    any_ = pl.BlockSpec(memory_space=pl.ANY)
    vmem = pl.BlockSpec(memory_space=pltpu.VMEM)
    row = jax.ShapeDtypeStruct((tok, width), BF16)
    rows = jax.ShapeDtypeStruct((n_dp, tok, width), BF16)
    return pl.pallas_call(
        functools.partial(gather_kernel, n_dp, n_f, downs, segs, pack and (pack[0], [None] * len(pack[1]), pack[2])),
        in_specs=[vmem] * 5 + ([vmem] * len(pack[1]) if pack else [any_] * streams),
        out_specs=[any_] * 4 + [vmem] * 3 + [any_] * streams,
        out_shape=[
            rows,
            jax.ShapeDtypeStruct((n_dp,) + lens.shape, lens.dtype),
            row,
            row,
            jax.ShapeDtypeStruct((tok, 128), F32),
            jax.ShapeDtypeStruct((8, tok), F32),
            jax.ShapeDtypeStruct((8, 128), F32),
        ]
        + [jax.ShapeDtypeStruct(side_by_side(n_f, *blocks[0].shape), BF16)]
        + [jax.ShapeDtypeStruct((n_f,) + b.shape, b.dtype) for b in blocks[1:]],
        scratch_shapes=[
            pltpu.VMEM(sent_x, BF16),
            pltpu.VMEM(sent_dy, BF16),
            pltpu.VMEM(sent_x, BF16),
            pltpu.VMEM(sent_dy, BF16),
            pltpu.VMEM((tok, width), BF16),
            pltpu.VMEM((tok, width), BF16),
            pltpu.SemaphoreType.DMA((2, 2)),
            pltpu.SemaphoreType.DMA((streams + 4,)),
            pltpu.SemaphoreType.DMA((2, n_dp)),
            pltpu.SemaphoreType.DMA((2, n_dp)),
            pltpu.SemaphoreType.DMA((streams, 2, hops)),
            pltpu.SemaphoreType.DMA((streams, 2, hops)),
        ]
        + ([pltpu.VMEM(b.shape, BF16) for b in blocks] if pack else []),
        compiler_params=pltpu.CompilerParams(
            collective_id=0, has_side_effects=True, vmem_limit_bytes=40 * 2**20
        ),
        cost_estimate=pl.CostEstimate(flops=10**10, bytes_accessed=2 * 10**8, transcendentals=0),
    )(x, dy, dest[None, :], dest[:, None], lens, *(pack[1] if pack else blocks))


def spread_kernel(cs, width, x_ref, w_ref, go_ref, small_ref, ride_ref, out_ref, sum_ref, go_out, rms_ref, *small_outs):
    total = jnp.zeros(sum_ref.shape, F32)
    n_dp = x_ref.shape[0]
    for f in range(x_ref.shape[2] // cs):
        for i in range(n_dp):
            part = x_ref[i, :, f * cs : (f + 1) * cs].astype(F32)
            cols = slice((f * n_dp + i) * cs, (f * n_dp + i + 1) * cs)
            out_ref[:, cols] = part
            product = part * w_ref[:, cols].astype(F32)
            for j in range(0, cs, 128):
                total = total + product[:, j : j + 128]
    go_out[...] = go_ref[...].astype(F32)

    @pl.when(pl.program_id(0) == 0)
    def _():
        sum_ref[...] = jnp.zeros_like(sum_ref)
        sums = jnp.sum(ride_ref[...].astype(F32), axis=0, keepdims=True)
        lane = lax.broadcasted_iota(jnp.int32, sums.shape, 1)
        squares = jnp.sum(jnp.where(lane < 2, sums, 0.0), axis=1, keepdims=True)
        count = jnp.sum(jnp.where((lane >= 2) & (lane < 4), sums, 0.0), axis=1, keepdims=True)
        rms_ref[...] = jnp.broadcast_to(jnp.sqrt(squares / (count * width)), rms_ref.shape)
        at = 0
        for out in small_outs:
            out[...] = small_ref[at : at + out.shape[0], :]
            at += out.shape[0]

    sum_ref[...] += total


def spread_columns(parts, w, go, small, heights, ride, width, cs):
    n_dp, height, cols = parts.shape
    if cs % 128:
        out = parts.reshape(n_dp, height, cols // cs, cs).transpose(1, 2, 0, 3).reshape(height, n_dp * cols).astype(F32)
        cuts = [small[sum(heights[:i]) : sum(heights[: i + 1])] for i in range(len(heights))]
        totals = jnp.sum(ride.astype(F32), axis=0)
        rms = jnp.sqrt((totals[0] + totals[1]) / ((totals[2] + totals[3]) * width))
        return out, jnp.sum(out * w.astype(F32), axis=1), go.astype(F32), rms, cuts
    wide = 2 * cs
    steps = cols // wide
    once = lambda f: (0, 0)
    go_block = (go.shape[0] // steps, go.shape[1])
    shaped = jax.ShapeDtypeStruct
    out, sums, go, rms, *cuts = pl.pallas_call(
        functools.partial(spread_kernel, cs, width),
        grid=(steps,),
        in_specs=[
            pl.BlockSpec((n_dp, height, wide), lambda f: (0, 0, f)),
            pl.BlockSpec((height, n_dp * wide), lambda f: (0, f)),
            pl.BlockSpec(go_block, lambda f: (f, 0)),
            pl.BlockSpec(small.shape, once),
            pl.BlockSpec(ride.shape, once),
        ],
        out_specs=[
            pl.BlockSpec((height, n_dp * wide), lambda f: (0, f)),
            pl.BlockSpec((height, 128), once),
            pl.BlockSpec(go_block, lambda f: (f, 0)),
            pl.BlockSpec((8, 128), once),
        ]
        + [pl.BlockSpec((h, small.shape[1]), once) for h in heights],
        out_shape=[shaped((height, n_dp * cols), F32), shaped((height, 128), F32), shaped(go.shape, F32)]
        + [shaped((8, 128), F32)]
        + [shaped((h, small.shape[1]), F32) for h in heights],
        compiler_params=pltpu.CompilerParams(vmem_limit_bytes=32 * 2**20),
        cost_estimate=pl.CostEstimate(flops=4 * height * cols * n_dp, bytes_accessed=8 * height * cols * n_dp, transcendentals=0),
    )(parts, w, go, small, ride)
    return out, jnp.sum(sums, axis=1), go, rms[0, 0], cuts


def per_device(
    tokens,
    cotangent,
    destination,
    lengths,
    norm_gain,
    in_weight,
    conv_weight,
    conv_bias,
    select_weight,
    step_weight,
    step_bias,
    decay_log,
    skip_gain,
    out_weight,
):
    n_dp = lax.axis_size("dp")
    n_f = lax.axis_size("fsdp")
    rows = n_dp * n_f
    tok = tokens.shape[0]
    width = tokens.shape[1]
    pair = tok // rows
    inner = conv_bias.shape[0] * n_f
    cs = conv_bias.shape[0] // n_dp
    ch = cs * n_f
    taps = conv_weight.shape[0]
    n = decay_log.shape[0]
    rank_of = step_weight.shape[0]
    dcols = width // n_f
    group = n_dp * tok
    both = ("dp", "fsdp")
    me_d = lax.axis_index("dp")
    me_f = lax.axis_index("fsdp")
    flat_dot = lambda a, b: jnp.dot(a, b, preferred_element_type=F32)
    nt_dot = lambda a, b: lax.dot_general(a, b, (((1,), (1,)), ((), ())), preferred_element_type=F32)
    tn_dot = lambda a, b: lax.dot_general(a, b, (((0,), (0,)), ((), ())), preferred_element_type=F32)

    segs = lengths.shape[1]
    lens_tile = jnp.pad(lengths, ((0, 7), (0, 128 - segs)))
    slots = jnp.arange(tok, dtype=jnp.int32)

    flat = lambda shard: shard.reshape(-1, n_dp * cs)
    smalls = [
        flat(v) for v in (select_weight, step_weight, decay_log, conv_weight, conv_bias, step_bias, skip_gain)
    ]
    gain_rows = dcols // cs
    gain_block = norm_gain.reshape(gain_rows, cs)
    used = sum(v.shape[0] for v in smalls) + gain_rows
    tall = used + -used % 16
    starts = [[h * inner + f * n_dp * cs for f in range(n_f)] for h in (0, 1)]
    if cs % 128:
        mine = lambda value, at: lax.dynamic_slice_in_dim(value, at + me_d * cs, cs, 1)
        blocks = [
            jnp.concatenate(
                [mine(v, 0) for v in smalls] + [gain_block, jnp.zeros((tall - used, cs), BF16)], axis=0
            )
        ] + [jnp.concatenate([mine(in_weight, at) for at in half], axis=1) for half in starts]
        pack = None
    else:
        blocks = [jax.ShapeDtypeStruct((tall, cs), BF16)] + [jax.ShapeDtypeStruct((dcols, ch), BF16)] * 2
        pack = (cs, [in_weight] + smalls + [gain_block], starts)
    wo_block = lax.dynamic_slice_in_dim(out_weight, me_d * cs, cs, 0)
    x_all, lens_all, x_own, dy_own, x_tags, ranks, ride, small_all, wx, wg = gather_all(
        tokens, cotangent, destination.astype(F32), lens_tile, segs, blocks, pack,
        [n_f // 2, n_f // 2, n_f - 1 - n_f // 2], n_dp, n_f,
    )
    x_all = x_all.reshape(group, width)
    lens = lens_all[:, 0, :segs]
    from_send = (ranks[0].astype(jnp.int32)[:, None] == slots[None, :]).astype(BF16)
    wx = wx.reshape(width, ch)
    wg = wg.reshape(width, ch)
    small = joined(small_all)
    at = select_weight.shape[0]
    sel = small[:at]
    stepw = small[at : at + rank_of]
    dlog = small[at + rank_of : at + rank_of + n]
    misc = small[at + rank_of + n :]
    conv_w, conv_b, step_b, skip = misc[:taps], misc[taps : taps + 1], misc[taps + 1 : taps + 2], misc[taps + 2 : taps + 3]
    gain = misc[taps + 3 : taps + 3 + gain_rows]
    gain = gain.reshape(gain_rows, n_f, cs).transpose(1, 0, 2).reshape(width).astype(F32)
    conv_w = conv_w.astype(F32)
    skip = skip.astype(F32)
    rate = -jnp.exp(dlog.astype(F32))

    normed, x_in, conv, act, gate, dbl, wo_next = enter(
        lens, x_all, gain[None], wx, wg, conv_w, conv_b.astype(F32), sel, wo_block, n_f
    )
    dbl = dbl.reshape(group, -1)
    rate2 = rate * LOG2E
    scan_out, states, delta, pre, wo, dy_all = scan_forward(
        lens, dbl, act, stepw, step_b.astype(F32), rate2, skip, wo_block, wo_next, dy_own, n_f, tok
    )
    dy_all = dy_all.reshape(group, width)
    wo = wo.reshape(ch, width)
    gate_silu = jax.nn.silu(gate)
    gated = (scan_out * gate_silu).astype(BF16)

    gated_grad = nt_dot(dy_all, wo)
    scan_grad = gated_grad * gate_silu
    gate_grad = (gated_grad * scan_out * silu_slope(gate)).astype(BF16)
    wg_grad = tn_dot(normed, gate_grad).astype(BF16)
    pre_grad, act_grad, dbl_grad, decay_sum, sums, step_grad, wg_own, wo_grad, wo_half, mixed = scan_backward(
        lens, dbl, delta, pre, act, scan_grad, stepw, rate2, skip, states,
        wg_grad.reshape(n_f, dcols, ch), gated, dy_all, wo, n_f, tok,
    )
    mix_back, dx_back, gin_all, go_all, small_full = leave(
        lens, act_grad, conv, x_in, act, dbl_grad, sel, conv_w, sums, decay_sum, rate, step_grad, normed, wx, wg,
        gate_grad, wo_grad, wo_half, wg_own, x_own, dy_own, mixed, gain[None], x_tags, ride[:1], n_f,
    )

    grad_in_weight, gain_sum, grad_out_weight, input_rms, cuts = spread_columns(
        gin_all, in_weight, go_all.reshape(n_dp * cs, width), joined(small_full),
        [select_weight.shape[0], rank_of, n, 8], mix_back[:, 0, width:], width, cs,
    )
    grad_select, grad_step, grad_decay, misc = cuts
    grad_norm_gain = gain_sum / norm_gain.astype(F32)

    back = mix_back.reshape(tok, width + 128)
    mixer_output = flat_dot(from_send, back[:, :width])
    layer_output = (tokens.astype(F32) + mixer_output).astype(BF16)
    mixer_output = mixer_output.astype(BF16)
    input_grad = flat_dot(from_send, dx_back.reshape(tok, width)).astype(BF16)
    return (
        layer_output,
        mixer_output,
        input_grad,
        input_rms,
        grad_norm_gain,
        grad_in_weight,
        misc[:taps],
        misc[taps],
        grad_select,
        grad_step,
        misc[taps + 1],
        grad_decay,
        misc[taps + 2],
        grad_out_weight,
    )


def solution(mesh):
    return jax.shard_map(
        per_device,
        mesh=mesh,
        in_specs=(
            P(("dp", "fsdp"), None),
            P(("dp", "fsdp"), None),
            P(("dp", "fsdp")),
            P(("dp", "fsdp"), None),
            P("fsdp"),
            P("fsdp", None),
            P(None, "fsdp"),
            P("fsdp"),
            P(None, "fsdp"),
            P(None, "fsdp"),
            P("fsdp"),
            P(None, "fsdp"),
            P("fsdp"),
            P("fsdp", None),
        ),
        out_specs=(
            P(("dp", "fsdp"), None),
            P(("dp", "fsdp"), None),
            P(("dp", "fsdp"), None),
            P(),
            P("fsdp"),
            P("fsdp", None),
            P(None, "fsdp"),
            P("fsdp"),
            P(None, "fsdp"),
            P(None, "fsdp"),
            P("fsdp"),
            P(None, "fsdp"),
            P("fsdp"),
            P("fsdp", None),
        ),
        check_vma=False,
    )
```
